32 devices in a mesh: maps: 2 (over y), row: 4 (over x, core), col: 4 (over z).
Axes of the slice: x: 2, y: 2, z: 4, core: 2. Of those that a mesh axis runs over, the one named last changes fastest.
Arguments:
- positions: float32 [512, 2, 384], P(('maps', 'row', 'col')), parts along dimension 0, may hold values from 0 to 127
- destination: int32 [512, 1], P(('maps', 'row', 'col')), parts along dimension 0, may hold values from 0 to 15; in each aligned block of 16 rows (0 to 15, 16 to 31, ...) at most 4 rows name the same one
- profile: float32 [65, 65], replicated, may hold values from 0.03 to 1
Outputs:
- magnification: float32 [1024, 512], P(('maps', 'row'), 'col'), parts along dimension 0
The draws below stay inside these ranges and needn't reach their ends.
There are 2 independent parts, one for each index of `maps`. The reference program is written for one: setup_inputs(seed, part) draws one part's arguments, and reference() takes and returns one part's arrays. A program takes and returns all parts, laid end to end along the dimension named above; an argument that names none is the same for every part. Nothing has to cross between parts.
Inputs may be any that keep to these rules, and one draw needn't show every extreme that they name: `destination`: at most 4 of the blocks of one device name one tile.
All inputs are finite; a program needn't handle non-finite values.
Results may differ from the reference program's by a relative error of at most 0.0003.
Values may be sent and summed in bfloat16 or wider, within the bound.
No kernel may reach another device: no remote copies, remote signals or barrier semaphores. Data moves between devices by JAX's collectives and lax.ppermute only.
A program may use at most 64 MiB of HBM per device.

```python
import math
import jax
import jax.numpy as jnp
import numpy as np
from jax import lax

TILE = 128
HALO = 32
DISC = 65
MOST = 4
R = 384
TCOLS = 4
TILES = 16
BLK_DEV = 16
BLOCKS = 256
NR = 512
NC = 512


def draw_positions(key, part):
    subkeys = jax.random.split(key, 3)
    low_log = 0.0
    spread = jnp.exp(jax.random.uniform(subkeys[0], (BLOCKS, 1, 1), jnp.float32, low_log, math.log(TILE - 1.0)))
    center = 0.5 * spread + jax.random.uniform(subkeys[1], (BLOCKS, 2, 1), jnp.float32) * (TILE - 1.0 - spread)
    offset = jax.random.uniform(subkeys[2], (BLOCKS, 2, R), jnp.float32) - 0.5
    return jnp.clip(center + spread * offset, 0.0, TILE - 1.0).astype(jnp.float32)


def deal_out(stream_key, own, number, rows, count, top, reach, lean):
    ranking = jax.random.permutation(stream_key, count)
    crowded, ordinary = portions_of(count, rows * top, reach, lean, True), portions_of(count, rows * top, reach, lean, False)
    places = jnp.arange(count)

    def named(lengths, turn):
        used = int((lengths > 0).sum())
        fixed = max(1, used // 4)
        moved = fixed + (places - fixed + turn * (used - fixed)) % max(1, count - fixed)
        return jnp.zeros((count,), jnp.int32).at[ranking[jnp.where(places < fixed, places, moved)]].set(jnp.asarray(lengths, jnp.int32))

    lengths = jnp.where(number % 4 == 0, named(crowded, number // 4), named(ordinary, number - number // 4 - 1))
    mixed = jax.random.permutation(jax.random.fold_in(own, 3), count)
    source_of, sink = mixed[0:count // 2 * 2:2], mixed[1:count // 2 * 2:2]
    slack = jnp.minimum(lengths[source_of] - 1, reach - lengths[sink]) // 2
    slack = jnp.where((source_of == ranking[0]) | (sink == ranking[0]) | (lengths[sink] == 0), 0, jnp.maximum(slack, 0))
    moved = jax.random.randint(jax.random.fold_in(own, 4), (count // 2,), 0, 1 << 20) % (slack + 1)
    lengths = lengths.at[source_of].add(-moved).at[sink].add(moved)
    items = jnp.searchsorted(jnp.cumsum(lengths), jnp.arange(rows * top), side="right").astype(jnp.int32)
    table = items.reshape(top, rows).T
    table = table[jax.random.permutation(jax.random.fold_in(own, 1), rows)]
    turn = jax.random.randint(jax.random.fold_in(own, 2), (rows, 1), 0, top)
    return jnp.take_along_axis(table, (jnp.arange(top)[None, :] + turn) % top, axis=1)


def portions_of(count, total, limit, slope, full):
    weights = [(1 << 20) // math.isqrt(rank ** slope) + 1 for rank in range(1, count + 1)]
    largest = limit if full else min(limit, max(-(-total // count), total * weights[0] // sum(weights)))
    least = 1 if total - largest >= count - 1 else 0
    given, spare = [largest] + [least] * (count - 1), total - largest - least * (count - 1)
    while spare > 0:
        movable = [i for i in range(1, count) if given[i] < largest] or [i for i in range(1, count) if given[i] < limit]
        pool, budget = sum([weights[i] for i in movable]), spare
        for i in movable:
            addition = min(limit - given[i], max(1, budget * weights[i] // pool), spare)
            given[i] = given[i] + addition
            spare = spare - addition
    return np.array(given)


def setup_inputs(seed: int = 0, part: int = 0) -> dict:
    keys = jax.random.split(jax.random.key(seed), 4)
    part_splits = jax.random.split(jax.random.fold_in(keys[3], part), 4)
    positions = draw_positions(jax.random.fold_in(jax.random.fold_in(keys[3], part), 71), part)
    destination_keys = jax.random.split(jax.random.fold_in(part_splits[1], 1), BLOCKS // BLK_DEV)
    destination_turns = jax.random.permutation(jax.random.fold_in(part_splits[1], 3), BLOCKS // BLK_DEV)
    destination = jax.vmap(lambda own, number: deal_out(jax.random.fold_in(part_splits[1], 2), own, number, BLK_DEV, TILES, 1, MOST, 1))(destination_keys, destination_turns).reshape((BLOCKS, 1))
    profile = jnp.clip(jnp.exp(jax.random.uniform(keys[2], (DISC, DISC), jnp.float32, math.log(0.03), math.log(1.0))), 0.03, 1.0)
    return dict(positions=positions, destination=destination, profile=profile)


def to_half(values):
    return lax.optimization_barrier(values.astype(jnp.bfloat16)).astype(jnp.float32)


def reference(positions, destination, profile):
    targets = destination[:, 0].astype(jnp.int32)
    base_row = (targets // TCOLS) * TILE
    base_col = (targets % TCOLS) * TILE
    first = positions[:, 0, :].astype(jnp.float32)
    second = positions[:, 1, :].astype(jnp.float32)
    low_first = jnp.floor(first)
    low_second = jnp.floor(second)
    total = jnp.zeros((NR * NC,), jnp.float32)
    for step_row in (0, 1):
        cell_row = low_first + float(step_row)
        hat_row = to_half(jnp.maximum(0.0, 1.0 - jnp.abs(first - cell_row)))
        row_index = jnp.minimum(cell_row.astype(jnp.int32), TILE - 1)
        row_inside = cell_row < TILE
        for step_col in (0, 1):
            cell_col = low_second + float(step_col)
            hat_col = to_half(jnp.maximum(0.0, 1.0 - jnp.abs(second - cell_col)))
            col_index = jnp.minimum(cell_col.astype(jnp.int32), TILE - 1)
            col_inside = cell_col < TILE
            weight = jnp.where(row_inside & col_inside, hat_row * hat_col, 0.0)
            flat = (base_row[:, None] + row_index) * NC + base_col[:, None] + col_index
            total = total.at[flat.reshape(-1).astype(jnp.int32)].add(weight.reshape(-1))
    source_map = to_half(total.reshape(NR, NC))
    span = jnp.arange(DISC).astype(jnp.float32) - HALO
    inside = (span[:, None] ** 2 + span[None, :] ** 2 <= HALO * HALO).astype(jnp.float32)
    weights = profile * inside
    kernel = to_half(weights / jnp.sum(weights))
    convolved = lax.conv_general_dilated(source_map[None, None], kernel[None, None], (1, 1), ((HALO, HALO), (HALO, HALO)), precision=lax.Precision.HIGHEST)[0, 0]
    return convolved / (BLK_DEV * R / (TILE * TILE))
```

```python
import jax
import jax.numpy as jnp
from jax import lax
from jax.sharding import PartitionSpec as P

TILE = 128
HALO = 32
MOST = 4


group_size = 16


def extended_2(cells, sides, width):
    for axis, dim in sides:
        count = lax.axis_size(axis)
        ends = count - 1
        head = lax.slice_in_dim(cells, 0, width, axis=dim)
        tail = lax.slice_in_dim(cells, cells.shape[dim] - width, cells.shape[dim], axis=dim)
        cells = jnp.concatenate(
            [
                lax.ppermute(tail, axis, [(i, (i + 1) % count) for i in range(ends)]),
                cells,
                lax.ppermute(head, axis, [((i + 1) % count, i) for i in range(ends)]),
            ],
            axis=dim,
        )
    return cells


def hat_table(coords, extent):
    cellular = jnp.arange(extent, dtype=jnp.float32)
    return jnp.maximum(0.0, 1.0 - jnp.abs(coords[:, None] - cellular[None, :])).astype(jnp.bfloat16)


def local_ranks(labels, extent):
    onehot = (labels[:, None] == jnp.arange(extent, dtype=jnp.int32)[None, :]).astype(jnp.int32)
    before = jnp.cumsum(onehot, axis=0) - onehot
    return jnp.sum(before * onehot, axis=1)


def deposit(received, recv_labels, wanted, extent):
    slot_count = recv_labels.shape[0]
    ray_count = received.shape[2]
    padded = jnp.concatenate([received, jnp.full((1, 2, ray_count), -2.0, jnp.float32)], axis=0)
    ordering = jnp.argsort((recv_labels != wanted).astype(jnp.int32), stable=True)
    ordering = jnp.concatenate([ordering, jnp.full((group_size,), slot_count, jnp.int32)])
    valid_count = jnp.sum((recv_labels == wanted).astype(jnp.int32))
    group_count = (valid_count + group_size - 1) // group_size

    def add_group(group_idx, group_total):
        picked = lax.dynamic_slice_in_dim(ordering, group_idx * group_size, group_size)
        within = group_idx * group_size + jnp.arange(group_size, dtype=jnp.int32) < valid_count
        picked = jnp.where(within, picked, slot_count)
        chosen = padded[picked]
        first_hat = hat_table(chosen[:, 0, :].reshape(-1), extent)
        second_hat = hat_table(chosen[:, 1, :].reshape(-1), extent)
        return group_total + lax.dot_general(
            first_hat, second_hat, (((0,), (0,)), ((), ())), preferred_element_type=jnp.float32
        )

    return lax.fori_loop(0, group_count, add_group, jnp.zeros((extent, extent), jnp.float32))


def shards(positions, destination, profile):
    row_count = lax.axis_size("row")
    col_count = lax.axis_size("col")
    tile_count = row_count * col_count
    block_count = positions.shape[0]
    ray_count = positions.shape[2]
    targets = destination[:, 0]
    if block_count <= 9 * MOST:
        received = lax.all_gather(positions, ("row", "col"), axis=0, tiled=True)
        recv_labels = lax.all_gather(targets, ("row", "col"), axis=0, tiled=True)
        wanted = lax.axis_index(("row", "col"))
    else:
        placed = targets * MOST + local_ranks(targets, tile_count)
        outgoing = (
            jnp.full((tile_count * MOST, 2, ray_count), -2.0, jnp.float32).at[placed].set(positions)
        )
        received = lax.all_to_all(
            outgoing.reshape(tile_count, MOST, 2, ray_count),
            ("row", "col"),
            split_axis=0,
            concat_axis=0,
            tiled=True,
        )
        received = received.reshape(tile_count * MOST, 2, ray_count)
        recv_labels = jnp.where(received[:, 0, 0] < -1.0, 1, 0)
        wanted = 0
    tile_sum = deposit(received, recv_labels, wanted, TILE)
    source_map = tile_sum.astype(jnp.bfloat16)
    extended = extended_2(source_map, (("row", 0), ("col", 1)), HALO)
    disc_side = 2 * HALO + 1
    span = jnp.arange(disc_side).astype(jnp.float32) - HALO
    inside = (span[:, None] ** 2 + span[None, :] ** 2 <= HALO * HALO).astype(jnp.float32)
    weights = profile * inside
    kernel = (weights / jnp.sum(weights)).astype(jnp.bfloat16)
    extent_wide = TILE + 2 * HALO
    lagged = (
        jnp.arange(extent_wide, dtype=jnp.int32)[:, None]
        - jnp.arange(TILE, dtype=jnp.int32)[None, :]
    )
    onehot = (lagged[None, :, :] == jnp.arange(disc_side, dtype=jnp.int32)[:, None, None]).astype(
        jnp.bfloat16
    )
    toeplitz = jnp.einsum("ab,bqj->qaj", kernel, onehot, preferred_element_type=jnp.float32).astype(
        jnp.bfloat16
    )
    lagged_sums = jnp.dot(
        extended,
        toeplitz.reshape(extent_wide, disc_side * TILE),
        preferred_element_type=jnp.float32,
    )
    stacked = lagged_sums.reshape(extent_wide * disc_side, TILE)
    column_index = jnp.arange(extent_wide * disc_side, dtype=jnp.int32)
    wide_row = column_index // disc_side
    disc_row = column_index % disc_side
    selector = (
        wide_row[None, :] == jnp.arange(TILE, dtype=jnp.int32)[:, None] + disc_row[None, :]
    ).astype(jnp.float32)
    convolved = jnp.dot(
        selector, stacked, precision=lax.Precision.HIGHEST, preferred_element_type=jnp.float32
    )
    density = block_count * ray_count / (TILE * TILE)
    return convolved / density


def solution(mesh):
    placed = (P(("maps", "row", "col"), None, None), P(("maps", "row", "col"), None), P())
    return jax.shard_map(
        shards, mesh=mesh, in_specs=placed, out_specs=P(("maps", "row"), "col"), check_vma=False
    )
```

```python
import functools

import jax
import jax.numpy as jnp
from jax import lax
from jax.experimental import pallas as pl
from jax.experimental.pallas import tpu as pltpu
from jax.sharding import PartitionSpec as P

TILE = 128
HALO = 32
MOST = 4
DISC = 2 * HALO + 1
STEP = 16
LONG = TILE + STEP
TURNS = 2 * HALO // STEP
WIDE = TILE + 2 * HALO
DEPTH = TURNS * WIDE

VMEM = pl.BlockSpec(memory_space=pltpu.VMEM)
SMEM = pl.BlockSpec(memory_space=pltpu.SMEM)


def place_kernel(dest_ref, rays_ref, out_ref, count_ref):
    blocks = rays_ref.shape[0]
    tiles = out_ref.shape[0] // MOST
    empty = jnp.full((MOST,) + rays_ref.shape[1:], -2.0, jnp.float32)

    def clear(t, carry):
        count_ref[t] = 0
        out_ref[pl.ds(t * MOST, MOST)] = empty
        return carry

    lax.fori_loop(0, tiles, clear, 0)

    def place(b, carry):
        t = dest_ref[b, 0]
        rank = count_ref[t]
        count_ref[t] = rank + 1
        out_ref[t * MOST + rank] = rays_ref[b]
        return carry

    lax.fori_loop(0, blocks, place, 0)


def table_kernel(profile_ref, pairs_ref, last_ref):
    a = lax.broadcasted_iota(jnp.int32, (DISC, DISC), 0) - HALO
    c = lax.broadcasted_iota(jnp.int32, (DISC, DISC), 1) - HALO
    weights = jnp.where(a * a + c * c <= HALO * HALO, profile_ref[...], 0.0)
    kernel = (weights / jnp.sum(weights)).astype(jnp.bfloat16)
    source = lax.broadcasted_iota(jnp.int32, (DISC, 2 * TILE), 0)
    target = lax.broadcasted_iota(jnp.int32, (DISC, 2 * TILE), 1)
    mirror = jnp.where((source + target) % (2 * TILE) == 0, 1.0, 0.0).astype(jnp.bfloat16)
    mirrored = jnp.dot(kernel, mirror, preferred_element_type=jnp.float32)

    def band(row, first, rows):
        wide = jnp.broadcast_to(mirrored[row : row + 1, :], (rows, 2 * TILE))
        rolled = pltpu.roll(wide, first, 1, stride=1, stride_axis=0)
        return rolled[:, :TILE].astype(jnp.bfloat16)

    for s in range(STEP):
        half = pl.ds((s % 2) * TILE, TILE)
        for u in range(TURNS):
            row = u * STEP + s
            pairs_ref[s // 2, pl.ds(u * TILE, TILE), half] = band(row, HALO, TILE)
            side = TURNS * TILE + u * 2 * HALO
            pairs_ref[s // 2, pl.ds(side, HALO), half] = band(row, 0, HALO)
            pairs_ref[s // 2, pl.ds(side + HALO, HALO), half] = band(row, HALO + TILE, HALO)
    last_ref[:TILE, :] = band(2 * HALO, HALO, TILE)
    last_ref[TILE : TILE + HALO, :] = band(2 * HALO, 0, HALO)
    last_ref[TILE + HALO :, :] = band(2 * HALO, HALO + TILE, HALO)


def deposit_kernel(rows_axis, cols_axis, rays_ref, tile_ref, send_ref):
    slots, _, rays = rays_ref.shape
    cell = lax.broadcasted_iota(jnp.int32, (TILE, rays), 0).astype(jnp.float32)

    def add(group, total):
        for k in range(MOST):
            block = rays_ref[group * MOST + k]
            first = jnp.maximum(0.0, 1.0 - jnp.abs(block[0:1, :] - cell)).astype(jnp.bfloat16)
            second = jnp.maximum(0.0, 1.0 - jnp.abs(block[1:2, :] - cell)).astype(jnp.bfloat16)
            total = total + lax.dot_general(
                first, second, (((1,), (1,)), ((), ())), preferred_element_type=jnp.float32
            )
        return total

    total = lax.fori_loop(0, slots // MOST, add, jnp.zeros((TILE, TILE), jnp.float32))
    tile = total.astype(jnp.bfloat16)
    turned = tile.astype(jnp.float32).T.astype(jnp.bfloat16)
    tile_ref[...] = tile
    send_ref[...] = jnp.zeros(send_ref.shape, jnp.bfloat16)
    row_count, col_count = lax.axis_size(rows_axis), lax.axis_size(cols_axis)
    row, col = lax.axis_index(rows_axis), lax.axis_index(cols_axis)
    low, high = slice(0, HALO), slice(TILE - HALO, TILE)
    for dr in (-1, 0, 1):
        for dc in (-1, 0, 1):
            if dr == 0 and dc == 0:
                continue
            if dr != 0:
                piece = tile[low if dr < 0 else high, :]
            else:
                piece = turned[low if dc < 0 else high, :]
            r, c = row + dr, col + dc

            @pl.when((r >= 0) & (r < row_count) & (c >= 0) & (c < col_count))
            def _(r=r, c=c, piece=piece):
                send_ref[r * col_count + c] = piece


def spread_kernel(rows_axis, cols_axis, scale, tile_ref, got_ref, pairs_ref, last_ref, out_ref,
                  own, side, left):
    row_count, col_count = lax.axis_size(rows_axis), lax.axis_size(cols_axis)
    row, col = lax.axis_index(rows_axis), lax.axis_index(cols_axis)

    def fetch(dr, dc):
        r, c = row + dr, col + dc
        inside = (r >= 0) & (r < row_count) & (c >= 0) & (c < col_count)
        index = jnp.where(inside, r * col_count + c, 0)
        piece = got_ref[index].astype(jnp.float32)
        return jnp.where(inside, piece, 0.0)

    own[:HALO, :] = fetch(-1, 0).astype(jnp.bfloat16)
    own[HALO : HALO + TILE, :] = tile_ref[...]
    own[HALO + TILE :, :] = fetch(1, 0).astype(jnp.bfloat16)
    for dr, at in ((-1, 0), (1, HALO + TILE)):
        lower = fetch(dr, -1)[:, TILE - HALO :]
        upper = fetch(dr, 1)[:, :HALO]
        side[at : at + HALO, :] = jnp.concatenate([lower, upper], axis=1).astype(jnp.bfloat16)
    strips = jnp.concatenate([fetch(0, -1), fetch(0, 1)], axis=0).T
    side[HALO : HALO + TILE, :] = strips.astype(jnp.bfloat16)
    for u in range(TURNS):
        left[:, u * TILE : (u + 1) * TILE] = own[u * STEP : u * STEP + LONG, :]
        at = TURNS * TILE + u * 2 * HALO
        left[:, at : at + 2 * HALO] = side[u * STEP : u * STEP + LONG, :]
    total = jnp.dot(own[2 * HALO :, :], last_ref[:TILE, :], preferred_element_type=jnp.float32)
    total = total + jnp.dot(
        side[2 * HALO :, :], last_ref[TILE:, :], preferred_element_type=jnp.float32
    )
    for p in range(STEP // 2):
        both = jnp.dot(left[...], pairs_ref[p], preferred_element_type=jnp.float32)
        total = total + both[2 * p : 2 * p + TILE, :TILE]
        total = total + both[2 * p + 1 : 2 * p + 1 + TILE, TILE:]
    out_ref[...] = total / scale


def shards(positions, destination, profile):
    tiles = lax.axis_size("row") * lax.axis_size("col")
    blocks, _, rays = positions.shape
    limit = pltpu.CompilerParams(vmem_limit_bytes=32 * 1024 * 1024)
    outgoing = pl.pallas_call(
        place_kernel,
        out_shape=jax.ShapeDtypeStruct((tiles * MOST, 2, rays), jnp.float32),
        in_specs=[SMEM, VMEM],
        out_specs=VMEM,
        scratch_shapes=[pltpu.SMEM((tiles,), jnp.int32)],
        compiler_params=limit,
        name="place",
    )(destination, positions)
    received = lax.all_to_all(
        outgoing.reshape(tiles, MOST, 2, rays), ("row", "col"), split_axis=0, concat_axis=0, tiled=True
    ).reshape(tiles * MOST, 2, rays)
    pairs, last = pl.pallas_call(
        table_kernel,
        out_shape=(
            jax.ShapeDtypeStruct((STEP // 2, DEPTH, 2 * TILE), jnp.bfloat16),
            jax.ShapeDtypeStruct((WIDE, TILE), jnp.bfloat16),
        ),
        in_specs=[VMEM],
        out_specs=(VMEM, VMEM),
        compiler_params=limit,
        cost_estimate=pl.CostEstimate(flops=10_000_000, bytes_accessed=6_000_000, transcendentals=0),
        name="table",
    )(profile)
    tile, send = pl.pallas_call(
        functools.partial(deposit_kernel, "row", "col"),
        out_shape=(
            jax.ShapeDtypeStruct((TILE, TILE), jnp.bfloat16),
            jax.ShapeDtypeStruct((tiles, HALO, TILE), jnp.bfloat16),
        ),
        in_specs=[VMEM],
        out_specs=(VMEM, VMEM),
        compiler_params=limit,
        name="deposit",
    )(received)
    got = lax.all_to_all(send, ("row", "col"), split_axis=0, concat_axis=0, tiled=True)
    scale = blocks * rays / (TILE * TILE)
    return pl.pallas_call(
        functools.partial(spread_kernel, "row", "col", scale),
        out_shape=jax.ShapeDtypeStruct((TILE, TILE), jnp.float32),
        in_specs=[VMEM, VMEM, VMEM, VMEM],
        out_specs=VMEM,
        scratch_shapes=[
            pltpu.VMEM((WIDE, TILE), jnp.bfloat16),
            pltpu.VMEM((WIDE, 2 * HALO), jnp.bfloat16),
            pltpu.VMEM((LONG, DEPTH), jnp.bfloat16),
        ],
        compiler_params=limit,
        name="spread",
    )(tile, got, pairs, last)


def solution(mesh):
    placed = (P(("maps", "row", "col"), None, None), P(("maps", "row", "col"), None), P())
    return jax.shard_map(
        shards, mesh=mesh, in_specs=placed, out_specs=P(("maps", "row"), "col"), check_vma=False
    )
```

```python
import functools

import jax
import jax.numpy as jnp
from jax import lax
from jax.experimental import pallas as pl
from jax.experimental.pallas import tpu as pltpu
from jax.sharding import PartitionSpec as P

TILE = 128
HALO = 32
MOST = 4
DISC = 2 * HALO + 1
STEP = 16
LONG = TILE + STEP
TURNS = 2 * HALO // STEP
WIDE = TILE + 2 * HALO
DEPTH = TURNS * WIDE
BITS = 16
BATCH = 8

VMEM = pl.BlockSpec(memory_space=pltpu.VMEM)
SMEM = pl.BlockSpec(memory_space=pltpu.SMEM)


def place_kernel(dest_ref, rays_ref, out_ref, count_ref):
    blocks = rays_ref.shape[0]
    tiles = out_ref.shape[0] // MOST
    empty = jnp.full((MOST,) + rays_ref.shape[1:], -2.0, jnp.float32)

    def clear(t, carry):
        count_ref[t] = 0
        out_ref[pl.ds(t * MOST, MOST)] = empty
        return carry

    lax.fori_loop(0, tiles, clear, 0)

    def place(b, carry):
        t = dest_ref[b, 0]
        rank = count_ref[t]
        count_ref[t] = rank + 1
        out_ref[t * MOST + rank] = rays_ref[b]
        return carry

    lax.fori_loop(0, blocks, place, 0)


def table_kernel(profile_ref, pairs_ref, last_ref):
    a = lax.broadcasted_iota(jnp.int32, (DISC, DISC), 0) - HALO
    c = lax.broadcasted_iota(jnp.int32, (DISC, DISC), 1) - HALO
    weights = jnp.where(a * a + c * c <= HALO * HALO, profile_ref[...], 0.0)
    kernel = (weights / jnp.sum(weights)).astype(jnp.bfloat16)
    source = lax.broadcasted_iota(jnp.int32, (DISC, 2 * TILE), 0)
    target = lax.broadcasted_iota(jnp.int32, (DISC, 2 * TILE), 1)
    mirror = jnp.where((source + target) % (2 * TILE) == 0, 1.0, 0.0).astype(jnp.bfloat16)
    mirrored = jnp.dot(kernel, mirror, preferred_element_type=jnp.float32)

    def band(row, first, rows):
        wide = jnp.broadcast_to(mirrored[row : row + 1, :], (rows, 2 * TILE))
        rolled = pltpu.roll(wide, first, 1, stride=1, stride_axis=0)
        return rolled[:, :TILE].astype(jnp.bfloat16)

    for s in range(STEP):
        half = pl.ds((s % 2) * TILE, TILE)
        for u in range(TURNS):
            row = u * STEP + s
            pairs_ref[s // 2, pl.ds(u * TILE, TILE), half] = band(row, HALO, TILE)
            side = TURNS * TILE + u * 2 * HALO
            pairs_ref[s // 2, pl.ds(side, HALO), half] = band(row, 0, HALO)
            pairs_ref[s // 2, pl.ds(side + HALO, HALO), half] = band(row, HALO + TILE, HALO)
    last_ref[:TILE, :] = band(2 * HALO, HALO, TILE)
    last_ref[TILE : TILE + HALO, :] = band(2 * HALO, 0, HALO)
    last_ref[TILE + HALO :, :] = band(2 * HALO, HALO + TILE, HALO)


def hats(coords, cell):
    low = jnp.floor(coords)
    near = jnp.maximum(0.0, 1.0 - jnp.abs(coords - low)).astype(jnp.bfloat16)
    far = jnp.maximum(0.0, 1.0 - jnp.abs(coords - (low + 1.0))).astype(jnp.bfloat16)
    low = low.astype(jnp.bfloat16)
    zero = jnp.zeros((), jnp.bfloat16)
    one = jnp.ones((), jnp.bfloat16)
    return jnp.where(cell == low, near, jnp.where(cell == low + one, far, zero))


def deposit_kernel(rows_axis, cols_axis, rays_ref, tile_ref, send_ref, list_ref):
    slots, _, rays = rays_ref.shape
    lane = lax.broadcasted_iota(jnp.int32, (BITS, 128), 1)
    place = lax.broadcasted_iota(jnp.int32, (BITS, 128), 0)
    power = jnp.where(lane == 0, (1 << place).astype(jnp.float32), 0.0)
    count, empty = jnp.int32(0), jnp.int32(0)
    for at in range(0, slots, BITS):
        heads = rays_ref[at : at + BITS, 0, :128]
        mask = jnp.sum(jnp.where(heads > -1.0, power, 0.0)).astype(jnp.int32)
        for k in range(BITS):
            filled = (mask >> k) & 1
            list_ref[count] = at + k
            empty = jnp.where(filled == 1, empty, at + k)
            count = count + filled
    for k in range(BATCH):
        list_ref[count + k] = empty

    cell = lax.broadcasted_iota(jnp.int32, (TILE, rays), 0).astype(jnp.float32)
    cell = cell.astype(jnp.bfloat16)

    def add(batch, total):
        for k in range(BATCH):
            block = rays_ref[list_ref[batch * BATCH + k]]
            total = total + lax.dot_general(
                hats(block[0:1, :], cell),
                hats(block[1:2, :], cell),
                (((1,), (1,)), ((), ())),
                preferred_element_type=jnp.float32,
            )
        return total

    batches = (count + BATCH - 1) // BATCH
    total = lax.fori_loop(0, batches, add, jnp.zeros((TILE, TILE), jnp.float32))
    tile = total.astype(jnp.bfloat16)
    turned = tile.astype(jnp.float32).T.astype(jnp.bfloat16)
    tile_ref[...] = tile
    send_ref[...] = jnp.zeros(send_ref.shape, jnp.bfloat16)
    row_count, col_count = lax.axis_size(rows_axis), lax.axis_size(cols_axis)
    row, col = lax.axis_index(rows_axis), lax.axis_index(cols_axis)
    low, high = slice(0, HALO), slice(TILE - HALO, TILE)
    for dr in (-1, 0, 1):
        for dc in (-1, 0, 1):
            if dr == 0 and dc == 0:
                continue
            if dr != 0:
                piece = tile[low if dr < 0 else high, :]
            else:
                piece = turned[low if dc < 0 else high, :]
            r, c = row + dr, col + dc

            @pl.when((r >= 0) & (r < row_count) & (c >= 0) & (c < col_count))
            def _(r=r, c=c, piece=piece):
                send_ref[r * col_count + c] = piece


def spread_kernel(rows_axis, cols_axis, scale, tile_ref, got_ref, pairs_ref, last_ref, out_ref,
                  own, side, left):
    row_count, col_count = lax.axis_size(rows_axis), lax.axis_size(cols_axis)
    row, col = lax.axis_index(rows_axis), lax.axis_index(cols_axis)

    def fetch(dr, dc):
        r, c = row + dr, col + dc
        inside = (r >= 0) & (r < row_count) & (c >= 0) & (c < col_count)
        index = jnp.where(inside, r * col_count + c, 0)
        piece = got_ref[index].astype(jnp.float32)
        return jnp.where(inside, piece, 0.0)

    own[:HALO, :] = fetch(-1, 0).astype(jnp.bfloat16)
    own[HALO : HALO + TILE, :] = tile_ref[...]
    own[HALO + TILE :, :] = fetch(1, 0).astype(jnp.bfloat16)
    for dr, at in ((-1, 0), (1, HALO + TILE)):
        lower = fetch(dr, -1)[:, TILE - HALO :]
        upper = fetch(dr, 1)[:, :HALO]
        side[at : at + HALO, :] = jnp.concatenate([lower, upper], axis=1).astype(jnp.bfloat16)
    strips = jnp.concatenate([fetch(0, -1), fetch(0, 1)], axis=0).T
    side[HALO : HALO + TILE, :] = strips.astype(jnp.bfloat16)
    for u in range(TURNS):
        left[:, u * TILE : (u + 1) * TILE] = own[u * STEP : u * STEP + LONG, :]
        at = TURNS * TILE + u * 2 * HALO
        left[:, at : at + 2 * HALO] = side[u * STEP : u * STEP + LONG, :]
    total = jnp.dot(own[2 * HALO :, :], last_ref[:TILE, :], preferred_element_type=jnp.float32)
    total = total + jnp.dot(
        side[2 * HALO :, :], last_ref[TILE:, :], preferred_element_type=jnp.float32
    )
    for p in range(STEP // 2):
        both = jnp.dot(left[...], pairs_ref[p], preferred_element_type=jnp.float32)
        total = total + both[2 * p : 2 * p + TILE, :TILE]
        total = total + both[2 * p + 1 : 2 * p + 1 + TILE, TILE:]
    out_ref[...] = total / scale


def shards(positions, destination, profile):
    tiles = lax.axis_size("row") * lax.axis_size("col")
    blocks, _, rays = positions.shape
    limit = pltpu.CompilerParams(vmem_limit_bytes=32 * 1024 * 1024)
    outgoing = pl.pallas_call(
        place_kernel,
        out_shape=jax.ShapeDtypeStruct((tiles * MOST, 2, rays), jnp.float32),
        in_specs=[SMEM, VMEM],
        out_specs=VMEM,
        scratch_shapes=[pltpu.SMEM((tiles,), jnp.int32)],
        compiler_params=limit,
        name="place",
    )(destination, positions)
    received = lax.all_to_all(
        outgoing.reshape(tiles, MOST, 2, rays), ("row", "col"), split_axis=0, concat_axis=0, tiled=True
    ).reshape(tiles * MOST, 2, rays)
    pairs, last = pl.pallas_call(
        table_kernel,
        out_shape=(
            jax.ShapeDtypeStruct((STEP // 2, DEPTH, 2 * TILE), jnp.bfloat16),
            jax.ShapeDtypeStruct((WIDE, TILE), jnp.bfloat16),
        ),
        in_specs=[VMEM],
        out_specs=(VMEM, VMEM),
        compiler_params=limit,
        cost_estimate=pl.CostEstimate(flops=10_000_000, bytes_accessed=6_000_000, transcendentals=0),
        name="table",
    )(profile)
    tile, send = pl.pallas_call(
        functools.partial(deposit_kernel, "row", "col"),
        out_shape=(
            jax.ShapeDtypeStruct((TILE, TILE), jnp.bfloat16),
            jax.ShapeDtypeStruct((tiles, HALO, TILE), jnp.bfloat16),
        ),
        in_specs=[VMEM],
        out_specs=(VMEM, VMEM),
        scratch_shapes=[pltpu.SMEM((tiles * MOST + BATCH,), jnp.int32)],
        compiler_params=limit,
        name="deposit",
    )(received)
    got = lax.all_to_all(send, ("row", "col"), split_axis=0, concat_axis=0, tiled=True)
    scale = blocks * rays / (TILE * TILE)
    return pl.pallas_call(
        functools.partial(spread_kernel, "row", "col", scale),
        out_shape=jax.ShapeDtypeStruct((TILE, TILE), jnp.float32),
        in_specs=[VMEM, VMEM, VMEM, VMEM],
        out_specs=VMEM,
        scratch_shapes=[
            pltpu.VMEM((WIDE, TILE), jnp.bfloat16),
            pltpu.VMEM((WIDE, 2 * HALO), jnp.bfloat16),
            pltpu.VMEM((LONG, DEPTH), jnp.bfloat16),
        ],
        compiler_params=limit,
        name="spread",
    )(tile, got, pairs, last)


def solution(mesh):
    placed = (P(("maps", "row", "col"), None, None), P(("maps", "row", "col"), None), P())
    return jax.shard_map(
        shards, mesh=mesh, in_specs=placed, out_specs=P(("maps", "row"), "col"), check_vma=False
    )
```

```python
import functools

import jax
import jax.numpy as jnp
from jax import lax
from jax.experimental import pallas as pl
from jax.experimental.pallas import tpu as pltpu
from jax.sharding import PartitionSpec as P

TILE = 128
HALO = 32
MOST = 4
DISC = 2 * HALO + 1
STEP = 16
LONG = TILE + STEP
TURNS = 2 * HALO // STEP
WIDE = TILE + 2 * HALO
DEPTH = TURNS * WIDE
BITS = 16
BATCH = 8

VMEM = pl.BlockSpec(memory_space=pltpu.VMEM)
SMEM = pl.BlockSpec(memory_space=pltpu.SMEM)


def place_kernel(dest_ref, rays_ref, out_ref, count_ref):
    blocks = rays_ref.shape[0]
    tiles = out_ref.shape[0] // MOST
    empty = jnp.full((MOST,) + rays_ref.shape[1:], -2.0, jnp.float32)

    def clear(t, carry):
        count_ref[t] = 0
        out_ref[pl.ds(t * MOST, MOST)] = empty
        return carry

    lax.fori_loop(0, tiles, clear, 0)

    def place(b, carry):
        t = dest_ref[b, 0]
        rank = count_ref[t]
        count_ref[t] = rank + 1
        out_ref[t * MOST + rank] = rays_ref[b]
        return carry

    lax.fori_loop(0, blocks, place, 0)


def table_kernel(profile_ref, pairs_ref, last_ref):
    a = lax.broadcasted_iota(jnp.int32, (DISC, DISC), 0) - HALO
    c = lax.broadcasted_iota(jnp.int32, (DISC, DISC), 1) - HALO
    weights = jnp.where(a * a + c * c <= HALO * HALO, profile_ref[...], 0.0)
    kernel = (weights / jnp.sum(weights)).astype(jnp.bfloat16)
    source = lax.broadcasted_iota(jnp.int32, (DISC, 2 * TILE), 0)
    target = lax.broadcasted_iota(jnp.int32, (DISC, 2 * TILE), 1)
    mirror = jnp.where((source + target) % (2 * TILE) == 0, 1.0, 0.0).astype(jnp.bfloat16)
    mirrored = jnp.dot(kernel, mirror, preferred_element_type=jnp.float32)

    def band(row, first, rows):
        wide = jnp.broadcast_to(mirrored[row : row + 1, :], (rows, 2 * TILE))
        rolled = pltpu.roll(wide, first, 1, stride=1, stride_axis=0)
        return rolled[:, :TILE].astype(jnp.bfloat16)

    for s in range(STEP):
        half = pl.ds((s % 2) * TILE, TILE)
        for u in range(TURNS):
            row = u * STEP + s
            pairs_ref[s // 2, pl.ds(u * TILE, TILE), half] = band(row, HALO, TILE)
            side = TURNS * TILE + u * 2 * HALO
            pairs_ref[s // 2, pl.ds(side, HALO), half] = band(row, 0, HALO)
            pairs_ref[s // 2, pl.ds(side + HALO, HALO), half] = band(row, HALO + TILE, HALO)
    last_ref[:TILE, :] = band(2 * HALO, HALO, TILE)
    last_ref[TILE : TILE + HALO, :] = band(2 * HALO, 0, HALO)
    last_ref[TILE + HALO :, :] = band(2 * HALO, HALO + TILE, HALO)


def hats(coords, cell):
    low = jnp.floor(coords)
    near = jnp.maximum(0.0, 1.0 - jnp.abs(coords - low)).astype(jnp.bfloat16)
    far = jnp.maximum(0.0, 1.0 - jnp.abs(coords - (low + 1.0))).astype(jnp.bfloat16)
    low = low.astype(jnp.bfloat16)
    zero = jnp.zeros((), jnp.bfloat16)
    one = jnp.ones((), jnp.bfloat16)
    return jnp.where(cell == low, near, jnp.where(cell == low + one, far, zero))


def deposit_kernel(rays_ref, tile_ref, low_ref, high_ref, list_ref):
    slots, _, rays = rays_ref.shape
    lane = lax.broadcasted_iota(jnp.int32, (BITS, 128), 1)
    place = lax.broadcasted_iota(jnp.int32, (BITS, 128), 0)
    power = jnp.where(lane == 0, (1 << place).astype(jnp.float32), 0.0)
    count, empty = jnp.int32(0), jnp.int32(0)
    for at in range(0, slots, BITS):
        heads = rays_ref[at : at + BITS, 0, :128]
        mask = jnp.sum(jnp.where(heads > -1.0, power, 0.0)).astype(jnp.int32)
        for k in range(BITS):
            filled = (mask >> k) & 1
            list_ref[count] = at + k
            empty = jnp.where(filled == 1, empty, at + k)
            count = count + filled
    for k in range(BATCH):
        list_ref[count + k] = empty

    cell = lax.broadcasted_iota(jnp.int32, (TILE, rays), 0).astype(jnp.float32)
    cell = cell.astype(jnp.bfloat16)

    def add(batch, total):
        for k in range(BATCH):
            block = rays_ref[list_ref[batch * BATCH + k]]
            total = total + lax.dot_general(
                hats(block[0:1, :], cell),
                hats(block[1:2, :], cell),
                (((1,), (1,)), ((), ())),
                preferred_element_type=jnp.float32,
            )
        return total

    batches = (count + BATCH - 1) // BATCH
    total = lax.fori_loop(0, batches, add, jnp.zeros((TILE, TILE), jnp.float32))
    tile = total.astype(jnp.bfloat16)
    tile_ref[...] = tile
    low_ref[...] = tile[:HALO, :]
    high_ref[...] = tile[TILE - HALO :, :]


def spread_kernel(scale, over_ref, tile_ref, under_ref, before_ref, after_ref, pairs_ref, last_ref,
                  out_ref, own, side, left):
    own[:HALO, :] = over_ref[...]
    own[HALO : HALO + TILE, :] = tile_ref[...]
    own[HALO + TILE :, :] = under_ref[...]
    side[:, :HALO] = before_ref[...]
    side[:, HALO:] = after_ref[...]
    for u in range(TURNS):
        left[:, u * TILE : (u + 1) * TILE] = own[u * STEP : u * STEP + LONG, :]
        at = TURNS * TILE + u * 2 * HALO
        left[:, at : at + 2 * HALO] = side[u * STEP : u * STEP + LONG, :]
    total = jnp.dot(own[2 * HALO :, :], last_ref[:TILE, :], preferred_element_type=jnp.float32)
    total = total + jnp.dot(
        side[2 * HALO :, :], last_ref[TILE:, :], preferred_element_type=jnp.float32
    )
    for p in range(STEP // 2):
        both = jnp.dot(left[...], pairs_ref[p], preferred_element_type=jnp.float32)
        total = total + both[2 * p : 2 * p + TILE, :TILE]
        total = total + both[2 * p + 1 : 2 * p + 1 + TILE, TILE:]
    out_ref[...] = total / scale


def shift(cells, axis, step):
    count = lax.axis_size(axis)
    pairs = [(i, i + step) for i in range(count) if 0 <= i + step < count]
    return lax.ppermute(cells, axis, pairs)


def shards(positions, destination, profile):
    tiles = lax.axis_size("row") * lax.axis_size("col")
    blocks, _, rays = positions.shape
    limit = pltpu.CompilerParams(vmem_limit_bytes=32 * 1024 * 1024)
    outgoing = pl.pallas_call(
        place_kernel,
        out_shape=jax.ShapeDtypeStruct((tiles * MOST, 2, rays), jnp.float32),
        in_specs=[SMEM, VMEM],
        out_specs=VMEM,
        scratch_shapes=[pltpu.SMEM((tiles,), jnp.int32)],
        compiler_params=limit,
        name="place",
    )(destination, positions)
    received = lax.all_to_all(
        outgoing.reshape(tiles, MOST, 2, rays), ("row", "col"), split_axis=0, concat_axis=0, tiled=True
    ).reshape(tiles * MOST, 2, rays)
    pairs, last = pl.pallas_call(
        table_kernel,
        out_shape=(
            jax.ShapeDtypeStruct((STEP // 2, DEPTH, 2 * TILE), jnp.bfloat16),
            jax.ShapeDtypeStruct((WIDE, TILE), jnp.bfloat16),
        ),
        in_specs=[VMEM],
        out_specs=(VMEM, VMEM),
        compiler_params=limit,
        cost_estimate=pl.CostEstimate(flops=10_000_000, bytes_accessed=6_000_000, transcendentals=0),
        name="table",
    )(profile)
    tile, low, high = pl.pallas_call(
        deposit_kernel,
        out_shape=(
            jax.ShapeDtypeStruct((TILE, TILE), jnp.bfloat16),
            jax.ShapeDtypeStruct((HALO, TILE), jnp.bfloat16),
            jax.ShapeDtypeStruct((HALO, TILE), jnp.bfloat16),
        ),
        in_specs=[VMEM],
        out_specs=(VMEM, VMEM, VMEM),
        scratch_shapes=[pltpu.SMEM((tiles * MOST + BATCH,), jnp.int32)],
        compiler_params=limit,
        name="deposit",
    )(received)
    over = shift(high, "row", 1)
    under = shift(low, "row", -1)
    tall = jnp.concatenate([over, tile, under], axis=0)
    before = shift(tall[:, TILE - HALO :], "col", 1)
    after = shift(tall[:, :HALO], "col", -1)
    scale = blocks * rays / (TILE * TILE)
    return pl.pallas_call(
        functools.partial(spread_kernel, scale),
        out_shape=jax.ShapeDtypeStruct((TILE, TILE), jnp.float32),
        in_specs=[VMEM] * 7,
        out_specs=VMEM,
        scratch_shapes=[
            pltpu.VMEM((WIDE, TILE), jnp.bfloat16),
            pltpu.VMEM((WIDE, 2 * HALO), jnp.bfloat16),
            pltpu.VMEM((LONG, DEPTH), jnp.bfloat16),
        ],
        compiler_params=limit,
        name="spread",
    )(over, tile, under, before, after, pairs, last)


def solution(mesh):
    placed = (P(("maps", "row", "col"), None, None), P(("maps", "row", "col"), None), P())
    return jax.shard_map(
        shards, mesh=mesh, in_specs=placed, out_specs=P(("maps", "row"), "col"), check_vma=False
    )
```

```python
import functools

import jax
import jax.numpy as jnp
from jax import lax
from jax.experimental import pallas as pl
from jax.experimental.pallas import tpu as pltpu
from jax.sharding import PartitionSpec as P

TILE = 128
HALO = 32
MOST = 4
DISC = 2 * HALO + 1
STEP = 16
LONG = TILE + STEP
TURNS = 2 * HALO // STEP
WIDE = TILE + 2 * HALO
DEPTH = TURNS * WIDE
BITS = 16
BATCH = 8

VMEM = pl.BlockSpec(memory_space=pltpu.VMEM)
SMEM = pl.BlockSpec(memory_space=pltpu.SMEM)


def place_kernel(dest_ref, rays_ref, out_ref, count_ref):
    blocks = rays_ref.shape[0]
    tiles = out_ref.shape[0] // MOST
    empty = jnp.full((MOST,) + rays_ref.shape[1:], -2.0, jnp.float32)

    def clear(t, carry):
        count_ref[t] = 0
        out_ref[pl.ds(t * MOST, MOST)] = empty
        return carry

    lax.fori_loop(0, tiles, clear, 0)

    def place(b, carry):
        t = dest_ref[b, 0]
        rank = count_ref[t]
        count_ref[t] = rank + 1
        out_ref[t * MOST + rank] = rays_ref[b]
        return carry

    lax.fori_loop(0, blocks, place, 0)


def table_kernel(profile_ref, pairs_ref, last_ref):
    a = lax.broadcasted_iota(jnp.int32, (DISC, DISC), 0) - HALO
    c = lax.broadcasted_iota(jnp.int32, (DISC, DISC), 1) - HALO
    weights = jnp.where(a * a + c * c <= HALO * HALO, profile_ref[...], 0.0)
    kernel = (weights / jnp.sum(weights)).astype(jnp.bfloat16)
    source = lax.broadcasted_iota(jnp.int32, (DISC, 2 * TILE), 0)
    target = lax.broadcasted_iota(jnp.int32, (DISC, 2 * TILE), 1)
    mirror = jnp.where((source + target) % (2 * TILE) == 0, 1.0, 0.0).astype(jnp.bfloat16)
    mirrored = jnp.dot(kernel, mirror, preferred_element_type=jnp.float32)

    def band(row, first, rows):
        wide = jnp.broadcast_to(mirrored[row : row + 1, :], (rows, 2 * TILE))
        rolled = pltpu.roll(wide, first, 1, stride=1, stride_axis=0)
        return rolled[:, :TILE].astype(jnp.bfloat16)

    for s in range(STEP):
        half = pl.ds((s % 2) * TILE, TILE)
        for u in range(TURNS):
            row = u * STEP + s
            pairs_ref[s // 2, pl.ds(u * TILE, TILE), half] = band(row, HALO, TILE)
            side = TURNS * TILE + u * 2 * HALO
            pairs_ref[s // 2, pl.ds(side, HALO), half] = band(row, 0, HALO)
            pairs_ref[s // 2, pl.ds(side + HALO, HALO), half] = band(row, HALO + TILE, HALO)
    last_ref[:TILE, :] = band(2 * HALO, HALO, TILE)
    last_ref[TILE : TILE + HALO, :] = band(2 * HALO, 0, HALO)
    last_ref[TILE + HALO :, :] = band(2 * HALO, HALO + TILE, HALO)


def hats(coords, cell):
    low = jnp.floor(coords)
    near = jnp.maximum(0.0, 1.0 - jnp.abs(coords - low)).astype(jnp.bfloat16)
    far = jnp.maximum(0.0, 1.0 - jnp.abs(coords - (low + 1.0))).astype(jnp.bfloat16)
    low = low.astype(jnp.bfloat16)
    zero = jnp.zeros((), jnp.bfloat16)
    one = jnp.ones((), jnp.bfloat16)
    return jnp.where(cell == low, near, jnp.where(cell == low + one, far, zero))


def deposit_kernel(cols_axis, rays_ref, tile_ref, send_ref, list_ref):
    slots, _, rays = rays_ref.shape
    lane = lax.broadcasted_iota(jnp.int32, (BITS, 128), 1)
    place = lax.broadcasted_iota(jnp.int32, (BITS, 128), 0)
    power = jnp.where(lane == 0, (1 << place).astype(jnp.float32), 0.0)
    count, empty = jnp.int32(0), jnp.int32(0)
    for at in range(0, slots, BITS):
        heads = rays_ref[at : at + BITS, 0, :128]
        mask = jnp.sum(jnp.where(heads > -1.0, power, 0.0)).astype(jnp.int32)
        for k in range(BITS):
            filled = (mask >> k) & 1
            list_ref[count] = at + k
            empty = jnp.where(filled == 1, empty, at + k)
            count = count + filled
    for k in range(BATCH):
        list_ref[count + k] = empty

    cell = lax.broadcasted_iota(jnp.int32, (TILE, rays), 0).astype(jnp.float32)
    cell = cell.astype(jnp.bfloat16)

    def add(batch, total):
        for k in range(BATCH):
            block = rays_ref[list_ref[batch * BATCH + k]]
            total = total + lax.dot_general(
                hats(block[0:1, :], cell),
                hats(block[1:2, :], cell),
                (((1,), (1,)), ((), ())),
                preferred_element_type=jnp.float32,
            )
        return total

    batches = (count + BATCH - 1) // BATCH
    total = lax.fori_loop(0, batches, add, jnp.zeros((TILE, TILE), jnp.float32))
    tile = total.astype(jnp.bfloat16)
    tile_ref[...] = tile
    turned = tile.astype(jnp.float32).T.astype(jnp.bfloat16)
    offer(cols_axis, send_ref, turned[:HALO, :], turned[TILE - HALO :, :])


def offer(axis, send_ref, low, high):
    count, me = lax.axis_size(axis), lax.axis_index(axis)
    send_ref[...] = jnp.zeros(send_ref.shape, jnp.bfloat16)

    @pl.when(me > 0)
    def _():
        send_ref[me - 1] = low

    @pl.when(me < count - 1)
    def _():
        send_ref[me + 1] = high


def fetch(axis, got_ref, step):
    count, me = lax.axis_size(axis), lax.axis_index(axis)
    at = me + step
    inside = (at >= 0) & (at < count)
    piece = got_ref[jnp.where(inside, at, 0)]
    return jnp.where(inside, piece, jnp.zeros((), jnp.bfloat16))


def rows_kernel(rows_axis, cols_axis, tile_ref, got_ref, side_ref, send_ref):
    before, after = fetch(cols_axis, got_ref, -1), fetch(cols_axis, got_ref, 1)
    side = jnp.concatenate([before, after], axis=0).astype(jnp.float32).T.astype(jnp.bfloat16)
    blank = jnp.zeros((HALO, 2 * HALO), jnp.bfloat16)
    side_ref[...] = side
    low = jnp.concatenate([tile_ref[:HALO, :], side[:HALO, :], blank], axis=1)
    high = jnp.concatenate([tile_ref[TILE - HALO :, :], side[TILE - HALO :, :], blank], axis=1)
    offer(rows_axis, send_ref, low, high)


def spread_kernel(rows_axis, scale, tile_ref, side_ref, got_ref, pairs_ref, last_ref, out_ref,
                  own, side, left):
    own[HALO : HALO + TILE, :] = tile_ref[...]
    side[HALO : HALO + TILE, :] = side_ref[...]
    for step, at in ((-1, 0), (1, HALO + TILE)):
        piece = fetch(rows_axis, got_ref, step)
        own[at : at + HALO, :] = piece[:, :TILE]
        side[at : at + HALO, :] = piece[:, TILE : TILE + 2 * HALO]
    for u in range(TURNS):
        left[:, u * TILE : (u + 1) * TILE] = own[u * STEP : u * STEP + LONG, :]
        at = TURNS * TILE + u * 2 * HALO
        left[:, at : at + 2 * HALO] = side[u * STEP : u * STEP + LONG, :]
    total = jnp.dot(own[2 * HALO :, :], last_ref[:TILE, :], preferred_element_type=jnp.float32)
    total = total + jnp.dot(
        side[2 * HALO :, :], last_ref[TILE:, :], preferred_element_type=jnp.float32
    )
    for p in range(STEP // 2):
        both = jnp.dot(left[...], pairs_ref[p], preferred_element_type=jnp.float32)
        total = total + both[2 * p : 2 * p + TILE, :TILE]
        total = total + both[2 * p + 1 : 2 * p + 1 + TILE, TILE:]
    out_ref[...] = total / scale


def shards(positions, destination, profile):
    tiles = lax.axis_size("row") * lax.axis_size("col")
    blocks, _, rays = positions.shape
    limit = pltpu.CompilerParams(vmem_limit_bytes=32 * 1024 * 1024)
    outgoing = pl.pallas_call(
        place_kernel,
        out_shape=jax.ShapeDtypeStruct((tiles * MOST, 2, rays), jnp.float32),
        in_specs=[SMEM, VMEM],
        out_specs=VMEM,
        scratch_shapes=[pltpu.SMEM((tiles,), jnp.int32)],
        compiler_params=limit,
        name="place",
    )(destination, positions)
    received = lax.all_to_all(
        outgoing.reshape(tiles, MOST, 2, rays), ("row", "col"), split_axis=0, concat_axis=0, tiled=True
    ).reshape(tiles * MOST, 2, rays)
    pairs, last = pl.pallas_call(
        table_kernel,
        out_shape=(
            jax.ShapeDtypeStruct((STEP // 2, DEPTH, 2 * TILE), jnp.bfloat16),
            jax.ShapeDtypeStruct((WIDE, TILE), jnp.bfloat16),
        ),
        in_specs=[VMEM],
        out_specs=(VMEM, VMEM),
        compiler_params=limit,
        cost_estimate=pl.CostEstimate(flops=10_000_000, bytes_accessed=6_000_000, transcendentals=0),
        name="table",
    )(profile)
    row_count, col_count = lax.axis_size("row"), lax.axis_size("col")
    tile, send = pl.pallas_call(
        functools.partial(deposit_kernel, "col"),
        out_shape=(
            jax.ShapeDtypeStruct((TILE, TILE), jnp.bfloat16),
            jax.ShapeDtypeStruct((col_count, HALO, TILE), jnp.bfloat16),
        ),
        in_specs=[VMEM],
        out_specs=(VMEM, VMEM),
        scratch_shapes=[pltpu.SMEM((tiles * MOST + BATCH,), jnp.int32)],
        compiler_params=limit,
        name="deposit",
    )(received)
    got = lax.all_to_all(send, "col", split_axis=0, concat_axis=0, tiled=True)
    side, send = pl.pallas_call(
        functools.partial(rows_kernel, "row", "col"),
        out_shape=(
            jax.ShapeDtypeStruct((TILE, 2 * HALO), jnp.bfloat16),
            jax.ShapeDtypeStruct((row_count, HALO, 2 * TILE), jnp.bfloat16),
        ),
        in_specs=[VMEM] * 2,
        out_specs=(VMEM, VMEM),
        compiler_params=limit,
        name="rows",
    )(tile, got)
    got = lax.all_to_all(send, "row", split_axis=0, concat_axis=0, tiled=True)
    scale = blocks * rays / (TILE * TILE)
    return pl.pallas_call(
        functools.partial(spread_kernel, "row", scale),
        out_shape=jax.ShapeDtypeStruct((TILE, TILE), jnp.float32),
        in_specs=[VMEM] * 5,
        out_specs=VMEM,
        scratch_shapes=[
            pltpu.VMEM((WIDE, TILE), jnp.bfloat16),
            pltpu.VMEM((WIDE, 2 * HALO), jnp.bfloat16),
            pltpu.VMEM((LONG, DEPTH), jnp.bfloat16),
        ],
        compiler_params=limit,
        name="spread",
    )(tile, side, got, pairs, last)


def solution(mesh):
    placed = (P(("maps", "row", "col"), None, None), P(("maps", "row", "col"), None), P())
    return jax.shard_map(
        shards, mesh=mesh, in_specs=placed, out_specs=P(("maps", "row"), "col"), check_vma=False
    )
```

```python
import functools

import jax
import jax.numpy as jnp
from jax import lax
from jax.experimental import pallas as pl
from jax.experimental.pallas import tpu as pltpu
from jax.sharding import PartitionSpec as P

TILE = 128
HALO = 32
MOST = 4
DISC = 2 * HALO + 1
STEP = 16
LONG = TILE + STEP
TURNS = 2 * HALO // STEP
WIDE = TILE + 2 * HALO
DEPTH = TURNS * WIDE
BITS = 16
BATCH = 8

VMEM = pl.BlockSpec(memory_space=pltpu.VMEM)
SMEM = pl.BlockSpec(memory_space=pltpu.SMEM)


def place_kernel(dest_ref, rays_ref, out_ref, count_ref, done):
    blocks = rays_ref.shape[0]
    tiles = out_ref.shape[0] // MOST
    empty = jnp.full((MOST,) + rays_ref.shape[1:], -2.0, jnp.float32)

    def clear(t, carry):
        count_ref[t] = 0
        out_ref[pl.ds(t * MOST, MOST)] = empty
        return carry

    lax.fori_loop(0, tiles, clear, 0, unroll=4)

    def place(b, carry):
        t = dest_ref[0, b]
        rank = count_ref[t]
        count_ref[t] = rank + 1
        pltpu.make_async_copy(rays_ref.at[b], out_ref.at[t * MOST + rank], done.at[b]).start()
        return carry

    lax.fori_loop(0, blocks, place, 0, unroll=4)

    def finish(b, carry):
        pltpu.make_async_copy(rays_ref.at[b], out_ref.at[b], done.at[b]).wait()
        return carry

    lax.fori_loop(0, blocks, finish, 0, unroll=4)


def table_kernel(profile_ref, pairs_ref, last_ref):
    a = lax.broadcasted_iota(jnp.int32, (DISC, DISC), 0) - HALO
    c = lax.broadcasted_iota(jnp.int32, (DISC, DISC), 1) - HALO
    weights = jnp.where(a * a + c * c <= HALO * HALO, profile_ref[...], 0.0)
    kernel = (weights / jnp.sum(weights)).astype(jnp.bfloat16)
    source = lax.broadcasted_iota(jnp.int32, (DISC, 2 * TILE), 0)
    target = lax.broadcasted_iota(jnp.int32, (DISC, 2 * TILE), 1)
    mirror = jnp.where((source + target) % (2 * TILE) == 0, 1.0, 0.0).astype(jnp.bfloat16)
    mirrored = jnp.dot(kernel, mirror, preferred_element_type=jnp.float32)

    def band(row, first, rows):
        wide = jnp.broadcast_to(mirrored[row : row + 1, :], (rows, 2 * TILE))
        rolled = pltpu.roll(wide, first, 1, stride=1, stride_axis=0)
        return rolled[:, :TILE].astype(jnp.bfloat16)

    for s in range(STEP):
        half = pl.ds((s % 2) * TILE, TILE)
        for u in range(TURNS):
            row = u * STEP + s
            pairs_ref[s // 2, pl.ds(u * TILE, TILE), half] = band(row, HALO, TILE)
            side = TURNS * TILE + u * 2 * HALO
            pairs_ref[s // 2, pl.ds(side, HALO), half] = band(row, 0, HALO)
            pairs_ref[s // 2, pl.ds(side + HALO, HALO), half] = band(row, HALO + TILE, HALO)
    last_ref[:TILE, :] = band(2 * HALO, HALO, TILE)
    last_ref[TILE : TILE + HALO, :] = band(2 * HALO, 0, HALO)
    last_ref[TILE + HALO :, :] = band(2 * HALO, HALO + TILE, HALO)


def hats(coords, cell):
    low = jnp.floor(coords)
    near = jnp.maximum(0.0, 1.0 - jnp.abs(coords - low)).astype(jnp.bfloat16)
    far = jnp.maximum(0.0, 1.0 - jnp.abs(coords - (low + 1.0))).astype(jnp.bfloat16)
    low = low.astype(jnp.bfloat16)
    zero = jnp.zeros((), jnp.bfloat16)
    one = jnp.ones((), jnp.bfloat16)
    return jnp.where(cell == low, near, jnp.where(cell == low + one, far, zero))


def deposit_kernel(rows_axis, cols_axis, rays_ref, tile_ref, send_ref, list_ref):
    slots, _, rays = rays_ref.shape
    lane = lax.broadcasted_iota(jnp.int32, (BITS, 128), 1)
    place = lax.broadcasted_iota(jnp.int32, (BITS, 128), 0)
    power = jnp.where(lane == 0, (1 << place).astype(jnp.float32), 0.0)
    count, empty = jnp.int32(0), jnp.int32(0)
    for at in range(0, slots, BITS):
        heads = rays_ref[at : at + BITS, 0, :128]
        mask = jnp.sum(jnp.where(heads > -1.0, power, 0.0)).astype(jnp.int32)
        for k in range(BITS):
            filled = (mask >> k) & 1
            list_ref[count] = at + k
            empty = jnp.where(filled == 1, empty, at + k)
            count = count + filled
    for k in range(BATCH):
        list_ref[count + k] = empty

    cell = lax.broadcasted_iota(jnp.int32, (TILE, rays), 0).astype(jnp.float32)
    cell = cell.astype(jnp.bfloat16)

    def add(batch, total):
        for k in range(BATCH):
            block = rays_ref[list_ref[batch * BATCH + k]]
            total = total + lax.dot_general(
                hats(block[0:1, :], cell),
                hats(block[1:2, :], cell),
                (((1,), (1,)), ((), ())),
                preferred_element_type=jnp.float32,
            )
        return total

    batches = (count + BATCH - 1) // BATCH
    total = lax.fori_loop(0, batches, add, jnp.zeros((TILE, TILE), jnp.float32))
    tile = total.astype(jnp.bfloat16)
    turned = tile.astype(jnp.float32).T.astype(jnp.bfloat16)
    tile_ref[...] = tile
    row_count, col_count = lax.axis_size(rows_axis), lax.axis_size(cols_axis)
    row, col = lax.axis_index(rows_axis), lax.axis_index(cols_axis)
    low, high = slice(0, HALO), slice(TILE - HALO, TILE)
    for dr in (-1, 0, 1):
        for dc in (-1, 0, 1):
            if dr == 0 and dc == 0:
                continue
            if dr != 0:
                piece = tile[low if dr < 0 else high, :]
            else:
                piece = turned[low if dc < 0 else high, :]
            r, c = row + dr, col + dc

            @pl.when((r >= 0) & (r < row_count) & (c >= 0) & (c < col_count))
            def _(r=r, c=c, piece=piece):
                send_ref[r * col_count + c] = piece


def spread_kernel(rows_axis, cols_axis, scale, tile_ref, got_ref, pairs_ref, last_ref, out_ref,
                  own, side, left):
    row_count, col_count = lax.axis_size(rows_axis), lax.axis_size(cols_axis)
    row, col = lax.axis_index(rows_axis), lax.axis_index(cols_axis)

    def fetch(dr, dc):
        r, c = row + dr, col + dc
        inside = (r >= 0) & (r < row_count) & (c >= 0) & (c < col_count)
        index = jnp.where(inside, r * col_count + c, 0)
        piece = got_ref[index].astype(jnp.float32)
        return jnp.where(inside, piece, 0.0)

    own[:HALO, :] = fetch(-1, 0).astype(jnp.bfloat16)
    own[HALO : HALO + TILE, :] = tile_ref[...]
    own[HALO + TILE :, :] = fetch(1, 0).astype(jnp.bfloat16)
    for dr, at in ((-1, 0), (1, HALO + TILE)):
        lower = fetch(dr, -1)[:, TILE - HALO :]
        upper = fetch(dr, 1)[:, :HALO]
        side[at : at + HALO, :] = jnp.concatenate([lower, upper], axis=1).astype(jnp.bfloat16)
    strips = jnp.concatenate([fetch(0, -1), fetch(0, 1)], axis=0).T
    side[HALO : HALO + TILE, :] = strips.astype(jnp.bfloat16)
    for u in range(TURNS):
        left[:, u * TILE : (u + 1) * TILE] = own[u * STEP : u * STEP + LONG, :]
        at = TURNS * TILE + u * 2 * HALO
        left[:, at : at + 2 * HALO] = side[u * STEP : u * STEP + LONG, :]
    total = jnp.dot(own[2 * HALO :, :], last_ref[:TILE, :], preferred_element_type=jnp.float32)
    total = total + jnp.dot(
        side[2 * HALO :, :], last_ref[TILE:, :], preferred_element_type=jnp.float32
    )
    for p in range(STEP // 2):
        both = jnp.dot(left[...], pairs_ref[p], preferred_element_type=jnp.float32)
        total = total + both[2 * p : 2 * p + TILE, :TILE]
        total = total + both[2 * p + 1 : 2 * p + 1 + TILE, TILE:]
    out_ref[...] = total / scale


def shards(positions, destination, profile):
    tiles = lax.axis_size("row") * lax.axis_size("col")
    blocks, _, rays = positions.shape
    limit = pltpu.CompilerParams(vmem_limit_bytes=32 * 1024 * 1024)
    outgoing = pl.pallas_call(
        place_kernel,
        out_shape=jax.ShapeDtypeStruct((tiles * MOST, 2, rays), jnp.float32),
        in_specs=[SMEM, pl.BlockSpec(memory_space=pltpu.HBM)],
        out_specs=VMEM,
        scratch_shapes=[pltpu.SMEM((tiles,), jnp.int32), pltpu.SemaphoreType.DMA((blocks,))],
        compiler_params=pltpu.CompilerParams(vmem_limit_bytes=56 * 1024 * 1024),
        name="place",
    )(destination.T, positions)
    received = lax.all_to_all(
        outgoing.reshape(tiles, MOST, 2, rays), ("row", "col"), split_axis=0, concat_axis=0, tiled=True
    ).reshape(tiles * MOST, 2, rays)
    pairs, last = pl.pallas_call(
        table_kernel,
        out_shape=(
            jax.ShapeDtypeStruct((STEP // 2, DEPTH, 2 * TILE), jnp.bfloat16),
            jax.ShapeDtypeStruct((WIDE, TILE), jnp.bfloat16),
        ),
        in_specs=[VMEM],
        out_specs=(VMEM, VMEM),
        compiler_params=limit,
        cost_estimate=pl.CostEstimate(flops=10_000_000, bytes_accessed=6_000_000, transcendentals=0),
        name="table",
    )(profile)
    received, pairs, last = lax.optimization_barrier((received, pairs, last))
    tile, send = pl.pallas_call(
        functools.partial(deposit_kernel, "row", "col"),
        out_shape=(
            jax.ShapeDtypeStruct((TILE, TILE), jnp.bfloat16),
            jax.ShapeDtypeStruct((tiles, HALO, TILE), jnp.bfloat16),
        ),
        in_specs=[VMEM],
        out_specs=(VMEM, VMEM),
        scratch_shapes=[pltpu.SMEM((tiles * MOST + BATCH,), jnp.int32)],
        compiler_params=limit,
        name="deposit",
    )(received)
    got = lax.all_to_all(send, ("row", "col"), split_axis=0, concat_axis=0, tiled=True)
    scale = blocks * rays / (TILE * TILE)
    return pl.pallas_call(
        functools.partial(spread_kernel, "row", "col", scale),
        out_shape=jax.ShapeDtypeStruct((TILE, TILE), jnp.float32),
        in_specs=[VMEM, VMEM, VMEM, VMEM],
        out_specs=VMEM,
        scratch_shapes=[
            pltpu.VMEM((WIDE, TILE), jnp.bfloat16),
            pltpu.VMEM((WIDE, 2 * HALO), jnp.bfloat16),
            pltpu.VMEM((LONG, DEPTH), jnp.bfloat16),
        ],
        compiler_params=limit,
        name="spread",
    )(tile, got, pairs, last)


def solution(mesh):
    placed = (P(("maps", "row", "col"), None, None), P(("maps", "row", "col"), None), P())
    return jax.shard_map(
        shards, mesh=mesh, in_specs=placed, out_specs=P(("maps", "row"), "col"), check_vma=False
    )
```

```python
import functools

import jax
import jax.numpy as jnp
from jax import lax
from jax.experimental import pallas as pl
from jax.experimental.pallas import tpu as pltpu
from jax.sharding import PartitionSpec as P

TILE = 128
HALO = 32
MOST = 4
DISC = 2 * HALO + 1
STEP = 16
LONG = TILE + STEP
TURNS = 2 * HALO // STEP
WIDE = TILE + 2 * HALO
DEPTH = TURNS * WIDE
LANES = 128
BATCH = 8

VMEM = pl.BlockSpec(memory_space=pltpu.VMEM)
LIMIT = pltpu.CompilerParams(vmem_limit_bytes=32 * 1024 * 1024)


def pack_kernel(dest_ref, rays_ref, out_ref, meta):
    blocks = rays_ref.shape[0]
    half = blocks // 2
    lane = lax.broadcasted_iota(jnp.int32, (blocks, LANES), 1)
    place = lax.broadcasted_iota(jnp.int32, (blocks, LANES), 0)

    def laid(column):
        return jnp.sum(jnp.where(lane == place, column, 0.0), axis=0, keepdims=True)

    meta[...] = jnp.zeros(meta.shape, jnp.float32)
    meta[0:1, :blocks] = dest_ref[...].astype(jnp.float32)
    for k in range(2):
        coords = rays_ref[:, k, :]
        meta[k : k + 1, LANES : 2 * LANES] = laid(jnp.min(coords, axis=1, keepdims=True))
        meta[k : k + 1, 2 * LANES : 3 * LANES] = laid(jnp.max(coords, axis=1, keepdims=True))
    col_count = lax.axis_size("col")
    for t in range(out_ref.shape[0]):
        at = (t // col_count) % 2 * half
        out_ref[t, :half] = rays_ref[at : at + half]
        out_ref[t, half] = meta[...]


def table_kernel(profile_ref, pairs_ref, last_ref):
    a = lax.broadcasted_iota(jnp.int32, (DISC, DISC), 0) - HALO
    c = lax.broadcasted_iota(jnp.int32, (DISC, DISC), 1) - HALO
    weights = jnp.where(a * a + c * c <= HALO * HALO, profile_ref[...], 0.0)
    kernel = (weights / jnp.sum(weights)).astype(jnp.bfloat16)
    source = lax.broadcasted_iota(jnp.int32, (DISC, 2 * TILE), 0)
    target = lax.broadcasted_iota(jnp.int32, (DISC, 2 * TILE), 1)
    mirror = jnp.where((source + target) % (2 * TILE) == 0, 1.0, 0.0).astype(jnp.bfloat16)
    mirrored = jnp.dot(kernel, mirror, preferred_element_type=jnp.float32)

    def band(row, first, rows):
        wide = jnp.broadcast_to(mirrored[row : row + 1, :], (rows, 2 * TILE))
        rolled = pltpu.roll(wide, first, 1, stride=1, stride_axis=0)
        return rolled[:, :TILE].astype(jnp.bfloat16)

    for s in range(STEP):
        half = pl.ds((s % 2) * TILE, TILE)
        for u in range(TURNS):
            row = u * STEP + s
            pairs_ref[s // 2, pl.ds(u * TILE, TILE), half] = band(row, HALO, TILE)
            side = TURNS * TILE + u * 2 * HALO
            pairs_ref[s // 2, pl.ds(side, HALO), half] = band(row, 0, HALO)
            pairs_ref[s // 2, pl.ds(side + HALO, HALO), half] = band(row, HALO + TILE, HALO)
    last_ref[:TILE, :] = band(2 * HALO, HALO, TILE)
    last_ref[TILE : TILE + HALO, :] = band(2 * HALO, 0, HALO)
    last_ref[TILE + HALO :, :] = band(2 * HALO, HALO + TILE, HALO)


def hats(coords, offset, cell):
    low = jnp.floor(coords)
    near = jnp.maximum(0.0, 1.0 - jnp.abs(coords - low)).astype(jnp.bfloat16)
    far = jnp.maximum(0.0, 1.0 - jnp.abs(coords - (low + 1.0))).astype(jnp.bfloat16)
    low = low + offset
    here, there = low.astype(jnp.bfloat16), (low + 1.0).astype(jnp.bfloat16)
    zero = jnp.zeros((), jnp.bfloat16)
    return jnp.where(cell == here, near, jnp.where(cell == there, far, zero))


def gather_codes(got_ref, codes, table, done):
    last = got_ref.shape[1] - 1
    row_count, col_count = lax.axis_size("row"), lax.axis_size("col")
    row, col = lax.axis_index("row"), lax.axis_index("col")
    tile = got_ref[:, last, 0, :LANES]
    tile_row = jnp.floor((tile + 0.5) / col_count)
    dr = tile_row - row.astype(jnp.float32)
    dc = tile - tile_row * col_count - col.astype(jnp.float32)

    def touches(d, k):
        least = got_ref[:, last, k, LANES : 2 * LANES]
        most = got_ref[:, last, k, 2 * LANES : 3 * LANES]
        before = (d == -1.0) & (most > TILE - HALO - 1.0)
        after = (d == 1.0) & (least < HALO)
        return (d == 0.0) | before | after

    reach = (tile >= 0.0) & touches(dr, 0) & touches(dc, 1)
    kind = jnp.where(dr == 0.0, 1.0, jnp.where(dr < 0.0, 2.0, 3.0))
    codes[...] = jnp.where(reach, 4.0 * kind + dc + 1.0, 0.0).astype(jnp.int32)
    copy = pltpu.make_async_copy(codes, table, done)
    copy.start()
    copy.wait()


def add_half(parity, got_ref, total, codes, table, done, lists):
    sources, held, _, rays = got_ref.shape
    half = held - 1
    gather_codes(got_ref, codes, table, done)
    room = sources * half + BATCH

    def sort(source, counts):
        one, two, three = counts
        for k in range(half):
            code = table[source, parity * half + k]
            entry = (source * held + k) * 4 + (code & 3)
            kind = code >> 2
            lists[one] = entry
            lists[room + two] = entry
            lists[2 * room + three] = entry
            one = one + (kind == 1).astype(jnp.int32)
            two = two + (kind == 2).astype(jnp.int32)
            three = three + (kind == 3).astype(jnp.int32)
        return one, two, three

    zero = jnp.int32(0)
    counts = lax.fori_loop(0, sources, sort, (zero, zero, zero))

    def steps(extent, start):
        cell = lax.broadcasted_iota(jnp.int32, (extent, rays), 0) + start
        return cell.astype(jnp.float32).astype(jnp.bfloat16)

    order = lax.broadcasted_iota(jnp.int32, (WIDE, rays), 0)
    order = jnp.where(order < TILE, order, jnp.where(order < TILE + HALO, order - WIDE + HALO, order - HALO))
    across = order.astype(jnp.float32).astype(jnp.bfloat16)

    for kind, (rows, start, at, batch) in enumerate(
        ((TILE, 0, HALO, BATCH), (HALO, TILE - HALO, 0, BATCH), (HALO, 0, HALO + TILE, BATCH))
    ):
        count, base = counts[kind], kind * room
        for k in range(batch):
            lists[base + count + k] = 3
        down = steps(rows, start)

        def add(step, sums, base=base, down=down, batch=batch):
            for k in range(batch):
                entry = lists[base + step * batch + k]
                slot = entry >> 2
                block = got_ref[slot // held, slot % held]
                offset = (((entry & 3) - 1) * TILE).astype(jnp.float32)
                sums = sums + lax.dot_general(
                    hats(block[0:1, :], 0.0, down),
                    hats(block[1:2, :], offset, across),
                    (((1,), (1,)), ((), ())),
                    preferred_element_type=jnp.float32,
                )
            return sums

        turns = (count + batch - 1) // batch
        total[at : at + rows, :] = lax.fori_loop(0, turns, add, total[at : at + rows, :])


def first_kernel(got_ref, total_ref, codes, table, done, lists):
    total_ref[...] = jnp.zeros(total_ref.shape, jnp.float32)
    add_half(lax.axis_index("row") % 2, got_ref, total_ref, codes, table, done, lists)


def second_kernel(scale, got_ref, total_ref, pairs_ref, last_ref, out_ref,
                  total, left, codes, table, done, lists):
    total[...] = total_ref[...]
    add_half(1 - lax.axis_index("row") % 2, got_ref, total, codes, table, done, lists)
    own = total[:, :TILE].astype(jnp.bfloat16)
    side = total[:, TILE:].astype(jnp.bfloat16)
    for u in range(TURNS):
        left[:, u * TILE : (u + 1) * TILE] = own[u * STEP : u * STEP + LONG, :]
        at = TURNS * TILE + u * 2 * HALO
        left[:, at : at + 2 * HALO] = side[u * STEP : u * STEP + LONG, :]
    sums = jnp.dot(own[2 * HALO :, :], last_ref[:TILE, :], preferred_element_type=jnp.float32)
    sums = sums + jnp.dot(side[2 * HALO :, :], last_ref[TILE:, :], preferred_element_type=jnp.float32)
    for p in range(STEP // 2):
        both = jnp.dot(left[...], pairs_ref[p], preferred_element_type=jnp.float32)
        sums = sums + both[2 * p : 2 * p + TILE, :TILE]
        sums = sums + both[2 * p + 1 : 2 * p + 1 + TILE, TILE:]
    out_ref[...] = sums / scale


def packed(positions, destination):
    row_count, col_count = lax.axis_size("row"), lax.axis_size("col")
    tiles = row_count * col_count
    blocks, _, rays = positions.shape
    if blocks <= 12 * MOST:
        return pl.pallas_call(
            pack_kernel,
            out_shape=jax.ShapeDtypeStruct((tiles, blocks // 2 + 1, 2, rays), jnp.float32),
            in_specs=[VMEM, VMEM],
            out_specs=VMEM,
            scratch_shapes=[pltpu.VMEM((2, rays), jnp.float32)],
            compiler_params=LIMIT,
            name="pack",
        )(destination.T, positions)
    room = 12 * MOST
    targets = destination[:, 0]
    pair = jnp.arange(row_count // 2, dtype=jnp.int32)[:, None, None]
    col = jnp.arange(col_count, dtype=jnp.int32)[None, :, None]
    down = targets // col_count - 2 * pair
    over = targets % col_count - col
    near = (down >= -1) & (down <= 2) & (jnp.abs(over) <= 1)
    picked = jnp.argsort(jnp.logical_not(near).astype(jnp.int32), axis=2, stable=True)[:, :, :room]
    valid = jnp.take_along_axis(near, picked, axis=2)
    label = jnp.where(valid, targets[picked], -1).astype(jnp.float32)
    least, most = jnp.min(positions, axis=2)[picked], jnp.max(positions, axis=2)[picked]
    spare = ((0, 0), (0, 0), (0, LANES - room))
    meta = jnp.stack(
        [
            jnp.concatenate([jnp.pad(row, spare) for row in (label, least[..., 0], most[..., 0])], 2),
            jnp.concatenate([jnp.pad(row, spare) for row in (label, least[..., 1], most[..., 1])], 2),
        ],
        axis=2,
    )
    halves = positions[picked].reshape(row_count // 2, col_count, 2, room // 2, 2, rays)
    halves = jnp.transpose(halves, (0, 2, 1, 3, 4, 5))
    metas = jnp.broadcast_to(meta[:, None, :, None], halves.shape[:3] + (1, 2, rays))
    return jnp.concatenate([halves, metas], axis=3).reshape(tiles, room // 2 + 1, 2, rays)


def shards(positions, destination, profile):
    blocks, _, rays = positions.shape
    outgoing = packed(positions, destination)
    sources, held = outgoing.shape[0], outgoing.shape[1]
    mine = lax.all_to_all(outgoing, ("row", "col"), split_axis=0, concat_axis=0, tiled=True)
    other = lax.ppermute(mine, "row", [(i, i ^ 1) for i in range(lax.axis_size("row"))])
    pairs, last = pl.pallas_call(
        table_kernel,
        out_shape=(
            jax.ShapeDtypeStruct((STEP // 2, DEPTH, 2 * TILE), jnp.bfloat16),
            jax.ShapeDtypeStruct((WIDE, TILE), jnp.bfloat16),
        ),
        in_specs=[VMEM],
        out_specs=(VMEM, VMEM),
        compiler_params=LIMIT,
        cost_estimate=pl.CostEstimate(flops=10_000_000, bytes_accessed=6_000_000, transcendentals=0),
        name="table",
    )(profile)
    scratch = [
        pltpu.VMEM((sources, LANES), jnp.int32),
        pltpu.SMEM((sources, LANES), jnp.int32),
        pltpu.SemaphoreType.DMA,
        pltpu.SMEM((3 * (sources * (held - 1) + BATCH),), jnp.int32),
    ]
    total = pl.pallas_call(
        first_kernel,
        out_shape=jax.ShapeDtypeStruct((WIDE, WIDE), jnp.float32),
        in_specs=[VMEM],
        out_specs=VMEM,
        scratch_shapes=scratch,
        compiler_params=LIMIT,
        cost_estimate=pl.CostEstimate(flops=2_000_000_000, bytes_accessed=4_000_000, transcendentals=0),
        name="first",
    )(mine)
    return pl.pallas_call(
        functools.partial(second_kernel, blocks * rays / (TILE * TILE)),
        out_shape=jax.ShapeDtypeStruct((TILE, TILE), jnp.float32),
        in_specs=[VMEM] * 4,
        out_specs=VMEM,
        scratch_shapes=[
            pltpu.VMEM((WIDE, WIDE), jnp.float32),
            pltpu.VMEM((LONG, DEPTH), jnp.bfloat16),
        ] + scratch,
        compiler_params=LIMIT,
        name="second",
    )(other, total, pairs, last)


def solution(mesh):
    placed = (P(("maps", "row", "col"), None, None), P(("maps", "row", "col"), None), P())
    return jax.shard_map(
        shards, mesh=mesh, in_specs=placed, out_specs=P(("maps", "row"), "col"), check_vma=False
    )
```

```python
import functools

import jax
import jax.numpy as jnp
from jax import lax
from jax.experimental import pallas as pl
from jax.experimental.pallas import tpu as pltpu
from jax.sharding import PartitionSpec as P

TILE = 128
HALO = 32
MOST = 4
DISC = 2 * HALO + 1
STEP = 16
LONG = TILE + STEP
TURNS = 2 * HALO // STEP
WIDE = TILE + 2 * HALO
DEPTH = TURNS * WIDE
LANES = 128
BATCH = 8

VMEM = pl.BlockSpec(memory_space=pltpu.VMEM)


def place_kernel(dest_ref, rays_ref, out_ref, labels, coords):
    blocks = rays_ref.shape[0]
    rows = out_ref.shape[0]
    shape = (blocks, blocks)
    earlier = lax.broadcasted_iota(jnp.int32, shape, 0)
    later = lax.broadcasted_iota(jnp.int32, shape, 1)
    across = jnp.broadcast_to(dest_ref[...].astype(jnp.float32), shape)
    down = jnp.sum(jnp.where(earlier == later, across, 0.0), axis=1, keepdims=True)
    same = jnp.where((down == across) & (earlier < later), 1.0, 0.0)
    rank = jnp.sum(same, axis=0, keepdims=True)
    place = (dest_ref[...].astype(jnp.float32) * (2.0 * MOST) + rank).astype(jnp.int32)
    labels[0:1, :blocks] = place
    labels[0:1, blocks : 2 * blocks] = place + MOST
    for b in range(blocks):
        coords[b : b + 1, :] = rays_ref[b, 0:1, :]
        coords[blocks + b : blocks + b + 1, :] = rays_ref[b, 1:2, :]
    target = lax.broadcasted_iota(jnp.int32, (rows, 2 * blocks), 0)
    chosen = labels[0:1, : 2 * blocks] == target
    select = jnp.where(chosen, 1.0, 0.0).astype(jnp.bfloat16)
    rest = coords[...]
    total = jnp.where(jnp.sum(jnp.where(chosen, 1.0, 0.0), axis=1, keepdims=True) > 0.0, 0.0, -2.0)
    for _ in range(3):
        part = rest.astype(jnp.bfloat16)
        rest = rest - part.astype(jnp.float32)
        total = total + jnp.dot(select, part, preferred_element_type=jnp.float32)
    out_ref[...] = total


def table_kernel(profile_ref, pairs_ref, last_ref):
    a = lax.broadcasted_iota(jnp.int32, (DISC, DISC), 0) - HALO
    c = lax.broadcasted_iota(jnp.int32, (DISC, DISC), 1) - HALO
    weights = jnp.where(a * a + c * c <= HALO * HALO, profile_ref[...], 0.0)
    kernel = (weights / jnp.sum(weights)).astype(jnp.bfloat16)
    source = lax.broadcasted_iota(jnp.int32, (DISC, 2 * TILE), 0)
    target = lax.broadcasted_iota(jnp.int32, (DISC, 2 * TILE), 1)
    mirror = jnp.where((source + target) % (2 * TILE) == 0, 1.0, 0.0).astype(jnp.bfloat16)
    mirrored = jnp.dot(kernel, mirror, preferred_element_type=jnp.float32)

    def band(row, first, rows):
        wide = jnp.broadcast_to(mirrored[row : row + 1, :], (rows, 2 * TILE))
        rolled = pltpu.roll(wide, first, 1, stride=1, stride_axis=0)
        return rolled[:, :TILE].astype(jnp.bfloat16)

    for s in range(STEP):
        half = pl.ds((s % 2) * TILE, TILE)
        for u in range(TURNS):
            row = u * STEP + s
            pairs_ref[s // 2, pl.ds(u * TILE, TILE), half] = band(row, HALO, TILE)
            side = TURNS * TILE + u * 2 * HALO
            pairs_ref[s // 2, pl.ds(side, HALO), half] = band(row, 0, HALO)
            pairs_ref[s // 2, pl.ds(side + HALO, HALO), half] = band(row, HALO + TILE, HALO)
    last_ref[:TILE, :] = band(2 * HALO, HALO, TILE)
    last_ref[TILE : TILE + HALO, :] = band(2 * HALO, 0, HALO)
    last_ref[TILE + HALO :, :] = band(2 * HALO, HALO + TILE, HALO)


def hats(coords, cell):
    low = jnp.floor(coords)
    near = jnp.maximum(0.0, 1.0 - jnp.abs(coords - low)).astype(jnp.bfloat16)
    far = jnp.maximum(0.0, 1.0 - jnp.abs(coords - (low + 1.0))).astype(jnp.bfloat16)
    low = low.astype(jnp.bfloat16)
    zero = jnp.zeros((), jnp.bfloat16)
    one = jnp.ones((), jnp.bfloat16)
    return jnp.where(cell == low, near, jnp.where(cell == low + one, far, zero))


def deposit_kernel(rows_axis, cols_axis, rays_ref, tile_ref, send_ref, list_ref):
    sources, held, rays = rays_ref.shape
    slots = sources * MOST
    step = 4 * held
    lane = lax.broadcasted_iota(jnp.int32, (step, LANES), 1)
    place = lax.broadcasted_iota(jnp.int32, (step, LANES), 0)
    bit = place // held * MOST + place % held
    power = jnp.where((lane == 0) & (place % held < MOST), (1 << bit).astype(jnp.float32), 0.0)
    count, empty = jnp.int32(0), jnp.int32(0)
    for at in range(0, sources, 4):
        heads = rays_ref[at : at + 4, :, :LANES].reshape(step, LANES)
        mask = jnp.sum(jnp.where(heads > -1.0, power, 0.0)).astype(jnp.int32)
        for k in range(4 * MOST):
            filled = (mask >> k) & 1
            entry = (at + k // MOST) * held + k % MOST
            list_ref[count] = entry
            empty = jnp.where(filled == 1, empty, entry)
            count = count + filled
    for k in range(BATCH):
        list_ref[count + k] = empty

    cell = lax.broadcasted_iota(jnp.int32, (TILE, rays), 0).astype(jnp.float32)
    cell = cell.astype(jnp.bfloat16)

    def add(batch, total):
        firsts, seconds = [], []
        for k in range(BATCH):
            entry = list_ref[batch * BATCH + k]
            source, slot = entry // held, entry % held
            firsts.append(hats(rays_ref[source, pl.ds(slot, 1), :], cell))
            seconds.append(hats(rays_ref[source, pl.ds(slot + MOST, 1), :], cell))
        return total + lax.dot_general(
            jnp.concatenate(firsts, axis=1),
            jnp.concatenate(seconds, axis=1),
            (((1,), (1,)), ((), ())),
            preferred_element_type=jnp.float32,
        )

    batches = (count + BATCH - 1) // BATCH
    total = lax.fori_loop(0, batches, add, jnp.zeros((TILE, TILE), jnp.float32))
    tile = total.astype(jnp.bfloat16)
    turned = tile.astype(jnp.float32).T.astype(jnp.bfloat16)
    tile_ref[...] = tile
    row_count, col_count = lax.axis_size(rows_axis), lax.axis_size(cols_axis)
    row, col = lax.axis_index(rows_axis), lax.axis_index(cols_axis)
    low, high = slice(0, HALO), slice(TILE - HALO, TILE)
    for dr in (-1, 0, 1):
        for dc in (-1, 0, 1):
            if dr == 0 and dc == 0:
                continue
            if dr != 0:
                piece = tile[low if dr < 0 else high, :]
            else:
                piece = turned[low if dc < 0 else high, :]
            r, c = row + dr, col + dc

            @pl.when((r >= 0) & (r < row_count) & (c >= 0) & (c < col_count))
            def _(r=r, c=c, piece=piece):
                send_ref[r * col_count + c] = piece


def spread_kernel(rows_axis, cols_axis, scale, tile_ref, got_ref, pairs_ref, last_ref, out_ref,
                  own, side, left):
    row_count, col_count = lax.axis_size(rows_axis), lax.axis_size(cols_axis)
    row, col = lax.axis_index(rows_axis), lax.axis_index(cols_axis)

    def fetch(dr, dc):
        r, c = row + dr, col + dc
        inside = (r >= 0) & (r < row_count) & (c >= 0) & (c < col_count)
        index = jnp.where(inside, r * col_count + c, 0)
        piece = got_ref[index].astype(jnp.float32)
        return jnp.where(inside, piece, 0.0)

    own[:HALO, :] = fetch(-1, 0).astype(jnp.bfloat16)
    own[HALO : HALO + TILE, :] = tile_ref[...]
    own[HALO + TILE :, :] = fetch(1, 0).astype(jnp.bfloat16)
    for dr, at in ((-1, 0), (1, HALO + TILE)):
        lower = fetch(dr, -1)[:, TILE - HALO :]
        upper = fetch(dr, 1)[:, :HALO]
        side[at : at + HALO, :] = jnp.concatenate([lower, upper], axis=1).astype(jnp.bfloat16)
    strips = jnp.concatenate([fetch(0, -1), fetch(0, 1)], axis=0).T
    side[HALO : HALO + TILE, :] = strips.astype(jnp.bfloat16)
    for u in range(TURNS):
        left[:, u * TILE : (u + 1) * TILE] = own[u * STEP : u * STEP + LONG, :]
        at = TURNS * TILE + u * 2 * HALO
        left[:, at : at + 2 * HALO] = side[u * STEP : u * STEP + LONG, :]
    total = jnp.dot(own[2 * HALO :, :], last_ref[:TILE, :], preferred_element_type=jnp.float32)
    total = total + jnp.dot(
        side[2 * HALO :, :], last_ref[TILE:, :], preferred_element_type=jnp.float32
    )
    for p in range(STEP // 2):
        both = jnp.dot(left[...], pairs_ref[p], preferred_element_type=jnp.float32)
        total = total + both[2 * p : 2 * p + TILE, :TILE]
        total = total + both[2 * p + 1 : 2 * p + 1 + TILE, TILE:]
    out_ref[...] = total / scale


def shards(positions, destination, profile):
    tiles = lax.axis_size("row") * lax.axis_size("col")
    blocks, _, rays = positions.shape
    limit = pltpu.CompilerParams(vmem_limit_bytes=32 * 1024 * 1024)
    outgoing = pl.pallas_call(
        place_kernel,
        out_shape=jax.ShapeDtypeStruct((tiles * 2 * MOST, rays), jnp.float32),
        in_specs=[VMEM, VMEM],
        out_specs=VMEM,
        scratch_shapes=[
            pltpu.VMEM((1, max(LANES, 2 * blocks)), jnp.int32),
            pltpu.VMEM((2 * blocks, rays), jnp.float32),
        ],
        compiler_params=pltpu.CompilerParams(vmem_limit_bytes=56 * 1024 * 1024),
        name="place",
    )(destination.T, positions)
    received = lax.all_to_all(
        outgoing.reshape(tiles, 2 * MOST, rays), ("row", "col"), split_axis=0, concat_axis=0, tiled=True
    )
    pairs, last = pl.pallas_call(
        table_kernel,
        out_shape=(
            jax.ShapeDtypeStruct((STEP // 2, DEPTH, 2 * TILE), jnp.bfloat16),
            jax.ShapeDtypeStruct((WIDE, TILE), jnp.bfloat16),
        ),
        in_specs=[VMEM],
        out_specs=(VMEM, VMEM),
        compiler_params=limit,
        cost_estimate=pl.CostEstimate(flops=10_000_000, bytes_accessed=6_000_000, transcendentals=0),
        name="table",
    )(profile)
    received, pairs, last = lax.optimization_barrier((received, pairs, last))
    tile, send = pl.pallas_call(
        functools.partial(deposit_kernel, "row", "col"),
        out_shape=(
            jax.ShapeDtypeStruct((TILE, TILE), jnp.bfloat16),
            jax.ShapeDtypeStruct((tiles, HALO, TILE), jnp.bfloat16),
        ),
        in_specs=[VMEM],
        out_specs=(VMEM, VMEM),
        scratch_shapes=[pltpu.SMEM((tiles * MOST + BATCH,), jnp.int32)],
        compiler_params=limit,
        name="deposit",
    )(received)
    got = lax.all_to_all(send, ("row", "col"), split_axis=0, concat_axis=0, tiled=True)
    scale = blocks * rays / (TILE * TILE)
    return pl.pallas_call(
        functools.partial(spread_kernel, "row", "col", scale),
        out_shape=jax.ShapeDtypeStruct((TILE, TILE), jnp.float32),
        in_specs=[VMEM, VMEM, VMEM, VMEM],
        out_specs=VMEM,
        scratch_shapes=[
            pltpu.VMEM((WIDE, TILE), jnp.bfloat16),
            pltpu.VMEM((WIDE, 2 * HALO), jnp.bfloat16),
            pltpu.VMEM((LONG, DEPTH), jnp.bfloat16),
        ],
        compiler_params=limit,
        name="spread",
    )(tile, got, pairs, last)


def solution(mesh):
    placed = (P(("maps", "row", "col"), None, None), P(("maps", "row", "col"), None), P())
    return jax.shard_map(
        shards, mesh=mesh, in_specs=placed, out_specs=P(("maps", "row"), "col"), check_vma=False
    )
```

```python
import functools

import jax
import jax.numpy as jnp
from jax import lax
from jax.experimental import pallas as pl
from jax.experimental.pallas import tpu as pltpu
from jax.sharding import PartitionSpec as P

TILE = 128
HALO = 32
MOST = 4
DISC = 2 * HALO + 1
STEP = 16
LONG = TILE + STEP
TURNS = 2 * HALO // STEP
WIDE = TILE + 2 * HALO
DEPTH = TURNS * WIDE
LANES = 128
BATCH = 8
ROOM = 5
NONE = 64.0

VMEM = pl.BlockSpec(memory_space=pltpu.VMEM)
SMEM = pl.BlockSpec(memory_space=pltpu.SMEM)
LIMIT = pltpu.CompilerParams(vmem_limit_bytes=32 * 1024 * 1024)


def touches(distance, least, most):
    before = (distance == -1.0) & (most > TILE - HALO - 1.0)
    after = (distance == 1.0) & (least < HALO)
    return (distance == 0.0) | before | after


def pack_kernel(turn_ref, dest_ref, rays_ref, out_ref, labels, parts):
    blocks, _, rays = rays_ref.shape
    tiles = out_ref.shape[0] // 8
    row_count, col_count = lax.axis_size("row"), lax.axis_size("col")
    lane = lax.broadcasted_iota(jnp.int32, (blocks, LANES), 1)
    place = lax.broadcasted_iota(jnp.int32, (blocks, LANES), 0)

    def laid(column):
        return jnp.sum(jnp.where(lane == place, column, 0.0), axis=0, keepdims=True)

    labels[...] = jnp.full(labels.shape, -1.0, jnp.float32)
    labels[0:1, :blocks] = dest_ref[...].astype(jnp.float32)
    label = labels[...]
    first, second = rays_ref[:, 0, :], rays_ref[:, 1, :]
    least_row, most_row = laid(jnp.min(first, 1, keepdims=True)), laid(jnp.max(first, 1, keepdims=True))
    least_col, most_col = laid(jnp.min(second, 1, keepdims=True)), laid(jnp.max(second, 1, keepdims=True))

    tile = lax.broadcasted_iota(jnp.int32, (tiles, LANES), 0)
    lane = lax.broadcasted_iota(jnp.int32, (tiles, LANES), 1)
    odd = (tile // col_count % 2).astype(jnp.float32)
    base = (tile // col_count).astype(jnp.float32) - odd
    label_row = jnp.floor((label + 0.5) / col_count)
    dc = label - label_row * col_count - (tile % col_count).astype(jnp.float32)
    aside = touches(dc, least_col, most_col) & (label >= 0.0)

    def coded(row):
        dr = label_row - row
        reach = aside & touches(dr, least_row, most_row)
        kind = jnp.where(dr == 0.0, 0.0, 2.0) + jnp.where(dc == 0.0, 0.0, 1.0)
        return reach, jnp.where(reach, 16.0 * kind + 4.0 * (dr + 1.0) + dc + 1.0, NONE)

    reach_even, code_even = coded(base)
    reach_odd, code_odd = coded(base + 1.0)
    reach = jnp.where(reach_even | reach_odd, 1.0, 0.0)
    earlier = lax.broadcasted_iota(jnp.int32, (LANES, LANES), 0)
    later = lax.broadcasted_iota(jnp.int32, (LANES, LANES), 1)
    before = jnp.where(earlier < later, 1.0, 0.0).astype(jnp.bfloat16)
    rank = jnp.dot(reach.astype(jnp.bfloat16), before, preferred_element_type=jnp.float32)
    most = jnp.max(jnp.max((rank + 1.0) * reach, axis=1, keepdims=True), axis=0, keepdims=True)
    turns = jnp.floor((most + (2.0 * ROOM - 0.5)) / (2.0 * ROOM))
    rank = rank - 2.0 * ROOM * turn_ref[0].astype(jnp.float32)
    slot = jnp.floor((rank - odd) * 0.5)
    mine = (reach > 0.0) & (slot * 2.0 + odd == rank) & (slot >= 0.0) & (slot < ROOM)
    slot = jnp.where(mine, slot, -1.0)

    meta = jnp.where(lane == 16, turns, NONE)
    for k in range(ROOM):
        for at, code in ((k, code_even), (8 + k, code_odd)):
            found = jnp.sum(jnp.where(slot == k, code - NONE, 0.0), axis=1, keepdims=True) + NONE
            meta = jnp.where(lane == at, found, meta)

    width = parts.shape[0]
    parts[...] = jnp.zeros(parts.shape, jnp.float32)
    parts[:blocks, :rays] = first
    parts[:blocks, rays:] = second[:, :LANES]
    parts[blocks : 2 * blocks, : 2 * LANES] = second[:, LANES:]
    parts[2 * blocks : 3 * blocks, 2 * LANES :] = second[:, LANES:]
    parts[3 * blocks : 3 * blocks + tiles, 2 * LANES : 3 * LANES] = meta

    source = lax.broadcasted_iota(jnp.int32, (LANES, width), 0)
    target = lax.broadcasted_iota(jnp.int32, (LANES, width), 1)
    wider = jnp.where((target % blocks == source) & (target < 3 * blocks), 1.0, 0.0)
    slot = jnp.dot(
        slot.astype(jnp.bfloat16), wider.astype(jnp.bfloat16), preferred_element_type=jnp.float32
    )
    source = lax.broadcasted_iota(jnp.int32, (8 * tiles, tiles), 1)
    target = lax.broadcasted_iota(jnp.int32, (8 * tiles, tiles), 0)
    taller = jnp.where(target // 8 == source, 1.0, 0.0).astype(jnp.bfloat16)
    slot = jnp.dot(taller, slot.astype(jnp.bfloat16), preferred_element_type=jnp.float32)
    row = lax.broadcasted_iota(jnp.int32, (8 * tiles, width), 0)
    group = lax.broadcasted_iota(jnp.int32, (8 * tiles, width), 1)
    within = row % 8
    low = (2 * (within - ROOM)).astype(jnp.float32)
    head = (group < blocks) & (within < ROOM) & (slot == within.astype(jnp.float32))
    even = (group >= blocks) & (group < 2 * blocks) & (within >= ROOM) & (slot == low)
    uneven = (group >= 2 * blocks) & (group < 3 * blocks) & (within >= ROOM) & (slot == low + 1.0)
    codes = (group - 3 * blocks == row // 8) & (group >= 3 * blocks) & (within == 7)
    select = jnp.where(head | even | uneven | codes, 1.0, 0.0).astype(jnp.bfloat16)
    rest = parts[...]
    total = jnp.zeros(out_ref.shape, jnp.float32)
    for _ in range(3):
        part = rest.astype(jnp.bfloat16)
        rest = rest - part.astype(jnp.float32)
        total = total + jnp.dot(select, part, preferred_element_type=jnp.float32)
    out_ref[...] = total


def table_kernel(profile_ref, pairs_ref, last_ref):
    a = lax.broadcasted_iota(jnp.int32, (DISC, DISC), 0) - HALO
    c = lax.broadcasted_iota(jnp.int32, (DISC, DISC), 1) - HALO
    weights = jnp.where(a * a + c * c <= HALO * HALO, profile_ref[...], 0.0)
    kernel = (weights / jnp.sum(weights)).astype(jnp.bfloat16)
    source = lax.broadcasted_iota(jnp.int32, (DISC, 2 * TILE), 0)
    target = lax.broadcasted_iota(jnp.int32, (DISC, 2 * TILE), 1)
    mirror = jnp.where((source + target) % (2 * TILE) == 0, 1.0, 0.0).astype(jnp.bfloat16)
    mirrored = jnp.dot(kernel, mirror, preferred_element_type=jnp.float32)

    def band(row, first, rows):
        wide = jnp.broadcast_to(mirrored[row : row + 1, :], (rows, 2 * TILE))
        rolled = pltpu.roll(wide, first, 1, stride=1, stride_axis=0)
        return rolled[:, :TILE].astype(jnp.bfloat16)

    for s in range(STEP):
        half = pl.ds((s % 2) * TILE, TILE)
        for u in range(TURNS):
            row = u * STEP + s
            pairs_ref[s // 2, pl.ds(u * TILE, TILE), half] = band(row, HALO, TILE)
            side = TURNS * TILE + u * 2 * HALO
            pairs_ref[s // 2, pl.ds(side, HALO), half] = band(row, 0, HALO)
            pairs_ref[s // 2, pl.ds(side + HALO, HALO), half] = band(row, HALO + TILE, HALO)
    last_ref[:TILE, :] = band(2 * HALO, HALO, TILE)
    last_ref[TILE : TILE + HALO, :] = band(2 * HALO, 0, HALO)
    last_ref[TILE + HALO :, :] = band(2 * HALO, HALO + TILE, HALO)


def hats(coords, offset, cell):
    low = jnp.floor(coords)
    near = jnp.maximum(0.0, 1.0 - jnp.abs(coords - low)).astype(jnp.bfloat16)
    far = jnp.maximum(0.0, 1.0 - jnp.abs(coords - (low + 1.0))).astype(jnp.bfloat16)
    low = low + offset
    here, there = low.astype(jnp.bfloat16), (low + 1.0).astype(jnp.bfloat16)
    zero = jnp.zeros((), jnp.bfloat16)
    return jnp.where(cell == here, near, jnp.where(cell == there, far, zero))


def add_half(got_ref, total, codes, table, done, lists):
    sources = got_ref.shape[0]
    rays = 3 * LANES
    codes[...] = got_ref[:, 7, 2 * LANES : 3 * LANES].astype(jnp.int32)
    copy = pltpu.make_async_copy(codes, table, done)
    copy.start()
    copy.wait()
    room = sources * ROOM + BATCH
    first_lane = lax.axis_index("row") % 2 * 8

    def sort(source, carry):
        turns, counts = carry[0], list(carry[1:])
        turns = jnp.maximum(turns, table[source, 16])
        for k in range(ROOM):
            code = table[source, first_lane + k]
            entry = (source * 8 + k) * 16 + (code & 15)
            kind = code >> 4
            for j in range(4):
                lists[j * room + counts[j]] = entry
                counts[j] = counts[j] + (kind == j).astype(jnp.int32)
        return (turns, *counts)

    turns, *counts = lax.fori_loop(0, sources, sort, (jnp.int32(0),) * 5)

    def cells(extent):
        cell = lax.broadcasted_iota(jnp.int32, (extent, rays), 0)
        if extent != TILE:
            cell = jnp.where(cell < HALO, cell - HALO, cell + (TILE - HALO))
        return cell.astype(jnp.float32).astype(jnp.bfloat16)

    own, halo = cells(TILE), cells(2 * HALO)
    inner, outer = slice(0, TILE), slice(TILE, WIDE)
    for kind, (rows, cols, down, across, batch) in enumerate(
        (
            (inner, inner, own, own, BATCH),
            (inner, outer, own, halo, BATCH // 2),
            (outer, inner, halo, own, BATCH // 2),
            (outer, outer, halo, halo, BATCH // 2),
        )
    ):
        count, base = counts[kind], kind * room
        for k in range(batch):
            lists[base + count + k] = 15

        def add(step, sums, base=base, down=down, across=across, batch=batch):
            firsts, seconds = [], []
            for k in range(batch):
                entry = lists[base + step * batch + k]
                source, slot = entry >> 7, (entry >> 4) & 7
                row_offset = ((((entry >> 2) & 3) - 1) * TILE).astype(jnp.float32)
                col_offset = (((entry & 3) - 1) * TILE).astype(jnp.float32)
                head = got_ref[source, pl.ds(slot, 1), :]
                tail = got_ref[source, pl.ds(ROOM + (slot >> 1), 1), :]
                tail = jnp.where((slot & 1) == 1, tail[:, 2 * LANES :], tail[:, : 2 * LANES])
                second = jnp.concatenate([head[:, rays:], tail], axis=1)
                firsts.append(hats(head[:, :rays], row_offset, down))
                seconds.append(hats(second, col_offset, across))
            return sums + lax.dot_general(
                jnp.concatenate(firsts, axis=1),
                jnp.concatenate(seconds, axis=1),
                (((1,), (1,)), ((), ())),
                preferred_element_type=jnp.float32,
            )

        total[rows, cols] = lax.fori_loop(0, (count + batch - 1) // batch, add, total[rows, cols])
    return turns


def first_kernel(got_ref, before_ref, total_ref, turns_ref, *scratch):
    if before_ref is None:
        total_ref[...] = jnp.zeros(total_ref.shape, jnp.float32)
    else:
        total_ref[...] = before_ref[...]
    turns_ref[0] = add_half(got_ref, total_ref, *scratch)


def second_kernel(scale, got_ref, before_ref, pairs_ref, last_ref, out_ref, total, left, *scratch):
    total[...] = before_ref[...]
    add_half(got_ref, total, *scratch)
    cells = total[...].astype(jnp.bfloat16)
    cells = jnp.concatenate([cells[TILE : TILE + HALO], cells[:TILE], cells[TILE + HALO :]], axis=0)
    own, side = cells[:, :TILE], cells[:, TILE:]
    for u in range(TURNS):
        left[:, u * TILE : (u + 1) * TILE] = own[u * STEP : u * STEP + LONG, :]
        at = TURNS * TILE + u * 2 * HALO
        left[:, at : at + 2 * HALO] = side[u * STEP : u * STEP + LONG, :]
    sums = jnp.dot(own[2 * HALO :, :], last_ref[:TILE, :], preferred_element_type=jnp.float32)
    sums = sums + jnp.dot(side[2 * HALO :, :], last_ref[TILE:, :], preferred_element_type=jnp.float32)
    for p in range(STEP // 2):
        both = jnp.dot(left[...], pairs_ref[p], preferred_element_type=jnp.float32)
        sums = sums + both[2 * p : 2 * p + TILE, :TILE]
        sums = sums + both[2 * p + 1 : 2 * p + 1 + TILE, TILE:]
    out_ref[...] = sums / scale


def shards(positions, destination, profile):
    blocks, _, rays = positions.shape
    row_count, col_count = lax.axis_size("row"), lax.axis_size("col")
    tiles = row_count * col_count
    width = -(-(3 * blocks + tiles) // LANES) * LANES

    def exchange(turn):
        outgoing = pl.pallas_call(
            pack_kernel,
            out_shape=jax.ShapeDtypeStruct((8 * tiles, rays + LANES), jnp.float32),
            in_specs=[SMEM, VMEM, VMEM],
            out_specs=VMEM,
            scratch_shapes=[
                pltpu.VMEM((1, LANES), jnp.float32),
                pltpu.VMEM((width, rays + LANES), jnp.float32),
            ],
            compiler_params=pltpu.CompilerParams(vmem_limit_bytes=56 * 1024 * 1024),
            name="pack",
        )(turn, destination.T, positions)
        return lax.all_to_all(
            outgoing.reshape(tiles, 8, rays + LANES), ("row", "col"), split_axis=0, concat_axis=0, tiled=True
        )

    scratch = [
        pltpu.VMEM((tiles, LANES), jnp.int32),
        pltpu.SMEM((tiles, LANES), jnp.int32),
        pltpu.SemaphoreType.DMA,
        pltpu.SMEM((4 * (tiles * ROOM + BATCH),), jnp.int32),
    ]

    def deposit(mine, before, pairs, last):
        other = lax.ppermute(mine, "row", [(i, i ^ 1) for i in range(row_count)])
        kernel, given = first_kernel, (mine, before)
        if before is None:
            kernel, given = lambda got, *refs: first_kernel(got, None, *refs), (mine,)
        total, turns = pl.pallas_call(
            kernel,
            out_shape=(
                jax.ShapeDtypeStruct((WIDE, WIDE), jnp.float32),
                jax.ShapeDtypeStruct((1,), jnp.int32),
            ),
            in_specs=[VMEM] * len(given),
            out_specs=(VMEM, SMEM),
            scratch_shapes=scratch,
            compiler_params=LIMIT,
            cost_estimate=pl.CostEstimate(flops=2_000_000_000, bytes_accessed=4_000_000, transcendentals=0),
            name="first",
        )(*given)
        out, total = pl.pallas_call(
            functools.partial(second_kernel, blocks * rays / (TILE * TILE)),
            out_shape=(
                jax.ShapeDtypeStruct((TILE, TILE), jnp.float32),
                jax.ShapeDtypeStruct((WIDE, WIDE), jnp.float32),
            ),
            in_specs=[VMEM] * 4,
            out_specs=(VMEM, VMEM),
            scratch_shapes=[pltpu.VMEM((LONG, DEPTH), jnp.bfloat16)] + scratch,
            compiler_params=LIMIT,
            name="second",
        )(other, total, pairs, last)
        return out, total, turns[0]

    mine = exchange(jnp.zeros((1,), jnp.int32))
    pairs, last = pl.pallas_call(
        table_kernel,
        out_shape=(
            jax.ShapeDtypeStruct((STEP // 2, DEPTH, 2 * TILE), jnp.bfloat16),
            jax.ShapeDtypeStruct((WIDE, TILE), jnp.bfloat16),
        ),
        in_specs=[VMEM],
        out_specs=(VMEM, VMEM),
        compiler_params=LIMIT,
        cost_estimate=pl.CostEstimate(flops=10_000_000, bytes_accessed=6_000_000, transcendentals=0),
        name="table",
    )(profile)
    mine, pairs, last = lax.optimization_barrier((mine, pairs, last))
    out, total, turns = deposit(mine, None, pairs, last)

    def more(state):
        turn, _, total = state
        out, total, _ = deposit(exchange(jnp.full((1,), turn, jnp.int32)), total, pairs, last)
        return turn + 1, out, total

    return lax.while_loop(lambda state: state[0] < turns, more, (jnp.int32(1), out, total))[1]


def solution(mesh):
    placed = (P(("maps", "row", "col"), None, None), P(("maps", "row", "col"), None), P())
    return jax.shard_map(
        shards, mesh=mesh, in_specs=placed, out_specs=P(("maps", "row"), "col"), check_vma=False
    )
```

```python
import functools

import jax
import jax.numpy as jnp
from jax import lax
from jax.experimental import pallas as pl
from jax.experimental.pallas import tpu as pltpu
from jax.sharding import PartitionSpec as P

TILE = 128
HALO = 32
MOST = 4
DISC = 2 * HALO + 1
STEP = 16
LONG = TILE + STEP
TURNS = 2 * HALO // STEP
WIDE = TILE + 2 * HALO
DEPTH = TURNS * WIDE
LANES = 128
BATCH = 8
ROOM = 5
NONE = 64.0

VMEM = pl.BlockSpec(memory_space=pltpu.VMEM)
SMEM = pl.BlockSpec(memory_space=pltpu.SMEM)
LIMIT = pltpu.CompilerParams(vmem_limit_bytes=32 * 1024 * 1024)


def touches(distance, least, most):
    before = (distance == -1.0) & (most > TILE - HALO - 1.0)
    after = (distance == 1.0) & (least < HALO)
    return (distance == 0.0) | before | after


def pack_kernel(turn_ref, dest_ref, rays_ref, out_ref, labels, parts):
    blocks, _, rays = rays_ref.shape
    tiles = out_ref.shape[0] // 8
    row_count, col_count = lax.axis_size("row"), lax.axis_size("col")
    lane = lax.broadcasted_iota(jnp.int32, (blocks, LANES), 1)
    place = lax.broadcasted_iota(jnp.int32, (blocks, LANES), 0)

    def laid(column):
        return jnp.sum(jnp.where(lane == place, column, 0.0), axis=0, keepdims=True)

    labels[...] = jnp.full(labels.shape, -1.0, jnp.float32)
    labels[0:1, :blocks] = dest_ref[...].astype(jnp.float32)
    label = labels[...]
    first, second = rays_ref[:, 0, :], rays_ref[:, 1, :]
    least_row, most_row = laid(jnp.min(first, 1, keepdims=True)), laid(jnp.max(first, 1, keepdims=True))
    least_col, most_col = laid(jnp.min(second, 1, keepdims=True)), laid(jnp.max(second, 1, keepdims=True))

    tile = lax.broadcasted_iota(jnp.int32, (tiles, LANES), 0)
    lane = lax.broadcasted_iota(jnp.int32, (tiles, LANES), 1)
    odd = (tile // col_count % 2).astype(jnp.float32)
    base = (tile // col_count).astype(jnp.float32) - odd
    label_row = jnp.floor((label + 0.5) / col_count)
    dc = label - label_row * col_count - (tile % col_count).astype(jnp.float32)
    aside = touches(dc, least_col, most_col) & (label >= 0.0)

    def coded(row):
        dr = label_row - row
        reach = aside & touches(dr, least_row, most_row)
        kind = jnp.where(dr == 0.0, 0.0, 2.0) + jnp.where(dc == 0.0, 0.0, 1.0)
        return reach, jnp.where(reach, 16.0 * kind + 4.0 * (dr + 1.0) + dc + 1.0, NONE)

    reach_even, code_even = coded(base)
    reach_odd, code_odd = coded(base + 1.0)
    reach = jnp.where(reach_even | reach_odd, 1.0, 0.0)
    earlier = lax.broadcasted_iota(jnp.int32, (LANES, LANES), 0)
    later = lax.broadcasted_iota(jnp.int32, (LANES, LANES), 1)
    before = jnp.where(earlier < later, 1.0, 0.0).astype(jnp.bfloat16)
    rank = jnp.dot(reach.astype(jnp.bfloat16), before, preferred_element_type=jnp.float32)
    most = jnp.max(jnp.max((rank + 1.0) * reach, axis=1, keepdims=True), axis=0, keepdims=True)
    turns = jnp.floor((most + (2.0 * ROOM - 0.5)) / (2.0 * ROOM))
    rank = rank - 2.0 * ROOM * turn_ref[0].astype(jnp.float32)
    slot = jnp.floor((rank - odd) * 0.5)
    mine = (reach > 0.0) & (slot * 2.0 + odd == rank) & (slot >= 0.0) & (slot < ROOM)
    slot = jnp.where(mine, slot, -1.0)

    meta = jnp.where(lane == 16, turns, NONE)
    for k in range(ROOM):
        for at, code in ((k, code_even), (8 + k, code_odd)):
            found = jnp.sum(jnp.where(slot == k, code - NONE, 0.0), axis=1, keepdims=True) + NONE
            meta = jnp.where(lane == at, found, meta)

    width = parts.shape[0]
    parts[...] = jnp.zeros(parts.shape, jnp.float32)
    parts[:blocks, :rays] = first
    parts[:blocks, rays:] = second[:, :LANES]
    parts[blocks : 2 * blocks, : 2 * LANES] = second[:, LANES:]
    parts[2 * blocks : 3 * blocks, 2 * LANES :] = second[:, LANES:]
    parts[3 * blocks : 3 * blocks + tiles, 2 * LANES : 3 * LANES] = meta

    source = lax.broadcasted_iota(jnp.int32, (LANES, width), 0)
    target = lax.broadcasted_iota(jnp.int32, (LANES, width), 1)
    wider = jnp.where((target % blocks == source) & (target < 3 * blocks), 1.0, 0.0)
    slot = jnp.dot(
        slot.astype(jnp.bfloat16), wider.astype(jnp.bfloat16), preferred_element_type=jnp.float32
    )
    source = lax.broadcasted_iota(jnp.int32, (8 * tiles, tiles), 1)
    target = lax.broadcasted_iota(jnp.int32, (8 * tiles, tiles), 0)
    taller = jnp.where(target // 8 == source, 1.0, 0.0).astype(jnp.bfloat16)
    slot = jnp.dot(taller, slot.astype(jnp.bfloat16), preferred_element_type=jnp.float32)
    row = lax.broadcasted_iota(jnp.int32, (8 * tiles, width), 0)
    group = lax.broadcasted_iota(jnp.int32, (8 * tiles, width), 1)
    within = row % 8
    low = (2 * (within - ROOM)).astype(jnp.float32)
    head = (group < blocks) & (within < ROOM) & (slot == within.astype(jnp.float32))
    even = (group >= blocks) & (group < 2 * blocks) & (within >= ROOM) & (slot == low)
    uneven = (group >= 2 * blocks) & (group < 3 * blocks) & (within >= ROOM) & (slot == low + 1.0)
    codes = (group - 3 * blocks == row // 8) & (group >= 3 * blocks) & (within == 7)
    select = jnp.where(head | even | uneven | codes, 1.0, 0.0).astype(jnp.bfloat16)
    rest = parts[...]
    total = jnp.zeros(out_ref.shape, jnp.float32)
    for _ in range(3):
        part = rest.astype(jnp.bfloat16)
        rest = rest - part.astype(jnp.float32)
        total = total + jnp.dot(select, part, preferred_element_type=jnp.float32)
    out_ref[...] = total


def table_kernel(profile_ref, pairs_ref, last_ref):
    a = lax.broadcasted_iota(jnp.int32, (DISC, DISC), 0) - HALO
    c = lax.broadcasted_iota(jnp.int32, (DISC, DISC), 1) - HALO
    weights = jnp.where(a * a + c * c <= HALO * HALO, profile_ref[...], 0.0)
    kernel = (weights / jnp.sum(weights)).astype(jnp.bfloat16)
    source = lax.broadcasted_iota(jnp.int32, (DISC, 2 * TILE), 0)
    target = lax.broadcasted_iota(jnp.int32, (DISC, 2 * TILE), 1)
    mirror = jnp.where((source + target) % (2 * TILE) == 0, 1.0, 0.0).astype(jnp.bfloat16)
    mirrored = jnp.dot(kernel, mirror, preferred_element_type=jnp.float32)

    def band(row, first, rows):
        wide = jnp.broadcast_to(mirrored[row : row + 1, :], (rows, 2 * TILE))
        rolled = pltpu.roll(wide, first, 1, stride=1, stride_axis=0)
        return rolled[:, :TILE].astype(jnp.bfloat16)

    for s in range(STEP):
        half = pl.ds((s % 2) * TILE, TILE)
        for u in range(TURNS):
            row = u * STEP + s
            pairs_ref[s // 2, pl.ds(u * TILE, TILE), half] = band(row, HALO, TILE)
            side = TURNS * TILE + u * 2 * HALO
            pairs_ref[s // 2, pl.ds(side, HALO), half] = band(row, 0, HALO)
            pairs_ref[s // 2, pl.ds(side + HALO, HALO), half] = band(row, HALO + TILE, HALO)
    last_ref[:TILE, :] = band(2 * HALO, HALO, TILE)
    last_ref[TILE : TILE + HALO, :] = band(2 * HALO, 0, HALO)
    last_ref[TILE + HALO :, :] = band(2 * HALO, HALO + TILE, HALO)


def hats(row, cell):
    near, far, here, there = (value.astype(jnp.bfloat16) for value in row)
    zero = jnp.zeros((), jnp.bfloat16)
    return jnp.maximum(zero, jnp.minimum((cell - here) + near, (there - cell) + far))


def add_half(got_ref, total, codes, table, done, lists, stage, facts):
    sources = got_ref.shape[0]
    rays = 3 * LANES
    codes[...] = got_ref[:, 7, 2 * LANES : 3 * LANES].astype(jnp.int32)
    copy = pltpu.make_async_copy(codes, table, done)
    copy.start()
    copy.wait()
    room = sources * ROOM + BATCH
    first_lane = lax.axis_index("row") % 2 * 8

    def sort(source, carry):
        counts = list(carry)
        for k in range(ROOM):
            code = table[source, first_lane + k]
            entry = (source * 8 + k) * 16 + (code & 15)
            kind = code >> 4
            for j in range(4):
                lists[j * room + counts[j]] = entry
                counts[j] = counts[j] + (kind == j).astype(jnp.int32)
        return tuple(counts)

    counts = lax.fori_loop(0, sources, sort, (jnp.int32(0),) * 4)

    def cells(extent):
        cell = lax.broadcasted_iota(jnp.int32, (extent, rays), 0)
        if extent != TILE:
            cell = jnp.where(cell < HALO, cell - HALO, cell + (TILE - HALO))
        return (2 * cell).astype(jnp.float32).astype(jnp.bfloat16)

    own, halo = cells(TILE), cells(2 * HALO)
    inner, outer = slice(0, TILE), slice(TILE, WIDE)
    for kind, (rows, cols, down, across, batch) in enumerate(
        (
            (inner, inner, own, own, BATCH),
            (inner, outer, own, halo, BATCH // 2),
            (outer, inner, halo, own, BATCH // 2),
            (outer, outer, halo, halo, BATCH // 2),
        )
    ):
        count, base = counts[kind], kind * room
        for k in range(batch):
            lists[base + count + k] = 15

        def add(step, sums, base=base, down=down, across=across, batch=batch):
            for k in range(batch):
                entry = lists[base + step * batch + k]
                source, slot = entry >> 7, (entry >> 4) & 7
                row_offset = ((((entry >> 2) & 3) - 1) * (2 * TILE)).astype(jnp.float32)
                col_offset = (((entry & 3) - 1) * (2 * TILE)).astype(jnp.float32)
                head = got_ref[source, pl.ds(slot, 1), :]
                tail = got_ref[source, pl.ds(ROOM + (slot >> 1), 1), :]
                stage[0, k : k + 1, :] = head[:, :rays]
                stage[1, k : k + 1, :LANES] = head[:, rays:]
                stage[1, k : k + 1, LANES:] = jnp.where(
                    (slot & 1) == 1, tail[:, 2 * LANES :], tail[:, : 2 * LANES]
                )
                stage[2, k : k + 1, :] = jnp.full((1, rays), row_offset)
                stage[3, k : k + 1, :] = jnp.full((1, rays), col_offset)
            for axis in range(2):
                coords = stage[axis]
                low = jnp.floor(coords)
                facts[4 * axis] = 1.0 - (coords - low)
                facts[4 * axis + 1] = 1.0 - ((low + 1.0) - coords)
                here = 2.0 * low + stage[2 + axis]
                facts[4 * axis + 2] = here
                facts[4 * axis + 3] = here + 2.0
            firsts, seconds = [], []
            for k in range(batch):
                row = [facts[j, k : k + 1, :] for j in range(8)]
                firsts.append(hats(row[:4], down))
                seconds.append(hats(row[4:], across))
            return sums + lax.dot_general(
                jnp.concatenate(firsts, axis=1),
                jnp.concatenate(seconds, axis=1),
                (((1,), (1,)), ((), ())),
                preferred_element_type=jnp.float32,
            )

        total[rows, cols] = lax.fori_loop(0, (count + batch - 1) // batch, add, total[rows, cols])


def first_kernel(got_ref, before_ref, total_ref, *scratch):
    if before_ref is None:
        total_ref[...] = jnp.zeros(total_ref.shape, jnp.float32)
    else:
        total_ref[...] = before_ref[...]
    add_half(got_ref, total_ref, *scratch)


def second_kernel(scale, got_ref, before_ref, pairs_ref, last_ref, out_ref, total, left, *scratch):
    total[...] = before_ref[...]
    add_half(got_ref, total, *scratch)
    cells = total[...].astype(jnp.bfloat16)
    cells = jnp.concatenate([cells[TILE : TILE + HALO], cells[:TILE], cells[TILE + HALO :]], axis=0)
    own, side = cells[:, :TILE], cells[:, TILE:]
    for u in range(TURNS):
        left[:, u * TILE : (u + 1) * TILE] = own[u * STEP : u * STEP + LONG, :]
        at = TURNS * TILE + u * 2 * HALO
        left[:, at : at + 2 * HALO] = side[u * STEP : u * STEP + LONG, :]
    sums = jnp.dot(own[2 * HALO :, :], last_ref[:TILE, :], preferred_element_type=jnp.float32)
    sums = sums + jnp.dot(side[2 * HALO :, :], last_ref[TILE:, :], preferred_element_type=jnp.float32)
    for p in range(STEP // 2):
        both = jnp.dot(left[...], pairs_ref[p], preferred_element_type=jnp.float32)
        sums = sums + both[2 * p : 2 * p + TILE, :TILE]
        sums = sums + both[2 * p + 1 : 2 * p + 1 + TILE, TILE:]
    out_ref[...] = sums / scale


def shards(positions, destination, profile):
    blocks, _, rays = positions.shape
    row_count, col_count = lax.axis_size("row"), lax.axis_size("col")
    tiles = row_count * col_count
    width = -(-(3 * blocks + tiles) // LANES) * LANES

    def exchange(turn):
        outgoing = pl.pallas_call(
            pack_kernel,
            out_shape=jax.ShapeDtypeStruct((8 * tiles, rays + LANES), jnp.float32),
            in_specs=[SMEM, VMEM, VMEM],
            out_specs=VMEM,
            scratch_shapes=[
                pltpu.VMEM((1, LANES), jnp.float32),
                pltpu.VMEM((width, rays + LANES), jnp.float32),
            ],
            compiler_params=pltpu.CompilerParams(vmem_limit_bytes=56 * 1024 * 1024),
            name="pack",
        )(turn, destination.T, positions)
        return lax.all_to_all(
            outgoing.reshape(tiles, 8, rays + LANES), ("row", "col"), split_axis=0, concat_axis=0, tiled=True
        )

    scratch = [
        pltpu.VMEM((tiles, LANES), jnp.int32),
        pltpu.SMEM((tiles, LANES), jnp.int32),
        pltpu.SemaphoreType.DMA,
        pltpu.SMEM((4 * (tiles * ROOM + BATCH),), jnp.int32),
        pltpu.VMEM((4, BATCH, rays), jnp.float32),
        pltpu.VMEM((8, BATCH, rays), jnp.float32),
    ]

    def deposit(mine, before, pairs, last):
        other = lax.ppermute(mine, "row", [(i, i ^ 1) for i in range(row_count)])
        kernel, given = first_kernel, (mine, before)
        if before is None:
            kernel, given = lambda got, *refs: first_kernel(got, None, *refs), (mine,)
        total = pl.pallas_call(
            kernel,
            out_shape=jax.ShapeDtypeStruct((WIDE, WIDE), jnp.float32),
            in_specs=[VMEM] * len(given),
            out_specs=VMEM,
            scratch_shapes=scratch,
            compiler_params=LIMIT,
            cost_estimate=pl.CostEstimate(flops=2_000_000_000, bytes_accessed=4_000_000, transcendentals=0),
            name="first",
        )(*given)
        out, total = pl.pallas_call(
            functools.partial(second_kernel, blocks * rays / (TILE * TILE)),
            out_shape=(
                jax.ShapeDtypeStruct((TILE, TILE), jnp.float32),
                jax.ShapeDtypeStruct((WIDE, WIDE), jnp.float32),
            ),
            in_specs=[VMEM] * 4,
            out_specs=(VMEM, VMEM),
            scratch_shapes=[pltpu.VMEM((LONG, DEPTH), jnp.bfloat16)] + scratch,
            compiler_params=LIMIT,
            name="second",
        )(other, total, pairs, last)
        return out, total

    mine = exchange(jnp.zeros((1,), jnp.int32))
    pairs, last = pl.pallas_call(
        table_kernel,
        out_shape=(
            jax.ShapeDtypeStruct((STEP // 2, DEPTH, 2 * TILE), jnp.bfloat16),
            jax.ShapeDtypeStruct((WIDE, TILE), jnp.bfloat16),
        ),
        in_specs=[VMEM],
        out_specs=(VMEM, VMEM),
        compiler_params=LIMIT,
        cost_estimate=pl.CostEstimate(flops=10_000_000, bytes_accessed=6_000_000, transcendentals=0),
        name="table",
    )(profile)
    mine, pairs, last = lax.optimization_barrier((mine, pairs, last))
    out, total = deposit(mine, None, pairs, last)
    turns = jnp.max(mine[:, 7, 2 * LANES + 16]).astype(jnp.int32)

    def more(state):
        turn, _, total = state
        out, total = deposit(exchange(jnp.full((1,), turn, jnp.int32)), total, pairs, last)
        return turn + 1, out, total

    return lax.while_loop(lambda state: state[0] < turns, more, (jnp.int32(1), out, total))[1]


def solution(mesh):
    placed = (P(("maps", "row", "col"), None, None), P(("maps", "row", "col"), None), P())
    return jax.shard_map(
        shards, mesh=mesh, in_specs=placed, out_specs=P(("maps", "row"), "col"), check_vma=False
    )
```

```python
import functools

import jax
import jax.numpy as jnp
from jax import lax
from jax.experimental import pallas as pl
from jax.experimental.pallas import tpu as pltpu
from jax.sharding import PartitionSpec as P

TILE = 128
HALO = 32
MOST = 4
DISC = 2 * HALO + 1
STEP = 16
LONG = TILE + STEP
TURNS = 2 * HALO // STEP
WIDE = TILE + 2 * HALO
LANES = 128
SPAN = 64
BATCH = 4
ROOM = 5
NONE = 64.0

VMEM = pl.BlockSpec(memory_space=pltpu.VMEM)
SMEM = pl.BlockSpec(memory_space=pltpu.SMEM)
LIMIT = pltpu.CompilerParams(vmem_limit_bytes=32 * 1024 * 1024)


def touches(distance, least, most):
    before = (distance == -1.0) & (most > TILE - HALO - 1.0)
    after = (distance == 1.0) & (least < HALO)
    return (distance == 0.0) | before | after


def pack_kernel(turn_ref, dest_ref, rays_ref, out_ref, labels, parts):
    blocks, _, rays = rays_ref.shape
    tiles = out_ref.shape[0] // 8
    width = parts.shape[0]
    col_count = lax.axis_size("col")
    skip = 0.0 if turn_ref is None else 2.0 * ROOM * turn_ref[0].astype(jnp.float32)
    lane = lax.broadcasted_iota(jnp.int32, (blocks, width), 1)
    place = lax.broadcasted_iota(jnp.int32, (blocks, width), 0)
    there = (lane % blocks == place) & (lane < 3 * blocks)

    def laid(column):
        return jnp.sum(jnp.where(there, column, 0.0), axis=0, keepdims=True)

    labels[...] = jnp.full(labels.shape, -1.0, jnp.float32)
    for g in range(3):
        labels[0:1, g * blocks : (g + 1) * blocks] = dest_ref[...].astype(jnp.float32)
    label = labels[...]
    label_row = jnp.floor((label + 0.5) / col_count)
    label_col = label - label_row * col_count
    first, second = rays_ref[:, 0, :], rays_ref[:, 1, :]
    least_row, most_row = laid(jnp.min(first, 1, keepdims=True)), laid(jnp.max(first, 1, keepdims=True))
    least_col, most_col = laid(jnp.min(second, 1, keepdims=True)), laid(jnp.max(second, 1, keepdims=True))
    earlier = lax.broadcasted_iota(jnp.int32, (width, width), 0)
    later = lax.broadcasted_iota(jnp.int32, (width, width), 1)
    earlier = jnp.where((earlier < later % blocks) & (later < 3 * blocks), 1.0, 0.0).astype(jnp.bfloat16)

    def chosen(tile):
        odd = (tile // col_count % 2).astype(jnp.float32)
        row = (tile // col_count).astype(jnp.float32) - odd
        dc = label_col - (tile % col_count).astype(jnp.float32)
        aside = touches(dc, least_col, most_col) & (label >= 0.0)

        def coded(dr):
            reach = aside & touches(dr, least_row, most_row)
            kind = jnp.where(dr == 0.0, 0.0, 16.0)
            return reach, jnp.where(reach, kind + 4.0 * (dr + 1.0) + dc + 1.0, NONE)

        reach_even, code_even = coded(label_row - row)
        reach_odd, code_odd = coded(label_row - row - 1.0)
        reach = jnp.where(reach_even | reach_odd, 1.0, 0.0)
        rank = jnp.dot(reach.astype(jnp.bfloat16), earlier, preferred_element_type=jnp.float32)
        left = rank - skip - odd
        slot = jnp.floor(left * 0.5)
        mine = (reach > 0.0) & (slot * 2.0 == left) & (slot >= 0.0) & (slot < ROOM)
        return jnp.where(mine, slot, -1.0), code_even, code_odd, (rank + 1.0) * reach

    slot, code_even, code_odd, most = chosen(lax.broadcasted_iota(jnp.int32, (tiles, width), 0))
    most = jnp.max(jnp.max(most, axis=1, keepdims=True), axis=0, keepdims=True)
    turns = jnp.floor((most + (2.0 * ROOM - 0.5)) / (2.0 * ROOM))
    lane = lax.broadcasted_iota(jnp.int32, (tiles, width), 1)
    meta = jnp.where(lane == 16, turns, NONE)
    for k in range(ROOM):
        for at, code in ((k, code_even), (8 + k, code_odd)):
            here = (slot == k) & (lane < blocks)
            found = jnp.sum(jnp.where(here, code - NONE, 0.0), axis=1, keepdims=True) + NONE
            meta = jnp.where(lane == at, found, meta)

    parts[...] = jnp.zeros(parts.shape, jnp.float32)
    parts[:blocks, :rays] = first
    parts[:blocks, rays:] = second[:, :LANES]
    parts[blocks : 2 * blocks, : 2 * LANES] = second[:, LANES:]
    parts[2 * blocks : 3 * blocks, 2 * LANES :] = second[:, LANES:]
    parts[3 * blocks : 3 * blocks + tiles, 2 * LANES : 3 * LANES] = meta[:, :LANES]

    row = lax.broadcasted_iota(jnp.int32, (8 * tiles, width), 0)
    group = lax.broadcasted_iota(jnp.int32, (8 * tiles, width), 1)
    slot = chosen(row // 8)[0]
    within = row % 8
    low = (2 * (within - ROOM)).astype(jnp.float32)
    head = (group < blocks) & (within < ROOM) & (slot == within.astype(jnp.float32))
    even = (group >= blocks) & (group < 2 * blocks) & (within >= ROOM) & (slot == low)
    uneven = (group >= 2 * blocks) & (group < 3 * blocks) & (within >= ROOM) & (slot == low + 1.0)
    codes = (group - 3 * blocks == row // 8) & (group >= 3 * blocks) & (within == 7)
    select = jnp.where(head | even | uneven | codes, 1.0, 0.0).astype(jnp.bfloat16)
    rest = parts[...]
    total = jnp.zeros(out_ref.shape, jnp.float32)
    for _ in range(3):
        part = rest.astype(jnp.bfloat16)
        rest = rest - part.astype(jnp.float32)
        total = total + jnp.dot(select, part, preferred_element_type=jnp.float32)
    out_ref[...] = total


def table_kernel(profile_ref, pairs_ref, last_ref):
    a = lax.broadcasted_iota(jnp.int32, (DISC, DISC), 0) - HALO
    c = lax.broadcasted_iota(jnp.int32, (DISC, DISC), 1) - HALO
    weights = jnp.where(a * a + c * c <= HALO * HALO, profile_ref[...], 0.0)
    kernel = (weights / jnp.sum(weights)).astype(jnp.bfloat16)
    source = lax.broadcasted_iota(jnp.int32, (DISC, LANES), 0)
    target = lax.broadcasted_iota(jnp.int32, (DISC, LANES), 1)
    mirror = jnp.where((source + target) % LANES == 0, 1.0, 0.0).astype(jnp.bfloat16)
    mirrored = jnp.dot(kernel, mirror, preferred_element_type=jnp.float32)
    left = lax.broadcasted_iota(jnp.int32, (LANES, LANES), 1) < SPAN

    def band(row, start):
        wide = jnp.broadcast_to(mirrored[row : row + 1, :], (LANES, LANES))
        return pltpu.roll(wide, start, 1, stride=1, stride_axis=0)

    for u in range(TURNS):
        for s in range(0, STEP, 2):
            row = u * STEP + s
            both = jnp.where(left, band(row, 0), band(row + 1, SPAN))
            pairs_ref[u * LANES : (u + 1) * LANES, s * SPAN : (s + 2) * SPAN] = both.astype(jnp.bfloat16)
    last_ref[...] = jnp.where(left, band(2 * HALO, 0), 0.0).astype(jnp.bfloat16)


def hats(row, cell):
    near, far, here, there = (value.astype(jnp.bfloat16) for value in row)
    zero = jnp.zeros((), jnp.bfloat16)
    return jnp.maximum(zero, jnp.minimum((cell - here) + near, (there - cell) + far))


def add_half(got_ref, total, codes, table, done, lists, stage, facts):
    sources = got_ref.shape[0]
    rays = 3 * LANES
    codes[...] = got_ref[:, 7, 2 * LANES : 3 * LANES].astype(jnp.int32)
    copy = pltpu.make_async_copy(codes, table, done)
    copy.start()
    copy.wait()
    room = sources * ROOM + BATCH
    first_lane = lax.axis_index("row") % 2 * 8

    def sort(source, carry):
        turns, inner, outer = carry
        turns = jnp.maximum(turns, table[source, 16])
        for k in range(ROOM):
            code = table[source, first_lane + k]
            entry = (source * 8 + k) * 16 + (code & 15)
            lists[inner] = entry
            lists[room + outer] = entry
            inner = inner + (code < 16).astype(jnp.int32)
            outer = outer + ((code >> 4) == 1).astype(jnp.int32)
        return turns, inner, outer

    turns, inner, outer = lax.fori_loop(0, sources, sort, (jnp.int32(0),) * 3)

    def doubled(cell):
        return (2 * cell).astype(jnp.float32).astype(jnp.bfloat16)

    across = doubled(lax.broadcasted_iota(jnp.int32, (WIDE, rays), 0) - HALO)
    own = doubled(lax.broadcasted_iota(jnp.int32, (TILE, rays), 0))
    edge = lax.broadcasted_iota(jnp.int32, (2 * HALO, rays), 0)
    edge = doubled(jnp.where(edge < HALO, edge - HALO, edge + (TILE - HALO)))

    def add(base, down, step, sums):
        for k in range(BATCH):
            entry = lists[base + step * BATCH + k]
            source, slot = entry >> 7, (entry >> 4) & 7
            head = got_ref[source, pl.ds(slot, 1), :]
            tail = got_ref[source, pl.ds(ROOM + (slot >> 1), 1), :]
            stage[0, k : k + 1, :] = head[:, :rays]
            stage[1, k : k + 1, :LANES] = head[:, rays:]
            stage[1, k : k + 1, LANES:] = jnp.where(
                (slot & 1) == 1, tail[:, 2 * LANES :], tail[:, : 2 * LANES]
            )
            for axis, shift in enumerate(((entry >> 2) & 3, entry & 3)):
                offset = ((shift - 1) * (2 * TILE)).astype(jnp.float32)
                stage[2 + axis, k : k + 1, :] = jnp.full((1, rays), offset)
        for axis in range(2):
            coords = stage[axis]
            low = jnp.floor(coords)
            facts[4 * axis] = 1.0 - (coords - low)
            facts[4 * axis + 1] = 1.0 - ((low + 1.0) - coords)
            here = 2.0 * low + stage[2 + axis]
            facts[4 * axis + 2] = here
            facts[4 * axis + 3] = here + 2.0
        firsts, seconds = [], []
        for k in range(BATCH):
            row = [facts[j, k : k + 1, :] for j in range(8)]
            firsts.append(hats(row[:4], down))
            seconds.append(hats(row[4:], across))
        return sums + lax.dot_general(
            jnp.concatenate(firsts, axis=1),
            jnp.concatenate(seconds, axis=1),
            (((1,), (1,)), ((), ())),
            preferred_element_type=jnp.float32,
        )

    top, middle, bottom = slice(0, HALO), slice(HALO, HALO + TILE), slice(HALO + TILE, WIDE)
    for count, base in ((inner, 0), (outer, room)):
        for k in range(BATCH):
            lists[base + count + k] = 15
    steps = (inner + BATCH - 1) // BATCH
    total[middle] = lax.fori_loop(0, steps, functools.partial(add, 0, own), total[middle])
    steps = (outer + BATCH - 1) // BATCH
    sums = jnp.concatenate([total[top], total[bottom]], axis=0)
    sums = lax.fori_loop(0, steps, functools.partial(add, room, edge), sums)
    total[top] = sums[:HALO]
    total[bottom] = sums[HALO:]
    return turns


def first_kernel(got_ref, before_ref, total_ref, turns_ref, *scratch):
    if before_ref is None:
        total_ref[...] = jnp.zeros(total_ref.shape, jnp.float32)
    else:
        total_ref[...] = before_ref[...]
    turns_ref[0] = add_half(got_ref, total_ref, *scratch)


def second_kernel(scale, got_ref, before_ref, pairs_ref, last_ref, out_ref, total, left, *scratch):
    total[...] = before_ref[...]
    add_half(got_ref, total, *scratch)
    cells = total[...]
    blocks = [cells[:, at : at + LANES].astype(jnp.bfloat16) for at in (0, SPAN)]
    for h in range(2):
        for u in range(TURNS):
            left[h * LONG : (h + 1) * LONG, u * LANES : (u + 1) * LANES] = blocks[h][
                u * STEP : u * STEP + LONG, :
            ]
    lowest = jnp.concatenate([block[2 * HALO :, :] for block in blocks], axis=0)
    ends = jnp.dot(lowest, last_ref[...], preferred_element_type=jnp.float32)
    evens = [ends[:TILE], ends[TILE:]]
    odds = [jnp.zeros((TILE, LANES), jnp.float32)] * 2
    for p in range(0, STEP * SPAN, 2 * LANES):
        both = jnp.dot(left[...], pairs_ref[:, p : p + 2 * LANES], preferred_element_type=jnp.float32)
        for h in range(2):
            for lanes in (0, LANES):
                s = (p + lanes) // SPAN
                part = both[h * LONG : (h + 1) * LONG, lanes : lanes + LANES]
                evens[h] = evens[h] + part[s : s + TILE]
                odds[h] = odds[h] + part[s + 1 : s + 1 + TILE]
    low = evens[0] + pltpu.roll(odds[0], SPAN, 1)
    high = pltpu.roll(evens[1], SPAN, 1) + odds[1]
    lane = lax.broadcasted_iota(jnp.int32, (TILE, LANES), 1)
    out_ref[...] = jnp.where(lane < SPAN, low, high) / scale


def shards(positions, destination, profile):
    blocks, _, rays = positions.shape
    row_count, col_count = lax.axis_size("row"), lax.axis_size("col")
    tiles = row_count * col_count
    width = -(-(3 * blocks + tiles) // LANES) * LANES

    def exchange(turn):
        kernel, given = pack_kernel, (turn, destination.T, positions)
        if turn is None:
            kernel, given = functools.partial(pack_kernel, None), (destination.T, positions)
        outgoing = pl.pallas_call(
            kernel,
            out_shape=jax.ShapeDtypeStruct((8 * tiles, rays + LANES), jnp.float32),
            in_specs=[SMEM, VMEM, VMEM][-len(given) :],
            out_specs=VMEM,
            scratch_shapes=[
                pltpu.VMEM((1, width), jnp.float32),
                pltpu.VMEM((width, rays + LANES), jnp.float32),
            ],
            compiler_params=pltpu.CompilerParams(vmem_limit_bytes=60 * 1024 * 1024),
            name="pack",
        )(*given)
        return lax.all_to_all(
            outgoing.reshape(tiles, 8, rays + LANES), ("row", "col"), split_axis=0, concat_axis=0, tiled=True
        )

    scratch = [
        pltpu.VMEM((tiles, LANES), jnp.int32),
        pltpu.SMEM((tiles, LANES), jnp.int32),
        pltpu.SemaphoreType.DMA,
        pltpu.SMEM((2 * (tiles * ROOM + BATCH),), jnp.int32),
        pltpu.VMEM((4, BATCH, rays), jnp.float32),
        pltpu.VMEM((8, BATCH, rays), jnp.float32),
    ]

    def deposit(mine, before, pairs, last):
        other = lax.ppermute(mine, "row", [(i, i ^ 1) for i in range(row_count)])
        kernel, given = first_kernel, (mine, before)
        if before is None:
            kernel, given = lambda got, *refs: first_kernel(got, None, *refs), (mine,)
        total, turns = pl.pallas_call(
            kernel,
            out_shape=(
                jax.ShapeDtypeStruct((WIDE, WIDE), jnp.float32),
                jax.ShapeDtypeStruct((1,), jnp.int32),
            ),
            in_specs=[VMEM] * len(given),
            out_specs=(VMEM, SMEM),
            scratch_shapes=scratch,
            compiler_params=LIMIT,
            cost_estimate=pl.CostEstimate(flops=2_000_000_000, bytes_accessed=4_000_000, transcendentals=0),
            name="first",
        )(*given)
        out, total = pl.pallas_call(
            functools.partial(second_kernel, blocks * rays / (TILE * TILE)),
            out_shape=(
                jax.ShapeDtypeStruct((TILE, TILE), jnp.float32),
                jax.ShapeDtypeStruct((WIDE, WIDE), jnp.float32),
            ),
            in_specs=[VMEM] * 4,
            out_specs=(VMEM, VMEM),
            scratch_shapes=[pltpu.VMEM((2 * LONG, TURNS * LANES), jnp.bfloat16)] + scratch,
            compiler_params=LIMIT,
            name="second",
        )(other, total, pairs, last)
        return out, total, turns[0]

    mine = exchange(None)
    pairs, last = pl.pallas_call(
        table_kernel,
        out_shape=(
            jax.ShapeDtypeStruct((TURNS * LANES, STEP * SPAN), jnp.bfloat16),
            jax.ShapeDtypeStruct((LANES, LANES), jnp.bfloat16),
        ),
        in_specs=[VMEM],
        out_specs=(VMEM, VMEM),
        compiler_params=LIMIT,
        cost_estimate=pl.CostEstimate(flops=10_000_000, bytes_accessed=6_000_000, transcendentals=0),
        name="table",
    )(profile)
    mine, pairs, last = lax.optimization_barrier((mine, pairs, last))
    out, total, turns = deposit(mine, None, pairs, last)

    def more(state):
        turn, _, total = state
        out, total, _ = deposit(exchange(jnp.full((1,), turn, jnp.int32)), total, pairs, last)
        return turn + 1, out, total

    return lax.while_loop(lambda state: state[0] < turns, more, (jnp.int32(1), out, total))[1]


def solution(mesh):
    placed = (P(("maps", "row", "col"), None, None), P(("maps", "row", "col"), None), P())
    return jax.shard_map(
        shards, mesh=mesh, in_specs=placed, out_specs=P(("maps", "row"), "col"), check_vma=False
    )
```

```python
import functools

import jax
import jax.numpy as jnp
from jax import lax
from jax.experimental import pallas as pl
from jax.experimental.pallas import tpu as pltpu
from jax.sharding import PartitionSpec as P

TILE = 128
HALO = 32
MOST = 4
DISC = 2 * HALO + 1
STEP = 16
LONG = TILE + STEP
TURNS = 2 * HALO // STEP
WIDE = TILE + 2 * HALO
LANES = 128
SPAN = 64
BATCH = 4
ROOM = 5
NONE = 64.0

VMEM = pl.BlockSpec(memory_space=pltpu.VMEM)
SMEM = pl.BlockSpec(memory_space=pltpu.SMEM)
LIMIT = pltpu.CompilerParams(vmem_limit_bytes=32 * 1024 * 1024)


def touches(distance, least, most):
    before = (distance == -1.0) & (most > TILE - HALO - 1.0)
    after = (distance == 1.0) & (least < HALO)
    return (distance == 0.0) | before | after


def pack_kernel(turn_ref, dest_ref, rays_ref, out_ref, labels, parts):
    blocks, _, rays = rays_ref.shape
    tiles = out_ref.shape[0] // 8
    width = parts.shape[0]
    col_count = lax.axis_size("col")
    skip = 0.0 if turn_ref is None else 2.0 * ROOM * turn_ref[0].astype(jnp.float32)
    lane = lax.broadcasted_iota(jnp.int32, (blocks, width), 1)
    place = lax.broadcasted_iota(jnp.int32, (blocks, width), 0)
    there = (lane % blocks == place) & (lane < 3 * blocks)

    def laid(column):
        return jnp.sum(jnp.where(there, column, 0.0), axis=0, keepdims=True)

    labels[...] = jnp.full(labels.shape, -1.0, jnp.float32)
    for g in range(3):
        labels[0:1, g * blocks : (g + 1) * blocks] = dest_ref[...].astype(jnp.float32)
    label = labels[...]
    label_row = jnp.floor((label + 0.5) / col_count)
    label_col = label - label_row * col_count
    first, second = rays_ref[:, 0, :], rays_ref[:, 1, :]
    least_row, most_row = laid(jnp.min(first, 1, keepdims=True)), laid(jnp.max(first, 1, keepdims=True))
    least_col, most_col = laid(jnp.min(second, 1, keepdims=True)), laid(jnp.max(second, 1, keepdims=True))
    earlier = lax.broadcasted_iota(jnp.int32, (width, width), 0)
    later = lax.broadcasted_iota(jnp.int32, (width, width), 1)
    earlier = jnp.where((earlier < later % blocks) & (later < 3 * blocks), 1.0, 0.0).astype(jnp.bfloat16)

    def chosen(tile):
        odd = (tile // col_count % 2).astype(jnp.float32)
        row = (tile // col_count).astype(jnp.float32) - odd
        dc = label_col - (tile % col_count).astype(jnp.float32)
        aside = touches(dc, least_col, most_col) & (label >= 0.0)

        def coded(dr):
            reach = aside & touches(dr, least_row, most_row)
            kind = jnp.where(dr == 0.0, 0.0, 16.0)
            return reach, jnp.where(reach, kind + 4.0 * (dr + 1.0) + dc + 1.0, NONE)

        reach_even, code_even = coded(label_row - row)
        reach_odd, code_odd = coded(label_row - row - 1.0)
        reach = jnp.where(reach_even | reach_odd, 1.0, 0.0)
        rank = jnp.dot(reach.astype(jnp.bfloat16), earlier, preferred_element_type=jnp.float32)
        left = rank - skip - odd
        slot = jnp.floor(left * 0.5)
        mine = (reach > 0.0) & (slot * 2.0 == left) & (slot >= 0.0) & (slot < ROOM)
        return jnp.where(mine, slot, -1.0), code_even, code_odd, (rank + 1.0) * reach

    slot, code_even, code_odd, most = chosen(lax.broadcasted_iota(jnp.int32, (tiles, width), 0))
    most = jnp.max(jnp.max(most, axis=1, keepdims=True), axis=0, keepdims=True)
    turns = jnp.floor((most + (2.0 * ROOM - 0.5)) / (2.0 * ROOM))
    lane = lax.broadcasted_iota(jnp.int32, (tiles, width), 1)
    meta = jnp.where(lane == 16, turns, NONE)
    for k in range(ROOM):
        for at, code in ((k, code_even), (8 + k, code_odd)):
            here = (slot == k) & (lane < blocks)
            found = jnp.sum(jnp.where(here, code - NONE, 0.0), axis=1, keepdims=True) + NONE
            meta = jnp.where(lane == at, found, meta)

    parts[...] = jnp.zeros(parts.shape, jnp.float32)
    parts[:blocks, :rays] = first
    parts[:blocks, rays:] = second[:, :LANES]
    parts[blocks : 2 * blocks, : 2 * LANES] = second[:, LANES:]
    parts[2 * blocks : 3 * blocks, 2 * LANES :] = second[:, LANES:]
    parts[3 * blocks : 3 * blocks + tiles, 2 * LANES : 3 * LANES] = meta[:, :LANES]

    row = lax.broadcasted_iota(jnp.int32, (8 * tiles, width), 0)
    group = lax.broadcasted_iota(jnp.int32, (8 * tiles, width), 1)
    slot = chosen(row // 8)[0]
    within = row % 8
    low = (2 * (within - ROOM)).astype(jnp.float32)
    head = (group < blocks) & (within < ROOM) & (slot == within.astype(jnp.float32))
    even = (group >= blocks) & (group < 2 * blocks) & (within >= ROOM) & (slot == low)
    uneven = (group >= 2 * blocks) & (group < 3 * blocks) & (within >= ROOM) & (slot == low + 1.0)
    codes = (group - 3 * blocks == row // 8) & (group >= 3 * blocks) & (within == 7)
    select = jnp.where(head | even | uneven | codes, 1.0, 0.0).astype(jnp.bfloat16)
    rest = parts[...]
    total = jnp.zeros(out_ref.shape, jnp.float32)
    for _ in range(3):
        part = rest.astype(jnp.bfloat16)
        rest = rest - part.astype(jnp.float32)
        total = total + jnp.dot(select, part, preferred_element_type=jnp.float32)
    out_ref[...] = total


def table_kernel(profile_ref, pairs_ref, last_ref):
    a = lax.broadcasted_iota(jnp.int32, (DISC, DISC), 0) - HALO
    c = lax.broadcasted_iota(jnp.int32, (DISC, DISC), 1) - HALO
    weights = jnp.where(a * a + c * c <= HALO * HALO, profile_ref[...], 0.0)
    kernel = (weights / jnp.sum(weights)).astype(jnp.bfloat16)
    source = lax.broadcasted_iota(jnp.int32, (DISC, LANES), 0)
    target = lax.broadcasted_iota(jnp.int32, (DISC, LANES), 1)
    mirror = jnp.where((source + target) % LANES == 0, 1.0, 0.0).astype(jnp.bfloat16)
    mirrored = jnp.dot(kernel, mirror, preferred_element_type=jnp.float32)
    left = lax.broadcasted_iota(jnp.int32, (LANES, LANES), 1) < SPAN

    def band(row, start):
        wide = jnp.broadcast_to(mirrored[row : row + 1, :], (LANES, LANES))
        return pltpu.roll(wide, start, 1, stride=1, stride_axis=0)

    for u in range(TURNS):
        for s in range(0, STEP, 2):
            row = u * STEP + s
            both = jnp.where(left, band(row, 0), band(row + 1, SPAN))
            pairs_ref[u * LANES : (u + 1) * LANES, s * SPAN : (s + 2) * SPAN] = both.astype(jnp.bfloat16)
    last_ref[...] = jnp.where(left, band(2 * HALO, 0), 0.0).astype(jnp.bfloat16)


def hats(row, cell):
    near, far, here, there = (value.astype(jnp.bfloat16) for value in row)
    zero = jnp.zeros((), jnp.bfloat16)
    return jnp.maximum(zero, jnp.minimum((cell - here) + near, (there - cell) + far))


def add_half(got_ref, total, codes, table, done, lists, stage, facts):
    sources = got_ref.shape[0]
    rays = 3 * LANES
    codes[...] = got_ref[:, 7, 2 * LANES : 3 * LANES].astype(jnp.int32)
    copy = pltpu.make_async_copy(codes, table, done)
    copy.start()
    copy.wait()
    room = sources * ROOM + BATCH
    first_lane = lax.axis_index("row") % 2 * 8

    def sort(source, carry):
        inner, outer = carry
        for k in range(ROOM):
            code = table[source, first_lane + k]
            entry = (source * 8 + k) * 16 + (code & 15)
            lists[inner] = entry
            lists[room + outer] = entry
            inner = inner + (code < 16).astype(jnp.int32)
            outer = outer + ((code >> 4) == 1).astype(jnp.int32)
        return inner, outer

    inner, outer = lax.fori_loop(0, sources, sort, (jnp.int32(0),) * 2)

    def doubled(cell):
        return (2 * cell).astype(jnp.float32).astype(jnp.bfloat16)

    across = doubled(lax.broadcasted_iota(jnp.int32, (WIDE, rays), 0) - HALO)
    own = doubled(lax.broadcasted_iota(jnp.int32, (TILE, rays), 0))
    edge = lax.broadcasted_iota(jnp.int32, (2 * HALO, rays), 0)
    edge = doubled(jnp.where(edge < HALO, edge - HALO, edge + (TILE - HALO)))

    def add(base, down, step, sums):
        for k in range(BATCH):
            entry = lists[base + step * BATCH + k]
            source, slot = entry >> 7, (entry >> 4) & 7
            head = got_ref[source, pl.ds(slot, 1), :]
            tail = got_ref[source, pl.ds(ROOM + (slot >> 1), 1), :]
            stage[0, k : k + 1, :] = head[:, :rays]
            stage[1, k : k + 1, :LANES] = head[:, rays:]
            stage[1, k : k + 1, LANES:] = jnp.where(
                (slot & 1) == 1, tail[:, 2 * LANES :], tail[:, : 2 * LANES]
            )
            for axis, shift in enumerate(((entry >> 2) & 3, entry & 3)):
                offset = ((shift - 1) * (2 * TILE)).astype(jnp.float32)
                stage[2 + axis, k : k + 1, :] = jnp.full((1, rays), offset)
        for axis in range(2):
            coords = stage[axis]
            low = jnp.floor(coords)
            facts[4 * axis] = 1.0 - (coords - low)
            facts[4 * axis + 1] = 1.0 - ((low + 1.0) - coords)
            here = 2.0 * low + stage[2 + axis]
            facts[4 * axis + 2] = here
            facts[4 * axis + 3] = here + 2.0
        firsts, seconds = [], []
        for k in range(BATCH):
            row = [facts[j, k : k + 1, :] for j in range(8)]
            firsts.append(hats(row[:4], down))
            seconds.append(hats(row[4:], across))
        return sums + lax.dot_general(
            jnp.concatenate(seconds, axis=1),
            jnp.concatenate(firsts, axis=1),
            (((1,), (1,)), ((), ())),
            preferred_element_type=jnp.float32,
        )

    for count, base in ((inner, 0), (outer, room)):
        for k in range(BATCH):
            lists[base + count + k] = 15
    for count, base, down, lanes in (
        (inner, 0, own, slice(0, TILE)),
        (outer, room, edge, slice(TILE, WIDE)),
    ):
        steps = (count + BATCH - 1) // BATCH
        total[:, lanes] = lax.fori_loop(0, steps, functools.partial(add, base, down), total[:, lanes])


def first_kernel(got_ref, before_ref, total_ref, *scratch):
    if before_ref is None:
        total_ref[...] = jnp.zeros(total_ref.shape, jnp.float32)
    else:
        total_ref[...] = before_ref[...]
    add_half(got_ref, total_ref, *scratch)


def second_kernel(scale, got_ref, before_ref, pairs_ref, last_ref, out_ref, total, left, *scratch):
    total[...] = before_ref[...]
    add_half(got_ref, total, *scratch)
    cells = total[...].T
    cells = jnp.concatenate([cells[TILE : TILE + HALO], cells[:TILE], cells[TILE + HALO :]], axis=0)
    blocks = [cells[:, at : at + LANES].astype(jnp.bfloat16) for at in (0, SPAN)]
    for h in range(2):
        for u in range(TURNS):
            left[h * LONG : (h + 1) * LONG, u * LANES : (u + 1) * LANES] = blocks[h][
                u * STEP : u * STEP + LONG, :
            ]
    lowest = jnp.concatenate([block[2 * HALO :, :] for block in blocks], axis=0)
    ends = jnp.dot(lowest, last_ref[...], preferred_element_type=jnp.float32)
    evens = [ends[:TILE], ends[TILE:]]
    odds = [jnp.zeros((TILE, LANES), jnp.float32)] * 2
    for p in range(0, STEP * SPAN, 2 * LANES):
        both = jnp.dot(left[...], pairs_ref[:, p : p + 2 * LANES], preferred_element_type=jnp.float32)
        for h in range(2):
            for lanes in (0, LANES):
                s = (p + lanes) // SPAN
                part = both[h * LONG : (h + 1) * LONG, lanes : lanes + LANES]
                evens[h] = evens[h] + part[s : s + TILE]
                odds[h] = odds[h] + part[s + 1 : s + 1 + TILE]
    low = evens[0] + pltpu.roll(odds[0], SPAN, 1)
    high = pltpu.roll(evens[1], SPAN, 1) + odds[1]
    lane = lax.broadcasted_iota(jnp.int32, (TILE, LANES), 1)
    out_ref[...] = jnp.where(lane < SPAN, low, high) / scale


def shards(positions, destination, profile):
    blocks, _, rays = positions.shape
    row_count, col_count = lax.axis_size("row"), lax.axis_size("col")
    tiles = row_count * col_count
    width = -(-(3 * blocks + tiles) // LANES) * LANES

    def exchange(turn):
        kernel, given = pack_kernel, (turn, destination.T, positions)
        if turn is None:
            kernel, given = functools.partial(pack_kernel, None), (destination.T, positions)
        outgoing = pl.pallas_call(
            kernel,
            out_shape=jax.ShapeDtypeStruct((8 * tiles, rays + LANES), jnp.float32),
            in_specs=[SMEM, VMEM, VMEM][-len(given) :],
            out_specs=VMEM,
            scratch_shapes=[
                pltpu.VMEM((1, width), jnp.float32),
                pltpu.VMEM((width, rays + LANES), jnp.float32),
            ],
            compiler_params=pltpu.CompilerParams(vmem_limit_bytes=60 * 1024 * 1024),
            name="pack",
        )(*given)
        return lax.all_to_all(
            outgoing.reshape(tiles, 8, rays + LANES), ("row", "col"), split_axis=0, concat_axis=0, tiled=True
        )

    scratch = [
        pltpu.VMEM((tiles, LANES), jnp.int32),
        pltpu.SMEM((tiles, LANES), jnp.int32),
        pltpu.SemaphoreType.DMA,
        pltpu.SMEM((2 * (tiles * ROOM + BATCH),), jnp.int32),
        pltpu.VMEM((4, BATCH, rays), jnp.float32),
        pltpu.VMEM((8, BATCH, rays), jnp.float32),
    ]

    def deposit(mine, before, pairs, last):
        other = lax.ppermute(mine, "row", [(i, i ^ 1) for i in range(row_count)])
        kernel, given = first_kernel, (mine, before)
        if before is None:
            kernel, given = lambda got, *refs: first_kernel(got, None, *refs), (mine,)
        total = pl.pallas_call(
            kernel,
            out_shape=jax.ShapeDtypeStruct((WIDE, WIDE), jnp.float32),
            in_specs=[VMEM] * len(given),
            out_specs=VMEM,
            scratch_shapes=scratch,
            compiler_params=LIMIT,
            cost_estimate=pl.CostEstimate(flops=2_000_000_000, bytes_accessed=4_000_000, transcendentals=0),
            name="first",
        )(*given)
        out, total = pl.pallas_call(
            functools.partial(second_kernel, blocks * rays / (TILE * TILE)),
            out_shape=(
                jax.ShapeDtypeStruct((TILE, TILE), jnp.float32),
                jax.ShapeDtypeStruct((WIDE, WIDE), jnp.float32),
            ),
            in_specs=[VMEM] * 4,
            out_specs=(VMEM, VMEM),
            scratch_shapes=[pltpu.VMEM((2 * LONG, TURNS * LANES), jnp.bfloat16)] + scratch,
            compiler_params=LIMIT,
            name="second",
        )(other, total, pairs, last)
        return out, total

    mine = exchange(None)
    pairs, last = pl.pallas_call(
        table_kernel,
        out_shape=(
            jax.ShapeDtypeStruct((TURNS * LANES, STEP * SPAN), jnp.bfloat16),
            jax.ShapeDtypeStruct((LANES, LANES), jnp.bfloat16),
        ),
        in_specs=[VMEM],
        out_specs=(VMEM, VMEM),
        compiler_params=LIMIT,
        cost_estimate=pl.CostEstimate(flops=10_000_000, bytes_accessed=6_000_000, transcendentals=0),
        name="table",
    )(profile)
    mine, pairs, last = lax.optimization_barrier((mine, pairs, last))
    turns = jnp.max(mine[:, 7, 2 * LANES + 16].astype(jnp.int32))
    out, total = deposit(mine, None, pairs, last)

    def more(state):
        turn, _, total = state
        out, total = deposit(exchange(jnp.full((1,), turn, jnp.int32)), total, pairs, last)
        return turn + 1, out, total

    return lax.while_loop(lambda state: state[0] < turns, more, (jnp.int32(1), out, total))[1]


def solution(mesh):
    placed = (P(("maps", "row", "col"), None, None), P(("maps", "row", "col"), None), P())
    return jax.shard_map(
        shards, mesh=mesh, in_specs=placed, out_specs=P(("maps", "row"), "col"), check_vma=False
    )
```

```python
import functools

import jax
import jax.numpy as jnp
from jax import lax
from jax.experimental import pallas as pl
from jax.experimental.pallas import tpu as pltpu
from jax.sharding import PartitionSpec as P

TILE = 128
HALO = 32
MOST = 4
DISC = 2 * HALO + 1
STEP = 16
LONG = TILE + STEP
TURNS = 2 * HALO // STEP
WIDE = TILE + 2 * HALO
LANES = 128
SPAN = 64
BATCH = 8
ROOM = 5
COUNT = 16
ROWS = 32
COLS = 64
FAR = 1024.0

VMEM = pl.BlockSpec(memory_space=pltpu.VMEM)
SMEM = pl.BlockSpec(memory_space=pltpu.SMEM)
LIMIT = pltpu.CompilerParams(vmem_limit_bytes=32 * 1024 * 1024)


def touches(distance, least, most):
    before = (distance == -1.0) & (most > TILE - HALO - 1.0)
    after = (distance == 1.0) & (least < HALO)
    return (distance == 0.0) | before | after


def pack_kernel(turn_ref, dest_ref, rays_ref, out_ref, labels, parts):
    blocks, _, rays = rays_ref.shape
    tiles = out_ref.shape[0] // 8
    width = parts.shape[0]
    col_count = lax.axis_size("col")
    skip = 0.0 if turn_ref is None else 2.0 * ROOM * turn_ref[0].astype(jnp.float32)
    lane = lax.broadcasted_iota(jnp.int32, (blocks, width), 1)
    place = lax.broadcasted_iota(jnp.int32, (blocks, width), 0)
    there = (lane % blocks == place) & (lane < 3 * blocks)

    def laid(column):
        return jnp.sum(jnp.where(there, column, 0.0), axis=0, keepdims=True)

    labels[...] = jnp.full(labels.shape, -1.0, jnp.float32)
    for g in range(3):
        labels[0:1, g * blocks : (g + 1) * blocks] = dest_ref[...].astype(jnp.float32)
    label = labels[...]
    label_row = jnp.floor((label + 0.5) / col_count)
    label_col = label - label_row * col_count
    first, second = rays_ref[:, 0, :], rays_ref[:, 1, :]
    least_row, most_row = laid(jnp.min(first, 1, keepdims=True)), laid(jnp.max(first, 1, keepdims=True))
    least_col, most_col = laid(jnp.min(second, 1, keepdims=True)), laid(jnp.max(second, 1, keepdims=True))
    earlier = lax.broadcasted_iota(jnp.int32, (width, width), 0)
    later = lax.broadcasted_iota(jnp.int32, (width, width), 1)
    earlier = jnp.where((earlier < later % blocks) & (later < 3 * blocks), 1.0, 0.0).astype(jnp.bfloat16)

    def chosen(tile):
        odd = (tile // col_count % 2).astype(jnp.float32)
        row = (tile // col_count).astype(jnp.float32) - odd
        dc = label_col - (tile % col_count).astype(jnp.float32)
        aside = touches(dc, least_col, most_col) & (label >= 0.0)

        def coded(dr):
            reach = aside & touches(dr, least_row, most_row)
            return reach, jnp.where(reach, jnp.where(dr == 0.0, 0.0, 1.0), FAR), dr

        even, odds = coded(label_row - row), coded(label_row - row - 1.0)
        reach = jnp.where(even[0] | odds[0], 1.0, 0.0)
        rank = jnp.dot(reach.astype(jnp.bfloat16), earlier, preferred_element_type=jnp.float32)
        left = rank - skip - odd
        slot = jnp.floor(left * 0.5)
        mine = (reach > 0.0) & (slot * 2.0 == left) & (slot >= 0.0) & (slot < ROOM)
        return jnp.where(mine, slot, -1.0), even, odds, dc, (rank + 1.0) * reach

    slot, even, odds, dc, most = chosen(lax.broadcasted_iota(jnp.int32, (tiles, width), 0))
    most = jnp.max(jnp.max(most, axis=1, keepdims=True), axis=0, keepdims=True)
    turns = jnp.floor((most + (2.0 * ROOM - 0.5)) / (2.0 * ROOM))
    lane = lax.broadcasted_iota(jnp.int32, (tiles, width), 1)
    meta = jnp.where(lane == COUNT, turns, FAR)
    for k in range(ROOM):
        here = (slot == k) & (lane < blocks)
        columns = [(COLS + k, dc * (2.0 * TILE)), (COLS + 8 + k, dc * (2.0 * TILE))]
        for at, (_, kind, dr) in ((k, even), (8 + k, odds)):
            columns += [(at, kind), (ROWS + at, dr * (2.0 * TILE))]
        for at, value in columns:
            found = jnp.sum(jnp.where(here, value - FAR, 0.0), axis=1, keepdims=True) + FAR
            meta = jnp.where(lane == at, found, meta)

    parts[...] = jnp.zeros(parts.shape, jnp.float32)
    parts[:blocks, :rays] = first
    parts[:blocks, rays:] = second[:, :LANES]
    parts[blocks : 2 * blocks, : 2 * LANES] = second[:, LANES:]
    parts[2 * blocks : 3 * blocks, 2 * LANES :] = second[:, LANES:]
    parts[3 * blocks : 3 * blocks + tiles, 2 * LANES : 3 * LANES] = meta[:, :LANES]

    row = lax.broadcasted_iota(jnp.int32, (8 * tiles, width), 0)
    group = lax.broadcasted_iota(jnp.int32, (8 * tiles, width), 1)
    slot = chosen(row // 8)[0]
    within = row % 8
    low = (2 * (within - ROOM)).astype(jnp.float32)
    head = (group < blocks) & (within < ROOM) & (slot == within.astype(jnp.float32))
    even = (group >= blocks) & (group < 2 * blocks) & (within >= ROOM) & (slot == low)
    uneven = (group >= 2 * blocks) & (group < 3 * blocks) & (within >= ROOM) & (slot == low + 1.0)
    codes = (group - 3 * blocks == row // 8) & (group >= 3 * blocks) & (within == 7)
    select = jnp.where(head | even | uneven | codes, 1.0, 0.0).astype(jnp.bfloat16)
    rest = parts[...]
    total = jnp.zeros(out_ref.shape, jnp.float32)
    for _ in range(3):
        part = rest.astype(jnp.bfloat16)
        rest = rest - part.astype(jnp.float32)
        total = total + jnp.dot(select, part, preferred_element_type=jnp.float32)
    out_ref[...] = total


def table_kernel(profile_ref, pairs_ref, last_ref):
    a = lax.broadcasted_iota(jnp.int32, (DISC, DISC), 0) - HALO
    c = lax.broadcasted_iota(jnp.int32, (DISC, DISC), 1) - HALO
    weights = jnp.where(a * a + c * c <= HALO * HALO, profile_ref[...], 0.0)
    kernel = (weights / jnp.sum(weights)).astype(jnp.bfloat16)
    source = lax.broadcasted_iota(jnp.int32, (DISC, LANES), 0)
    target = lax.broadcasted_iota(jnp.int32, (DISC, LANES), 1)
    mirror = jnp.where((source + target) % LANES == 0, 1.0, 0.0).astype(jnp.bfloat16)
    mirrored = jnp.dot(kernel, mirror, preferred_element_type=jnp.float32)
    left = lax.broadcasted_iota(jnp.int32, (LANES, LANES), 1) < SPAN

    def band(row, start):
        wide = jnp.broadcast_to(mirrored[row : row + 1, :], (LANES, LANES))
        return pltpu.roll(wide, start, 1, stride=1, stride_axis=0)

    for u in range(TURNS):
        for s in range(0, STEP, 2):
            row = u * STEP + s
            both = jnp.where(left, band(row, 0), band(row + 1, SPAN))
            pairs_ref[u * LANES : (u + 1) * LANES, s * SPAN : (s + 2) * SPAN] = both.astype(jnp.bfloat16)
    last_ref[...] = jnp.where(left, band(2 * HALO, 0), 0.0).astype(jnp.bfloat16)


def hats(row, cell):
    near, far, here, there = (value.astype(jnp.bfloat16) for value in row)
    zero = jnp.zeros((), jnp.bfloat16)
    return jnp.maximum(zero, jnp.minimum((cell - here) + near, (there - cell) + far))


def add_blocks(total, both, lists, stage, shifts, facts):
    sources = both.shape[0]
    rays = 3 * LANES
    first_lane = lax.axis_index("row") % 2 * 8
    room = sources * ROOM + 1
    kinds = both[:, 7, 2 * LANES :][:, :LANES]
    lane = lax.broadcasted_iota(jnp.int32, (sources, LANES), 1) - first_lane
    source = lax.broadcasted_iota(jnp.int32, (sources, LANES), 0)
    power = (1 << jnp.clip(lane + source % 4 * ROOM, 0, 23)).astype(jnp.float32)
    power = jnp.where((lane >= 0) & (lane < ROOM), power, 0.0)
    masks = []
    for kind in range(2):
        bits = jnp.where(kinds == kind, power, 0.0)
        masks.append(
            [jnp.sum(bits[at : at + 4]).astype(jnp.int32) for at in range(0, sources, 4)]
        )
    counts = []
    for kind in range(2):
        count = jnp.int32(0)
        for at in range(sources):
            for k in range(ROOM):
                lists[kind * room + count] = at * 8 + k
                count = count + ((masks[kind][at // 4] >> (at % 4 * ROOM + k)) & 1)
        lists[kind * room + count] = ROOM
        counts.append(count)

    def doubled(cell):
        return (2 * cell).astype(jnp.float32).astype(jnp.bfloat16)

    across = doubled(lax.broadcasted_iota(jnp.int32, (WIDE, rays), 0) - HALO)
    own = doubled(lax.broadcasted_iota(jnp.int32, (TILE, rays), 0))
    edge = lax.broadcasted_iota(jnp.int32, (2 * HALO, rays), 0)
    edge = doubled(jnp.where(edge < HALO, edge - HALO, edge + (TILE - HALO)))
    lane = lax.broadcasted_iota(jnp.int32, (1, LANES), 1) - first_lane
    batches = (BATCH, BATCH // 2)
    starts = (0, BATCH)

    def load(kind, step):
        for k in range(batches[kind]):
            at = starts[kind] + k
            entry = lists[kind * room + jnp.minimum(step * batches[kind] + k, counts[kind])]
            source, slot = entry >> 3, entry & 7
            head = both[source, pl.ds(slot, 1), :]
            tail = both[source, pl.ds(ROOM + (slot >> 1), 1), :]
            meta = both[source, 7:8, :][:, 2 * LANES : 3 * LANES]
            stage[0, at : at + 1, :] = head[:, :rays]
            stage[1, at : at + 1, :LANES] = head[:, rays:]
            stage[1, at : at + 1, LANES:] = jnp.where(
                (slot & 1) == 1, tail[:, 2 * LANES :], tail[:, : 2 * LANES]
            )
            shifts[0, at : at + 1, :] = jnp.where(lane == slot + ROWS, meta, 0.0)
            shifts[1, at : at + 1, :] = jnp.where(lane == slot + COLS, meta, 0.0)

    def prepare(begin, end):
        for axis in range(2):
            coords = stage[axis, begin:end, :]
            low = jnp.floor(coords)
            facts[4 * axis, begin:end, :] = 1.0 - (coords - low)
            facts[4 * axis + 1, begin:end, :] = 1.0 - ((low + 1.0) - coords)
            here = 2.0 * low + jnp.sum(shifts[axis, begin:end, :], axis=1, keepdims=True)
            facts[4 * axis + 2, begin:end, :] = here
            facts[4 * axis + 3, begin:end, :] = here + 2.0

    def product(kind, down):
        firsts, seconds = [], []
        for at in range(starts[kind], starts[kind] + batches[kind]):
            row = [facts[j, at : at + 1, :] for j in range(8)]
            firsts.append(hats(row[:4], down))
            seconds.append(hats(row[4:], across))
        return lax.dot_general(
            jnp.concatenate(firsts, axis=1),
            jnp.concatenate(seconds, axis=1),
            (((1,), (1,)), ((), ())),
            preferred_element_type=jnp.float32,
        )

    def add_both(step, sums):
        load(0, step)
        load(1, step)
        prepare(0, 2 * BATCH)
        return sums[0] + product(0, own), sums[1] + product(1, edge)

    def add_own(step, sums):
        load(0, step)
        prepare(0, BATCH)
        return sums + product(0, own)

    def add_edge(step, sums):
        load(1, step)
        prepare(BATCH, 2 * BATCH)
        return sums + product(1, edge)

    top, middle, bottom = slice(0, HALO), slice(HALO, HALO + TILE), slice(HALO + TILE, WIDE)
    steps = [(counts[kind] + batches[kind] - 1) // batches[kind] for kind in range(2)]
    shared = jnp.minimum(steps[0], steps[1])
    inner, outer = lax.fori_loop(
        0, shared, add_both, (total[middle], jnp.concatenate([total[top], total[bottom]], axis=0))
    )
    total[middle] = lax.fori_loop(shared, steps[0], add_own, inner)
    outer = lax.fori_loop(shared, steps[1], add_edge, outer)
    total[top] = outer[:HALO]
    total[bottom] = outer[HALO:]


def spread_kernel(scale, mine_ref, other_ref, before_ref, pairs_ref, last_ref, out_ref, total,
                  left, both, *scratch):
    sources = mine_ref.shape[0]
    both[:sources] = mine_ref[...]
    both[sources:] = other_ref[...]
    if before_ref is None:
        total[...] = jnp.zeros(total.shape, jnp.float32)
    else:
        total[...] = before_ref[...]
    add_blocks(total, both, *scratch)
    cells = total[...]
    blocks = [cells[:, at : at + LANES].astype(jnp.bfloat16) for at in (0, SPAN)]
    for h in range(2):
        for u in range(TURNS):
            left[h * LONG : (h + 1) * LONG, u * LANES : (u + 1) * LANES] = blocks[h][
                u * STEP : u * STEP + LONG, :
            ]
    lowest = jnp.concatenate([block[2 * HALO :, :] for block in blocks], axis=0)
    ends = jnp.dot(lowest, last_ref[...], preferred_element_type=jnp.float32)
    evens = [ends[:TILE], ends[TILE:]]
    odds = [jnp.zeros((TILE, LANES), jnp.float32)] * 2
    for p in range(0, STEP * SPAN, 2 * LANES):
        both = jnp.dot(left[...], pairs_ref[:, p : p + 2 * LANES], preferred_element_type=jnp.float32)
        for h in range(2):
            for lanes in (0, LANES):
                s = (p + lanes) // SPAN
                part = both[h * LONG : (h + 1) * LONG, lanes : lanes + LANES]
                evens[h] = evens[h] + part[s : s + TILE]
                odds[h] = odds[h] + part[s + 1 : s + 1 + TILE]
    low = evens[0] + pltpu.roll(odds[0], SPAN, 1)
    high = pltpu.roll(evens[1], SPAN, 1) + odds[1]
    lane = lax.broadcasted_iota(jnp.int32, (TILE, LANES), 1)
    out_ref[...] = jnp.where(lane < SPAN, low, high) / scale


def shards(positions, destination, profile):
    blocks, _, rays = positions.shape
    row_count, col_count = lax.axis_size("row"), lax.axis_size("col")
    tiles = row_count * col_count
    width = -(-(3 * blocks + tiles) // LANES) * LANES

    def exchange(turn):
        kernel, given = pack_kernel, (turn, destination.T, positions)
        if turn is None:
            kernel, given = functools.partial(pack_kernel, None), (destination.T, positions)
        outgoing = pl.pallas_call(
            kernel,
            out_shape=jax.ShapeDtypeStruct((8 * tiles, rays + LANES), jnp.float32),
            in_specs=[SMEM, VMEM, VMEM][-len(given) :],
            out_specs=VMEM,
            scratch_shapes=[
                pltpu.VMEM((1, width), jnp.float32),
                pltpu.VMEM((width, rays + LANES), jnp.float32),
            ],
            compiler_params=pltpu.CompilerParams(vmem_limit_bytes=63_400_000),
            name="pack",
        )(*given)
        return lax.all_to_all(
            outgoing.reshape(tiles, 8, rays + LANES), ("row", "col"), split_axis=0, concat_axis=0, tiled=True
        )

    def deposit(mine, before, pairs, last):
        other = lax.ppermute(mine, "row", [(i, i ^ 1) for i in range(row_count)])
        scale = blocks * rays / (TILE * TILE)
        kernel, given = functools.partial(spread_kernel, scale), (mine, other, before, pairs, last)
        if before is None:
            kernel = lambda mine, other, *refs: spread_kernel(scale, mine, other, None, *refs)
            given = (mine, other, pairs, last)
        return pl.pallas_call(
            kernel,
            out_shape=(
                jax.ShapeDtypeStruct((TILE, TILE), jnp.float32),
                jax.ShapeDtypeStruct((WIDE, WIDE), jnp.float32),
            ),
            in_specs=[VMEM] * len(given),
            out_specs=(VMEM, VMEM),
            scratch_shapes=[
                pltpu.VMEM((2 * LONG, TURNS * LANES), jnp.bfloat16),
                pltpu.VMEM((2 * tiles, 8, rays + LANES), jnp.float32),
                pltpu.SMEM((2 * (2 * tiles * ROOM + 1),), jnp.int32),
                pltpu.VMEM((2, 2 * BATCH, rays), jnp.float32),
                pltpu.VMEM((2, 2 * BATCH, LANES), jnp.float32),
                pltpu.VMEM((8, 2 * BATCH, rays), jnp.float32),
            ],
            compiler_params=LIMIT,
            name="spread",
        )(*given)

    mine = exchange(None)
    pairs, last = pl.pallas_call(
        table_kernel,
        out_shape=(
            jax.ShapeDtypeStruct((TURNS * LANES, STEP * SPAN), jnp.bfloat16),
            jax.ShapeDtypeStruct((LANES, LANES), jnp.bfloat16),
        ),
        in_specs=[VMEM],
        out_specs=(VMEM, VMEM),
        compiler_params=LIMIT,
        cost_estimate=pl.CostEstimate(flops=10_000_000, bytes_accessed=6_000_000, transcendentals=0),
        name="table",
    )(profile)
    mine, pairs, last = lax.optimization_barrier((mine, pairs, last))
    turns = jnp.max(mine[:, 7, 2 * LANES + COUNT]).astype(jnp.int32)
    out, total = deposit(mine, None, pairs, last)

    def more(state):
        turn, _, total = state
        out, total = deposit(exchange(jnp.full((1,), turn, jnp.int32)), total, pairs, last)
        return turn + 1, out, total

    return lax.while_loop(lambda state: state[0] < turns, more, (jnp.int32(1), out, total))[1]


def solution(mesh):
    placed = (P(("maps", "row", "col"), None, None), P(("maps", "row", "col"), None), P())
    return jax.shard_map(
        shards, mesh=mesh, in_specs=placed, out_specs=P(("maps", "row"), "col"), check_vma=False
    )
```

```python
import functools

import jax
import jax.numpy as jnp
from jax import lax
from jax.experimental import pallas as pl
from jax.experimental.pallas import tpu as pltpu
from jax.sharding import PartitionSpec as P

TILE = 128
HALO = 32
MOST = 4
DISC = 2 * HALO + 1
STEP = 16
LONG = TILE + STEP
TURNS = 2 * HALO // STEP
WIDE = TILE + 2 * HALO
LANES = 128
SPAN = 64
BATCH = 8
ROOM = 5
COUNT = 16
ROWS = 32
COLS = 64
FAR = 1024.0

VMEM = pl.BlockSpec(memory_space=pltpu.VMEM)
SMEM = pl.BlockSpec(memory_space=pltpu.SMEM)
LIMIT = pltpu.CompilerParams(vmem_limit_bytes=32 * 1024 * 1024)


def touches(distance, least, most):
    before = (distance == -1.0) & (most > TILE - HALO - 1.0)
    after = (distance == 1.0) & (least < HALO)
    return (distance == 0.0) | before | after


def pack_kernel(turn_ref, dest_ref, rays_ref, out_ref, labels, parts):
    blocks, _, rays = rays_ref.shape
    tiles = out_ref.shape[0] // 8
    width = parts.shape[0]
    col_count = lax.axis_size("col")
    skip = 0.0 if turn_ref is None else 2.0 * ROOM * turn_ref[0].astype(jnp.float32)
    lane = lax.broadcasted_iota(jnp.int32, (blocks, width), 1)
    place = lax.broadcasted_iota(jnp.int32, (blocks, width), 0)
    there = (lane % blocks == place) & (lane < 3 * blocks)

    def laid(column):
        return jnp.sum(jnp.where(there, column, 0.0), axis=0, keepdims=True)

    labels[...] = jnp.full(labels.shape, -1.0, jnp.float32)
    for g in range(3):
        labels[0:1, g * blocks : (g + 1) * blocks] = dest_ref[...].astype(jnp.float32)
    label = labels[...]
    label_row = jnp.floor((label + 0.5) / col_count)
    label_col = label - label_row * col_count
    first, second = rays_ref[:, 0, :], rays_ref[:, 1, :]
    least_row, most_row = laid(jnp.min(first, 1, keepdims=True)), laid(jnp.max(first, 1, keepdims=True))
    least_col, most_col = laid(jnp.min(second, 1, keepdims=True)), laid(jnp.max(second, 1, keepdims=True))
    earlier = lax.broadcasted_iota(jnp.int32, (width, width), 0)
    later = lax.broadcasted_iota(jnp.int32, (width, width), 1)
    earlier = jnp.where((earlier < later % blocks) & (later < 3 * blocks), 1.0, 0.0).astype(jnp.bfloat16)

    def chosen(tile):
        odd = (tile // col_count % 2).astype(jnp.float32)
        row = (tile // col_count).astype(jnp.float32) - odd
        dc = label_col - (tile % col_count).astype(jnp.float32)
        aside = touches(dc, least_col, most_col) & (label >= 0.0)

        def coded(dr):
            reach = aside & touches(dr, least_row, most_row)
            return reach, jnp.where(reach, jnp.where(dr == 0.0, 0.0, 1.0), FAR), dr

        even, odds = coded(label_row - row), coded(label_row - row - 1.0)
        reach = jnp.where(even[0] | odds[0], 1.0, 0.0)
        rank = jnp.dot(reach.astype(jnp.bfloat16), earlier, preferred_element_type=jnp.float32)
        left = rank - skip - odd
        slot = jnp.floor(left * 0.5)
        mine = (reach > 0.0) & (slot * 2.0 == left) & (slot >= 0.0) & (slot < ROOM)
        return jnp.where(mine, slot, -1.0), even, odds, dc, (rank + 1.0) * reach

    slot, even, odds, dc, most = chosen(lax.broadcasted_iota(jnp.int32, (tiles, width), 0))
    most = jnp.max(jnp.max(most, axis=1, keepdims=True), axis=0, keepdims=True)
    turns = jnp.floor((most + (2.0 * ROOM - 0.5)) / (2.0 * ROOM))
    lane = lax.broadcasted_iota(jnp.int32, (tiles, width), 1)
    meta = jnp.where(lane == COUNT, turns, FAR)
    for k in range(ROOM):
        here = (slot == k) & (lane < blocks)
        columns = [(COLS + k, dc * (2.0 * TILE)), (COLS + 8 + k, dc * (2.0 * TILE))]
        for at, (_, kind, dr) in ((k, even), (8 + k, odds)):
            columns += [(at, kind), (ROWS + at, dr * (2.0 * TILE))]
        for at, value in columns:
            found = jnp.sum(jnp.where(here, value - FAR, 0.0), axis=1, keepdims=True) + FAR
            meta = jnp.where(lane == at, found, meta)

    parts[...] = jnp.zeros(parts.shape, jnp.float32)
    parts[:blocks, :rays] = first
    parts[:blocks, rays:] = second[:, :LANES]
    parts[blocks : 2 * blocks, : 2 * LANES] = second[:, LANES:]
    parts[2 * blocks : 3 * blocks, 2 * LANES :] = second[:, LANES:]
    parts[3 * blocks : 3 * blocks + tiles, 2 * LANES : 3 * LANES] = meta[:, :LANES]

    row = lax.broadcasted_iota(jnp.int32, (8 * tiles, width), 0)
    group = lax.broadcasted_iota(jnp.int32, (8 * tiles, width), 1)
    slot = chosen(row // 8)[0]
    within = row % 8
    low = (2 * (within - ROOM)).astype(jnp.float32)
    head = (group < blocks) & (within < ROOM) & (slot == within.astype(jnp.float32))
    even = (group >= blocks) & (group < 2 * blocks) & (within >= ROOM) & (slot == low)
    uneven = (group >= 2 * blocks) & (group < 3 * blocks) & (within >= ROOM) & (slot == low + 1.0)
    codes = (group - 3 * blocks == row // 8) & (group >= 3 * blocks) & (within == 7)
    select = jnp.where(head | even | uneven | codes, 1.0, 0.0).astype(jnp.bfloat16)
    rest = parts[...]
    total = jnp.zeros(out_ref.shape, jnp.float32)
    for _ in range(3):
        part = rest.astype(jnp.bfloat16)
        rest = rest - part.astype(jnp.float32)
        total = total + jnp.dot(select, part, preferred_element_type=jnp.float32)
    out_ref[...] = total


def table_kernel(profile_ref, pairs_ref, last_ref):
    a = lax.broadcasted_iota(jnp.int32, (DISC, DISC), 0) - HALO
    c = lax.broadcasted_iota(jnp.int32, (DISC, DISC), 1) - HALO
    weights = jnp.where(a * a + c * c <= HALO * HALO, profile_ref[...], 0.0)
    kernel = (weights / jnp.sum(weights)).astype(jnp.bfloat16)
    source = lax.broadcasted_iota(jnp.int32, (DISC, LANES), 0)
    target = lax.broadcasted_iota(jnp.int32, (DISC, LANES), 1)
    mirror = jnp.where((source + target) % LANES == 0, 1.0, 0.0).astype(jnp.bfloat16)
    mirrored = jnp.dot(kernel, mirror, preferred_element_type=jnp.float32)
    left = lax.broadcasted_iota(jnp.int32, (LANES, LANES), 1) < SPAN

    def band(row, start):
        wide = jnp.broadcast_to(mirrored[row : row + 1, :], (LANES, LANES))
        return pltpu.roll(wide, start, 1, stride=1, stride_axis=0)

    for u in range(TURNS):
        for s in range(0, STEP, 2):
            row = u * STEP + s
            both = jnp.where(left, band(row, 0), band(row + 1, SPAN))
            pairs_ref[u * LANES : (u + 1) * LANES, s * SPAN : (s + 2) * SPAN] = both.astype(jnp.bfloat16)
    last_ref[...] = jnp.where(left, band(2 * HALO, 0), 0.0).astype(jnp.bfloat16)


def hats(row, cell):
    near, far, here, there = (value.astype(jnp.bfloat16) for value in row)
    zero = jnp.zeros((), jnp.bfloat16)
    return jnp.where(cell == here, near, jnp.where(cell == there, far, zero))


def add_blocks(total, both, lists, stage, shifts, facts):
    sources = both.shape[0]
    rays = 3 * LANES
    first_lane = lax.axis_index("row") % 2 * 8
    room = sources * ROOM + 1
    kinds = both[:, 7, 2 * LANES :][:, :LANES]
    lane = lax.broadcasted_iota(jnp.int32, (sources, LANES), 1) - first_lane
    source = lax.broadcasted_iota(jnp.int32, (sources, LANES), 0)
    power = (1 << jnp.clip(lane + source % 4 * ROOM, 0, 23)).astype(jnp.float32)
    power = jnp.where((lane >= 0) & (lane < ROOM), power, 0.0)
    masks = []
    for kind in range(2):
        bits = jnp.where(kinds == kind, power, 0.0)
        masks.append(
            [jnp.sum(bits[at : at + 4]).astype(jnp.int32) for at in range(0, sources, 4)]
        )
    counts = []
    for kind in range(2):
        count = jnp.int32(0)
        for at in range(sources):
            for k in range(ROOM):
                lists[kind * room + count] = at * 8 + k
                count = count + ((masks[kind][at // 4] >> (at % 4 * ROOM + k)) & 1)
        lists[kind * room + count] = ROOM
        counts.append(count)

    def doubled(cell):
        return (2 * cell).astype(jnp.float32).astype(jnp.bfloat16)

    across = doubled(lax.broadcasted_iota(jnp.int32, (WIDE, rays), 0) - HALO)
    own = doubled(lax.broadcasted_iota(jnp.int32, (TILE, rays), 0))
    edge = lax.broadcasted_iota(jnp.int32, (2 * HALO, rays), 0)
    edge = doubled(jnp.where(edge < HALO, edge - HALO, edge + (TILE - HALO)))
    lane = lax.broadcasted_iota(jnp.int32, (1, LANES), 1) - first_lane
    batches = (BATCH, BATCH // 2)
    starts = (0, BATCH)

    def load(kind, step):
        for k in range(batches[kind]):
            at = starts[kind] + k
            entry = lists[kind * room + jnp.minimum(step * batches[kind] + k, counts[kind])]
            source, slot = entry >> 3, entry & 7
            head = both[source, pl.ds(slot, 1), :]
            tail = both[source, pl.ds(ROOM + (slot >> 1), 1), :]
            meta = both[source, 7:8, :][:, 2 * LANES : 3 * LANES]
            stage[0, at : at + 1, :] = head[:, :rays]
            stage[1, at : at + 1, :LANES] = head[:, rays:]
            stage[1, at : at + 1, LANES:] = jnp.where(
                (slot & 1) == 1, tail[:, 2 * LANES :], tail[:, : 2 * LANES]
            )
            shifts[0, at : at + 1, :] = jnp.where(lane == slot + ROWS, meta, 0.0)
            shifts[1, at : at + 1, :] = jnp.where(lane == slot + COLS, meta, 0.0)

    def prepare(begin, end):
        for axis in range(2):
            coords = stage[axis, begin:end, :]
            low = jnp.floor(coords)
            facts[4 * axis, begin:end, :] = 1.0 - (coords - low)
            facts[4 * axis + 1, begin:end, :] = 1.0 - ((low + 1.0) - coords)
            here = 2.0 * low + jnp.sum(shifts[axis, begin:end, :], axis=1, keepdims=True)
            facts[4 * axis + 2, begin:end, :] = here
            facts[4 * axis + 3, begin:end, :] = here + 2.0

    def product(kind, down):
        firsts, seconds = [], []
        for at in range(starts[kind], starts[kind] + batches[kind]):
            row = [facts[j, at : at + 1, :] for j in range(8)]
            firsts.append(hats(row[:4], down))
            seconds.append(hats(row[4:], across))
        return lax.dot_general(
            jnp.concatenate(firsts, axis=1),
            jnp.concatenate(seconds, axis=1),
            (((1,), (1,)), ((), ())),
            preferred_element_type=jnp.float32,
        )

    def add_both(step, sums):
        load(0, step)
        load(1, step)
        prepare(0, 2 * BATCH)
        return sums[0] + product(0, own), sums[1] + product(1, edge)

    def add_own(step, sums):
        load(0, step)
        prepare(0, BATCH)
        return sums + product(0, own)

    def add_edge(step, sums):
        load(1, step)
        prepare(BATCH, 2 * BATCH)
        return sums + product(1, edge)

    top, middle, bottom = slice(0, HALO), slice(HALO, HALO + TILE), slice(HALO + TILE, WIDE)
    steps = [(counts[kind] + batches[kind] - 1) // batches[kind] for kind in range(2)]
    shared = jnp.minimum(steps[0], steps[1])
    inner, outer = lax.fori_loop(
        0, shared, add_both, (total[middle], jnp.concatenate([total[top], total[bottom]], axis=0))
    )
    total[middle] = lax.fori_loop(shared, steps[0], add_own, inner)
    outer = lax.fori_loop(shared, steps[1], add_edge, outer)
    total[top] = outer[:HALO]
    total[bottom] = outer[HALO:]


def spread_kernel(scale, mine_ref, other_ref, before_ref, pairs_ref, last_ref, out_ref, total,
                  left, both, *scratch):
    sources = mine_ref.shape[0]
    both[:sources] = mine_ref[...]
    both[sources:] = other_ref[...]
    if before_ref is None:
        total[...] = jnp.zeros(total.shape, jnp.float32)
    else:
        total[...] = before_ref[...]
    add_blocks(total, both, *scratch)
    cells = total[...]
    blocks = [cells[:, at : at + LANES].astype(jnp.bfloat16) for at in (0, SPAN)]
    for h in range(2):
        for u in range(TURNS):
            left[h * LONG : (h + 1) * LONG, u * LANES : (u + 1) * LANES] = blocks[h][
                u * STEP : u * STEP + LONG, :
            ]
    lowest = jnp.concatenate([block[2 * HALO :, :] for block in blocks], axis=0)
    ends = jnp.dot(lowest, last_ref[...], preferred_element_type=jnp.float32)
    evens = [ends[:TILE], ends[TILE:]]
    odds = [jnp.zeros((TILE, LANES), jnp.float32)] * 2
    for p in range(0, STEP * SPAN, 2 * LANES):
        both = jnp.dot(left[...], pairs_ref[:, p : p + 2 * LANES], preferred_element_type=jnp.float32)
        for h in range(2):
            for lanes in (0, LANES):
                s = (p + lanes) // SPAN
                part = both[h * LONG : (h + 1) * LONG, lanes : lanes + LANES]
                evens[h] = evens[h] + part[s : s + TILE]
                odds[h] = odds[h] + part[s + 1 : s + 1 + TILE]
    low = evens[0] + pltpu.roll(odds[0], SPAN, 1)
    high = pltpu.roll(evens[1], SPAN, 1) + odds[1]
    lane = lax.broadcasted_iota(jnp.int32, (TILE, LANES), 1)
    out_ref[...] = jnp.where(lane < SPAN, low, high) / scale


def shards(positions, destination, profile):
    blocks, _, rays = positions.shape
    row_count, col_count = lax.axis_size("row"), lax.axis_size("col")
    tiles = row_count * col_count
    width = -(-(3 * blocks + tiles) // LANES) * LANES

    def exchange(turn):
        kernel, given = pack_kernel, (turn, destination.T, positions)
        if turn is None:
            kernel, given = functools.partial(pack_kernel, None), (destination.T, positions)
        outgoing = pl.pallas_call(
            kernel,
            out_shape=jax.ShapeDtypeStruct((8 * tiles, rays + LANES), jnp.float32),
            in_specs=[SMEM, VMEM, VMEM][-len(given) :],
            out_specs=VMEM,
            scratch_shapes=[
                pltpu.VMEM((1, width), jnp.float32),
                pltpu.VMEM((width, rays + LANES), jnp.float32),
            ],
            compiler_params=pltpu.CompilerParams(vmem_limit_bytes=67_104_000),
            name="pack",
        )(*given)
        return lax.all_to_all(
            outgoing.reshape(tiles, 8, rays + LANES), ("row", "col"), split_axis=0, concat_axis=0, tiled=True
        )

    def deposit(mine, before, pairs, last):
        other = lax.ppermute(mine, "row", [(i, i ^ 1) for i in range(row_count)])
        scale = blocks * rays / (TILE * TILE)
        kernel, given = functools.partial(spread_kernel, scale), (mine, other, before, pairs, last)
        if before is None:
            kernel = lambda mine, other, *refs: spread_kernel(scale, mine, other, None, *refs)
            given = (mine, other, pairs, last)
        return pl.pallas_call(
            kernel,
            out_shape=(
                jax.ShapeDtypeStruct((TILE, TILE), jnp.float32),
                jax.ShapeDtypeStruct((WIDE, WIDE), jnp.float32),
            ),
            in_specs=[VMEM] * len(given),
            out_specs=(VMEM, VMEM),
            scratch_shapes=[
                pltpu.VMEM((2 * LONG, TURNS * LANES), jnp.bfloat16),
                pltpu.VMEM((2 * tiles, 8, rays + LANES), jnp.float32),
                pltpu.SMEM((2 * (2 * tiles * ROOM + 1),), jnp.int32),
                pltpu.VMEM((2, 2 * BATCH, rays), jnp.float32),
                pltpu.VMEM((2, 2 * BATCH, LANES), jnp.float32),
                pltpu.VMEM((8, 2 * BATCH, rays), jnp.float32),
            ],
            compiler_params=LIMIT,
            name="spread",
        )(*given)

    mine = exchange(None)
    pairs, last = pl.pallas_call(
        table_kernel,
        out_shape=(
            jax.ShapeDtypeStruct((TURNS * LANES, STEP * SPAN), jnp.bfloat16),
            jax.ShapeDtypeStruct((LANES, LANES), jnp.bfloat16),
        ),
        in_specs=[VMEM],
        out_specs=(VMEM, VMEM),
        compiler_params=LIMIT,
        cost_estimate=pl.CostEstimate(flops=10_000_000, bytes_accessed=6_000_000, transcendentals=0),
        name="table",
    )(profile)
    mine, pairs, last = lax.optimization_barrier((mine, pairs, last))
    turns = jnp.max(mine[:, 7, 2 * LANES + COUNT]).astype(jnp.int32)
    out, total = deposit(mine, None, pairs, last)

    def more(state):
        turn, _, total = state
        out, total = deposit(exchange(jnp.full((1,), turn, jnp.int32)), total, pairs, last)
        return turn + 1, out, total

    return lax.while_loop(lambda state: state[0] < turns, more, (jnp.int32(1), out, total))[1]


def solution(mesh):
    placed = (P(("maps", "row", "col"), None, None), P(("maps", "row", "col"), None), P())
    return jax.shard_map(
        shards, mesh=mesh, in_specs=placed, out_specs=P(("maps", "row"), "col"), check_vma=False
    )
```

```python
import functools

import jax
import jax.numpy as jnp
from jax import lax
from jax.experimental import pallas as pl
from jax.experimental.pallas import tpu as pltpu
from jax.sharding import PartitionSpec as P

TILE = 128
HALO = 32
MOST = 4
DISC = 2 * HALO + 1
STEP = 16
LONG = TILE + STEP
TURNS = 2 * HALO // STEP
WIDE = TILE + 2 * HALO
LANES = 128
SPAN = 64
BATCH = 8
ROOM = 5
COUNT = 16
ROWS = 32
COLS = 64
FAR = 1024.0

VMEM = pl.BlockSpec(memory_space=pltpu.VMEM)
SMEM = pl.BlockSpec(memory_space=pltpu.SMEM)
ALONE = pltpu.CompilerParams(vmem_limit_bytes=67_104_000)
LIMIT = pltpu.CompilerParams(vmem_limit_bytes=32 * 1024 * 1024)


def touches(distance, least, most):
    before = (distance == -1.0) & (most > TILE - HALO - 1.0)
    after = (distance == 1.0) & (least < HALO)
    return (distance == 0.0) | before | after


def pack_kernel(turn_ref, dest_ref, rays_ref, out_ref, labels, parts):
    blocks, _, rays = rays_ref.shape
    tiles = out_ref.shape[0] // 8
    width = parts.shape[0]
    col_count = lax.axis_size("col")
    skip = 0.0 if turn_ref is None else 2.0 * ROOM * turn_ref[0].astype(jnp.float32)
    lane = lax.broadcasted_iota(jnp.int32, (blocks, width), 1)
    place = lax.broadcasted_iota(jnp.int32, (blocks, width), 0)
    there = (lane % blocks == place) & (lane < 3 * blocks)

    def laid(column):
        return jnp.sum(jnp.where(there, column, 0.0), axis=0, keepdims=True)

    labels[...] = jnp.full(labels.shape, -1.0, jnp.float32)
    for g in range(3):
        labels[0:1, g * blocks : (g + 1) * blocks] = dest_ref[...].astype(jnp.float32)
    label = labels[...]
    label_row = jnp.floor((label + 0.5) / col_count)
    label_col = label - label_row * col_count
    first, second = rays_ref[:, 0, :], rays_ref[:, 1, :]
    least_row, most_row = laid(jnp.min(first, 1, keepdims=True)), laid(jnp.max(first, 1, keepdims=True))
    least_col, most_col = laid(jnp.min(second, 1, keepdims=True)), laid(jnp.max(second, 1, keepdims=True))
    earlier = lax.broadcasted_iota(jnp.int32, (width, width), 0)
    later = lax.broadcasted_iota(jnp.int32, (width, width), 1)
    earlier = jnp.where((earlier < later % blocks) & (later < 3 * blocks), 1.0, 0.0).astype(jnp.bfloat16)

    def chosen(tile):
        odd = (tile // col_count % 2).astype(jnp.float32)
        row = (tile // col_count).astype(jnp.float32) - odd
        dc = label_col - (tile % col_count).astype(jnp.float32)
        aside = touches(dc, least_col, most_col) & (label >= 0.0)

        def coded(dr):
            reach = aside & touches(dr, least_row, most_row)
            return reach, jnp.where(reach, jnp.where(dr == 0.0, 0.0, 2.0) + jnp.where(dc == 0.0, 0.0, 1.0), FAR), dr

        even, odds = coded(label_row - row), coded(label_row - row - 1.0)
        reach = jnp.where(even[0] | odds[0], 1.0, 0.0)
        rank = jnp.dot(reach.astype(jnp.bfloat16), earlier, preferred_element_type=jnp.float32)
        left = rank - skip - odd
        slot = jnp.floor(left * 0.5)
        mine = (reach > 0.0) & (slot * 2.0 == left) & (slot >= 0.0) & (slot < ROOM)
        return jnp.where(mine, slot, -1.0), even, odds, dc, (rank + 1.0) * reach

    slot, even, odds, dc, most = chosen(lax.broadcasted_iota(jnp.int32, (tiles, width), 0))
    most = jnp.max(jnp.max(most, axis=1, keepdims=True), axis=0, keepdims=True)
    turns = jnp.floor((most + (2.0 * ROOM - 0.5)) / (2.0 * ROOM))
    lane = lax.broadcasted_iota(jnp.int32, (tiles, width), 1)
    meta = jnp.where(lane == COUNT, turns, FAR)
    for k in range(ROOM):
        here = (slot == k) & (lane < blocks)
        columns = [(COLS + k, dc * (2.0 * TILE)), (COLS + 8 + k, dc * (2.0 * TILE))]
        for at, (_, kind, dr) in ((k, even), (8 + k, odds)):
            columns += [(at, kind), (ROWS + at, dr * (2.0 * TILE))]
        for at, value in columns:
            found = jnp.sum(jnp.where(here, value - FAR, 0.0), axis=1, keepdims=True) + FAR
            meta = jnp.where(lane == at, found, meta)

    parts[...] = jnp.zeros(parts.shape, jnp.float32)
    parts[:blocks, :rays] = first
    parts[:blocks, rays:] = second[:, :LANES]
    parts[blocks : 2 * blocks, : 2 * LANES] = second[:, LANES:]
    parts[2 * blocks : 3 * blocks, 2 * LANES :] = second[:, LANES:]
    parts[3 * blocks : 3 * blocks + tiles, 2 * LANES : 3 * LANES] = meta[:, :LANES]

    row = lax.broadcasted_iota(jnp.int32, (8 * tiles, width), 0)
    group = lax.broadcasted_iota(jnp.int32, (8 * tiles, width), 1)
    slot = chosen(row // 8)[0]
    within = row % 8
    low = (2 * (within - ROOM)).astype(jnp.float32)
    head = (group < blocks) & (within < ROOM) & (slot == within.astype(jnp.float32))
    even = (group >= blocks) & (group < 2 * blocks) & (within >= ROOM) & (slot == low)
    uneven = (group >= 2 * blocks) & (group < 3 * blocks) & (within >= ROOM) & (slot == low + 1.0)
    codes = (group - 3 * blocks == row // 8) & (group >= 3 * blocks) & (within == 7)
    select = jnp.where(head | even | uneven | codes, 1.0, 0.0).astype(jnp.bfloat16)
    rest = parts[...]
    total = jnp.zeros(out_ref.shape, jnp.float32)
    for _ in range(3):
        part = rest.astype(jnp.bfloat16)
        rest = rest - part.astype(jnp.float32)
        total = total + jnp.dot(select, part, preferred_element_type=jnp.float32)
    out_ref[...] = total


def table_kernel(profile_ref, pairs_ref, last_ref):
    a = lax.broadcasted_iota(jnp.int32, (DISC, DISC), 0) - HALO
    c = lax.broadcasted_iota(jnp.int32, (DISC, DISC), 1) - HALO
    weights = jnp.where(a * a + c * c <= HALO * HALO, profile_ref[...], 0.0)
    kernel = (weights / jnp.sum(weights)).astype(jnp.bfloat16)
    source = lax.broadcasted_iota(jnp.int32, (DISC, LANES), 0)
    target = lax.broadcasted_iota(jnp.int32, (DISC, LANES), 1)
    mirror = jnp.where((source + target) % LANES == 0, 1.0, 0.0).astype(jnp.bfloat16)
    mirrored = jnp.dot(kernel, mirror, preferred_element_type=jnp.float32)
    left = lax.broadcasted_iota(jnp.int32, (LANES, LANES), 1) < SPAN

    def band(row, start):
        wide = jnp.broadcast_to(mirrored[row : row + 1, :], (LANES, LANES))
        return pltpu.roll(wide, start, 1, stride=1, stride_axis=0)

    for u in range(TURNS):
        for s in range(0, STEP, 2):
            row = u * STEP + s
            both = jnp.where(left, band(row, 0), band(row + 1, SPAN))
            pairs_ref[u * LANES : (u + 1) * LANES, s * SPAN : (s + 2) * SPAN] = both.astype(jnp.bfloat16)
    last_ref[...] = jnp.where(left, band(2 * HALO, 0), 0.0).astype(jnp.bfloat16)


def hats(row, cell):
    near, far, here, there = (value.astype(jnp.bfloat16) for value in row)
    zero = jnp.zeros((), jnp.bfloat16)
    return jnp.where(cell == here, near, jnp.where(cell == there, far, zero))


def deposited(both, lists, stage, shifts, facts):
    sources = both.shape[0]
    rays = 3 * LANES
    first_lane = lax.axis_index("row") % 2 * 8
    room = sources * ROOM + 1
    kinds = both[:, 7, 2 * LANES :][:, :LANES]
    lane = lax.broadcasted_iota(jnp.int32, (sources, LANES), 1) - first_lane
    source = lax.broadcasted_iota(jnp.int32, (sources, LANES), 0)
    power = (1 << jnp.clip(lane + source % 4 * ROOM, 0, 23)).astype(jnp.float32)
    power = jnp.where((lane >= 0) & (lane < ROOM), power, 0.0)

    def bits(chosen):
        held = jnp.where(chosen, power, 0.0)
        return [jnp.sum(held[at : at + 4]).astype(jnp.int32) for at in range(0, sources, 4)]

    reached, outer = bits(kinds < 4.0), bits((kinds == 2.0) | (kinds == 3.0))
    beside = bits((kinds == 1.0) | (kinds == 3.0))
    masks = [
        [r & ~(o | b) for r, o, b in zip(reached, outer, beside)],
        [b & ~o for o, b in zip(outer, beside)],
        [o & ~b for o, b in zip(outer, beside)],
        [o & b for o, b in zip(outer, beside)],
    ]
    counts = []
    for kind in range(4):
        count = jnp.int32(0)
        for at in range(sources):
            for k in range(ROOM):
                lists[kind * room + count] = at * 8 + k
                count = count + ((masks[kind][at // 4] >> (at % 4 * ROOM + k)) & 1)
        lists[kind * room + count] = ROOM
        counts.append(count)

    def doubled(cell):
        return (2 * cell).astype(jnp.float32).astype(jnp.bfloat16)

    own = doubled(lax.broadcasted_iota(jnp.int32, (TILE, rays), 0))
    edge = lax.broadcasted_iota(jnp.int32, (2 * HALO, rays), 0)
    edge = doubled(jnp.where(edge < HALO, edge - HALO, edge + (TILE - HALO)))
    lane = lax.broadcasted_iota(jnp.int32, (1, LANES), 1) - first_lane

    def load(kind, step, batch, start):
        for k in range(batch):
            at = start + k
            entry = lists[kind * room + jnp.minimum(step * batch + k, counts[kind])]
            source, slot = entry >> 3, entry & 7
            head = both[source, pl.ds(slot, 1), :]
            tail = both[source, pl.ds(ROOM + (slot >> 1), 1), :]
            meta = both[source, 7:8, :][:, 2 * LANES : 3 * LANES]
            stage[0, at : at + 1, :] = head[:, :rays]
            stage[1, at : at + 1, :LANES] = head[:, rays:]
            stage[1, at : at + 1, LANES:] = jnp.where(
                (slot & 1) == 1, tail[:, 2 * LANES :], tail[:, : 2 * LANES]
            )
            shifts[0, at : at + 1, :] = jnp.where(lane == slot + ROWS, meta, 0.0)
            shifts[1, at : at + 1, :] = jnp.where(lane == slot + COLS, meta, 0.0)

    def prepare(begin, end):
        for axis in range(2):
            coords = stage[axis, begin:end, :]
            low = jnp.floor(coords)
            facts[4 * axis, begin:end, :] = 1.0 - (coords - low)
            facts[4 * axis + 1, begin:end, :] = 1.0 - ((low + 1.0) - coords)
            here = 2.0 * low + jnp.sum(shifts[axis, begin:end, :], axis=1, keepdims=True)
            facts[4 * axis + 2, begin:end, :] = here
            facts[4 * axis + 3, begin:end, :] = here + 2.0

    def product(kind, batch, start):
        down, across = (own, edge)[kind // 2], (own, edge)[kind % 2]
        firsts, seconds = [], []
        for at in range(start, start + batch):
            row = [facts[j, at : at + 1, :] for j in range(8)]
            firsts.append(hats(row[:4], down))
            seconds.append(hats(row[4:], across))
        return lax.dot_general(
            jnp.concatenate(firsts, axis=1),
            jnp.concatenate(seconds, axis=1),
            (((1,), (1,)), ((), ())),
            preferred_element_type=jnp.float32,
        )

    def together(one, two):
        def step_one(step, sums, given=one):
            load(given[0], step, given[1], given[2])
            prepare(given[2], given[2] + 8)
            return sums + product(*given)

        def step_both(step, sums):
            load(one[0], step, one[1], one[2])
            load(two[0], step, two[1], two[2])
            prepare(0, 2 * BATCH)
            return sums[0] + product(*one), sums[1] + product(*two)

        zeros = [
            jnp.zeros(((TILE, 2 * HALO)[kind // 2], (TILE, 2 * HALO)[kind % 2]), jnp.float32)
            for kind in (one[0], two[0])
        ]
        steps = [(counts[kind] + batch - 1) // batch for kind, batch, _ in (one, two)]
        shared = jnp.minimum(steps[0], steps[1])
        sums = lax.fori_loop(0, shared, step_both, tuple(zeros))
        return [
            lax.fori_loop(shared, steps[j], functools.partial(step_one, given=(one, two)[j]), sums[j])
            for j in range(2)
        ]

    inside, corners = together((0, BATCH, 0), (3, BATCH // 2, BATCH))
    beside, above = together((1, BATCH // 2, 0), (2, BATCH // 2, BATCH))

    def wide(middle, ends):
        return jnp.concatenate([ends[:, :HALO], middle, ends[:, HALO:]], axis=1)

    middle, ends = wide(inside, beside), wide(above, corners)
    return jnp.concatenate([ends[:HALO], middle, ends[HALO:]], axis=0)


def spread_kernel(scale, mine_ref, other_ref, before_ref, pairs_ref, last_ref, out_ref, total_ref,
                  left, both, *scratch):
    sources = mine_ref.shape[0]
    both[:sources] = mine_ref[...]
    both[sources:] = other_ref[...]
    cells = deposited(both, *scratch)
    if before_ref is not None:
        cells = cells + before_ref[...]
    total_ref[...] = cells
    blocks = [cells[:, at : at + LANES].astype(jnp.bfloat16) for at in (0, SPAN)]
    for h in range(2):
        for u in range(TURNS):
            left[h * LONG : (h + 1) * LONG, u * LANES : (u + 1) * LANES] = blocks[h][
                u * STEP : u * STEP + LONG, :
            ]
    lowest = jnp.concatenate([block[2 * HALO :, :] for block in blocks], axis=0)
    ends = jnp.dot(lowest, last_ref[...], preferred_element_type=jnp.float32)
    evens = [ends[:TILE], ends[TILE:]]
    odds = [jnp.zeros((TILE, LANES), jnp.float32)] * 2
    for p in range(0, STEP * SPAN, 2 * LANES):
        both = jnp.dot(left[...], pairs_ref[:, p : p + 2 * LANES], preferred_element_type=jnp.float32)
        for h in range(2):
            for lanes in (0, LANES):
                s = (p + lanes) // SPAN
                part = both[h * LONG : (h + 1) * LONG, lanes : lanes + LANES]
                evens[h] = evens[h] + part[s : s + TILE]
                odds[h] = odds[h] + part[s + 1 : s + 1 + TILE]
    low = evens[0] + pltpu.roll(odds[0], SPAN, 1)
    high = pltpu.roll(evens[1], SPAN, 1) + odds[1]
    lane = lax.broadcasted_iota(jnp.int32, (TILE, LANES), 1)
    out_ref[...] = jnp.where(lane < SPAN, low, high) / scale


def shards(positions, destination, profile):
    blocks, _, rays = positions.shape
    row_count, col_count = lax.axis_size("row"), lax.axis_size("col")
    tiles = row_count * col_count
    width = -(-(3 * blocks + tiles) // LANES) * LANES

    def exchange(turn):
        kernel, given = pack_kernel, (turn, destination.T, positions)
        if turn is None:
            kernel, given = functools.partial(pack_kernel, None), (destination.T, positions)
        outgoing = pl.pallas_call(
            kernel,
            out_shape=jax.ShapeDtypeStruct((8 * tiles, rays + LANES), jnp.float32),
            in_specs=[SMEM, VMEM, VMEM][-len(given) :],
            out_specs=VMEM,
            scratch_shapes=[
                pltpu.VMEM((1, width), jnp.float32),
                pltpu.VMEM((width, rays + LANES), jnp.float32),
            ],
            compiler_params=ALONE if turn is None else LIMIT,
            name="pack",
        )(*given)
        return lax.all_to_all(
            outgoing.reshape(tiles, 8, rays + LANES), ("row", "col"), split_axis=0, concat_axis=0, tiled=True
        )

    def deposit(mine, before, pairs, last):
        other = lax.ppermute(mine, "row", [(i, i ^ 1) for i in range(row_count)])
        scale = blocks * rays / (TILE * TILE)
        kernel, given = functools.partial(spread_kernel, scale), (mine, other, before, pairs, last)
        if before is None:
            kernel = lambda mine, other, *refs: spread_kernel(scale, mine, other, None, *refs)
            given = (mine, other, pairs, last)
        return pl.pallas_call(
            kernel,
            out_shape=(
                jax.ShapeDtypeStruct((TILE, TILE), jnp.float32),
                jax.ShapeDtypeStruct((WIDE, WIDE), jnp.float32),
            ),
            in_specs=[VMEM] * len(given),
            out_specs=(VMEM, VMEM),
            scratch_shapes=[
                pltpu.VMEM((2 * LONG, TURNS * LANES), jnp.bfloat16),
                pltpu.VMEM((2 * tiles, 8, rays + LANES), jnp.float32),
                pltpu.SMEM((4 * (2 * tiles * ROOM + 1),), jnp.int32),
                pltpu.VMEM((2, 2 * BATCH, rays), jnp.float32),
                pltpu.VMEM((2, 2 * BATCH, LANES), jnp.float32),
                pltpu.VMEM((8, 2 * BATCH, rays), jnp.float32),
            ],
            compiler_params=LIMIT,
            name="spread",
        )(*given)

    mine = exchange(None)
    pairs, last = pl.pallas_call(
        table_kernel,
        out_shape=(
            jax.ShapeDtypeStruct((TURNS * LANES, STEP * SPAN), jnp.bfloat16),
            jax.ShapeDtypeStruct((LANES, LANES), jnp.bfloat16),
        ),
        in_specs=[VMEM],
        out_specs=(VMEM, VMEM),
        compiler_params=LIMIT,
        cost_estimate=pl.CostEstimate(flops=10_000_000, bytes_accessed=6_000_000, transcendentals=0),
        name="table",
    )(profile)
    mine, pairs, last = lax.optimization_barrier((mine, pairs, last))
    turns = jnp.max(mine[:, 7, 2 * LANES + COUNT]).astype(jnp.int32)
    out, total = deposit(mine, None, pairs, last)

    def more(state):
        turn, _, total = state
        out, total = deposit(exchange(jnp.full((1,), turn, jnp.int32)), total, pairs, last)
        return turn + 1, out, total

    return lax.while_loop(lambda state: state[0] < turns, more, (jnp.int32(1), out, total))[1]


def solution(mesh):
    placed = (P(("maps", "row", "col"), None, None), P(("maps", "row", "col"), None), P())
    return jax.shard_map(
        shards, mesh=mesh, in_specs=placed, out_specs=P(("maps", "row"), "col"), check_vma=False
    )
```

```python
import functools

import jax
import jax.numpy as jnp
from jax import lax
from jax.experimental import pallas as pl
from jax.experimental.pallas import tpu as pltpu
from jax.sharding import PartitionSpec as P

TILE = 128
HALO = 32
MOST = 4
DISC = 2 * HALO + 1
STEP = 16
LONG = TILE + STEP
TURNS = 2 * HALO // STEP
WIDE = TILE + 2 * HALO
LANES = 128
SPAN = 64
BATCH = 8
ROOM = 5
COUNT = 16
ROWS = 32
COLS = 64
FAR = 1024.0

VMEM = pl.BlockSpec(memory_space=pltpu.VMEM)
SMEM = pl.BlockSpec(memory_space=pltpu.SMEM)
ALONE = pltpu.CompilerParams(vmem_limit_bytes=67_104_000)
LIMIT = pltpu.CompilerParams(vmem_limit_bytes=32 * 1024 * 1024)


def touches(distance, least, most):
    before = (distance == -1.0) & (most > TILE - HALO - 1.0)
    after = (distance == 1.0) & (least < HALO)
    return (distance == 0.0) | before | after


def pack_kernel(turn_ref, dest_ref, rays_ref, out_ref, labels, parts):
    blocks, _, rays = rays_ref.shape
    tiles = out_ref.shape[0] // 8
    width = parts.shape[0]
    col_count = lax.axis_size("col")
    skip = 0.0 if turn_ref is None else 2.0 * ROOM * turn_ref[0].astype(jnp.float32)
    lane = lax.broadcasted_iota(jnp.int32, (blocks, width), 1)
    place = lax.broadcasted_iota(jnp.int32, (blocks, width), 0)
    there = (lane % blocks == place) & (lane < 3 * blocks)

    def laid(column):
        return jnp.sum(jnp.where(there, column, 0.0), axis=0, keepdims=True)

    labels[...] = jnp.full(labels.shape, -1.0, jnp.float32)
    for g in range(3):
        labels[0:1, g * blocks : (g + 1) * blocks] = dest_ref[...].astype(jnp.float32)
    label = labels[...]
    label_row = jnp.floor((label + 0.5) / col_count)
    label_col = label - label_row * col_count
    first, second = rays_ref[:, 0, :], rays_ref[:, 1, :]
    least_row, most_row = laid(jnp.min(first, 1, keepdims=True)), laid(jnp.max(first, 1, keepdims=True))
    least_col, most_col = laid(jnp.min(second, 1, keepdims=True)), laid(jnp.max(second, 1, keepdims=True))
    earlier = lax.broadcasted_iota(jnp.int32, (width, width), 0)
    later = lax.broadcasted_iota(jnp.int32, (width, width), 1)
    earlier = jnp.where((earlier < later % blocks) & (later < 3 * blocks), 1.0, 0.0).astype(jnp.bfloat16)

    def chosen(tile):
        odd = (tile // col_count % 2).astype(jnp.float32)
        row = (tile // col_count).astype(jnp.float32) - odd
        dc = label_col - (tile % col_count).astype(jnp.float32)
        aside = touches(dc, least_col, most_col) & (label >= 0.0)

        def coded(dr):
            reach = aside & touches(dr, least_row, most_row)
            return reach, jnp.where(reach, jnp.where(dr == 0.0, 0.0, 2.0) + jnp.where(dc == 0.0, 0.0, 1.0), FAR), dr

        even, odds = coded(label_row - row), coded(label_row - row - 1.0)
        reach = jnp.where(even[0] | odds[0], 1.0, 0.0)
        rank = jnp.dot(reach.astype(jnp.bfloat16), earlier, preferred_element_type=jnp.float32)
        left = rank - skip - odd
        slot = jnp.floor(left * 0.5)
        mine = (reach > 0.0) & (slot * 2.0 == left) & (slot >= 0.0) & (slot < ROOM)
        return jnp.where(mine, slot, -1.0), even, odds, dc, (rank + 1.0) * reach

    slot, even, odds, dc, most = chosen(lax.broadcasted_iota(jnp.int32, (tiles, width), 0))
    most = jnp.max(jnp.max(most, axis=1, keepdims=True), axis=0, keepdims=True)
    turns = jnp.floor((most + (2.0 * ROOM - 0.5)) / (2.0 * ROOM))
    lane = lax.broadcasted_iota(jnp.int32, (tiles, width), 1)
    meta = jnp.where(lane == COUNT, turns, FAR)
    for k in range(ROOM):
        here = (slot == k) & (lane < blocks)
        columns = [(COLS + k, dc * (2.0 * TILE)), (COLS + 8 + k, dc * (2.0 * TILE))]
        for at, (_, kind, dr) in ((k, even), (8 + k, odds)):
            columns += [(at, kind), (ROWS + at, dr * (2.0 * TILE))]
        for at, value in columns:
            found = jnp.sum(jnp.where(here, value - FAR, 0.0), axis=1, keepdims=True) + FAR
            meta = jnp.where(lane == at, found, meta)

    parts[...] = jnp.zeros(parts.shape, jnp.float32)
    parts[:blocks, :rays] = first
    parts[:blocks, rays:] = second[:, :LANES]
    parts[blocks : 2 * blocks, : 2 * LANES] = second[:, LANES:]
    parts[2 * blocks : 3 * blocks, 2 * LANES :] = second[:, LANES:]
    parts[3 * blocks : 3 * blocks + tiles, 2 * LANES : 3 * LANES] = meta[:, :LANES]

    row = lax.broadcasted_iota(jnp.int32, (8 * tiles, width), 0)
    group = lax.broadcasted_iota(jnp.int32, (8 * tiles, width), 1)
    slot = chosen(row // 8)[0]
    within = row % 8
    low = (2 * (within - ROOM)).astype(jnp.float32)
    head = (group < blocks) & (within < ROOM) & (slot == within.astype(jnp.float32))
    even = (group >= blocks) & (group < 2 * blocks) & (within >= ROOM) & (slot == low)
    uneven = (group >= 2 * blocks) & (group < 3 * blocks) & (within >= ROOM) & (slot == low + 1.0)
    codes = (group - 3 * blocks == row // 8) & (group >= 3 * blocks) & (within == 7)
    select = jnp.where(head | even | uneven | codes, 1.0, 0.0).astype(jnp.bfloat16)
    rest = parts[...]
    total = jnp.zeros(out_ref.shape, jnp.float32)
    for _ in range(3):
        part = rest.astype(jnp.bfloat16)
        rest = rest - part.astype(jnp.float32)
        total = total + jnp.dot(select, part, preferred_element_type=jnp.float32)
    out_ref[...] = total


def table_kernel(profile_ref, dest_ref, rays_ref, pairs_ref, last_ref, dest_copy, rays_copy):
    dest_copy[...] = dest_ref[...]
    rays_copy[...] = rays_ref[...]
    a = lax.broadcasted_iota(jnp.int32, (DISC, DISC), 0) - HALO
    c = lax.broadcasted_iota(jnp.int32, (DISC, DISC), 1) - HALO
    weights = jnp.where(a * a + c * c <= HALO * HALO, profile_ref[...], 0.0)
    kernel = (weights / jnp.sum(weights)).astype(jnp.bfloat16)
    source = lax.broadcasted_iota(jnp.int32, (DISC, LANES), 0)
    target = lax.broadcasted_iota(jnp.int32, (DISC, LANES), 1)
    mirror = jnp.where((source + target) % LANES == 0, 1.0, 0.0).astype(jnp.bfloat16)
    mirrored = jnp.dot(kernel, mirror, preferred_element_type=jnp.float32)
    left = lax.broadcasted_iota(jnp.int32, (LANES, LANES), 1) < SPAN

    def band(row, start):
        wide = jnp.broadcast_to(mirrored[row : row + 1, :], (LANES, LANES))
        return pltpu.roll(wide, start, 1, stride=1, stride_axis=0)

    for u in range(TURNS):
        for s in range(0, STEP, 2):
            row = u * STEP + s
            both = jnp.where(left, band(row, 0), band(row + 1, SPAN))
            pairs_ref[u * LANES : (u + 1) * LANES, s * SPAN : (s + 2) * SPAN] = both.astype(jnp.bfloat16)
    last_ref[...] = jnp.where(left, band(2 * HALO, 0), 0.0).astype(jnp.bfloat16)


def hats(row, cell):
    near, far, here, there = (value.astype(jnp.bfloat16) for value in row)
    zero = jnp.zeros((), jnp.bfloat16)
    return jnp.where(cell == here, near, jnp.where(cell == there, far, zero))


def deposited(both, lists, stage, shifts, facts):
    sources = both.shape[0]
    rays = 3 * LANES
    first_lane = lax.axis_index("row") % 2 * 8
    room = sources * ROOM + 1
    kinds = both[:, 7, 2 * LANES :][:, :LANES]
    lane = lax.broadcasted_iota(jnp.int32, (sources, LANES), 1) - first_lane
    source = lax.broadcasted_iota(jnp.int32, (sources, LANES), 0)
    power = (1 << jnp.clip(lane + source % 4 * ROOM, 0, 23)).astype(jnp.float32)
    power = jnp.where((lane >= 0) & (lane < ROOM), power, 0.0)

    def bits(chosen):
        held = jnp.where(chosen, power, 0.0)
        return [jnp.sum(held[at : at + 4]).astype(jnp.int32) for at in range(0, sources, 4)]

    reached, outer = bits(kinds < 4.0), bits((kinds == 2.0) | (kinds == 3.0))
    beside = bits((kinds == 1.0) | (kinds == 3.0))
    masks = [
        [r & ~(o | b) for r, o, b in zip(reached, outer, beside)],
        [b & ~o for o, b in zip(outer, beside)],
        [o & ~b for o, b in zip(outer, beside)],
        [o & b for o, b in zip(outer, beside)],
    ]
    def listed(counts, slots):
        counts = list(counts)
        for kind in range(4):
            for at in range(sources):
                for k in slots:
                    lists[kind * room + counts[kind]] = at * 8 + k
                    bit = (masks[kind][at // 4] >> (at % 4 * ROOM + k)) & 1
                    counts[kind] = counts[kind] + bit
        return tuple(counts)

    rare = sum(1 << (at * ROOM + k) for at in range(4) for k in range(3, ROOM))
    seldom = functools.reduce(jnp.bitwise_or, reached) & rare
    counts = listed((jnp.int32(0),) * 4, range(3))
    counts = lax.cond(seldom != 0, lambda held: listed(held, range(3, ROOM)), lambda held: held, counts)
    for kind in range(4):
        lists[kind * room + counts[kind]] = ROOM

    def doubled(cell):
        return (2 * cell).astype(jnp.float32).astype(jnp.bfloat16)

    own = doubled(lax.broadcasted_iota(jnp.int32, (TILE, rays), 0))
    edge = lax.broadcasted_iota(jnp.int32, (2 * HALO, rays), 0)
    edge = doubled(jnp.where(edge < HALO, edge - HALO, edge + (TILE - HALO)))
    lane = lax.broadcasted_iota(jnp.int32, (1, LANES), 1) - first_lane

    def load(kind, step, batch, start):
        for k in range(batch):
            at = start + k
            entry = lists[kind * room + jnp.minimum(step * batch + k, counts[kind])]
            source, slot = entry >> 3, entry & 7
            head = both[source, pl.ds(slot, 1), :]
            tail = both[source, pl.ds(ROOM + (slot >> 1), 1), :]
            meta = both[source, 7:8, :][:, 2 * LANES : 3 * LANES]
            stage[0, at : at + 1, :] = head[:, :rays]
            stage[1, at : at + 1, :LANES] = head[:, rays:]
            stage[1, at : at + 1, LANES:] = jnp.where(
                (slot & 1) == 1, tail[:, 2 * LANES :], tail[:, : 2 * LANES]
            )
            shifts[0, at : at + 1, :] = jnp.where(lane == slot + ROWS, meta, 0.0)
            shifts[1, at : at + 1, :] = jnp.where(lane == slot + COLS, meta, 0.0)

    def prepare(begin, end):
        for axis in range(2):
            coords = stage[axis, begin:end, :]
            low = jnp.floor(coords)
            facts[4 * axis, begin:end, :] = 1.0 - (coords - low)
            facts[4 * axis + 1, begin:end, :] = 1.0 - ((low + 1.0) - coords)
            here = 2.0 * low + jnp.sum(shifts[axis, begin:end, :], axis=1, keepdims=True)
            facts[4 * axis + 2, begin:end, :] = here
            facts[4 * axis + 3, begin:end, :] = here + 2.0

    def product(kind, batch, start):
        down, across = (own, edge)[kind // 2], (own, edge)[kind % 2]
        firsts, seconds = [], []
        for at in range(start, start + batch):
            row = [facts[j, at : at + 1, :] for j in range(8)]
            firsts.append(hats(row[:4], down))
            seconds.append(hats(row[4:], across))
        return lax.dot_general(
            jnp.concatenate(firsts, axis=1),
            jnp.concatenate(seconds, axis=1),
            (((1,), (1,)), ((), ())),
            preferred_element_type=jnp.float32,
        )

    def together(one, two):
        def ready(step, *given):
            for kind, batch, start in given:
                load(kind, step, batch, start)
            prepare(given[0][2], given[-1][2] + 8)

        def step_one(step, sums, given=one):
            sums = sums + product(*given)
            ready(step + 1, given)
            return sums

        def step_both(step, sums):
            sums = sums[0] + product(*one), sums[1] + product(*two)
            ready(step + 1, one, two)
            return sums

        ready(0, one, two)
        zeros = [
            jnp.zeros(((TILE, 2 * HALO)[kind // 2], (TILE, 2 * HALO)[kind % 2]), jnp.float32)
            for kind in (one[0], two[0])
        ]
        steps = [(counts[kind] + batch - 1) // batch for kind, batch, _ in (one, two)]
        shared = jnp.minimum(steps[0], steps[1])
        sums = lax.fori_loop(0, shared, step_both, tuple(zeros))
        return [
            lax.fori_loop(shared, steps[j], functools.partial(step_one, given=(one, two)[j]), sums[j])
            for j in range(2)
        ]

    inside, corners = together((0, BATCH, 0), (3, BATCH // 2, BATCH))
    beside, above = together((1, BATCH // 2, 0), (2, BATCH // 2, BATCH))

    def wide(middle, ends):
        return jnp.concatenate([ends[:, :HALO], middle, ends[:, HALO:]], axis=1)

    middle, ends = wide(inside, beside), wide(above, corners)
    return jnp.concatenate([ends[:HALO], middle, ends[HALO:]], axis=0)


def spread_kernel(scale, mine_ref, other_ref, before_ref, pairs_ref, last_ref, out_ref, total_ref,
                  left, both, *scratch):
    sources = mine_ref.shape[0]
    both[:sources] = mine_ref[...]
    both[sources:] = other_ref[...]
    cells = deposited(both, *scratch)
    if before_ref is not None:
        cells = cells + before_ref[...]
    total_ref[...] = cells
    blocks = [cells[:, at : at + LANES].astype(jnp.bfloat16) for at in (0, SPAN)]
    for h in range(2):
        for u in range(TURNS):
            left[h * LONG : (h + 1) * LONG, u * LANES : (u + 1) * LANES] = blocks[h][
                u * STEP : u * STEP + LONG, :
            ]
    lowest = jnp.concatenate([block[2 * HALO :, :] for block in blocks], axis=0)
    ends = jnp.dot(lowest, last_ref[...], preferred_element_type=jnp.float32)
    evens = [ends[:TILE], ends[TILE:]]
    odds = [jnp.zeros((TILE, LANES), jnp.float32)] * 2
    for p in range(0, STEP * SPAN, 2 * LANES):
        both = jnp.dot(left[...], pairs_ref[:, p : p + 2 * LANES], preferred_element_type=jnp.float32)
        for h in range(2):
            for lanes in (0, LANES):
                s = (p + lanes) // SPAN
                part = both[h * LONG : (h + 1) * LONG, lanes : lanes + LANES]
                evens[h] = evens[h] + part[s : s + TILE]
                odds[h] = odds[h] + part[s + 1 : s + 1 + TILE]
    low = evens[0] + pltpu.roll(odds[0], SPAN, 1)
    high = pltpu.roll(evens[1], SPAN, 1) + odds[1]
    lane = lax.broadcasted_iota(jnp.int32, (TILE, LANES), 1)
    out_ref[...] = jnp.where(lane < SPAN, low, high) / scale


def shards(positions, destination, profile):
    blocks, _, rays = positions.shape
    row_count, col_count = lax.axis_size("row"), lax.axis_size("col")
    tiles = row_count * col_count
    width = -(-(3 * blocks + tiles) // LANES) * LANES

    def exchange(turn, labels, coords):
        kernel, given = pack_kernel, (turn, labels, coords)
        if turn is None:
            kernel, given = functools.partial(pack_kernel, None), (labels, coords)
        outgoing = pl.pallas_call(
            kernel,
            out_shape=jax.ShapeDtypeStruct((8 * tiles, rays + LANES), jnp.float32),
            in_specs=[SMEM, VMEM, VMEM][-len(given) :],
            out_specs=VMEM,
            scratch_shapes=[
                pltpu.VMEM((1, width), jnp.float32),
                pltpu.VMEM((width, rays + LANES), jnp.float32),
            ],
            compiler_params=ALONE if turn is None else LIMIT,
            name="pack",
        )(*given)
        return lax.all_to_all(
            outgoing.reshape(tiles, 8, rays + LANES), ("row", "col"), split_axis=0, concat_axis=0, tiled=True
        )

    def deposit(mine, before, pairs, last):
        other = lax.ppermute(mine, "row", [(i, i ^ 1) for i in range(row_count)])
        scale = blocks * rays / (TILE * TILE)
        kernel, given = functools.partial(spread_kernel, scale), (mine, other, before, pairs, last)
        if before is None:
            kernel = lambda mine, other, *refs: spread_kernel(scale, mine, other, None, *refs)
            given = (mine, other, pairs, last)
        return pl.pallas_call(
            kernel,
            out_shape=(
                jax.ShapeDtypeStruct((TILE, TILE), jnp.float32),
                jax.ShapeDtypeStruct((WIDE, WIDE), jnp.float32),
            ),
            in_specs=[VMEM] * len(given),
            out_specs=(VMEM, VMEM),
            scratch_shapes=[
                pltpu.VMEM((2 * LONG, TURNS * LANES), jnp.bfloat16),
                pltpu.VMEM((2 * tiles, 8, rays + LANES), jnp.float32),
                pltpu.SMEM((4 * (2 * tiles * ROOM + 1),), jnp.int32),
                pltpu.VMEM((2, 2 * BATCH, rays), jnp.float32),
                pltpu.VMEM((2, 2 * BATCH, LANES), jnp.float32),
                pltpu.VMEM((8, 2 * BATCH, rays), jnp.float32),
            ],
            compiler_params=LIMIT,
            name="spread",
        )(*given)

    mine = exchange(None, destination.T, positions)
    pairs, last, labels, coords = pl.pallas_call(
        table_kernel,
        out_shape=(
            jax.ShapeDtypeStruct((TURNS * LANES, STEP * SPAN), jnp.bfloat16),
            jax.ShapeDtypeStruct((LANES, LANES), jnp.bfloat16),
            jax.ShapeDtypeStruct((1, blocks), jnp.int32),
            jax.ShapeDtypeStruct(positions.shape, jnp.float32),
        ),
        in_specs=[VMEM] * 3,
        out_specs=(VMEM,) * 4,
        compiler_params=LIMIT,
        cost_estimate=pl.CostEstimate(flops=10_000_000, bytes_accessed=6_000_000, transcendentals=0),
        name="table",
    )(profile, destination.T, positions)
    mine, pairs, last, labels, coords = lax.optimization_barrier((mine, pairs, last, labels, coords))
    turns = jnp.max(mine[:, 7, 2 * LANES + COUNT]).astype(jnp.int32)
    out, total = deposit(mine, None, pairs, last)

    def more(state):
        turn, _, total = state
        out, total = deposit(
            exchange(jnp.full((1,), turn, jnp.int32), labels, coords), total, pairs, last
        )
        return turn + 1, out, total

    return lax.while_loop(lambda state: state[0] < turns, more, (jnp.int32(1), out, total))[1]


def solution(mesh):
    placed = (P(("maps", "row", "col"), None, None), P(("maps", "row", "col"), None), P())
    return jax.shard_map(
        shards, mesh=mesh, in_specs=placed, out_specs=P(("maps", "row"), "col"), check_vma=False
    )
```

```python
import functools

import jax
import jax.numpy as jnp
from jax import lax
from jax.experimental import pallas as pl
from jax.experimental.pallas import tpu as pltpu
from jax.sharding import PartitionSpec as P

TILE = 128
HALO = 32
MOST = 4
DISC = 2 * HALO + 1
STEP = 16
LONG = TILE + STEP
TURNS = 2 * HALO // STEP
WIDE = TILE + 2 * HALO
LANES = 128
SPAN = 64
BATCH = 8
ROOM = 5
COUNT = 16
ROWS = 32
COLS = 64
FAR = 1024.0

VMEM = pl.BlockSpec(memory_space=pltpu.VMEM)
SMEM = pl.BlockSpec(memory_space=pltpu.SMEM)
ALONE = pltpu.CompilerParams(vmem_limit_bytes=67_104_000)
LIMIT = pltpu.CompilerParams(vmem_limit_bytes=32 * 1024 * 1024)


def touches(distance, least, most):
    before = (distance == -1.0) & (most > TILE - HALO - 1.0)
    after = (distance == 1.0) & (least < HALO)
    return (distance == 0.0) | before | after


def pack_kernel(turn_ref, dest_ref, rays_ref, out_ref, labels, parts):
    blocks, _, rays = rays_ref.shape
    tiles = out_ref.shape[0] // 8
    width = parts.shape[0]
    col_count = lax.axis_size("col")
    skip = 0.0 if turn_ref is None else 2.0 * ROOM * turn_ref[0].astype(jnp.float32)
    lane = lax.broadcasted_iota(jnp.int32, (blocks, width), 1)
    place = lax.broadcasted_iota(jnp.int32, (blocks, width), 0)
    there = (lane % blocks == place) & (lane < 3 * blocks)

    def laid(column):
        return jnp.sum(jnp.where(there, column, 0.0), axis=0, keepdims=True)

    labels[...] = jnp.full(labels.shape, -1.0, jnp.float32)
    for g in range(3):
        labels[0:1, g * blocks : (g + 1) * blocks] = dest_ref[...].astype(jnp.float32)
    label = labels[...]
    label_row = jnp.floor((label + 0.5) / col_count)
    label_col = label - label_row * col_count
    first, second = rays_ref[:, 0, :], rays_ref[:, 1, :]
    least_row, most_row = laid(jnp.min(first, 1, keepdims=True)), laid(jnp.max(first, 1, keepdims=True))
    least_col, most_col = laid(jnp.min(second, 1, keepdims=True)), laid(jnp.max(second, 1, keepdims=True))
    earlier = lax.broadcasted_iota(jnp.int32, (width, width), 0)
    later = lax.broadcasted_iota(jnp.int32, (width, width), 1)
    earlier = jnp.where((earlier < later % blocks) & (later < 3 * blocks), 1.0, 0.0).astype(jnp.bfloat16)

    def chosen(tile):
        odd = (tile // col_count % 2).astype(jnp.float32)
        row = (tile // col_count).astype(jnp.float32) - odd
        dc = label_col - (tile % col_count).astype(jnp.float32)
        aside = touches(dc, least_col, most_col) & (label >= 0.0)

        def coded(dr):
            reach = aside & touches(dr, least_row, most_row)
            return reach, jnp.where(reach, jnp.where(dr == 0.0, 0.0, 2.0) + jnp.where(dc == 0.0, 0.0, 1.0), FAR), dr

        even, odds = coded(label_row - row), coded(label_row - row - 1.0)
        reach = jnp.where(even[0] | odds[0], 1.0, 0.0)
        rank = jnp.dot(reach.astype(jnp.bfloat16), earlier, preferred_element_type=jnp.float32)
        left = rank - skip - odd
        slot = jnp.floor(left * 0.5)
        mine = (reach > 0.0) & (slot * 2.0 == left) & (slot >= 0.0) & (slot < ROOM)
        return jnp.where(mine, slot, -1.0), even, odds, dc, (rank + 1.0) * reach

    slot, even, odds, dc, most = chosen(lax.broadcasted_iota(jnp.int32, (tiles, width), 0))
    most = jnp.max(jnp.max(most, axis=1, keepdims=True), axis=0, keepdims=True)
    turns = jnp.floor((most + (2.0 * ROOM - 0.5)) / (2.0 * ROOM))
    lane = lax.broadcasted_iota(jnp.int32, (tiles, width), 1)
    meta = jnp.where(lane == COUNT, turns, FAR)
    for k in range(ROOM):
        here = (slot == k) & (lane < blocks)
        columns = [(COLS + k, dc * (2.0 * TILE)), (COLS + 8 + k, dc * (2.0 * TILE))]
        for at, (_, kind, dr) in ((k, even), (8 + k, odds)):
            columns += [(at, kind), (ROWS + at, dr * (2.0 * TILE))]
        for at, value in columns:
            found = jnp.sum(jnp.where(here, value - FAR, 0.0), axis=1, keepdims=True) + FAR
            meta = jnp.where(lane == at, found, meta)

    parts[...] = jnp.zeros(parts.shape, jnp.float32)
    parts[:blocks, :rays] = first
    parts[:blocks, rays:] = second[:, :LANES]
    parts[blocks : 2 * blocks, : 2 * LANES] = second[:, LANES:]
    parts[2 * blocks : 3 * blocks, 2 * LANES :] = second[:, LANES:]
    parts[3 * blocks : 3 * blocks + tiles, 2 * LANES : 3 * LANES] = meta[:, :LANES]

    row = lax.broadcasted_iota(jnp.int32, (8 * tiles, width), 0)
    group = lax.broadcasted_iota(jnp.int32, (8 * tiles, width), 1)
    slot = chosen(row // 8)[0]
    within = row % 8
    low = (2 * (within - ROOM)).astype(jnp.float32)
    head = (group < blocks) & (within < ROOM) & (slot == within.astype(jnp.float32))
    even = (group >= blocks) & (group < 2 * blocks) & (within >= ROOM) & (slot == low)
    uneven = (group >= 2 * blocks) & (group < 3 * blocks) & (within >= ROOM) & (slot == low + 1.0)
    codes = (group - 3 * blocks == row // 8) & (group >= 3 * blocks) & (within == 7)
    select = jnp.where(head | even | uneven | codes, 1.0, 0.0).astype(jnp.bfloat16)
    rest = parts[...]
    total = jnp.zeros(out_ref.shape, jnp.float32)
    for _ in range(3):
        part = rest.astype(jnp.bfloat16)
        rest = rest - part.astype(jnp.float32)
        total = total + jnp.dot(select, part, preferred_element_type=jnp.float32)
    out_ref[...] = total


def build_table(profile_ref, pairs_ref, last_ref):
    a = lax.broadcasted_iota(jnp.int32, (DISC, DISC), 0) - HALO
    c = lax.broadcasted_iota(jnp.int32, (DISC, DISC), 1) - HALO
    weights = jnp.where(a * a + c * c <= HALO * HALO, profile_ref[...], 0.0)
    kernel = (weights / jnp.sum(weights)).astype(jnp.bfloat16)
    source = lax.broadcasted_iota(jnp.int32, (DISC, LANES), 0)
    target = lax.broadcasted_iota(jnp.int32, (DISC, LANES), 1)
    mirror = jnp.where((source + target) % LANES == 0, 1.0, 0.0).astype(jnp.bfloat16)
    mirrored = jnp.dot(kernel, mirror, preferred_element_type=jnp.float32)
    left = lax.broadcasted_iota(jnp.int32, (LANES, LANES), 1) < SPAN

    def band(row, start):
        wide = jnp.broadcast_to(mirrored[row : row + 1, :], (LANES, LANES))
        return pltpu.roll(wide, start, 1, stride=1, stride_axis=0)

    for u in range(TURNS):
        for s in range(0, STEP, 2):
            row = u * STEP + s
            both = jnp.where(left, band(row, 0), band(row + 1, SPAN))
            pairs_ref[u * LANES : (u + 1) * LANES, s * SPAN : (s + 2) * SPAN] = both.astype(jnp.bfloat16)
    last_ref[...] = jnp.where(left, band(2 * HALO, 0), 0.0).astype(jnp.bfloat16)


def hats(row, cell):
    near, far, here, there = (value.astype(jnp.bfloat16) for value in row)
    zero = jnp.zeros((), jnp.bfloat16)
    return jnp.where(cell == here, near, jnp.where(cell == there, far, zero))


def deposited(both, build, lists, stage, shifts, facts):
    sources = both.shape[0]
    rays = 3 * LANES
    first_lane = lax.axis_index("row") % 2 * 8
    room = sources * ROOM + 1
    kinds = both[:, 7, 2 * LANES :][:, :LANES]
    lane = lax.broadcasted_iota(jnp.int32, (sources, LANES), 1) - first_lane
    source = lax.broadcasted_iota(jnp.int32, (sources, LANES), 0)
    power = (1 << jnp.clip(lane + source % 4 * ROOM, 0, 23)).astype(jnp.float32)
    power = jnp.where((lane >= 0) & (lane < ROOM), power, 0.0)

    def bits(chosen):
        held = jnp.where(chosen, power, 0.0)
        return [jnp.sum(held[at : at + 4]).astype(jnp.int32) for at in range(0, sources, 4)]

    reached, outer = bits(kinds < 4.0), bits((kinds == 2.0) | (kinds == 3.0))
    beside = bits((kinds == 1.0) | (kinds == 3.0))
    masks = [
        [r & ~(o | b) for r, o, b in zip(reached, outer, beside)],
        [b & ~o for o, b in zip(outer, beside)],
        [o & ~b for o, b in zip(outer, beside)],
        [o & b for o, b in zip(outer, beside)],
    ]
    def listed(counts, slots):
        counts = list(counts)
        for kind in range(4):
            for at in range(sources):
                for k in slots:
                    lists[kind * room + counts[kind]] = at * 8 + k
                    bit = (masks[kind][at // 4] >> (at % 4 * ROOM + k)) & 1
                    counts[kind] = counts[kind] + bit
        return tuple(counts)

    build()
    rare = sum(1 << (at * ROOM + k) for at in range(4) for k in range(3, ROOM))
    seldom = functools.reduce(jnp.bitwise_or, reached) & rare
    counts = listed((jnp.int32(0),) * 4, range(3))
    counts = lax.cond(seldom != 0, lambda held: listed(held, range(3, ROOM)), lambda held: held, counts)
    for kind in range(4):
        lists[kind * room + counts[kind]] = ROOM

    def doubled(cell):
        return (2 * cell).astype(jnp.float32).astype(jnp.bfloat16)

    own = doubled(lax.broadcasted_iota(jnp.int32, (TILE, rays), 0))
    edge = lax.broadcasted_iota(jnp.int32, (2 * HALO, rays), 0)
    edge = doubled(jnp.where(edge < HALO, edge - HALO, edge + (TILE - HALO)))
    lane = lax.broadcasted_iota(jnp.int32, (1, LANES), 1) - first_lane

    def load(kind, step, batch, start):
        for k in range(batch):
            at = start + k
            entry = lists[kind * room + jnp.minimum(step * batch + k, counts[kind])]
            source, slot = entry >> 3, entry & 7
            head = both[source, pl.ds(slot, 1), :]
            tail = both[source, pl.ds(ROOM + (slot >> 1), 1), :]
            meta = both[source, 7:8, :][:, 2 * LANES : 3 * LANES]
            stage[0, at : at + 1, :] = head[:, :rays]
            stage[1, at : at + 1, :LANES] = head[:, rays:]
            stage[1, at : at + 1, LANES:] = jnp.where(
                (slot & 1) == 1, tail[:, 2 * LANES :], tail[:, : 2 * LANES]
            )
            shifts[0, at : at + 1, :] = jnp.where(lane == slot + ROWS, meta, 0.0)
            shifts[1, at : at + 1, :] = jnp.where(lane == slot + COLS, meta, 0.0)

    def prepare(begin, end):
        for axis in range(2):
            coords = stage[axis, begin:end, :]
            low = jnp.floor(coords)
            facts[4 * axis, begin:end, :] = 1.0 - (coords - low)
            facts[4 * axis + 1, begin:end, :] = 1.0 - ((low + 1.0) - coords)
            here = 2.0 * low + jnp.sum(shifts[axis, begin:end, :], axis=1, keepdims=True)
            facts[4 * axis + 2, begin:end, :] = here
            facts[4 * axis + 3, begin:end, :] = here + 2.0

    def product(kind, batch, start):
        down, across = (own, edge)[kind // 2], (own, edge)[kind % 2]
        firsts, seconds = [], []
        for at in range(start, start + batch):
            row = [facts[j, at : at + 1, :] for j in range(8)]
            firsts.append(hats(row[:4], down))
            seconds.append(hats(row[4:], across))
        return lax.dot_general(
            jnp.concatenate(firsts, axis=1),
            jnp.concatenate(seconds, axis=1),
            (((1,), (1,)), ((), ())),
            preferred_element_type=jnp.float32,
        )

    def together(one, two):
        def ready(step, *given):
            for kind, batch, start in given:
                load(kind, step, batch, start)
            prepare(given[0][2], given[-1][2] + 8)

        def step_one(step, sums, given=one):
            sums = sums + product(*given)
            ready(step + 1, given)
            return sums

        def step_both(step, sums):
            sums = sums[0] + product(*one), sums[1] + product(*two)
            ready(step + 1, one, two)
            return sums

        ready(0, one, two)
        zeros = [
            jnp.zeros(((TILE, 2 * HALO)[kind // 2], (TILE, 2 * HALO)[kind % 2]), jnp.float32)
            for kind in (one[0], two[0])
        ]
        steps = [(counts[kind] + batch - 1) // batch for kind, batch, _ in (one, two)]
        shared = jnp.minimum(steps[0], steps[1])
        sums = lax.fori_loop(0, shared, step_both, tuple(zeros))
        return [
            lax.fori_loop(shared, steps[j], functools.partial(step_one, given=(one, two)[j]), sums[j])
            for j in range(2)
        ]

    inside, corners = together((0, BATCH, 0), (3, BATCH // 2, BATCH))
    beside, above = together((1, BATCH // 2, 0), (2, BATCH // 2, BATCH))

    def wide(middle, ends):
        return jnp.concatenate([ends[:, :HALO], middle, ends[:, HALO:]], axis=1)

    middle, ends = wide(inside, beside), wide(above, corners)
    return jnp.concatenate([ends[:HALO], middle, ends[HALO:]], axis=0)


def spread_kernel(scale, mine_ref, other_ref, profile_ref, dest_ref, rays_ref, before_ref, out_ref,
                  total_ref, dest_copy, rays_copy, pairs_ref, last_ref, left, both, *scratch):
    sources = mine_ref.shape[0]
    both[:sources] = mine_ref[...]
    both[sources:] = other_ref[...]
    dest_copy[...] = dest_ref[...]
    rays_copy[...] = rays_ref[...]
    build = functools.partial(build_table, profile_ref, pairs_ref, last_ref)
    cells = deposited(both, build, *scratch)
    if before_ref is not None:
        cells = cells + before_ref[...]
    total_ref[...] = cells
    blocks = [cells[:, at : at + LANES].astype(jnp.bfloat16) for at in (0, SPAN)]
    for h in range(2):
        for u in range(TURNS):
            left[h * LONG : (h + 1) * LONG, u * LANES : (u + 1) * LANES] = blocks[h][
                u * STEP : u * STEP + LONG, :
            ]
    lowest = jnp.concatenate([block[2 * HALO :, :] for block in blocks], axis=0)
    ends = jnp.dot(lowest, last_ref[...], preferred_element_type=jnp.float32)
    evens = [ends[:TILE], ends[TILE:]]
    odds = [jnp.zeros((TILE, LANES), jnp.float32)] * 2
    for p in range(0, STEP * SPAN, 2 * LANES):
        both = jnp.dot(left[...], pairs_ref[:, p : p + 2 * LANES], preferred_element_type=jnp.float32)
        for h in range(2):
            for lanes in (0, LANES):
                s = (p + lanes) // SPAN
                part = both[h * LONG : (h + 1) * LONG, lanes : lanes + LANES]
                evens[h] = evens[h] + part[s : s + TILE]
                odds[h] = odds[h] + part[s + 1 : s + 1 + TILE]
    low = evens[0] + pltpu.roll(odds[0], SPAN, 1)
    high = pltpu.roll(evens[1], SPAN, 1) + odds[1]
    lane = lax.broadcasted_iota(jnp.int32, (TILE, LANES), 1)
    out_ref[...] = jnp.where(lane < SPAN, low, high) / scale


def shards(positions, destination, profile):
    blocks, _, rays = positions.shape
    row_count, col_count = lax.axis_size("row"), lax.axis_size("col")
    tiles = row_count * col_count
    width = -(-(3 * blocks + tiles) // LANES) * LANES

    def exchange(turn, labels, coords):
        kernel, given = pack_kernel, (turn, labels, coords)
        if turn is None:
            kernel, given = functools.partial(pack_kernel, None), (labels, coords)
        outgoing = pl.pallas_call(
            kernel,
            out_shape=jax.ShapeDtypeStruct((8 * tiles, rays + LANES), jnp.float32),
            in_specs=[SMEM, VMEM, VMEM][-len(given) :],
            out_specs=VMEM,
            scratch_shapes=[
                pltpu.VMEM((1, width), jnp.float32),
                pltpu.VMEM((width, rays + LANES), jnp.float32),
            ],
            compiler_params=ALONE if turn is None else LIMIT,
            name="pack",
        )(*given)
        return lax.all_to_all(
            outgoing.reshape(tiles, 8, rays + LANES), ("row", "col"), split_axis=0, concat_axis=0, tiled=True
        )

    def deposit(mine, labels, coords, before):
        other = lax.ppermute(mine, "row", [(i, i ^ 1) for i in range(row_count)])
        scale = blocks * rays / (TILE * TILE)
        kernel, given = functools.partial(spread_kernel, scale), (mine, other, profile, labels, coords, before)
        if before is None:
            kernel = lambda *refs: spread_kernel(scale, *refs[:5], None, *refs[5:])
            given = given[:5]
        return pl.pallas_call(
            kernel,
            out_shape=(
                jax.ShapeDtypeStruct((TILE, TILE), jnp.float32),
                jax.ShapeDtypeStruct((WIDE, WIDE), jnp.float32),
                jax.ShapeDtypeStruct((1, blocks), jnp.int32),
                jax.ShapeDtypeStruct(positions.shape, jnp.float32),
            ),
            in_specs=[VMEM] * len(given),
            out_specs=(VMEM,) * 4,
            scratch_shapes=[
                pltpu.VMEM((TURNS * LANES, STEP * SPAN), jnp.bfloat16),
                pltpu.VMEM((LANES, LANES), jnp.bfloat16),
                pltpu.VMEM((2 * LONG, TURNS * LANES), jnp.bfloat16),
                pltpu.VMEM((2 * tiles, 8, rays + LANES), jnp.float32),
                pltpu.SMEM((4 * (2 * tiles * ROOM + 1),), jnp.int32),
                pltpu.VMEM((2, 2 * BATCH, rays), jnp.float32),
                pltpu.VMEM((2, 2 * BATCH, LANES), jnp.float32),
                pltpu.VMEM((8, 2 * BATCH, rays), jnp.float32),
            ],
            compiler_params=LIMIT,
            name="spread",
        )(*given)

    mine = exchange(None, destination.T, positions)
    turns = jnp.max(mine[:, 7, 2 * LANES + COUNT]).astype(jnp.int32)
    out, total, labels, coords = deposit(mine, destination.T, positions, None)

    def more(state):
        turn, _, total, labels, coords = state
        mine = exchange(jnp.full((1,), turn, jnp.int32), labels, coords)
        return (turn + 1, *deposit(mine, labels, coords, total))

    state = (jnp.int32(1), out, total, labels, coords)
    return lax.while_loop(lambda state: state[0] < turns, more, state)[1]


def solution(mesh):
    placed = (P(("maps", "row", "col"), None, None), P(("maps", "row", "col"), None), P())
    return jax.shard_map(
        shards, mesh=mesh, in_specs=placed, out_specs=P(("maps", "row"), "col"), check_vma=False
    )
```

```python
import functools

import jax
import jax.numpy as jnp
from jax import lax
from jax.experimental import pallas as pl
from jax.experimental.pallas import tpu as pltpu
from jax.sharding import PartitionSpec as P

TILE = 128
HALO = 32
MOST = 4
DISC = 2 * HALO + 1
STEP = 16
LONG = TILE + STEP
TURNS = 2 * HALO // STEP
WIDE = TILE + 2 * HALO
LANES = 128
SPAN = 64
BATCH = 8
ROOM = 5
COUNT = 16
FAR = 1024.0

VMEM = pl.BlockSpec(memory_space=pltpu.VMEM)
SMEM = pl.BlockSpec(memory_space=pltpu.SMEM)
LIMIT = pltpu.CompilerParams(vmem_limit_bytes=32 * 1024 * 1024)


def touches(distance, least, most):
    before = (distance == -1.0) & (most > TILE - HALO - 1.0)
    after = (distance == 1.0) & (least < HALO)
    return (distance == 0.0) | before | after


def lay_kernel(rays_ref, parts_ref, bounds_ref):
    blocks, _, rays = rays_ref.shape
    width = bounds_ref.shape[1]
    lane = lax.broadcasted_iota(jnp.int32, (blocks, width), 1)
    place = lax.broadcasted_iota(jnp.int32, (blocks, width), 0)
    there = (lane % blocks == place) & (lane < 3 * blocks)
    first, second = rays_ref[:, 0, :], rays_ref[:, 1, :]
    for row, column in enumerate(
        (
            jnp.min(first, 1, keepdims=True),
            jnp.max(first, 1, keepdims=True),
            jnp.min(second, 1, keepdims=True),
            jnp.max(second, 1, keepdims=True),
        )
    ):
        bounds_ref[row : row + 1, :] = jnp.sum(jnp.where(there, column, 0.0), axis=0, keepdims=True)
    parts = parts_ref.at[0]
    parts_ref[...] = jnp.zeros(parts_ref.shape, jnp.bfloat16)
    for part in range(3):
        one, two = first.astype(jnp.bfloat16), second.astype(jnp.bfloat16)
        first, second = first - one.astype(jnp.float32), second - two.astype(jnp.float32)
        parts = parts_ref.at[part]
        parts[:blocks, :rays] = one
        parts[:blocks, rays:] = two[:, :LANES]
        parts[blocks : 2 * blocks, : 2 * LANES] = two[:, LANES:]
        parts[2 * blocks : 3 * blocks, 2 * LANES :] = two[:, LANES:]


def pack_kernel(turn_ref, dest_ref, parts_ref, bounds_ref, out_ref, labels):
    blocks = dest_ref.shape[1]
    tiles = out_ref.shape[0] // 8
    width = parts_ref.shape[1]
    col_count = lax.axis_size("col")
    skip = 0.0 if turn_ref is None else 2.0 * ROOM * turn_ref[0].astype(jnp.float32)
    labels[...] = jnp.full(labels.shape, -1.0, jnp.float32)
    for g in range(3):
        labels[0:1, g * blocks : (g + 1) * blocks] = dest_ref[...].astype(jnp.float32)
    label = labels[...]
    label_row = jnp.floor((label + 0.5) / col_count)
    label_col = label - label_row * col_count
    least_row, most_row, least_col, most_col = (bounds_ref[j : j + 1, :] for j in range(4))
    earlier = lax.broadcasted_iota(jnp.int32, (width, width), 0)
    later = lax.broadcasted_iota(jnp.int32, (width, width), 1)
    earlier = jnp.where((earlier < later % blocks) & (later < 3 * blocks), 1.0, 0.0).astype(jnp.bfloat16)

    def chosen(tile):
        odd = (tile // col_count % 2).astype(jnp.float32)
        row = (tile // col_count).astype(jnp.float32) - odd
        dc = label_col - (tile % col_count).astype(jnp.float32)
        aside = touches(dc, least_col, most_col) & (label >= 0.0)

        def coded(dr):
            reach = aside & touches(dr, least_row, most_row)
            return reach, jnp.where(reach, 3.0 * dr + dc + 4.0, FAR)

        even, odds = coded(label_row - row), coded(label_row - row - 1.0)
        reach = jnp.where(even[0] | odds[0], 1.0, 0.0)
        rank = jnp.dot(reach.astype(jnp.bfloat16), earlier, preferred_element_type=jnp.float32)
        left = rank - skip - odd
        slot = jnp.floor(left * 0.5)
        mine = (reach > 0.0) & (slot * 2.0 == left) & (slot >= 0.0) & (slot < ROOM)
        return jnp.where(mine, slot, -1.0), even[1], odds[1], (rank + 1.0) * reach

    row = lax.broadcasted_iota(jnp.int32, (8 * tiles, width), 0)
    group = lax.broadcasted_iota(jnp.int32, (8 * tiles, width), 1)
    slot = chosen(row // 8)[0]
    within = row % 8
    low = (2 * (within - ROOM)).astype(jnp.float32)
    head = (group < blocks) & (within < ROOM) & (slot == within.astype(jnp.float32))
    even = (group >= blocks) & (group < 2 * blocks) & (within >= ROOM) & (slot == low)
    uneven = (group >= 2 * blocks) & (group < 3 * blocks) & (within >= ROOM) & (slot == low + 1.0)
    select = jnp.where(head | even | uneven, 1.0, 0.0).astype(jnp.bfloat16)
    total = jnp.dot(select, parts_ref[0], preferred_element_type=jnp.float32)
    for part in range(1, 3):
        total = total + jnp.dot(select, parts_ref[part], preferred_element_type=jnp.float32)
    out_ref[...] = total

    slot, even, odds, most = chosen(lax.broadcasted_iota(jnp.int32, (tiles, width), 0))
    most = jnp.max(jnp.max(most, axis=1, keepdims=True), axis=0, keepdims=True)
    turns = jnp.floor((most + (2.0 * ROOM - 0.5)) / (2.0 * ROOM))
    lane = lax.broadcasted_iota(jnp.int32, (tiles, width), 1)
    meta = jnp.where(lane == COUNT, turns, FAR)
    for k in range(ROOM):
        here = (slot == k) & (lane < blocks)
        for at, code in ((k, even), (8 + k, odds)):
            found = jnp.sum(jnp.where(here, code - FAR, 0.0), axis=1, keepdims=True) + FAR
            meta = jnp.where(lane == at, found, meta)
    for t in range(tiles):
        out_ref[8 * t + 7 : 8 * t + 8, 2 * LANES : 3 * LANES] = meta[t : t + 1, :LANES]


def build_table(profile_ref, pairs_ref, last_ref):
    a = lax.broadcasted_iota(jnp.int32, (DISC, DISC), 0) - HALO
    c = lax.broadcasted_iota(jnp.int32, (DISC, DISC), 1) - HALO
    weights = jnp.where(a * a + c * c <= HALO * HALO, profile_ref[...], 0.0)
    kernel = (weights / jnp.sum(weights)).astype(jnp.bfloat16)
    source = lax.broadcasted_iota(jnp.int32, (DISC, LANES), 0)
    target = lax.broadcasted_iota(jnp.int32, (DISC, LANES), 1)
    mirror = jnp.where((source + target) % LANES == 0, 1.0, 0.0).astype(jnp.bfloat16)
    mirrored = jnp.dot(kernel, mirror, preferred_element_type=jnp.float32)
    left = lax.broadcasted_iota(jnp.int32, (LANES, LANES), 1) < SPAN

    def band(row, start):
        wide = jnp.broadcast_to(mirrored[row : row + 1, :], (LANES, LANES))
        return pltpu.roll(wide, start, 1, stride=1, stride_axis=0)

    for u in range(TURNS):
        for s in range(0, STEP, 2):
            row = u * STEP + s
            both = jnp.where(left, band(row, 0), band(row + 1, SPAN))
            pairs_ref[u * LANES : (u + 1) * LANES, s * SPAN : (s + 2) * SPAN] = both.astype(jnp.bfloat16)
    last_ref[...] = jnp.where(left, band(2 * HALO, 0), 0.0).astype(jnp.bfloat16)


def hats(row, cell):
    near, far, here, there = (value.astype(jnp.bfloat16) for value in row)
    zero = jnp.zeros((), jnp.bfloat16)
    return jnp.where(cell == here, near, jnp.where(cell == there, far, zero))


def deposited(both, build, lists, stage, shifts, facts):
    sources = both.shape[0]
    rays = 3 * LANES
    first_lane = lax.axis_index("row") % 2 * 8
    room = sources * ROOM + 1
    code = both[:, 7, 2 * LANES :][:, :LANES]
    rowwise = jnp.floor((code + 0.5) / 3.0)
    held, above, aside = code < 9.0, rowwise != 1.0, code - 3.0 * rowwise != 1.0
    lane = lax.broadcasted_iota(jnp.int32, (sources, LANES), 1) - first_lane
    source = lax.broadcasted_iota(jnp.int32, (sources, LANES), 0)
    power = (1 << jnp.clip(lane + source % 4 * ROOM, 0, 23)).astype(jnp.float32)
    power = jnp.where((lane >= 0) & (lane < ROOM), power, 0.0)

    def bits(chosen):
        value = jnp.where(chosen, power, 0.0)
        return [jnp.sum(value[at : at + 4]).astype(jnp.int32) for at in range(0, sources, 4)]

    reached, outer, beside = bits(held), bits(held & above), bits(held & aside)
    masks = [
        [r & ~(o | b) for r, o, b in zip(reached, outer, beside)],
        [b & ~o for o, b in zip(outer, beside)],
        [o & ~b for o, b in zip(outer, beside)],
        [o & b for o, b in zip(outer, beside)],
    ]
    def listed(counts, slots):
        counts = list(counts)
        for kind in range(4):
            for at in range(sources):
                for k in slots:
                    lists[kind * room + counts[kind]] = at * 8 + k
                    bit = (masks[kind][at // 4] >> (at % 4 * ROOM + k)) & 1
                    counts[kind] = counts[kind] + bit
        return tuple(counts)

    build()
    rare = sum(1 << (at * ROOM + k) for at in range(4) for k in range(3, ROOM))
    seldom = functools.reduce(jnp.bitwise_or, reached) & rare
    counts = listed((jnp.int32(0),) * 4, range(3))
    counts = lax.cond(seldom != 0, lambda held: listed(held, range(3, ROOM)), lambda held: held, counts)
    for kind in range(4):
        lists[kind * room + counts[kind]] = ROOM

    def doubled(cell):
        return (2 * cell).astype(jnp.float32).astype(jnp.bfloat16)

    own = doubled(lax.broadcasted_iota(jnp.int32, (TILE, rays), 0))
    edge = lax.broadcasted_iota(jnp.int32, (2 * HALO, rays), 0)
    edge = doubled(jnp.where(edge < HALO, edge - HALO, edge + (TILE - HALO)))
    lane = lax.broadcasted_iota(jnp.int32, (1, LANES), 1) - first_lane

    def load(kind, step, batch, start):
        for k in range(batch):
            at = start + k
            entry = lists[kind * room + jnp.minimum(step * batch + k, counts[kind])]
            source, slot = entry >> 3, entry & 7
            head = both[source, pl.ds(slot, 1), :]
            tail = both[source, pl.ds(ROOM + (slot >> 1), 1), :]
            meta = both[source, 7:8, :][:, 2 * LANES : 3 * LANES]
            stage[0, at : at + 1, :] = head[:, :rays]
            stage[1, at : at + 1, :LANES] = head[:, rays:]
            stage[1, at : at + 1, LANES:] = jnp.where(
                (slot & 1) == 1, tail[:, 2 * LANES :], tail[:, : 2 * LANES]
            )
            shifts[at : at + 1, :] = jnp.where(lane == slot, meta, 0.0)

    def prepare(begin, end):
        code = jnp.sum(shifts[begin:end, :], axis=1, keepdims=True)
        rowwise = jnp.floor((code + 0.5) / 3.0)
        offsets = (rowwise - 1.0) * (2.0 * TILE), (code - 3.0 * rowwise - 1.0) * (2.0 * TILE)
        for axis in range(2):
            coords = stage[axis, begin:end, :]
            low = jnp.floor(coords)
            facts[4 * axis, begin:end, :] = 1.0 - (coords - low)
            facts[4 * axis + 1, begin:end, :] = 1.0 - ((low + 1.0) - coords)
            here = 2.0 * low + offsets[axis]
            facts[4 * axis + 2, begin:end, :] = here
            facts[4 * axis + 3, begin:end, :] = here + 2.0

    def product(kind, batch, start):
        down, across = (own, edge)[kind // 2], (own, edge)[kind % 2]
        firsts, seconds = [], []
        for at in range(start, start + batch):
            row = [facts[j, at : at + 1, :] for j in range(8)]
            firsts.append(hats(row[:4], down))
            seconds.append(hats(row[4:], across))
        return lax.dot_general(
            jnp.concatenate(firsts, axis=1),
            jnp.concatenate(seconds, axis=1),
            (((1,), (1,)), ((), ())),
            preferred_element_type=jnp.float32,
        )

    def together(one, two):
        def ready(step, *given):
            for kind, batch, start in given:
                load(kind, step, batch, start)
            prepare(given[0][2], given[-1][2] + 8)

        def step_one(step, sums, given=one):
            sums = sums + product(*given)
            ready(step + 1, given)
            return sums

        def step_both(step, sums):
            sums = sums[0] + product(*one), sums[1] + product(*two)
            ready(step + 1, one, two)
            return sums

        ready(0, one, two)
        zeros = [
            jnp.zeros(((TILE, 2 * HALO)[kind // 2], (TILE, 2 * HALO)[kind % 2]), jnp.float32)
            for kind in (one[0], two[0])
        ]
        steps = [(counts[kind] + batch - 1) // batch for kind, batch, _ in (one, two)]
        shared = jnp.minimum(steps[0], steps[1])
        sums = lax.fori_loop(0, shared, step_both, tuple(zeros))
        return [
            lax.fori_loop(shared, steps[j], functools.partial(step_one, given=(one, two)[j]), sums[j])
            for j in range(2)
        ]

    inside, corners = together((0, BATCH, 0), (3, BATCH // 2, BATCH))
    beside, above = together((1, BATCH // 2, 0), (2, BATCH // 2, BATCH))

    def wide(middle, ends):
        return jnp.concatenate([ends[:, :HALO], middle, ends[:, HALO:]], axis=1)

    middle, ends = wide(inside, beside), wide(above, corners)
    return jnp.concatenate([ends[:HALO], middle, ends[HALO:]], axis=0)


def spread_kernel(scale, mine_ref, other_ref, profile_ref, dest_ref, rays_ref, before_ref, out_ref,
                  total_ref, dest_copy, rays_copy, pairs_ref, last_ref, left, both, *scratch):
    sources = mine_ref.shape[0]
    both[:sources] = mine_ref[...]
    both[sources:] = other_ref[...]
    dest_copy[...] = dest_ref[...]
    rays_copy[...] = rays_ref[...]
    build = functools.partial(build_table, profile_ref, pairs_ref, last_ref)
    cells = deposited(both, build, *scratch)
    if before_ref is not None:
        cells = cells + before_ref[...]
    total_ref[...] = cells
    blocks = [cells[:, at : at + LANES].astype(jnp.bfloat16) for at in (0, SPAN)]
    for h in range(2):
        for u in range(TURNS):
            left[h * LONG : (h + 1) * LONG, u * LANES : (u + 1) * LANES] = blocks[h][
                u * STEP : u * STEP + LONG, :
            ]
    lowest = jnp.concatenate([block[2 * HALO :, :] for block in blocks], axis=0)
    ends = jnp.dot(lowest, last_ref[...], preferred_element_type=jnp.float32)
    evens = [ends[:TILE], ends[TILE:]]
    odds = [jnp.zeros((TILE, LANES), jnp.float32)] * 2
    for p in range(0, STEP * SPAN, 2 * LANES):
        both = jnp.dot(left[...], pairs_ref[:, p : p + 2 * LANES], preferred_element_type=jnp.float32)
        for h in range(2):
            for lanes in (0, LANES):
                s = (p + lanes) // SPAN
                part = both[h * LONG : (h + 1) * LONG, lanes : lanes + LANES]
                evens[h] = evens[h] + part[s : s + TILE]
                odds[h] = odds[h] + part[s + 1 : s + 1 + TILE]
    low = evens[0] + pltpu.roll(odds[0], SPAN, 1)
    high = pltpu.roll(evens[1], SPAN, 1) + odds[1]
    lane = lax.broadcasted_iota(jnp.int32, (TILE, LANES), 1)
    out_ref[...] = jnp.where(lane < SPAN, low, high) / scale


def shards(positions, destination, profile):
    blocks, _, rays = positions.shape
    row_count, col_count = lax.axis_size("row"), lax.axis_size("col")
    tiles = row_count * col_count
    width = -(-3 * blocks // LANES) * LANES

    def exchange(turn, labels, coords):
        laid = pl.pallas_call(
            lay_kernel,
            out_shape=(
                jax.ShapeDtypeStruct((3, width, rays + LANES), jnp.bfloat16),
                jax.ShapeDtypeStruct((4, width), jnp.float32),
            ),
            in_specs=[VMEM],
            out_specs=(VMEM, VMEM),
            compiler_params=LIMIT,
            name="lay",
        )(coords)
        kernel, given = pack_kernel, (turn, labels, *laid)
        if turn is None:
            kernel, given = functools.partial(pack_kernel, None), (labels, *laid)
        outgoing = pl.pallas_call(
            kernel,
            out_shape=jax.ShapeDtypeStruct((8 * tiles, rays + LANES), jnp.float32),
            in_specs=[SMEM, VMEM, VMEM, VMEM][-len(given) :],
            out_specs=VMEM,
            scratch_shapes=[pltpu.VMEM((1, width), jnp.float32)],
            compiler_params=LIMIT,
            name="pack",
        )(*given)
        return lax.all_to_all(
            outgoing.reshape(tiles, 8, rays + LANES), ("row", "col"), split_axis=0, concat_axis=0, tiled=True
        )

    def deposit(mine, labels, coords, before):
        other = lax.ppermute(mine, "row", [(i, i ^ 1) for i in range(row_count)])
        scale = blocks * rays / (TILE * TILE)
        kernel, given = functools.partial(spread_kernel, scale), (mine, other, profile, labels, coords, before)
        if before is None:
            kernel = lambda *refs: spread_kernel(scale, *refs[:5], None, *refs[5:])
            given = given[:5]
        return pl.pallas_call(
            kernel,
            out_shape=(
                jax.ShapeDtypeStruct((TILE, TILE), jnp.float32),
                jax.ShapeDtypeStruct((WIDE, WIDE), jnp.float32),
                jax.ShapeDtypeStruct((1, blocks), jnp.int32),
                jax.ShapeDtypeStruct(positions.shape, jnp.float32),
            ),
            in_specs=[VMEM] * len(given),
            out_specs=(VMEM,) * 4,
            scratch_shapes=[
                pltpu.VMEM((TURNS * LANES, STEP * SPAN), jnp.bfloat16),
                pltpu.VMEM((LANES, LANES), jnp.bfloat16),
                pltpu.VMEM((2 * LONG, TURNS * LANES), jnp.bfloat16),
                pltpu.VMEM((2 * tiles, 8, rays + LANES), jnp.float32),
                pltpu.SMEM((4 * (2 * tiles * ROOM + 1),), jnp.int32),
                pltpu.VMEM((2, 2 * BATCH, rays), jnp.float32),
                pltpu.VMEM((2 * BATCH, LANES), jnp.float32),
                pltpu.VMEM((8, 2 * BATCH, rays), jnp.float32),
            ],
            compiler_params=LIMIT,
            name="spread",
        )(*given)

    mine = exchange(None, destination.T, positions)
    turns = jnp.max(mine[:, 7, 2 * LANES + COUNT]).astype(jnp.int32)
    out, total, labels, coords = deposit(mine, destination.T, positions, None)

    def more(state):
        turn, _, total, labels, coords = state
        mine = exchange(jnp.full((1,), turn, jnp.int32), labels, coords)
        return (turn + 1, *deposit(mine, labels, coords, total))

    state = (jnp.int32(1), out, total, labels, coords)
    return lax.while_loop(lambda state: state[0] < turns, more, state)[1]


def solution(mesh):
    placed = (P(("maps", "row", "col"), None, None), P(("maps", "row", "col"), None), P())
    return jax.shard_map(
        shards, mesh=mesh, in_specs=placed, out_specs=P(("maps", "row"), "col"), check_vma=False
    )
```

```python
import functools

import jax
import jax.numpy as jnp
from jax import lax
from jax.experimental import pallas as pl
from jax.experimental.pallas import tpu as pltpu
from jax.sharding import PartitionSpec as P

TILE = 128
HALO = 32
MOST = 4
DISC = 2 * HALO + 1
STEP = 16
LONG = TILE + STEP
TURNS = 2 * HALO // STEP
WIDE = TILE + 2 * HALO
LANES = 128
SPAN = 64
BATCH = 8
ROOM = 5
COUNT = 16
KINDS = 18
FAR = 1024.0

VMEM = pl.BlockSpec(memory_space=pltpu.VMEM)
SMEM = pl.BlockSpec(memory_space=pltpu.SMEM)
ALONE = pltpu.CompilerParams(vmem_limit_bytes=67_104_000)
LIMIT = pltpu.CompilerParams(vmem_limit_bytes=32 * 1024 * 1024)


def touches(distance, least, most):
    before = (distance == -1.0) & (most > TILE - HALO - 1.0)
    after = (distance == 1.0) & (least < HALO)
    return (distance == 0.0) | before | after


def pack_kernel(turn_ref, dest_ref, rays_ref, out_ref, labels, parts):
    blocks, _, rays = rays_ref.shape
    tiles = out_ref.shape[0] // 8
    width = labels.shape[1]
    col_count = lax.axis_size("col")
    skip = 0.0 if turn_ref is None else 2.0 * ROOM * turn_ref[0].astype(jnp.float32)
    labels[...] = jnp.full(labels.shape, -1.0, jnp.float32)
    for g in range(3):
        labels[0:1, g * blocks : (g + 1) * blocks] = dest_ref[...].astype(jnp.float32)
    label = labels[...]
    label_row = jnp.floor((label + 0.5) / col_count)
    label_col = label - label_row * col_count
    lane = lax.broadcasted_iota(jnp.int32, (blocks, width), 1)
    place = lax.broadcasted_iota(jnp.int32, (blocks, width), 0)
    there = (lane % blocks == place) & (lane < 3 * blocks)

    def laid(column):
        return jnp.sum(jnp.where(there, column, 0.0), axis=0, keepdims=True)

    first, second = rays_ref[:, 0, :], rays_ref[:, 1, :]
    least_row, most_row = laid(jnp.min(first, 1, keepdims=True)), laid(jnp.max(first, 1, keepdims=True))
    least_col, most_col = laid(jnp.min(second, 1, keepdims=True)), laid(jnp.max(second, 1, keepdims=True))
    parts[...] = jnp.zeros(parts.shape, jnp.bfloat16)
    for at in range(0, 9 * blocks, 3 * blocks):
        one, two = first.astype(jnp.bfloat16), second.astype(jnp.bfloat16)
        first, second = first - one.astype(jnp.float32), second - two.astype(jnp.float32)
        parts[at : at + blocks, :rays] = one
        parts[at : at + blocks, rays:] = two[:, :LANES]
        parts[at + blocks : at + 2 * blocks, : 2 * LANES] = two[:, LANES:]
        parts[at + 2 * blocks : at + 3 * blocks, 2 * LANES :] = two[:, LANES:]
    earlier = lax.broadcasted_iota(jnp.int32, (width, width), 0)
    later = lax.broadcasted_iota(jnp.int32, (width, width), 1)
    earlier = jnp.where((earlier < later % blocks) & (later < 3 * blocks), 1.0, 0.0).astype(jnp.bfloat16)

    def chosen(tile):
        odd = (tile // col_count % 2).astype(jnp.float32)
        row = (tile // col_count).astype(jnp.float32) - odd
        dc = label_col - (tile % col_count).astype(jnp.float32)
        aside = touches(dc, least_col, most_col) & (label >= 0.0)

        def coded(dr):
            reach = aside & touches(dr, least_row, most_row)
            return reach, jnp.where(reach, 3.0 * dr + dc + 4.0, FAR)

        even, odds = coded(label_row - row), coded(label_row - row - 1.0)
        reach = jnp.where(even[0] | odds[0], 1.0, 0.0)
        rank = jnp.dot(reach.astype(jnp.bfloat16), earlier, preferred_element_type=jnp.float32)
        left = rank - skip - odd
        slot = jnp.floor(left * 0.5)
        mine = (reach > 0.0) & (slot * 2.0 == left) & (slot >= 0.0) & (slot < ROOM)
        return jnp.where(mine, slot, -1.0), even[1], odds[1], (rank + 1.0) * reach

    row = lax.broadcasted_iota(jnp.int32, (8 * tiles, width), 0)
    group = lax.broadcasted_iota(jnp.int32, (8 * tiles, width), 1)
    slot = chosen(row // 8)[0]
    within = row % 8
    low = (2 * (within - ROOM)).astype(jnp.float32)
    head = (group < blocks) & (within < ROOM) & (slot == within.astype(jnp.float32))
    even = (group >= blocks) & (group < 2 * blocks) & (within >= ROOM) & (slot == low)
    uneven = (group >= 2 * blocks) & (group < 3 * blocks) & (within >= ROOM) & (slot == low + 1.0)
    select = jnp.where(head | even | uneven, 1.0, 0.0)[:, : 3 * blocks]
    select = jnp.concatenate([select] * 3, axis=1).astype(jnp.bfloat16)
    out_ref[...] = jnp.dot(select, parts[...], preferred_element_type=jnp.float32)

    slot, even, odds, most = chosen(lax.broadcasted_iota(jnp.int32, (tiles, width), 0))
    most = jnp.max(jnp.max(most, axis=1, keepdims=True), axis=0, keepdims=True)
    turns = jnp.floor((most + (2.0 * ROOM - 0.5)) / (2.0 * ROOM))
    lane = lax.broadcasted_iota(jnp.int32, (tiles, width), 1)
    meta = jnp.where(lane == COUNT, turns, FAR)
    for at, code in ((KINDS, even), (KINDS + 1, odds)):
        rowwise = jnp.floor((code + 0.5) / 3.0)
        kind = jnp.where(rowwise == 1.0, 0.0, 2.0) + jnp.where(code - 3.0 * rowwise == 1.0, 0.0, 1.0)
        bit = 1 << jnp.clip(5.0 * kind + slot, 0.0, 23.0).astype(jnp.int32)
        here = (slot >= 0.0) & (code < FAR) & (lane < blocks)
        word = jnp.sum(jnp.where(here, bit.astype(jnp.float32), 0.0), axis=1, keepdims=True)
        meta = jnp.where(lane == at, word, meta)
    for k in range(ROOM):
        here = (slot == k) & (lane < blocks)
        for at, code in ((k, even), (8 + k, odds)):
            found = jnp.sum(jnp.where(here, code - FAR, 0.0), axis=1, keepdims=True) + FAR
            meta = jnp.where(lane == at, found, meta)
    for t in range(tiles):
        out_ref[8 * t + 7 : 8 * t + 8, 2 * LANES : 3 * LANES] = meta[t : t + 1, :LANES]


def table_kernel(profile_ref, dest_ref, rays_ref, pairs_ref, last_ref, dest_copy, rays_copy):
    dest_copy[...] = dest_ref[...]
    rays_copy[...] = rays_ref[...]
    a = lax.broadcasted_iota(jnp.int32, (DISC, DISC), 0) - HALO
    c = lax.broadcasted_iota(jnp.int32, (DISC, DISC), 1) - HALO
    weights = jnp.where(a * a + c * c <= HALO * HALO, profile_ref[...], 0.0)
    kernel = (weights / jnp.sum(weights)).astype(jnp.bfloat16)
    source = lax.broadcasted_iota(jnp.int32, (DISC, LANES), 0)
    target = lax.broadcasted_iota(jnp.int32, (DISC, LANES), 1)
    mirror = jnp.where((source + target) % LANES == 0, 1.0, 0.0).astype(jnp.bfloat16)
    mirrored = jnp.dot(kernel, mirror, preferred_element_type=jnp.float32)
    left = lax.broadcasted_iota(jnp.int32, (LANES, LANES), 1) < SPAN

    def band(row, start):
        wide = jnp.broadcast_to(mirrored[row : row + 1, :], (LANES, LANES))
        return pltpu.roll(wide, start, 1, stride=1, stride_axis=0)

    for u in range(TURNS):
        for s in range(0, STEP, 2):
            row = u * STEP + s
            both = jnp.where(left, band(row, 0), band(row + 1, SPAN))
            pairs_ref[u * LANES : (u + 1) * LANES, s * SPAN : (s + 2) * SPAN] = both.astype(jnp.bfloat16)
    last_ref[...] = jnp.where(left, band(2 * HALO, 0), 0.0).astype(jnp.bfloat16)


def hats(row, cell):
    near, far, here, there = (value.astype(jnp.bfloat16) for value in row)
    zero = jnp.zeros((), jnp.bfloat16)
    return jnp.where(cell == here, near, jnp.where(cell == there, far, zero))


def deposited(both, lists, stage, shifts, facts):
    sources = both.shape[0]
    rays = 3 * LANES
    first_lane = lax.axis_index("row") % 2 * 8
    room = sources * ROOM + 1
    lane = lax.broadcasted_iota(jnp.int32, (sources, LANES), 1)
    parity = lax.axis_index("row") % 2
    words = jnp.where(lane == KINDS + parity, both[:, 7, 2 * LANES :][:, :LANES], 0.0)
    words = jnp.sum(words, axis=1, keepdims=True).astype(jnp.int32)
    words = [words[at, 0] for at in range(sources)]

    def listed(counts, slots):
        counts = list(counts)
        for kind in range(4):
            for at in range(sources):
                for k in slots:
                    lists[kind * room + counts[kind]] = at * 8 + k
                    bit = (words[at] >> (ROOM * kind + k)) & 1
                    counts[kind] = counts[kind] + bit
        return tuple(counts)

    rare = sum(1 << (ROOM * kind + k) for kind in range(4) for k in range(3, ROOM))
    seldom = functools.reduce(jnp.bitwise_or, words) & rare
    counts = listed((jnp.int32(0),) * 4, range(3))
    counts = lax.cond(seldom != 0, lambda held: listed(held, range(3, ROOM)), lambda held: held, counts)
    for kind in range(4):
        lists[kind * room + counts[kind]] = ROOM

    def doubled(cell):
        return (2 * cell).astype(jnp.float32).astype(jnp.bfloat16)

    own = doubled(lax.broadcasted_iota(jnp.int32, (TILE, rays), 0))
    edge = lax.broadcasted_iota(jnp.int32, (2 * HALO, rays), 0)
    edge = doubled(jnp.where(edge < HALO, edge - HALO, edge + (TILE - HALO)))
    lane = lax.broadcasted_iota(jnp.int32, (1, LANES), 1) - first_lane

    def load(kind, step, batch, start):
        for k in range(batch):
            at = start + k
            entry = lists[kind * room + jnp.minimum(step * batch + k, counts[kind])]
            source, slot = entry >> 3, entry & 7
            head = both[source, pl.ds(slot, 1), :]
            tail = both[source, pl.ds(ROOM + (slot >> 1), 1), :]
            meta = both[source, 7:8, :][:, 2 * LANES : 3 * LANES]
            stage[0, at : at + 1, :] = head[:, :rays]
            stage[1, at : at + 1, :LANES] = head[:, rays:]
            stage[1, at : at + 1, LANES:] = jnp.where(
                (slot & 1) == 1, tail[:, 2 * LANES :], tail[:, : 2 * LANES]
            )
            shifts[at : at + 1, :] = jnp.where(lane == slot, meta, 0.0)

    def prepare(begin, end):
        code = jnp.sum(shifts[begin:end, :], axis=1, keepdims=True)
        rowwise = jnp.floor((code + 0.5) / 3.0)
        offsets = (rowwise - 1.0) * (2.0 * TILE), (code - 3.0 * rowwise - 1.0) * (2.0 * TILE)
        for axis in range(2):
            coords = stage[axis, begin:end, :]
            low = jnp.floor(coords)
            facts[4 * axis, begin:end, :] = 1.0 - (coords - low)
            facts[4 * axis + 1, begin:end, :] = 1.0 - ((low + 1.0) - coords)
            here = 2.0 * low + offsets[axis]
            facts[4 * axis + 2, begin:end, :] = here
            facts[4 * axis + 3, begin:end, :] = here + 2.0

    def product(kind, batch, start):
        down, across = (own, edge)[kind // 2], (own, edge)[kind % 2]
        firsts, seconds = [], []
        for at in range(start, start + batch):
            row = [facts[j, at : at + 1, :] for j in range(8)]
            firsts.append(hats(row[:4], down))
            seconds.append(hats(row[4:], across))
        return lax.dot_general(
            jnp.concatenate(firsts, axis=1),
            jnp.concatenate(seconds, axis=1),
            (((1,), (1,)), ((), ())),
            preferred_element_type=jnp.float32,
        )

    def together(one, two):
        def ready(step, *given):
            for kind, batch, start in given:
                load(kind, step, batch, start)
            prepare(given[0][2], given[-1][2] + 8)

        def step_one(step, sums, given=one):
            sums = sums + product(*given)
            ready(step + 1, given)
            return sums

        def step_both(step, sums):
            sums = sums[0] + product(*one), sums[1] + product(*two)
            ready(step + 1, one, two)
            return sums

        ready(0, one, two)
        zeros = [
            jnp.zeros(((TILE, 2 * HALO)[kind // 2], (TILE, 2 * HALO)[kind % 2]), jnp.float32)
            for kind in (one[0], two[0])
        ]
        steps = [(counts[kind] + batch - 1) // batch for kind, batch, _ in (one, two)]
        shared = jnp.minimum(steps[0], steps[1])
        sums = lax.fori_loop(0, shared, step_both, tuple(zeros))
        return [
            lax.fori_loop(shared, steps[j], functools.partial(step_one, given=(one, two)[j]), sums[j])
            for j in range(2)
        ]

    inside, corners = together((0, BATCH, 0), (3, BATCH // 2, BATCH))
    beside, above = together((1, BATCH // 2, 0), (2, BATCH // 2, BATCH))

    def wide(middle, ends):
        return jnp.concatenate([ends[:, :HALO], middle, ends[:, HALO:]], axis=1)

    middle, ends = wide(inside, beside), wide(above, corners)
    return jnp.concatenate([ends[:HALO], middle, ends[HALO:]], axis=0)


def spread_kernel(scale, mine_ref, other_ref, before_ref, pairs_ref, last_ref, out_ref, total_ref,
                  left, both, *scratch):
    sources = mine_ref.shape[0]
    both[:sources] = mine_ref[...]
    both[sources:] = other_ref[...]
    cells = deposited(both, *scratch)
    if before_ref is not None:
        cells = cells + before_ref[...]
    total_ref[...] = cells
    blocks = [cells[:, at : at + LANES].astype(jnp.bfloat16) for at in (0, SPAN)]
    for h in range(2):
        for u in range(TURNS):
            left[h * LONG : (h + 1) * LONG, u * LANES : (u + 1) * LANES] = blocks[h][
                u * STEP : u * STEP + LONG, :
            ]
    lowest = jnp.concatenate([block[2 * HALO :, :] for block in blocks], axis=0)
    ends = jnp.dot(lowest, last_ref[...], preferred_element_type=jnp.float32)
    evens = [ends[:TILE], ends[TILE:]]
    odds = [jnp.zeros((TILE, LANES), jnp.float32)] * 2
    for p in range(0, STEP * SPAN, 2 * LANES):
        both = jnp.dot(left[...], pairs_ref[:, p : p + 2 * LANES], preferred_element_type=jnp.float32)
        for h in range(2):
            for lanes in (0, LANES):
                s = (p + lanes) // SPAN
                part = both[h * LONG : (h + 1) * LONG, lanes : lanes + LANES]
                evens[h] = evens[h] + part[s : s + TILE]
                odds[h] = odds[h] + part[s + 1 : s + 1 + TILE]
    low = evens[0] + pltpu.roll(odds[0], SPAN, 1)
    high = pltpu.roll(evens[1], SPAN, 1) + odds[1]
    lane = lax.broadcasted_iota(jnp.int32, (TILE, LANES), 1)
    out_ref[...] = jnp.where(lane < SPAN, low, high) / scale


def shards(positions, destination, profile):
    blocks, _, rays = positions.shape
    row_count, col_count = lax.axis_size("row"), lax.axis_size("col")
    tiles = row_count * col_count
    width = -(-3 * blocks // LANES) * LANES

    def exchange(turn, labels, coords):
        kernel, given = pack_kernel, (turn, labels, coords)
        if turn is None:
            kernel, given = functools.partial(pack_kernel, None), (labels, coords)
        outgoing = pl.pallas_call(
            kernel,
            out_shape=jax.ShapeDtypeStruct((8 * tiles, rays + LANES), jnp.float32),
            in_specs=[SMEM, VMEM, VMEM][-len(given) :],
            out_specs=VMEM,
            scratch_shapes=[
                pltpu.VMEM((1, width), jnp.float32),
                pltpu.VMEM((9 * blocks, rays + LANES), jnp.bfloat16),
            ],
            compiler_params=ALONE if turn is None else LIMIT,
            name="pack",
        )(*given)
        return lax.all_to_all(
            outgoing.reshape(tiles, 8, rays + LANES), ("row", "col"), split_axis=0, concat_axis=0, tiled=True
        )

    def deposit(mine, before, pairs, last):
        other = lax.ppermute(mine, "row", [(i, i ^ 1) for i in range(row_count)])
        scale = blocks * rays / (TILE * TILE)
        kernel, given = functools.partial(spread_kernel, scale), (mine, other, before, pairs, last)
        if before is None:
            kernel = lambda mine, other, *refs: spread_kernel(scale, mine, other, None, *refs)
            given = (mine, other, pairs, last)
        return pl.pallas_call(
            kernel,
            out_shape=(
                jax.ShapeDtypeStruct((TILE, TILE), jnp.float32),
                jax.ShapeDtypeStruct((WIDE, WIDE), jnp.float32),
            ),
            in_specs=[VMEM] * len(given),
            out_specs=(VMEM, VMEM),
            scratch_shapes=[
                pltpu.VMEM((2 * LONG, TURNS * LANES), jnp.bfloat16),
                pltpu.VMEM((2 * tiles, 8, rays + LANES), jnp.float32),
                pltpu.SMEM((4 * (2 * tiles * ROOM + 1),), jnp.int32),
                pltpu.VMEM((2, 2 * BATCH, rays), jnp.float32),
                pltpu.VMEM((2 * BATCH, LANES), jnp.float32),
                pltpu.VMEM((8, 2 * BATCH, rays), jnp.float32),
            ],
            compiler_params=LIMIT,
            name="spread",
        )(*given)

    mine = exchange(None, destination.T, positions)
    pairs, last, labels, coords = pl.pallas_call(
        table_kernel,
        out_shape=(
            jax.ShapeDtypeStruct((TURNS * LANES, STEP * SPAN), jnp.bfloat16),
            jax.ShapeDtypeStruct((LANES, LANES), jnp.bfloat16),
            jax.ShapeDtypeStruct((1, blocks), jnp.int32),
            jax.ShapeDtypeStruct(positions.shape, jnp.float32),
        ),
        in_specs=[VMEM] * 3,
        out_specs=(VMEM,) * 4,
        compiler_params=LIMIT,
        cost_estimate=pl.CostEstimate(flops=10_000_000, bytes_accessed=6_000_000, transcendentals=0),
        name="table",
    )(profile, destination.T, positions)
    mine, pairs, last, labels, coords = lax.optimization_barrier((mine, pairs, last, labels, coords))
    turns = jnp.max(mine[:, 7, 2 * LANES + COUNT]).astype(jnp.int32)
    out, total = deposit(mine, None, pairs, last)

    def more(state):
        turn, _, total = state
        out, total = deposit(
            exchange(jnp.full((1,), turn, jnp.int32), labels, coords), total, pairs, last
        )
        return turn + 1, out, total

    return lax.while_loop(lambda state: state[0] < turns, more, (jnp.int32(1), out, total))[1]


def solution(mesh):
    placed = (P(("maps", "row", "col"), None, None), P(("maps", "row", "col"), None), P())
    return jax.shard_map(
        shards, mesh=mesh, in_specs=placed, out_specs=P(("maps", "row"), "col"), check_vma=False
    )
```

```python
import functools

import jax
import jax.numpy as jnp
from jax import lax
from jax.experimental import pallas as pl
from jax.experimental.pallas import tpu as pltpu
from jax.sharding import PartitionSpec as P

TILE = 128
HALO = 32
MOST = 4
DISC = 2 * HALO + 1
STEP = 16
LONG = TILE + STEP
TURNS = 2 * HALO // STEP
WIDE = TILE + 2 * HALO
LANES = 128
SPAN = 64
BATCH = 8
ROOM = 5
COUNT = 16
KINDS = 18
FAR = 1024.0

VMEM = pl.BlockSpec(memory_space=pltpu.VMEM)
SMEM = pl.BlockSpec(memory_space=pltpu.SMEM)
ALONE = pltpu.CompilerParams(vmem_limit_bytes=67_104_000)
LIMIT = pltpu.CompilerParams(vmem_limit_bytes=32 * 1024 * 1024)


def touches(distance, least, most):
    before = (distance == -1.0) & (most > TILE - HALO - 1.0)
    after = (distance == 1.0) & (least < HALO)
    return (distance == 0.0) | before | after


def split(index, size):
    index = index.astype(jnp.float32)
    quotient = jnp.floor((index + 0.5) * (1.0 / size))
    return quotient, index - size * quotient


def pack_kernel(turn_ref, dest_ref, rays_ref, out_ref, labels, parts):
    blocks, _, rays = rays_ref.shape
    tiles = out_ref.shape[0] // 8
    width = parts.shape[0]
    col_count = lax.axis_size("col")
    skip = 0.0 if turn_ref is None else 2.0 * ROOM * turn_ref[0].astype(jnp.float32)
    copy, own = split(lax.broadcasted_iota(jnp.int32, (blocks, width), 1), blocks)
    place = lax.broadcasted_iota(jnp.int32, (blocks, width), 0).astype(jnp.float32)
    there = (own == place) & (copy < 3.0)

    def laid(column):
        return jnp.sum(jnp.where(there, column, 0.0), axis=0, keepdims=True)

    labels[...] = jnp.full(labels.shape, -1.0, jnp.float32)
    for g in range(3):
        labels[0:1, g * blocks : (g + 1) * blocks] = dest_ref[...].astype(jnp.float32)
    label = labels[...]
    label_row = jnp.floor((label + 0.5) * (1.0 / col_count))
    label_col = label - label_row * col_count
    first, second = rays_ref[:, 0, :], rays_ref[:, 1, :]
    least_row, most_row = laid(jnp.min(first, 1, keepdims=True)), laid(jnp.max(first, 1, keepdims=True))
    least_col, most_col = laid(jnp.min(second, 1, keepdims=True)), laid(jnp.max(second, 1, keepdims=True))
    earlier = lax.broadcasted_iota(jnp.int32, (width, width), 0).astype(jnp.float32)
    copy, own = split(lax.broadcasted_iota(jnp.int32, (width, width), 1), blocks)
    earlier = jnp.where((earlier < own) & (copy < 3.0), 1.0, 0.0).astype(jnp.bfloat16)

    def chosen(row, col):
        odd = split(row, 2)[1]
        row = row - odd
        dc = label_col - col
        aside = touches(dc, least_col, most_col) & (label >= 0.0)

        def coded(dr):
            reach = aside & touches(dr, least_row, most_row)
            return reach, jnp.where(reach, 3.0 * dr + dc + 4.0, FAR)

        even, odds = coded(label_row - row), coded(label_row - row - 1.0)
        reach = jnp.where(even[0] | odds[0], 1.0, 0.0)
        rank = jnp.dot(reach.astype(jnp.bfloat16), earlier, preferred_element_type=jnp.float32)
        left = rank - skip - odd
        slot = jnp.floor(left * 0.5)
        mine = (reach > 0.0) & (slot * 2.0 == left) & (slot >= 0.0) & (slot < ROOM)
        return jnp.where(mine, slot, -1.0), even[1], odds[1], (rank + 1.0) * reach

    tile = lax.broadcasted_iota(jnp.int32, (tiles, width), 0)
    slot, even, odds, most = chosen(*split(tile, col_count))
    most = jnp.max(jnp.max(most, axis=1, keepdims=True), axis=0, keepdims=True)
    turns = jnp.floor((most + (2.0 * ROOM - 0.5)) / (2.0 * ROOM))
    lane = lax.broadcasted_iota(jnp.int32, (tiles, width), 1)
    meta = jnp.where(lane == COUNT, turns, FAR)
    for k in range(ROOM):
        here = (slot == k) & (lane < blocks)
        for at, code in ((k, even), (8 + k, odds)):
            found = jnp.sum(jnp.where(here, code - FAR, 0.0), axis=1, keepdims=True) + FAR
            meta = jnp.where(lane == at, found, meta)
    for at, code in ((KINDS, even), (KINDS + 1, odds)):
        rowwise, colwise = split(code, 3)
        kind = jnp.where(rowwise == 1.0, 0.0, 2.0) + jnp.where(colwise == 1.0, 0.0, 1.0)
        bit = 1 << jnp.clip(5.0 * kind + slot, 0.0, 23.0).astype(jnp.int32)
        here = (slot >= 0.0) & (code < FAR) & (lane < blocks)
        word = jnp.sum(jnp.where(here, bit.astype(jnp.float32), 0.0), axis=1, keepdims=True)
        meta = jnp.where(lane == at, word, meta)

    parts[...] = jnp.zeros(parts.shape, jnp.float32)
    parts[:blocks, :rays] = first
    parts[:blocks, rays:] = second[:, :LANES]
    parts[blocks : 2 * blocks, : 2 * LANES] = second[:, LANES:]
    parts[2 * blocks : 3 * blocks, 2 * LANES :] = second[:, LANES:]
    parts[3 * blocks : 3 * blocks + tiles, 2 * LANES : 3 * LANES] = meta[:, :LANES]

    tile, within = split(lax.broadcasted_iota(jnp.int32, (8 * tiles, width), 0), 8)
    lane = lax.broadcasted_iota(jnp.int32, (8 * tiles, width), 1)
    copy = split(lane, blocks)[0]
    slot = chosen(*split(tile, col_count))[0]
    low = 2.0 * (within - ROOM)
    wanted = jnp.where(copy == 0.0, within, jnp.where(copy == 1.0, low, low + 1.0))
    place = ((copy == 0.0) & (within < ROOM)) | ((copy > 0.0) & (copy < 3.0) & (within >= ROOM))
    codes = (lane.astype(jnp.float32) - 3.0 * blocks == tile) & (within == 7.0)
    select = jnp.where((place & (slot == wanted)) | codes, 1.0, 0.0).astype(jnp.bfloat16)
    rest = parts[...]
    total = jnp.zeros(out_ref.shape, jnp.float32)
    for _ in range(3):
        part = rest.astype(jnp.bfloat16)
        rest = rest - part.astype(jnp.float32)
        total = total + jnp.dot(select, part, preferred_element_type=jnp.float32)
    out_ref[...] = total


def table_kernel(profile_ref, dest_ref, rays_ref, pairs_ref, last_ref, dest_copy, rays_copy):
    dest_copy[...] = dest_ref[...]
    rays_copy[...] = rays_ref[...]
    a = lax.broadcasted_iota(jnp.int32, (DISC, DISC), 0) - HALO
    c = lax.broadcasted_iota(jnp.int32, (DISC, DISC), 1) - HALO
    weights = jnp.where(a * a + c * c <= HALO * HALO, profile_ref[...], 0.0)
    kernel = (weights / jnp.sum(weights)).astype(jnp.bfloat16)
    source = lax.broadcasted_iota(jnp.int32, (DISC, LANES), 0)
    target = lax.broadcasted_iota(jnp.int32, (DISC, LANES), 1)
    mirror = jnp.where((source + target) % LANES == 0, 1.0, 0.0).astype(jnp.bfloat16)
    mirrored = jnp.dot(kernel, mirror, preferred_element_type=jnp.float32)
    left = lax.broadcasted_iota(jnp.int32, (LANES, LANES), 1) < SPAN

    def band(row, start):
        wide = jnp.broadcast_to(mirrored[row : row + 1, :], (LANES, LANES))
        return pltpu.roll(wide, start, 1, stride=1, stride_axis=0)

    for u in range(TURNS):
        for s in range(0, STEP, 2):
            row = u * STEP + s
            both = jnp.where(left, band(row, 0), band(row + 1, SPAN))
            pairs_ref[u * LANES : (u + 1) * LANES, s * SPAN : (s + 2) * SPAN] = both.astype(jnp.bfloat16)
    last_ref[...] = jnp.where(left, band(2 * HALO, 0), 0.0).astype(jnp.bfloat16)


def hats(row, cell):
    near, far, here, there = (value.astype(jnp.bfloat16) for value in row)
    zero = jnp.zeros((), jnp.bfloat16)
    return jnp.where(cell == here, near, jnp.where(cell == there, far, zero))


def deposited(both, lists, stage, shifts, facts):
    sources = both.shape[0]
    rays = 3 * LANES
    first_lane = lax.axis_index("row") % 2 * 8
    room = sources * ROOM + 1
    lane = lax.broadcasted_iota(jnp.int32, (sources, LANES), 1)
    parity = lax.axis_index("row") % 2
    words = jnp.where(lane == KINDS + parity, both[:, 7, 2 * LANES :][:, :LANES], 0.0)
    words = jnp.sum(words, axis=1, keepdims=True).astype(jnp.int32)
    words = [words[at, 0] for at in range(sources)]

    def listed(counts, slots):
        counts = list(counts)
        for kind in range(4):
            for at in range(sources):
                for k in slots:
                    lists[kind * room + counts[kind]] = at * 8 + k
                    bit = (words[at] >> (ROOM * kind + k)) & 1
                    counts[kind] = counts[kind] + bit
        return tuple(counts)

    rare = sum(1 << (ROOM * kind + k) for kind in range(4) for k in range(3, ROOM))
    seldom = functools.reduce(jnp.bitwise_or, words) & rare
    counts = listed((jnp.int32(0),) * 4, range(3))
    counts = lax.cond(seldom != 0, lambda held: listed(held, range(3, ROOM)), lambda held: held, counts)
    for kind in range(4):
        lists[kind * room + counts[kind]] = ROOM

    def doubled(cell):
        return (2 * cell).astype(jnp.float32).astype(jnp.bfloat16)

    own = doubled(lax.broadcasted_iota(jnp.int32, (TILE, rays), 0))
    edge = lax.broadcasted_iota(jnp.int32, (2 * HALO, rays), 0)
    edge = doubled(jnp.where(edge < HALO, edge - HALO, edge + (TILE - HALO)))
    lane = lax.broadcasted_iota(jnp.int32, (1, LANES), 1) - first_lane

    def load(kind, step, batch, start):
        for k in range(batch):
            at = start + k
            entry = lists[kind * room + jnp.minimum(step * batch + k, counts[kind])]
            source, slot = entry >> 3, entry & 7
            head = both[source, pl.ds(slot, 1), :]
            tail = both[source, pl.ds(ROOM + (slot >> 1), 1), :]
            meta = both[source, 7:8, :][:, 2 * LANES : 3 * LANES]
            stage[0, at : at + 1, :] = head[:, :rays]
            stage[1, at : at + 1, :LANES] = head[:, rays:]
            stage[1, at : at + 1, LANES:] = jnp.where(
                (slot & 1) == 1, tail[:, 2 * LANES :], tail[:, : 2 * LANES]
            )
            shifts[at : at + 1, :] = jnp.where(lane == slot, meta, 0.0)

    def prepare(begin, end):
        code = jnp.sum(shifts[begin:end, :], axis=1, keepdims=True)
        rowwise = jnp.floor((code + 0.5) / 3.0)
        offsets = (rowwise - 1.0) * (2.0 * TILE), (code - 3.0 * rowwise - 1.0) * (2.0 * TILE)
        for axis in range(2):
            coords = stage[axis, begin:end, :]
            low = jnp.floor(coords)
            facts[4 * axis, begin:end, :] = 1.0 - (coords - low)
            facts[4 * axis + 1, begin:end, :] = 1.0 - ((low + 1.0) - coords)
            here = 2.0 * low + offsets[axis]
            facts[4 * axis + 2, begin:end, :] = here
            facts[4 * axis + 3, begin:end, :] = here + 2.0

    def product(kind, batch, start):
        down, across = (own, edge)[kind // 2], (own, edge)[kind % 2]
        firsts, seconds = [], []
        for at in range(start, start + batch):
            row = [facts[j, at : at + 1, :] for j in range(8)]
            firsts.append(hats(row[:4], down))
            seconds.append(hats(row[4:], across))
        return lax.dot_general(
            jnp.concatenate(firsts, axis=1),
            jnp.concatenate(seconds, axis=1),
            (((1,), (1,)), ((), ())),
            preferred_element_type=jnp.float32,
        )

    def together(one, two):
        def ready(step, *given):
            for kind, batch, start in given:
                load(kind, step, batch, start)
            prepare(given[0][2], given[-1][2] + 8)

        def step_one(step, sums, given=one):
            sums = sums + product(*given)
            ready(step + 1, given)
            return sums

        def step_both(step, sums):
            sums = sums[0] + product(*one), sums[1] + product(*two)
            ready(step + 1, one, two)
            return sums

        ready(0, one, two)
        zeros = [
            jnp.zeros(((TILE, 2 * HALO)[kind // 2], (TILE, 2 * HALO)[kind % 2]), jnp.float32)
            for kind in (one[0], two[0])
        ]
        steps = [(counts[kind] + batch - 1) // batch for kind, batch, _ in (one, two)]
        shared = jnp.minimum(steps[0], steps[1])
        sums = lax.fori_loop(0, shared, step_both, tuple(zeros))
        return [
            lax.fori_loop(shared, steps[j], functools.partial(step_one, given=(one, two)[j]), sums[j])
            for j in range(2)
        ]

    inside, corners = together((0, BATCH, 0), (3, BATCH // 2, BATCH))
    beside, above = together((1, BATCH // 2, 0), (2, BATCH // 2, BATCH))

    def wide(middle, ends):
        return jnp.concatenate([ends[:, :HALO], middle, ends[:, HALO:]], axis=1)

    middle, ends = wide(inside, beside), wide(above, corners)
    return jnp.concatenate([ends[:HALO], middle, ends[HALO:]], axis=0)


def spread_kernel(scale, mine_ref, other_ref, before_ref, pairs_ref, last_ref, out_ref, total_ref,
                  left, both, *scratch):
    sources = mine_ref.shape[0]
    both[:sources] = mine_ref[...]
    both[sources:] = other_ref[...]
    cells = deposited(both, *scratch)
    if before_ref is not None:
        cells = cells + before_ref[...]
    total_ref[...] = cells
    blocks = [cells[:, at : at + LANES].astype(jnp.bfloat16) for at in (0, SPAN)]
    for h in range(2):
        for u in range(TURNS):
            left[h * LONG : (h + 1) * LONG, u * LANES : (u + 1) * LANES] = blocks[h][
                u * STEP : u * STEP + LONG, :
            ]
    lowest = jnp.concatenate([block[2 * HALO :, :] for block in blocks], axis=0)
    ends = jnp.dot(lowest, last_ref[...], preferred_element_type=jnp.float32)
    evens = [ends[:TILE], ends[TILE:]]
    odds = [jnp.zeros((TILE, LANES), jnp.float32)] * 2
    for p in range(0, STEP * SPAN, 2 * LANES):
        both = jnp.dot(left[...], pairs_ref[:, p : p + 2 * LANES], preferred_element_type=jnp.float32)
        for h in range(2):
            for lanes in (0, LANES):
                s = (p + lanes) // SPAN
                part = both[h * LONG : (h + 1) * LONG, lanes : lanes + LANES]
                evens[h] = evens[h] + part[s : s + TILE]
                odds[h] = odds[h] + part[s + 1 : s + 1 + TILE]
    low = evens[0] + pltpu.roll(odds[0], SPAN, 1)
    high = pltpu.roll(evens[1], SPAN, 1) + odds[1]
    lane = lax.broadcasted_iota(jnp.int32, (TILE, LANES), 1)
    out_ref[...] = jnp.where(lane < SPAN, low, high) / scale


def shards(positions, destination, profile):
    blocks, _, rays = positions.shape
    row_count, col_count = lax.axis_size("row"), lax.axis_size("col")
    tiles = row_count * col_count
    width = -(-(3 * blocks + tiles) // LANES) * LANES

    def exchange(turn, labels, coords):
        kernel, given = pack_kernel, (turn, labels, coords)
        if turn is None:
            kernel, given = functools.partial(pack_kernel, None), (labels, coords)
        outgoing = pl.pallas_call(
            kernel,
            out_shape=jax.ShapeDtypeStruct((8 * tiles, rays + LANES), jnp.float32),
            in_specs=[SMEM, VMEM, VMEM][-len(given) :],
            out_specs=VMEM,
            scratch_shapes=[
                pltpu.VMEM((1, width), jnp.float32),
                pltpu.VMEM((width, rays + LANES), jnp.float32),
            ],
            compiler_params=ALONE if turn is None else LIMIT,
            name="pack",
        )(*given)
        return lax.all_to_all(
            outgoing.reshape(tiles, 8, rays + LANES), ("row", "col"), split_axis=0, concat_axis=0, tiled=True
        )

    def deposit(mine, before, pairs, last):
        other = lax.ppermute(mine, "row", [(i, i ^ 1) for i in range(row_count)])
        scale = blocks * rays / (TILE * TILE)
        kernel, given = functools.partial(spread_kernel, scale), (mine, other, before, pairs, last)
        if before is None:
            kernel = lambda mine, other, *refs: spread_kernel(scale, mine, other, None, *refs)
            given = (mine, other, pairs, last)
        return pl.pallas_call(
            kernel,
            out_shape=(
                jax.ShapeDtypeStruct((TILE, TILE), jnp.float32),
                jax.ShapeDtypeStruct((WIDE, WIDE), jnp.float32),
            ),
            in_specs=[VMEM] * len(given),
            out_specs=(VMEM, VMEM),
            scratch_shapes=[
                pltpu.VMEM((2 * LONG, TURNS * LANES), jnp.bfloat16),
                pltpu.VMEM((2 * tiles, 8, rays + LANES), jnp.float32),
                pltpu.SMEM((4 * (2 * tiles * ROOM + 1),), jnp.int32),
                pltpu.VMEM((2, 2 * BATCH, rays), jnp.float32),
                pltpu.VMEM((2 * BATCH, LANES), jnp.float32),
                pltpu.VMEM((8, 2 * BATCH, rays), jnp.float32),
            ],
            compiler_params=LIMIT,
            name="spread",
        )(*given)

    mine = exchange(None, destination.T, positions)
    pairs, last, labels, coords = pl.pallas_call(
        table_kernel,
        out_shape=(
            jax.ShapeDtypeStruct((TURNS * LANES, STEP * SPAN), jnp.bfloat16),
            jax.ShapeDtypeStruct((LANES, LANES), jnp.bfloat16),
            jax.ShapeDtypeStruct((1, blocks), jnp.int32),
            jax.ShapeDtypeStruct(positions.shape, jnp.float32),
        ),
        in_specs=[VMEM] * 3,
        out_specs=(VMEM,) * 4,
        compiler_params=LIMIT,
        cost_estimate=pl.CostEstimate(flops=10_000_000, bytes_accessed=6_000_000, transcendentals=0),
        name="table",
    )(profile, destination.T, positions)
    mine, pairs, last, labels, coords = lax.optimization_barrier((mine, pairs, last, labels, coords))
    turns = jnp.max(mine[:, 7, 2 * LANES + COUNT]).astype(jnp.int32)
    out, total = deposit(mine, None, pairs, last)

    def more(state):
        turn, _, total = state
        out, total = deposit(
            exchange(jnp.full((1,), turn, jnp.int32), labels, coords), total, pairs, last
        )
        return turn + 1, out, total

    return lax.while_loop(lambda state: state[0] < turns, more, (jnp.int32(1), out, total))[1]


def solution(mesh):
    placed = (P(("maps", "row", "col"), None, None), P(("maps", "row", "col"), None), P())
    return jax.shard_map(
        shards, mesh=mesh, in_specs=placed, out_specs=P(("maps", "row"), "col"), check_vma=False
    )
```

```python
import functools

import jax
import jax.numpy as jnp
from jax import lax
from jax.experimental import pallas as pl
from jax.experimental.pallas import tpu as pltpu
from jax.sharding import PartitionSpec as P

TILE = 128
HALO = 32
MOST = 4
DISC = 2 * HALO + 1
STEP = 16
LONG = TILE + STEP
TURNS = 2 * HALO // STEP
WIDE = TILE + 2 * HALO
LANES = 128
SPAN = 64
BATCH = 8
ROOM = 5
COUNT = 16
KINDS = 18
FAR = 1024.0

VMEM = pl.BlockSpec(memory_space=pltpu.VMEM)
SMEM = pl.BlockSpec(memory_space=pltpu.SMEM)
ALONE = pltpu.CompilerParams(vmem_limit_bytes=67_104_000)
LIMIT = pltpu.CompilerParams(vmem_limit_bytes=32 * 1024 * 1024)


def touches(distance, least, most):
    before = (distance == -1.0) & (most > TILE - HALO - 1.0)
    after = (distance == 1.0) & (least < HALO)
    return (distance == 0.0) | before | after


def split(index, size):
    index = index.astype(jnp.float32)
    quotient = jnp.floor((index + 0.5) * (1.0 / size))
    return quotient, index - size * quotient


def pack_kernel(turn_ref, dest_ref, rays_ref, out_ref, labels, parts):
    blocks, _, rays = rays_ref.shape
    tiles = out_ref.shape[0] // 8
    width = parts.shape[0]
    col_count = lax.axis_size("col")
    skip = 0.0 if turn_ref is None else 2.0 * ROOM * turn_ref[0].astype(jnp.float32)
    copy, own = split(lax.broadcasted_iota(jnp.int32, (blocks, width), 1), blocks)
    place = lax.broadcasted_iota(jnp.int32, (blocks, width), 0).astype(jnp.float32)
    there = (own == place) & (copy < 3.0)

    def laid(column):
        return jnp.sum(jnp.where(there, column, 0.0), axis=0, keepdims=True)

    labels[...] = jnp.full(labels.shape, -1.0, jnp.float32)
    for g in range(3):
        labels[0:1, g * blocks : (g + 1) * blocks] = dest_ref[...].astype(jnp.float32)
    label = labels[...]
    label_row = jnp.floor((label + 0.5) * (1.0 / col_count))
    label_col = label - label_row * col_count
    first, second = rays_ref[:, 0, :], rays_ref[:, 1, :]
    least_row, most_row = laid(jnp.min(first, 1, keepdims=True)), laid(jnp.max(first, 1, keepdims=True))
    least_col, most_col = laid(jnp.min(second, 1, keepdims=True)), laid(jnp.max(second, 1, keepdims=True))
    earlier = lax.broadcasted_iota(jnp.int32, (width, width), 0).astype(jnp.float32)
    copy, own = split(lax.broadcasted_iota(jnp.int32, (width, width), 1), blocks)
    earlier = jnp.where((earlier < own) & (copy < 3.0), 1.0, 0.0).astype(jnp.bfloat16)

    def chosen(row, col):
        odd = split(row, 2)[1]
        row = row - odd
        dc = label_col - col
        aside = touches(dc, least_col, most_col) & (label >= 0.0)

        def coded(dr):
            reach = aside & touches(dr, least_row, most_row)
            return reach, jnp.where(reach, 3.0 * dr + dc + 4.0, FAR)

        even, odds = coded(label_row - row), coded(label_row - row - 1.0)
        reach = jnp.where(even[0] | odds[0], 1.0, 0.0)
        rank = jnp.dot(reach.astype(jnp.bfloat16), earlier, preferred_element_type=jnp.float32)
        left = rank - skip - odd
        slot = jnp.floor(left * 0.5)
        mine = (reach > 0.0) & (slot * 2.0 == left) & (slot >= 0.0) & (slot < ROOM)
        return jnp.where(mine, slot, -1.0), even[1], odds[1], (rank + 1.0) * reach

    tile = lax.broadcasted_iota(jnp.int32, (tiles, width), 0)
    slot, even, odds, most = chosen(*split(tile, col_count))
    most = jnp.max(jnp.max(most, axis=1, keepdims=True), axis=0, keepdims=True)
    turns = jnp.floor((most + (2.0 * ROOM - 0.5)) / (2.0 * ROOM))
    lane = lax.broadcasted_iota(jnp.int32, (tiles, width), 1)
    meta = jnp.where(lane == COUNT, turns, FAR)
    for k in range(ROOM):
        here = (slot == k) & (lane < blocks)
        for at, code in ((k, even), (8 + k, odds)):
            found = jnp.sum(jnp.where(here, code - FAR, 0.0), axis=1, keepdims=True) + FAR
            meta = jnp.where(lane == at, found, meta)
    for at, code in ((KINDS, even), (KINDS + 1, odds)):
        rowwise, colwise = split(code, 3)
        kind = jnp.where(rowwise == 1.0, 0.0, 2.0) + jnp.where(colwise == 1.0, 0.0, 1.0)
        bit = 1 << jnp.clip(5.0 * kind + slot, 0.0, 23.0).astype(jnp.int32)
        here = (slot >= 0.0) & (code < FAR) & (lane < blocks)
        word = jnp.sum(jnp.where(here, bit.astype(jnp.float32), 0.0), axis=1, keepdims=True)
        meta = jnp.where(lane == at, word, meta)

    parts[...] = jnp.zeros(parts.shape, jnp.float32)
    parts[:blocks, :rays] = first
    parts[:blocks, rays:] = second[:, :LANES]
    parts[blocks : 2 * blocks, : 2 * LANES] = second[:, LANES:]
    parts[2 * blocks : 3 * blocks, 2 * LANES :] = second[:, LANES:]
    parts[3 * blocks : 3 * blocks + tiles, 2 * LANES : 3 * LANES] = meta[:, :LANES]

    tile, within = split(lax.broadcasted_iota(jnp.int32, (8 * tiles, width), 0), 8)
    lane = lax.broadcasted_iota(jnp.int32, (8 * tiles, width), 1)
    copy = split(lane, blocks)[0]
    slot = chosen(*split(tile, col_count))[0]
    low = 2.0 * (within - ROOM)
    wanted = jnp.where(copy == 0.0, within, jnp.where(copy == 1.0, low, low + 1.0))
    place = ((copy == 0.0) & (within < ROOM)) | ((copy > 0.0) & (copy < 3.0) & (within >= ROOM))
    codes = (lane.astype(jnp.float32) - 3.0 * blocks == tile) & (within == 7.0)
    select = jnp.where((place & (slot == wanted)) | codes, 1.0, 0.0).astype(jnp.bfloat16)
    rest = parts[...]
    total = jnp.zeros(out_ref.shape, jnp.float32)
    for _ in range(3):
        part = rest.astype(jnp.bfloat16)
        rest = rest - part.astype(jnp.float32)
        total = total + jnp.dot(select, part, preferred_element_type=jnp.float32)
    out_ref[...] = total


def table_kernel(profile_ref, dest_ref, rays_ref, pairs_ref, last_ref, dest_copy, rays_copy):
    dest_copy[...] = dest_ref[...]
    rays_copy[...] = rays_ref[...]
    a = lax.broadcasted_iota(jnp.int32, (DISC, DISC), 0) - HALO
    c = lax.broadcasted_iota(jnp.int32, (DISC, DISC), 1) - HALO
    weights = jnp.where(a * a + c * c <= HALO * HALO, profile_ref[...], 0.0)
    kernel = (weights / jnp.sum(weights)).astype(jnp.bfloat16)
    source = lax.broadcasted_iota(jnp.int32, (DISC, LANES), 0)
    target = lax.broadcasted_iota(jnp.int32, (DISC, LANES), 1)
    mirror = jnp.where((source + target) % LANES == 0, 1.0, 0.0).astype(jnp.bfloat16)
    mirrored = jnp.dot(kernel, mirror, preferred_element_type=jnp.float32)
    left = lax.broadcasted_iota(jnp.int32, (LANES, LANES), 1) < SPAN

    def band(row, start):
        wide = jnp.broadcast_to(mirrored[row : row + 1, :], (LANES, LANES))
        return pltpu.roll(wide, start, 1, stride=1, stride_axis=0)

    for u in range(TURNS):
        for s in range(0, STEP, 2):
            row = u * STEP + s
            both = jnp.where(left, band(row, 0), band(row + 1, SPAN))
            pairs_ref[u * LANES : (u + 1) * LANES, s * SPAN : (s + 2) * SPAN] = both.astype(jnp.bfloat16)
    last_ref[...] = jnp.where(left, band(2 * HALO, 0), 0.0).astype(jnp.bfloat16)


def hats(row, cell):
    near, far, here, there = (value.astype(jnp.bfloat16) for value in row)
    zero = jnp.zeros((), jnp.bfloat16)
    return jnp.where(cell == here, near, jnp.where(cell == there, far, zero))


def deposited(both, lists, stage, shifts, facts):
    sources = both.shape[0]
    rays = 3 * LANES
    first_lane = lax.axis_index("row") % 2 * 8
    room = sources * ROOM + 1
    lane = lax.broadcasted_iota(jnp.int32, (sources, LANES), 1)
    parity = lax.axis_index("row") % 2
    words = jnp.where(lane == KINDS + parity, both[:, 7, 2 * LANES :][:, :LANES], 0.0)
    words = jnp.sum(words, axis=1, keepdims=True).astype(jnp.int32)
    words = [words[at, 0] for at in range(sources)]

    def listed(counts, kinds, slots):
        counts = list(counts)
        for kind in kinds:
            for at in range(sources):
                for k in slots:
                    lists[kind * room + counts[kind]] = at * 8 + k
                    bit = (words[at] >> (ROOM * kind + k)) & 1
                    counts[kind] = counts[kind] + bit
        return tuple(counts)

    rare = sum(1 << (ROOM * kind + k) for kind in range(4) for k in range(3, ROOM))
    seldom = functools.reduce(jnp.bitwise_or, words) & rare
    counts = lax.cond(
        seldom != 0,
        lambda held: listed(held, range(4), range(3, ROOM)),
        lambda held: held,
        (jnp.int32(0),) * 4,
    )

    def doubled(cell):
        return (2 * cell).astype(jnp.float32).astype(jnp.bfloat16)

    own = doubled(lax.broadcasted_iota(jnp.int32, (TILE, rays), 0))
    edge = lax.broadcasted_iota(jnp.int32, (2 * HALO, rays), 0)
    edge = doubled(jnp.where(edge < HALO, edge - HALO, edge + (TILE - HALO)))
    lane = lax.broadcasted_iota(jnp.int32, (1, LANES), 1) - first_lane

    def load(kind, step, batch, start):
        for k in range(batch):
            at = start + k
            entry = lists[kind * room + jnp.minimum(step * batch + k, counts[kind])]
            source, slot = entry >> 3, entry & 7
            head = both[source, pl.ds(slot, 1), :]
            tail = both[source, pl.ds(ROOM + (slot >> 1), 1), :]
            meta = both[source, 7:8, :][:, 2 * LANES : 3 * LANES]
            stage[0, at : at + 1, :] = head[:, :rays]
            stage[1, at : at + 1, :LANES] = head[:, rays:]
            stage[1, at : at + 1, LANES:] = jnp.where(
                (slot & 1) == 1, tail[:, 2 * LANES :], tail[:, : 2 * LANES]
            )
            shifts[at : at + 1, :] = jnp.where(lane == slot, meta, 0.0)

    def prepare(begin, end):
        code = jnp.sum(shifts[begin:end, :], axis=1, keepdims=True)
        rowwise = jnp.floor((code + 0.5) / 3.0)
        offsets = (rowwise - 1.0) * (2.0 * TILE), (code - 3.0 * rowwise - 1.0) * (2.0 * TILE)
        for axis in range(2):
            coords = stage[axis, begin:end, :]
            low = jnp.floor(coords)
            facts[4 * axis, begin:end, :] = 1.0 - (coords - low)
            facts[4 * axis + 1, begin:end, :] = 1.0 - ((low + 1.0) - coords)
            here = 2.0 * low + offsets[axis]
            facts[4 * axis + 2, begin:end, :] = here
            facts[4 * axis + 3, begin:end, :] = here + 2.0

    def product(kind, batch, start):
        down, across = (own, edge)[kind // 2], (own, edge)[kind % 2]
        firsts, seconds = [], []
        for at in range(start, start + batch):
            row = [facts[j, at : at + 1, :] for j in range(8)]
            firsts.append(hats(row[:4], down))
            seconds.append(hats(row[4:], across))
        return lax.dot_general(
            jnp.concatenate(firsts, axis=1),
            jnp.concatenate(seconds, axis=1),
            (((1,), (1,)), ((), ())),
            preferred_element_type=jnp.float32,
        )

    def ready(step, *given):
        for kind, batch, start in given:
            load(kind, step, batch, start)
        prepare(given[0][2], given[-1][2] + BATCH)

    def together(one, two):
        def step_one(step, sums, given=one):
            sums = sums + product(*given)
            ready(step + 1, given)
            return sums

        def step_both(step, sums):
            sums = sums[0] + product(*one), sums[1] + product(*two)
            ready(step + 1, one, two)
            return sums

        zeros = [
            jnp.zeros(((TILE, 2 * HALO)[kind // 2], (TILE, 2 * HALO)[kind % 2]), jnp.float32)
            for kind in (one[0], two[0])
        ]
        steps = [(counts[kind] + batch - 1) // batch for kind, batch, _ in (one, two)]
        shared = jnp.minimum(steps[0], steps[1])
        sums = lax.fori_loop(0, shared, step_both, tuple(zeros))
        return [
            lax.fori_loop(shared, steps[j], functools.partial(step_one, given=(one, two)[j]), sums[j])
            for j in range(2)
        ]

    pairs = (
        ((0, BATCH, 0), (3, BATCH // 2, BATCH)),
        ((1, BATCH // 2, 2 * BATCH), (2, BATCH // 2, 3 * BATCH)),
    )
    for pair in pairs:
        kinds = [kind for kind, _, _ in pair]
        counts = listed(counts, kinds, range(3))
        for kind in kinds:
            lists[kind * room + counts[kind]] = ROOM
        ready(0, *pair)
    inside, corners = together(*pairs[0])
    beside, above = together(*pairs[1])

    def wide(middle, ends):
        return jnp.concatenate([ends[:, :HALO], middle, ends[:, HALO:]], axis=1)

    middle, ends = wide(inside, beside), wide(above, corners)
    return jnp.concatenate([ends[:HALO], middle, ends[HALO:]], axis=0)


def spread_kernel(scale, mine_ref, other_ref, before_ref, pairs_ref, last_ref, out_ref, total_ref,
                  left, both, *scratch):
    sources = mine_ref.shape[0]
    both[:sources] = mine_ref[...]
    both[sources:] = other_ref[...]
    cells = deposited(both, *scratch)
    if before_ref is not None:
        cells = cells + before_ref[...]
    total_ref[...] = cells
    blocks = [cells[:, at : at + LANES].astype(jnp.bfloat16) for at in (0, SPAN)]
    for h in range(2):
        for u in range(TURNS):
            left[h * LONG : (h + 1) * LONG, u * LANES : (u + 1) * LANES] = blocks[h][
                u * STEP : u * STEP + LONG, :
            ]
    lowest = jnp.concatenate([block[2 * HALO :, :] for block in blocks], axis=0)
    ends = jnp.dot(lowest, last_ref[...], preferred_element_type=jnp.float32)
    evens = [ends[:TILE], ends[TILE:]]
    odds = [jnp.zeros((TILE, LANES), jnp.float32)] * 2
    for p in range(0, STEP * SPAN, 2 * LANES):
        both = jnp.dot(left[...], pairs_ref[:, p : p + 2 * LANES], preferred_element_type=jnp.float32)
        for h in range(2):
            for lanes in (0, LANES):
                s = (p + lanes) // SPAN
                part = both[h * LONG : (h + 1) * LONG, lanes : lanes + LANES]
                evens[h] = evens[h] + part[s : s + TILE]
                odds[h] = odds[h] + part[s + 1 : s + 1 + TILE]
    low = evens[0] + pltpu.roll(odds[0], SPAN, 1)
    high = pltpu.roll(evens[1], SPAN, 1) + odds[1]
    lane = lax.broadcasted_iota(jnp.int32, (TILE, LANES), 1)
    out_ref[...] = jnp.where(lane < SPAN, low, high) / scale


def shards(positions, destination, profile):
    blocks, _, rays = positions.shape
    row_count, col_count = lax.axis_size("row"), lax.axis_size("col")
    tiles = row_count * col_count
    width = -(-(3 * blocks + tiles) // LANES) * LANES

    def exchange(turn, labels, coords):
        kernel, given = pack_kernel, (turn, labels, coords)
        if turn is None:
            kernel, given = functools.partial(pack_kernel, None), (labels, coords)
        outgoing = pl.pallas_call(
            kernel,
            out_shape=jax.ShapeDtypeStruct((8 * tiles, rays + LANES), jnp.float32),
            in_specs=[SMEM, VMEM, VMEM][-len(given) :],
            out_specs=VMEM,
            scratch_shapes=[
                pltpu.VMEM((1, width), jnp.float32),
                pltpu.VMEM((width, rays + LANES), jnp.float32),
            ],
            compiler_params=ALONE if turn is None else LIMIT,
            name="pack",
        )(*given)
        return lax.all_to_all(
            outgoing.reshape(tiles, 8, rays + LANES), ("row", "col"), split_axis=0, concat_axis=0, tiled=True
        )

    def deposit(mine, before, pairs, last):
        other = lax.ppermute(mine, "row", [(i, i ^ 1) for i in range(row_count)])
        scale = blocks * rays / (TILE * TILE)
        kernel, given = functools.partial(spread_kernel, scale), (mine, other, before, pairs, last)
        if before is None:
            kernel = lambda mine, other, *refs: spread_kernel(scale, mine, other, None, *refs)
            given = (mine, other, pairs, last)
        return pl.pallas_call(
            kernel,
            out_shape=(
                jax.ShapeDtypeStruct((TILE, TILE), jnp.float32),
                jax.ShapeDtypeStruct((WIDE, WIDE), jnp.float32),
            ),
            in_specs=[VMEM] * len(given),
            out_specs=(VMEM, VMEM),
            scratch_shapes=[
                pltpu.VMEM((2 * LONG, TURNS * LANES), jnp.bfloat16),
                pltpu.VMEM((2 * tiles, 8, rays + LANES), jnp.float32),
                pltpu.SMEM((4 * (2 * tiles * ROOM + 1),), jnp.int32),
                pltpu.VMEM((2, 4 * BATCH, rays), jnp.float32),
                pltpu.VMEM((4 * BATCH, LANES), jnp.float32),
                pltpu.VMEM((8, 4 * BATCH, rays), jnp.float32),
            ],
            compiler_params=LIMIT,
            name="spread",
        )(*given)

    mine = exchange(None, destination.T, positions)
    pairs, last, labels, coords = pl.pallas_call(
        table_kernel,
        out_shape=(
            jax.ShapeDtypeStruct((TURNS * LANES, STEP * SPAN), jnp.bfloat16),
            jax.ShapeDtypeStruct((LANES, LANES), jnp.bfloat16),
            jax.ShapeDtypeStruct((1, blocks), jnp.int32),
            jax.ShapeDtypeStruct(positions.shape, jnp.float32),
        ),
        in_specs=[VMEM] * 3,
        out_specs=(VMEM,) * 4,
        compiler_params=LIMIT,
        cost_estimate=pl.CostEstimate(flops=10_000_000, bytes_accessed=6_000_000, transcendentals=0),
        name="table",
    )(profile, destination.T, positions)
    mine, pairs, last, labels, coords = lax.optimization_barrier((mine, pairs, last, labels, coords))
    turns = jnp.max(mine[:, 7, 2 * LANES + COUNT]).astype(jnp.int32)
    out, total = deposit(mine, None, pairs, last)

    def more(state):
        turn, _, total = state
        out, total = deposit(
            exchange(jnp.full((1,), turn, jnp.int32), labels, coords), total, pairs, last
        )
        return turn + 1, out, total

    return lax.while_loop(lambda state: state[0] < turns, more, (jnp.int32(1), out, total))[1]


def solution(mesh):
    placed = (P(("maps", "row", "col"), None, None), P(("maps", "row", "col"), None), P())
    return jax.shard_map(
        shards, mesh=mesh, in_specs=placed, out_specs=P(("maps", "row"), "col"), check_vma=False
    )
```

```python
import functools

import jax
import jax.numpy as jnp
from jax import lax
from jax.experimental import pallas as pl
from jax.experimental.pallas import tpu as pltpu
from jax.sharding import PartitionSpec as P

TILE = 128
HALO = 32
MOST = 4
DISC = 2 * HALO + 1
STEP = 16
LONG = TILE + STEP
TURNS = 2 * HALO // STEP
WIDE = TILE + 2 * HALO
LANES = 128
SPAN = 64
BATCH = 8
ROOM = 5
COMMON = 3
COUNT = 16
KINDS = 18
FAR = 1024.0

VMEM = pl.BlockSpec(memory_space=pltpu.VMEM)
SMEM = pl.BlockSpec(memory_space=pltpu.SMEM)
ALONE = pltpu.CompilerParams(vmem_limit_bytes=67_104_000)
LIMIT = pltpu.CompilerParams(vmem_limit_bytes=32 * 1024 * 1024)


def touches(distance, least, most):
    before = (distance == -1.0) & (most > TILE - HALO - 1.0)
    after = (distance == 1.0) & (least < HALO)
    return (distance == 0.0) | before | after


def split(index, size):
    index = index.astype(jnp.float32)
    quotient = jnp.floor((index + 0.5) * (1.0 / size))
    return quotient, index - size * quotient


def pack_kernel(turn_ref, dest_ref, rays_ref, out_ref, labels, parts):
    blocks, _, rays = rays_ref.shape
    tiles = out_ref.shape[0] // 8
    width = parts.shape[0]
    col_count = lax.axis_size("col")
    skip = 0.0 if turn_ref is None else 2.0 * ROOM * turn_ref[0].astype(jnp.float32)
    copy, own = split(lax.broadcasted_iota(jnp.int32, (blocks, width), 1), blocks)
    place = lax.broadcasted_iota(jnp.int32, (blocks, width), 0).astype(jnp.float32)
    there = (own == place) & (copy < 3.0)

    def laid(column):
        return jnp.sum(jnp.where(there, column, 0.0), axis=0, keepdims=True)

    labels[...] = jnp.full(labels.shape, -1.0, jnp.float32)
    for g in range(3):
        labels[0:1, g * blocks : (g + 1) * blocks] = dest_ref[...].astype(jnp.float32)
    label = labels[...]
    label_row = jnp.floor((label + 0.5) * (1.0 / col_count))
    label_col = label - label_row * col_count
    first, second = rays_ref[:, 0, :], rays_ref[:, 1, :]
    least_row, most_row = laid(jnp.min(first, 1, keepdims=True)), laid(jnp.max(first, 1, keepdims=True))
    least_col, most_col = laid(jnp.min(second, 1, keepdims=True)), laid(jnp.max(second, 1, keepdims=True))
    earlier = lax.broadcasted_iota(jnp.int32, (width, width), 0).astype(jnp.float32)
    copy, own = split(lax.broadcasted_iota(jnp.int32, (width, width), 1), blocks)
    earlier = jnp.where((earlier < own) & (copy < 3.0), 1.0, 0.0).astype(jnp.bfloat16)

    def chosen(row, col):
        odd = split(row, 2)[1]
        row = row - odd
        dc = label_col - col
        aside = touches(dc, least_col, most_col) & (label >= 0.0)

        def coded(dr):
            reach = aside & touches(dr, least_row, most_row)
            return reach, jnp.where(reach, 3.0 * dr + dc + 4.0, FAR)

        even, odds = coded(label_row - row), coded(label_row - row - 1.0)
        reach = jnp.where(even[0] | odds[0], 1.0, 0.0)
        rank = jnp.dot(reach.astype(jnp.bfloat16), earlier, preferred_element_type=jnp.float32)
        left = rank - skip - odd
        slot = jnp.floor(left * 0.5)
        mine = (reach > 0.0) & (slot * 2.0 == left) & (slot >= 0.0) & (slot < ROOM)
        return jnp.where(mine, slot, -1.0), even[1], odds[1], (rank + 1.0) * reach

    tile = lax.broadcasted_iota(jnp.int32, (tiles, width), 0)
    slot, even, odds, most = chosen(*split(tile, col_count))
    most = jnp.max(jnp.max(most, axis=1, keepdims=True), axis=0, keepdims=True)
    turns = jnp.floor((most + (2.0 * ROOM - 0.5)) / (2.0 * ROOM))
    lane = lax.broadcasted_iota(jnp.int32, (tiles, width), 1)
    meta = jnp.where(lane == COUNT, turns, FAR)
    for k in range(ROOM):
        here = (slot == k) & (lane < blocks)
        for at, code in ((k, even), (8 + k, odds)):
            found = jnp.sum(jnp.where(here, code - FAR, 0.0), axis=1, keepdims=True) + FAR
            meta = jnp.where(lane == at, found, meta)
    for at, code in ((KINDS, even), (KINDS + 1, odds)):
        rowwise, colwise = split(code, 3)
        kind = jnp.where(rowwise == 1.0, 0.0, 2.0) + jnp.where(colwise == 1.0, 0.0, 1.0)
        bit = 1 << jnp.clip(5.0 * kind + slot, 0.0, 23.0).astype(jnp.int32)
        here = (slot >= 0.0) & (code < FAR) & (lane < blocks)
        word = jnp.sum(jnp.where(here, bit.astype(jnp.float32), 0.0), axis=1, keepdims=True)
        meta = jnp.where(lane == at, word, meta)

    parts[...] = jnp.zeros(parts.shape, jnp.float32)
    parts[:blocks, :rays] = first
    parts[:blocks, rays:] = second[:, :LANES]
    parts[blocks : 2 * blocks, : 2 * LANES] = second[:, LANES:]
    parts[2 * blocks : 3 * blocks, 2 * LANES :] = second[:, LANES:]
    parts[3 * blocks : 3 * blocks + tiles, 2 * LANES : 3 * LANES] = meta[:, :LANES]

    tile, within = split(lax.broadcasted_iota(jnp.int32, (8 * tiles, width), 0), 8)
    lane = lax.broadcasted_iota(jnp.int32, (8 * tiles, width), 1)
    copy = split(lane, blocks)[0]
    slot = chosen(*split(tile, col_count))[0]
    low = 2.0 * (within - ROOM)
    wanted = jnp.where(copy == 0.0, within, jnp.where(copy == 1.0, low, low + 1.0))
    place = ((copy == 0.0) & (within < ROOM)) | ((copy > 0.0) & (copy < 3.0) & (within >= ROOM))
    codes = (lane.astype(jnp.float32) - 3.0 * blocks == tile) & (within == 7.0)
    select = jnp.where((place & (slot == wanted)) | codes, 1.0, 0.0).astype(jnp.bfloat16)
    rest = parts[...]
    total = jnp.zeros(out_ref.shape, jnp.float32)
    for _ in range(3):
        part = rest.astype(jnp.bfloat16)
        rest = rest - part.astype(jnp.float32)
        total = total + jnp.dot(select, part, preferred_element_type=jnp.float32)
    out_ref[...] = total


def table_kernel(profile_ref, dest_ref, rays_ref, pairs_ref, last_ref, dest_copy, rays_copy):
    dest_copy[...] = dest_ref[...]
    rays_copy[...] = rays_ref[...]
    a = lax.broadcasted_iota(jnp.int32, (DISC, DISC), 0) - HALO
    c = lax.broadcasted_iota(jnp.int32, (DISC, DISC), 1) - HALO
    weights = jnp.where(a * a + c * c <= HALO * HALO, profile_ref[...], 0.0)
    kernel = (weights / jnp.sum(weights)).astype(jnp.bfloat16)
    source = lax.broadcasted_iota(jnp.int32, (DISC, LANES), 0)
    target = lax.broadcasted_iota(jnp.int32, (DISC, LANES), 1)
    mirror = jnp.where((source + target) % LANES == 0, 1.0, 0.0).astype(jnp.bfloat16)
    mirrored = jnp.dot(kernel, mirror, preferred_element_type=jnp.float32)
    left = lax.broadcasted_iota(jnp.int32, (LANES, LANES), 1) < SPAN

    def band(row, start):
        wide = jnp.broadcast_to(mirrored[row : row + 1, :], (LANES, LANES))
        return pltpu.roll(wide, start, 1, stride=1, stride_axis=0)

    for u in range(TURNS):
        for s in range(0, STEP, 2):
            row = u * STEP + s
            both = jnp.where(left, band(row, 0), band(row + 1, SPAN))
            pairs_ref[u * LANES : (u + 1) * LANES, s * SPAN : (s + 2) * SPAN] = both.astype(jnp.bfloat16)
    last_ref[...] = jnp.where(left, band(2 * HALO, 0), 0.0).astype(jnp.bfloat16)


def hats(row, cell):
    near, far, here, there = (value.astype(jnp.bfloat16) for value in row)
    zero = jnp.zeros((), jnp.bfloat16)
    return jnp.where(cell == here, near, jnp.where(cell == there, far, zero))


def deposited(both, lists, stage, shifts, facts):
    sources = both.shape[0]
    rays = 3 * LANES
    first_lane = lax.axis_index("row") % 2 * 8
    room = sources * ROOM + 1
    lane = lax.broadcasted_iota(jnp.int32, (sources, LANES), 1)
    parity = lax.axis_index("row") % 2
    words = jnp.where(lane == KINDS + parity, both[:, 7, 2 * LANES :][:, :LANES], 0.0)
    words = jnp.sum(words, axis=1, keepdims=True).astype(jnp.int32)
    words = [words[at, 0] for at in range(sources)]

    def listed(counts, kinds, slots):
        counts = list(counts)
        for kind in kinds:
            for at in range(sources):
                for k in slots:
                    lists[kind * room + counts[kind]] = at * 8 + k
                    bit = (words[at] >> (ROOM * kind + k)) & 1
                    counts[kind] = counts[kind] + bit
        return tuple(counts)

    counts = (jnp.int32(0),) * 4
    used = functools.reduce(jnp.bitwise_or, words)
    for slot in range(COMMON, ROOM):
        counts = lax.cond(
            used & sum(1 << (ROOM * kind + slot) for kind in range(4)) != 0,
            lambda held, slot=slot: listed(held, range(4), (slot,)),
            lambda held: held,
            counts,
        )

    def doubled(cell):
        return (2 * cell).astype(jnp.float32).astype(jnp.bfloat16)

    own = doubled(lax.broadcasted_iota(jnp.int32, (TILE, rays), 0))
    edge = lax.broadcasted_iota(jnp.int32, (2 * HALO, rays), 0)
    edge = doubled(jnp.where(edge < HALO, edge - HALO, edge + (TILE - HALO)))
    lane = lax.broadcasted_iota(jnp.int32, (1, LANES), 1) - first_lane

    def load(kind, step, batch, start):
        for k in range(batch):
            at = start + k
            entry = lists[kind * room + jnp.minimum(step * batch + k, counts[kind])]
            source, slot = entry >> 3, entry & 7
            head = both[source, pl.ds(slot, 1), :]
            tail = both[source, pl.ds(ROOM + (slot >> 1), 1), :]
            meta = both[source, 7:8, :][:, 2 * LANES : 3 * LANES]
            stage[0, at : at + 1, :] = head[:, :rays]
            stage[1, at : at + 1, :LANES] = head[:, rays:]
            stage[1, at : at + 1, LANES:] = jnp.where(
                (slot & 1) == 1, tail[:, 2 * LANES :], tail[:, : 2 * LANES]
            )
            shifts[at : at + 1, :] = jnp.where(lane == slot, meta, 0.0)

    def prepare(begin, end):
        code = jnp.sum(shifts[begin:end, :], axis=1, keepdims=True)
        rowwise = jnp.floor((code + 0.5) / 3.0)
        offsets = (rowwise - 1.0) * (2.0 * TILE), (code - 3.0 * rowwise - 1.0) * (2.0 * TILE)
        for axis in range(2):
            coords = stage[axis, begin:end, :]
            low = jnp.floor(coords)
            facts[4 * axis, begin:end, :] = 1.0 - (coords - low)
            facts[4 * axis + 1, begin:end, :] = 1.0 - ((low + 1.0) - coords)
            here = 2.0 * low + offsets[axis]
            facts[4 * axis + 2, begin:end, :] = here
            facts[4 * axis + 3, begin:end, :] = here + 2.0

    def product(kind, batch, start):
        down, across = (own, edge)[kind // 2], (own, edge)[kind % 2]
        firsts, seconds = [], []
        for at in range(start, start + batch):
            row = [facts[j, at : at + 1, :] for j in range(8)]
            firsts.append(hats(row[:4], down))
            seconds.append(hats(row[4:], across))
        return lax.dot_general(
            jnp.concatenate(firsts, axis=1),
            jnp.concatenate(seconds, axis=1),
            (((1,), (1,)), ((), ())),
            preferred_element_type=jnp.float32,
        )

    def ready(step, *given):
        for kind, batch, start in given:
            load(kind, step, batch, start)
        prepare(given[0][2], given[-1][2] + BATCH)

    def together(one, two):
        def step_one(step, sums, given=one):
            sums = sums + product(*given)
            ready(step + 1, given)
            return sums

        def step_both(step, sums):
            sums = sums[0] + product(*one), sums[1] + product(*two)
            ready(step + 1, one, two)
            return sums

        zeros = [
            jnp.zeros(((TILE, 2 * HALO)[kind // 2], (TILE, 2 * HALO)[kind % 2]), jnp.float32)
            for kind in (one[0], two[0])
        ]
        steps = [(counts[kind] + batch - 1) // batch for kind, batch, _ in (one, two)]
        shared = jnp.minimum(steps[0], steps[1])
        sums = lax.fori_loop(0, shared, step_both, tuple(zeros))
        return [
            lax.fori_loop(shared, steps[j], functools.partial(step_one, given=(one, two)[j]), sums[j])
            for j in range(2)
        ]

    pairs = (
        ((0, 6, 0), (3, 3, BATCH)),
        ((1, BATCH // 2, 2 * BATCH), (2, BATCH // 2, 3 * BATCH)),
    )
    for pair in pairs:
        kinds = [kind for kind, _, _ in pair]
        counts = listed(counts, kinds, range(COMMON))
        for kind in kinds:
            lists[kind * room + counts[kind]] = ROOM
        ready(0, *pair)
    inside, corners = together(*pairs[0])
    beside, above = together(*pairs[1])

    def wide(middle, ends):
        return jnp.concatenate([ends[:, :HALO], middle, ends[:, HALO:]], axis=1)

    middle, ends = wide(inside, beside), wide(above, corners)
    return jnp.concatenate([ends[:HALO], middle, ends[HALO:]], axis=0)


def spread_kernel(scale, mine_ref, other_ref, before_ref, pairs_ref, last_ref, out_ref, total_ref,
                  left, both, *scratch):
    sources = mine_ref.shape[0]
    both[:sources] = mine_ref[...]
    both[sources:] = other_ref[...]
    cells = deposited(both, *scratch)
    if before_ref is not None:
        cells = cells + before_ref[...]
    total_ref[...] = cells
    blocks = [cells[:, at : at + LANES].astype(jnp.bfloat16) for at in (0, SPAN)]
    for h in range(2):
        for u in range(TURNS):
            left[h * LONG : (h + 1) * LONG, u * LANES : (u + 1) * LANES] = blocks[h][
                u * STEP : u * STEP + LONG, :
            ]
    lowest = jnp.concatenate([block[2 * HALO :, :] for block in blocks], axis=0)
    ends = jnp.dot(lowest, last_ref[...], preferred_element_type=jnp.float32)
    evens = [ends[:TILE], ends[TILE:]]
    odds = [jnp.zeros((TILE, LANES), jnp.float32)] * 2
    for p in range(0, STEP * SPAN, 2 * LANES):
        both = jnp.dot(left[...], pairs_ref[:, p : p + 2 * LANES], preferred_element_type=jnp.float32)
        for h in range(2):
            for lanes in (0, LANES):
                s = (p + lanes) // SPAN
                part = both[h * LONG : (h + 1) * LONG, lanes : lanes + LANES]
                evens[h] = evens[h] + part[s : s + TILE]
                odds[h] = odds[h] + part[s + 1 : s + 1 + TILE]
    low = evens[0] + pltpu.roll(odds[0], SPAN, 1)
    high = pltpu.roll(evens[1], SPAN, 1) + odds[1]
    lane = lax.broadcasted_iota(jnp.int32, (TILE, LANES), 1)
    out_ref[...] = jnp.where(lane < SPAN, low, high) / scale


def shards(positions, destination, profile):
    blocks, _, rays = positions.shape
    row_count, col_count = lax.axis_size("row"), lax.axis_size("col")
    tiles = row_count * col_count
    width = -(-(3 * blocks + tiles) // LANES) * LANES

    def exchange(turn, labels, coords):
        kernel, given = pack_kernel, (turn, labels, coords)
        if turn is None:
            kernel, given = functools.partial(pack_kernel, None), (labels, coords)
        outgoing = pl.pallas_call(
            kernel,
            out_shape=jax.ShapeDtypeStruct((8 * tiles, rays + LANES), jnp.float32),
            in_specs=[SMEM, VMEM, VMEM][-len(given) :],
            out_specs=VMEM,
            scratch_shapes=[
                pltpu.VMEM((1, width), jnp.float32),
                pltpu.VMEM((width, rays + LANES), jnp.float32),
            ],
            compiler_params=ALONE if turn is None else LIMIT,
            name="pack",
        )(*given)
        return lax.all_to_all(
            outgoing.reshape(tiles, 8, rays + LANES), ("row", "col"), split_axis=0, concat_axis=0, tiled=True
        )

    def deposit(mine, before, pairs, last):
        other = lax.ppermute(mine, "row", [(i, i ^ 1) for i in range(row_count)])
        scale = blocks * rays / (TILE * TILE)
        kernel, given = functools.partial(spread_kernel, scale), (mine, other, before, pairs, last)
        if before is None:
            kernel = lambda mine, other, *refs: spread_kernel(scale, mine, other, None, *refs)
            given = (mine, other, pairs, last)
        return pl.pallas_call(
            kernel,
            out_shape=(
                jax.ShapeDtypeStruct((TILE, TILE), jnp.float32),
                jax.ShapeDtypeStruct((WIDE, WIDE), jnp.float32),
            ),
            in_specs=[VMEM] * len(given),
            out_specs=(VMEM, VMEM),
            scratch_shapes=[
                pltpu.VMEM((2 * LONG, TURNS * LANES), jnp.bfloat16),
                pltpu.VMEM((2 * tiles, 8, rays + LANES), jnp.float32),
                pltpu.SMEM((4 * (2 * tiles * ROOM + 1),), jnp.int32),
                pltpu.VMEM((2, 4 * BATCH, rays), jnp.float32),
                pltpu.VMEM((4 * BATCH, LANES), jnp.float32),
                pltpu.VMEM((8, 4 * BATCH, rays), jnp.float32),
            ],
            compiler_params=LIMIT,
            name="spread",
        )(*given)

    mine = exchange(None, destination.T, positions)
    pairs, last, labels, coords = pl.pallas_call(
        table_kernel,
        out_shape=(
            jax.ShapeDtypeStruct((TURNS * LANES, STEP * SPAN), jnp.bfloat16),
            jax.ShapeDtypeStruct((LANES, LANES), jnp.bfloat16),
            jax.ShapeDtypeStruct((1, blocks), jnp.int32),
            jax.ShapeDtypeStruct(positions.shape, jnp.float32),
        ),
        in_specs=[VMEM] * 3,
        out_specs=(VMEM,) * 4,
        compiler_params=LIMIT,
        cost_estimate=pl.CostEstimate(flops=10_000_000, bytes_accessed=6_000_000, transcendentals=0),
        name="table",
    )(profile, destination.T, positions)
    mine, pairs, last, labels, coords = lax.optimization_barrier((mine, pairs, last, labels, coords))
    turns = jnp.max(mine[:, 7, 2 * LANES + COUNT]).astype(jnp.int32)
    out, total = deposit(mine, None, pairs, last)

    def more(state):
        turn, _, total = state
        out, total = deposit(
            exchange(jnp.full((1,), turn, jnp.int32), labels, coords), total, pairs, last
        )
        return turn + 1, out, total

    return lax.while_loop(lambda state: state[0] < turns, more, (jnp.int32(1), out, total))[1]


def solution(mesh):
    placed = (P(("maps", "row", "col"), None, None), P(("maps", "row", "col"), None), P())
    return jax.shard_map(
        shards, mesh=mesh, in_specs=placed, out_specs=P(("maps", "row"), "col"), check_vma=False
    )
```

```python
import functools

import jax
import jax.numpy as jnp
from jax import lax
from jax.experimental import pallas as pl
from jax.experimental.pallas import tpu as pltpu
from jax.sharding import PartitionSpec as P

TILE = 128
HALO = 32
MOST = 4
DISC = 2 * HALO + 1
STEP = 16
LONG = TILE + STEP
TURNS = 2 * HALO // STEP
WIDE = TILE + 2 * HALO
LANES = 128
SPAN = 64
BATCH = 8
ROOM = 5
COMMON = 3
COUNT = 16
KINDS = 18
FAR = 1024.0

VMEM = pl.BlockSpec(memory_space=pltpu.VMEM)
SMEM = pl.BlockSpec(memory_space=pltpu.SMEM)
ALONE = pltpu.CompilerParams(vmem_limit_bytes=67_104_000)
LIMIT = pltpu.CompilerParams(vmem_limit_bytes=32 * 1024 * 1024)


def touches(distance, least, most):
    before = (distance == -1.0) & (most > TILE - HALO - 1.0)
    after = (distance == 1.0) & (least < HALO)
    return (distance == 0.0) | before | after


def split(index, size):
    index = index.astype(jnp.float32)
    quotient = jnp.floor((index + 0.5) * (1.0 / size))
    return quotient, index - size * quotient


def pack_kernel(turn_ref, dest_ref, rays_ref, out_ref, labels, parts):
    blocks, _, rays = rays_ref.shape
    tiles = out_ref.shape[0] // 8
    width = parts.shape[0]
    col_count = lax.axis_size("col")
    skip = 0.0 if turn_ref is None else 2.0 * ROOM * turn_ref[0].astype(jnp.float32)
    copy, own = split(lax.broadcasted_iota(jnp.int32, (blocks, width), 1), blocks)
    place = lax.broadcasted_iota(jnp.int32, (blocks, width), 0).astype(jnp.float32)
    there = (own == place) & (copy < 3.0)

    def laid(column):
        return jnp.sum(jnp.where(there, column, 0.0), axis=0, keepdims=True)

    labels[...] = jnp.full(labels.shape, -1.0, jnp.float32)
    for g in range(3):
        labels[0:1, g * blocks : (g + 1) * blocks] = dest_ref[...].astype(jnp.float32)
    label = labels[...]
    label_row = jnp.floor((label + 0.5) * (1.0 / col_count))
    label_col = label - label_row * col_count
    first, second = rays_ref[:, 0, :], rays_ref[:, 1, :]
    least_row, most_row = laid(jnp.min(first, 1, keepdims=True)), laid(jnp.max(first, 1, keepdims=True))
    least_col, most_col = laid(jnp.min(second, 1, keepdims=True)), laid(jnp.max(second, 1, keepdims=True))
    earlier = lax.broadcasted_iota(jnp.int32, (width, width), 0).astype(jnp.float32)
    copy, own = split(lax.broadcasted_iota(jnp.int32, (width, width), 1), blocks)
    earlier = jnp.where((earlier < own) & (copy < 3.0), 1.0, 0.0).astype(jnp.bfloat16)

    def chosen(row, col):
        odd = split(row, 2)[1]
        row = row - odd
        dc = label_col - col
        aside = touches(dc, least_col, most_col) & (label >= 0.0)

        def coded(dr):
            reach = aside & touches(dr, least_row, most_row)
            return reach, jnp.where(reach, 3.0 * dr + dc + 4.0, FAR)

        even, odds = coded(label_row - row), coded(label_row - row - 1.0)
        reach = jnp.where(even[0] | odds[0], 1.0, 0.0)
        rank = jnp.dot(reach.astype(jnp.bfloat16), earlier, preferred_element_type=jnp.float32)
        left = rank - skip - odd
        slot = jnp.floor(left * 0.5)
        mine = (reach > 0.0) & (slot * 2.0 == left) & (slot >= 0.0) & (slot < ROOM)
        return jnp.where(mine, slot, -1.0), even[1], odds[1], (rank + 1.0) * reach

    tile = lax.broadcasted_iota(jnp.int32, (tiles, width), 0)
    slot, even, odds, most = chosen(*split(tile, col_count))
    most = jnp.max(jnp.max(most, axis=1, keepdims=True), axis=0, keepdims=True)
    turns = jnp.floor((most + (2.0 * ROOM - 0.5)) / (2.0 * ROOM))
    lane = lax.broadcasted_iota(jnp.int32, (tiles, width), 1)
    meta = jnp.where(lane == COUNT, turns, FAR)
    for k in range(ROOM):
        here = (slot == k) & (lane < blocks)
        for at, code in ((k, even), (8 + k, odds)):
            found = jnp.sum(jnp.where(here, code - FAR, 0.0), axis=1, keepdims=True) + FAR
            meta = jnp.where(lane == at, found, meta)
    for at, code in ((KINDS, even), (KINDS + 1, odds)):
        rowwise, colwise = split(code, 3)
        kind = jnp.where(rowwise == 1.0, 0.0, 2.0) + jnp.where(colwise == 1.0, 0.0, 1.0)
        bit = 1 << jnp.clip(5.0 * kind + slot, 0.0, 23.0).astype(jnp.int32)
        here = (slot >= 0.0) & (code < FAR) & (lane < blocks)
        word = jnp.sum(jnp.where(here, bit.astype(jnp.float32), 0.0), axis=1, keepdims=True)
        meta = jnp.where(lane == at, word, meta)

    parts[...] = jnp.zeros(parts.shape, jnp.float32)
    parts[:blocks, :rays] = first
    parts[:blocks, rays:] = second[:, :LANES]
    parts[blocks : 2 * blocks, : 2 * LANES] = second[:, LANES:]
    parts[2 * blocks : 3 * blocks, 2 * LANES :] = second[:, LANES:]
    parts[3 * blocks : 3 * blocks + tiles, 2 * LANES : 3 * LANES] = meta[:, :LANES]

    tile, within = split(lax.broadcasted_iota(jnp.int32, (8 * tiles, width), 0), 8)
    lane = lax.broadcasted_iota(jnp.int32, (8 * tiles, width), 1)
    copy = split(lane, blocks)[0]
    slot = chosen(*split(tile, col_count))[0]
    low = 2.0 * (within - ROOM)
    wanted = jnp.where(copy == 0.0, within, jnp.where(copy == 1.0, low, low + 1.0))
    place = ((copy == 0.0) & (within < ROOM)) | ((copy > 0.0) & (copy < 3.0) & (within >= ROOM))
    codes = (lane.astype(jnp.float32) - 3.0 * blocks == tile) & (within == 7.0)
    select = jnp.where((place & (slot == wanted)) | codes, 1.0, 0.0).astype(jnp.bfloat16)
    rest = parts[...]
    total = jnp.zeros(out_ref.shape, jnp.float32)
    for _ in range(3):
        part = rest.astype(jnp.bfloat16)
        rest = rest - part.astype(jnp.float32)
        total = total + jnp.dot(select, part, preferred_element_type=jnp.float32)
    out_ref[...] = total


def table_kernel(profile_ref, dest_ref, rays_ref, pairs_ref, last_ref, dest_copy, rays_copy):
    dest_copy[...] = dest_ref[...]
    rays_copy[...] = rays_ref[...]
    a = lax.broadcasted_iota(jnp.int32, (DISC, DISC), 0) - HALO
    c = lax.broadcasted_iota(jnp.int32, (DISC, DISC), 1) - HALO
    weights = jnp.where(a * a + c * c <= HALO * HALO, profile_ref[...], 0.0)
    kernel = (weights / jnp.sum(weights)).astype(jnp.bfloat16)
    source = lax.broadcasted_iota(jnp.int32, (DISC, LANES), 0)
    target = lax.broadcasted_iota(jnp.int32, (DISC, LANES), 1)
    mirror = jnp.where((source + target) % LANES == 0, 1.0, 0.0).astype(jnp.bfloat16)
    mirrored = jnp.dot(kernel, mirror, preferred_element_type=jnp.float32)
    left = lax.broadcasted_iota(jnp.int32, (LANES, LANES), 1) < SPAN

    def band(row, start):
        wide = jnp.broadcast_to(mirrored[row : row + 1, :], (LANES, LANES))
        return pltpu.roll(wide, start, 1, stride=1, stride_axis=0)

    for u in range(TURNS):
        for s in range(0, STEP, 2):
            row = u * STEP + s
            both = jnp.where(left, band(row, 0), band(row + 1, SPAN))
            pairs_ref[u * LANES : (u + 1) * LANES, s * SPAN : (s + 2) * SPAN] = both.astype(jnp.bfloat16)
    last_ref[...] = jnp.where(left, band(2 * HALO, 0), 0.0).astype(jnp.bfloat16)


def hats(row, cell):
    near, far, here, there = (value.astype(jnp.bfloat16) for value in row)
    zero = jnp.zeros((), jnp.bfloat16)
    return jnp.where(cell == here, near, jnp.where(cell == there, far, zero))


def deposited(both, lists, stage, shifts, facts):
    sources = both.shape[0]
    rays = 3 * LANES
    first_lane = lax.axis_index("row") % 2 * 8
    room = sources * ROOM + 1
    lane = lax.broadcasted_iota(jnp.int32, (sources, LANES), 1)
    parity = lax.axis_index("row") % 2
    words = jnp.where(lane == KINDS + parity, both[:, 7, 2 * LANES :][:, :LANES], 0.0)
    words = jnp.sum(words, axis=1, keepdims=True).astype(jnp.int32)
    words = [words[at, 0] for at in range(sources)]

    def listed(counts, kinds, slots):
        counts = list(counts)
        for kind in kinds:
            for at in range(sources):
                for k in slots:
                    lists[counts[kind]] = at * 8 + k
                    bit = (words[at] >> (ROOM * kind + k)) & 1
                    counts[kind] = counts[kind] + bit
        return tuple(counts)

    counts = tuple(jnp.int32(kind * room) for kind in range(4))
    used = functools.reduce(jnp.bitwise_or, words)
    for slot in range(COMMON, ROOM):
        counts = lax.cond(
            used & sum(1 << (ROOM * kind + slot) for kind in range(4)) != 0,
            lambda held, slot=slot: listed(held, range(4), (slot,)),
            lambda held: held,
            counts,
        )

    def doubled(cell):
        return (2 * cell).astype(jnp.float32).astype(jnp.bfloat16)

    own = doubled(lax.broadcasted_iota(jnp.int32, (TILE, rays), 0))
    edge = lax.broadcasted_iota(jnp.int32, (2 * HALO, rays), 0)
    edge = doubled(jnp.where(edge < HALO, edge - HALO, edge + (TILE - HALO)))
    lane = lax.broadcasted_iota(jnp.int32, (1, LANES), 1) - first_lane

    def load(kind, step, batch, start):
        for k in range(batch):
            at = start + k
            entry = lists[jnp.minimum(kind * room + k + step * batch, counts[kind])]
            source, slot = entry >> 3, entry & 7
            head = both[source, pl.ds(slot, 1), :]
            tail = both[source, pl.ds(ROOM + (slot >> 1), 1), :]
            meta = both[source, 7:8, :][:, 2 * LANES : 3 * LANES]
            stage[0, at : at + 1, :] = head[:, :rays]
            stage[1, at : at + 1, :LANES] = head[:, rays:]
            stage[1, at : at + 1, LANES:] = jnp.where(
                (slot & 1) == 1, tail[:, 2 * LANES :], tail[:, : 2 * LANES]
            )
            shifts[at : at + 1, :] = jnp.where(lane == slot, meta, 0.0)

    def prepare(begin, end):
        code = jnp.sum(shifts[begin:end, :], axis=1, keepdims=True)
        rowwise = jnp.floor((code + 0.5) / 3.0)
        offsets = (rowwise - 1.0) * (2.0 * TILE), (code - 3.0 * rowwise - 1.0) * (2.0 * TILE)
        for axis in range(2):
            coords = stage[axis, begin:end, :]
            low = jnp.floor(coords)
            facts[4 * axis, begin:end, :] = 1.0 - (coords - low)
            facts[4 * axis + 1, begin:end, :] = 1.0 - ((low + 1.0) - coords)
            here = 2.0 * low + offsets[axis]
            facts[4 * axis + 2, begin:end, :] = here
            facts[4 * axis + 3, begin:end, :] = here + 2.0

    def product(kind, batch, start):
        down, across = (own, edge)[kind // 2], (own, edge)[kind % 2]
        firsts, seconds = [], []
        for at in range(start, start + batch):
            row = [facts[j, at : at + 1, :] for j in range(8)]
            firsts.append(hats(row[:4], down))
            seconds.append(hats(row[4:], across))
        return lax.dot_general(
            jnp.concatenate(firsts, axis=1),
            jnp.concatenate(seconds, axis=1),
            (((1,), (1,)), ((), ())),
            preferred_element_type=jnp.float32,
        )

    def ready(step, *given):
        for kind, batch, start in given:
            load(kind, step, batch, start)
        prepare(given[0][2], given[-1][2] + BATCH)

    def together(one, two):
        def step_one(step, sums, given=one):
            sums = sums + product(*given)
            ready(step + 1, given)
            return sums

        def step_both(step, sums):
            sums = sums[0] + product(*one), sums[1] + product(*two)
            ready(step + 1, one, two)
            return sums

        zeros = [
            jnp.zeros(((TILE, 2 * HALO)[kind // 2], (TILE, 2 * HALO)[kind % 2]), jnp.float32)
            for kind in (one[0], two[0])
        ]
        steps = [(counts[kind] - kind * room + batch - 1) // batch for kind, batch, _ in (one, two)]
        shared = jnp.minimum(steps[0], steps[1])
        sums = lax.fori_loop(0, shared, step_both, tuple(zeros))
        return [
            lax.fori_loop(shared, steps[j], functools.partial(step_one, given=(one, two)[j]), sums[j])
            for j in range(2)
        ]

    pairs = (
        ((0, BATCH, 0), (3, BATCH // 2, BATCH)),
        ((1, BATCH // 2, 2 * BATCH), (2, BATCH // 2, 3 * BATCH)),
    )
    for pair in pairs:
        kinds = [kind for kind, _, _ in pair]
        counts = listed(counts, kinds, range(COMMON))
        for kind in kinds:
            lists[counts[kind]] = ROOM
        ready(0, *pair)
    inside, corners = together(*pairs[0])
    beside, above = together(*pairs[1])

    def wide(middle, ends):
        return jnp.concatenate([ends[:, :HALO], middle, ends[:, HALO:]], axis=1)

    middle, ends = wide(inside, beside), wide(above, corners)
    return jnp.concatenate([ends[:HALO], middle, ends[HALO:]], axis=0)


def spread_kernel(scale, mine_ref, other_ref, before_ref, pairs_ref, last_ref, out_ref, total_ref,
                  left, both, *scratch):
    sources = mine_ref.shape[0]
    both[:sources] = mine_ref[...]
    both[sources:] = other_ref[...]
    cells = deposited(both, *scratch)
    if before_ref is not None:
        cells = cells + before_ref[...]
    total_ref[...] = cells
    blocks = [cells[:, at : at + LANES].astype(jnp.bfloat16) for at in (0, SPAN)]
    for h in range(2):
        for u in range(TURNS):
            left[h * LONG : (h + 1) * LONG, u * LANES : (u + 1) * LANES] = blocks[h][
                u * STEP : u * STEP + LONG, :
            ]
    lowest = jnp.concatenate([block[2 * HALO :, :] for block in blocks], axis=0)
    ends = jnp.dot(lowest, last_ref[...], preferred_element_type=jnp.float32)
    evens = [ends[:TILE], ends[TILE:]]
    odds = [jnp.zeros((TILE, LANES), jnp.float32)] * 2
    for p in range(0, STEP * SPAN, 2 * LANES):
        both = jnp.dot(left[...], pairs_ref[:, p : p + 2 * LANES], preferred_element_type=jnp.float32)
        for h in range(2):
            for lanes in (0, LANES):
                s = (p + lanes) // SPAN
                part = both[h * LONG : (h + 1) * LONG, lanes : lanes + LANES]
                evens[h] = evens[h] + part[s : s + TILE]
                odds[h] = odds[h] + part[s + 1 : s + 1 + TILE]
    low = evens[0] + pltpu.roll(odds[0], SPAN, 1)
    high = pltpu.roll(evens[1], SPAN, 1) + odds[1]
    lane = lax.broadcasted_iota(jnp.int32, (TILE, LANES), 1)
    out_ref[...] = jnp.where(lane < SPAN, low, high) / scale


def shards(positions, destination, profile):
    blocks, _, rays = positions.shape
    row_count, col_count = lax.axis_size("row"), lax.axis_size("col")
    tiles = row_count * col_count
    width = -(-(3 * blocks + tiles) // LANES) * LANES

    def exchange(turn, labels, coords):
        kernel, given = pack_kernel, (turn, labels, coords)
        if turn is None:
            kernel, given = functools.partial(pack_kernel, None), (labels, coords)
        outgoing = pl.pallas_call(
            kernel,
            out_shape=jax.ShapeDtypeStruct((8 * tiles, rays + LANES), jnp.float32),
            in_specs=[SMEM, VMEM, VMEM][-len(given) :],
            out_specs=VMEM,
            scratch_shapes=[
                pltpu.VMEM((1, width), jnp.float32),
                pltpu.VMEM((width, rays + LANES), jnp.float32),
            ],
            compiler_params=ALONE if turn is None else LIMIT,
            name="pack",
        )(*given)
        return lax.all_to_all(
            outgoing.reshape(tiles, 8, rays + LANES), ("row", "col"), split_axis=0, concat_axis=0, tiled=True
        )

    def deposit(mine, before, pairs, last):
        other = lax.ppermute(mine, "row", [(i, i ^ 1) for i in range(row_count)])
        scale = blocks * rays / (TILE * TILE)
        kernel, given = functools.partial(spread_kernel, scale), (mine, other, before, pairs, last)
        if before is None:
            kernel = lambda mine, other, *refs: spread_kernel(scale, mine, other, None, *refs)
            given = (mine, other, pairs, last)
        return pl.pallas_call(
            kernel,
            out_shape=(
                jax.ShapeDtypeStruct((TILE, TILE), jnp.float32),
                jax.ShapeDtypeStruct((WIDE, WIDE), jnp.float32),
            ),
            in_specs=[VMEM] * len(given),
            out_specs=(VMEM, VMEM),
            scratch_shapes=[
                pltpu.VMEM((2 * LONG, TURNS * LANES), jnp.bfloat16),
                pltpu.VMEM((2 * tiles, 8, rays + LANES), jnp.float32),
                pltpu.SMEM((4 * (2 * tiles * ROOM + 1),), jnp.int32),
                pltpu.VMEM((2, 4 * BATCH, rays), jnp.float32),
                pltpu.VMEM((4 * BATCH, LANES), jnp.float32),
                pltpu.VMEM((8, 4 * BATCH, rays), jnp.float32),
            ],
            compiler_params=LIMIT,
            name="spread",
        )(*given)

    mine = exchange(None, destination.T, positions)
    pairs, last, labels, coords = pl.pallas_call(
        table_kernel,
        out_shape=(
            jax.ShapeDtypeStruct((TURNS * LANES, STEP * SPAN), jnp.bfloat16),
            jax.ShapeDtypeStruct((LANES, LANES), jnp.bfloat16),
            jax.ShapeDtypeStruct((1, blocks), jnp.int32),
            jax.ShapeDtypeStruct(positions.shape, jnp.float32),
        ),
        in_specs=[VMEM] * 3,
        out_specs=(VMEM,) * 4,
        compiler_params=LIMIT,
        cost_estimate=pl.CostEstimate(flops=10_000_000, bytes_accessed=6_000_000, transcendentals=0),
        name="table",
    )(profile, destination.T, positions)
    mine, pairs, last, labels, coords = lax.optimization_barrier((mine, pairs, last, labels, coords))
    turns = jnp.max(mine[:, 7, 2 * LANES + COUNT]).astype(jnp.int32)
    out, total = deposit(mine, None, pairs, last)

    def more(state):
        turn, _, total = state
        out, total = deposit(
            exchange(jnp.full((1,), turn, jnp.int32), labels, coords), total, pairs, last
        )
        return turn + 1, out, total

    return lax.while_loop(lambda state: state[0] < turns, more, (jnp.int32(1), out, total))[1]


def solution(mesh):
    placed = (P(("maps", "row", "col"), None, None), P(("maps", "row", "col"), None), P())
    return jax.shard_map(
        shards, mesh=mesh, in_specs=placed, out_specs=P(("maps", "row"), "col"), check_vma=False
    )
```

```python
import functools

import jax
import jax.numpy as jnp
from jax import lax
from jax.experimental import pallas as pl
from jax.experimental.pallas import tpu as pltpu
from jax.sharding import PartitionSpec as P

TILE = 128
HALO = 32
MOST = 4
DISC = 2 * HALO + 1
STEP = 16
LONG = TILE + STEP
TURNS = 2 * HALO // STEP
WIDE = TILE + 2 * HALO
LANES = 128
SPAN = 64
BATCH = 8
ROOM = 5
COMMON = 3
COUNT = 16
KINDS = 18
FAR = 1024.0

VMEM = pl.BlockSpec(memory_space=pltpu.VMEM)
SMEM = pl.BlockSpec(memory_space=pltpu.SMEM)
ALONE = pltpu.CompilerParams(vmem_limit_bytes=67_104_000)
LIMIT = pltpu.CompilerParams(vmem_limit_bytes=32 * 1024 * 1024)


def touches(distance, least, most):
    before = (distance == -1.0) & (most > TILE - HALO - 1.0)
    after = (distance == 1.0) & (least < HALO)
    return (distance == 0.0) | before | after


def split(index, size):
    index = index.astype(jnp.float32)
    quotient = jnp.floor((index + 0.5) * (1.0 / size))
    return quotient, index - size * quotient


def pack_kernel(turn_ref, dest_ref, rays_ref, out_ref, labels, parts):
    blocks, _, rays = rays_ref.shape
    tiles = out_ref.shape[0] // 8
    width = parts.shape[0]
    col_count = lax.axis_size("col")
    skip = 0.0 if turn_ref is None else 2.0 * ROOM * turn_ref[0].astype(jnp.float32)
    copy, own = split(lax.broadcasted_iota(jnp.int32, (blocks, width), 1), blocks)
    place = lax.broadcasted_iota(jnp.int32, (blocks, width), 0).astype(jnp.float32)
    there = (own == place) & (copy < 3.0)

    def laid(column):
        return jnp.sum(jnp.where(there, column, 0.0), axis=0, keepdims=True)

    labels[...] = jnp.full(labels.shape, -1.0, jnp.float32)
    for g in range(3):
        labels[0:1, g * blocks : (g + 1) * blocks] = dest_ref[...].astype(jnp.float32)
    label = labels[...]
    label_row = jnp.floor((label + 0.5) * (1.0 / col_count))
    label_col = label - label_row * col_count
    first, second = rays_ref[:, 0, :], rays_ref[:, 1, :]
    least_row, most_row = laid(jnp.min(first, 1, keepdims=True)), laid(jnp.max(first, 1, keepdims=True))
    least_col, most_col = laid(jnp.min(second, 1, keepdims=True)), laid(jnp.max(second, 1, keepdims=True))
    earlier = lax.broadcasted_iota(jnp.int32, (width, width), 0).astype(jnp.float32)
    copy, own = split(lax.broadcasted_iota(jnp.int32, (width, width), 1), blocks)
    earlier = jnp.where((earlier < own) & (copy < 3.0), 1.0, 0.0).astype(jnp.bfloat16)

    def chosen(row, col):
        odd = split(row, 2)[1]
        row = row - odd
        dc = label_col - col
        aside = touches(dc, least_col, most_col) & (label >= 0.0)

        def coded(dr):
            reach = aside & touches(dr, least_row, most_row)
            return reach, jnp.where(reach, 3.0 * dr + dc + 4.0, FAR)

        even, odds = coded(label_row - row), coded(label_row - row - 1.0)
        reach = jnp.where(even[0] | odds[0], 1.0, 0.0)
        rank = jnp.dot(reach.astype(jnp.bfloat16), earlier, preferred_element_type=jnp.float32)
        left = rank - skip - odd
        slot = jnp.floor(left * 0.5)
        mine = (reach > 0.0) & (slot * 2.0 == left) & (slot >= 0.0) & (slot < ROOM)
        return jnp.where(mine, slot, -1.0), even[1], odds[1], (rank + 1.0) * reach

    tile = lax.broadcasted_iota(jnp.int32, (tiles, width), 0)
    slot, even, odds, most = chosen(*split(tile, col_count))
    most = jnp.max(jnp.max(most, axis=1, keepdims=True), axis=0, keepdims=True)
    turns = jnp.floor((most + (2.0 * ROOM - 0.5)) / (2.0 * ROOM))
    lane = lax.broadcasted_iota(jnp.int32, (tiles, width), 1)
    meta = jnp.where(lane == COUNT, turns, FAR)
    for k in range(ROOM):
        here = (slot == k) & (lane < blocks)
        for at, code in ((k, even), (8 + k, odds)):
            found = jnp.sum(jnp.where(here, code - FAR, 0.0), axis=1, keepdims=True) + FAR
            meta = jnp.where(lane == at, found, meta)
    for at, code in ((KINDS, even), (KINDS + 1, odds)):
        rowwise, colwise = split(code, 3)
        kind = jnp.where(rowwise == 1.0, 0.0, 2.0) + jnp.where(colwise == 1.0, 0.0, 1.0)
        bit = 1 << jnp.clip(5.0 * kind + slot, 0.0, 23.0).astype(jnp.int32)
        here = (slot >= 0.0) & (code < FAR) & (lane < blocks)
        word = jnp.sum(jnp.where(here, bit.astype(jnp.float32), 0.0), axis=1, keepdims=True)
        meta = jnp.where(lane == at, word, meta)

    parts[...] = jnp.zeros(parts.shape, jnp.float32)
    parts[:blocks, :rays] = first
    parts[:blocks, rays:] = second[:, :LANES]
    parts[blocks : 2 * blocks, : 2 * LANES] = second[:, LANES:]
    parts[2 * blocks : 3 * blocks, 2 * LANES :] = second[:, LANES:]
    parts[3 * blocks : 3 * blocks + tiles, 2 * LANES : 3 * LANES] = meta[:, :LANES]

    tile, within = split(lax.broadcasted_iota(jnp.int32, (8 * tiles, width), 0), 8)
    lane = lax.broadcasted_iota(jnp.int32, (8 * tiles, width), 1)
    copy = split(lane, blocks)[0]
    slot = chosen(*split(tile, col_count))[0]
    low = 2.0 * (within - ROOM)
    wanted = jnp.where(copy == 0.0, within, jnp.where(copy == 1.0, low, low + 1.0))
    place = ((copy == 0.0) & (within < ROOM)) | ((copy > 0.0) & (copy < 3.0) & (within >= ROOM))
    codes = (lane.astype(jnp.float32) - 3.0 * blocks == tile) & (within == 7.0)
    select = jnp.where((place & (slot == wanted)) | codes, 1.0, 0.0).astype(jnp.bfloat16)
    rest = parts[...]
    total = jnp.zeros(out_ref.shape, jnp.float32)
    for _ in range(3):
        part = rest.astype(jnp.bfloat16)
        rest = rest - part.astype(jnp.float32)
        total = total + jnp.dot(select, part, preferred_element_type=jnp.float32)
    out_ref[...] = total


def table_kernel(profile_ref, dest_ref, rays_ref, pairs_ref, last_ref, dest_copy, rays_copy):
    dest_copy[...] = dest_ref[...]
    rays_copy[...] = rays_ref[...]
    a = lax.broadcasted_iota(jnp.int32, (DISC, DISC), 0) - HALO
    c = lax.broadcasted_iota(jnp.int32, (DISC, DISC), 1) - HALO
    weights = jnp.where(a * a + c * c <= HALO * HALO, profile_ref[...], 0.0)
    kernel = (weights / jnp.sum(weights)).astype(jnp.bfloat16)
    source = lax.broadcasted_iota(jnp.int32, (DISC, LANES), 0)
    target = lax.broadcasted_iota(jnp.int32, (DISC, LANES), 1)
    mirror = jnp.where((source + target) % LANES == 0, 1.0, 0.0).astype(jnp.bfloat16)
    mirrored = jnp.dot(kernel, mirror, preferred_element_type=jnp.float32)
    left = lax.broadcasted_iota(jnp.int32, (LANES, LANES), 1) < SPAN

    def band(row, start):
        wide = jnp.broadcast_to(mirrored[row : row + 1, :], (LANES, LANES))
        return pltpu.roll(wide, start, 1, stride=1, stride_axis=0)

    for u in range(TURNS):
        for s in range(0, STEP, 2):
            row = u * STEP + s
            both = jnp.where(left, band(row, 0), band(row + 1, SPAN))
            pairs_ref[u * LANES : (u + 1) * LANES, s * SPAN : (s + 2) * SPAN] = both.astype(jnp.bfloat16)
    last_ref[...] = jnp.where(left, band(2 * HALO, 0), 0.0).astype(jnp.bfloat16)


def hats(row, cell):
    near, far, here, there = (value.astype(jnp.bfloat16) for value in row)
    zero = jnp.zeros((), jnp.bfloat16)
    return jnp.where(cell == here, near, jnp.where(cell == there, far, zero))


def deposited(both, lists, stage, shifts, facts):
    sources = both.shape[0]
    rays = 3 * LANES
    first_lane = lax.axis_index("row") % 2 * 8
    room = sources * ROOM + 1
    lane = lax.broadcasted_iota(jnp.int32, (sources, LANES), 1)
    parity = lax.axis_index("row") % 2
    words = jnp.where(lane == KINDS + parity, both[:, 7, 2 * LANES :][:, :LANES], 0.0)
    words = jnp.sum(words, axis=1, keepdims=True).astype(jnp.int32)
    words = [words[at, 0] for at in range(sources)]

    def listed(counts, kinds, slots):
        counts = list(counts)
        for kind in kinds:
            for at in range(sources):
                for k in slots:
                    lists[counts[kind]] = at * 8 + k
                    bit = (words[at] >> (ROOM * kind + k)) & 1
                    counts[kind] = counts[kind] + bit
        return tuple(counts)

    counts = tuple(jnp.int32(kind * room) for kind in range(4))
    used = functools.reduce(jnp.bitwise_or, words)
    for slot in range(COMMON, ROOM):
        counts = lax.cond(
            used & sum(1 << (ROOM * kind + slot) for kind in range(4)) != 0,
            lambda held, slot=slot: listed(held, range(4), (slot,)),
            lambda held: held,
            counts,
        )

    def doubled(cell):
        return (2 * cell).astype(jnp.float32).astype(jnp.bfloat16)

    own = doubled(lax.broadcasted_iota(jnp.int32, (TILE, rays), 0))
    edge = lax.broadcasted_iota(jnp.int32, (2 * HALO, rays), 0)
    edge = doubled(jnp.where(edge < HALO, edge - HALO, edge + (TILE - HALO)))
    lane = lax.broadcasted_iota(jnp.int32, (1, LANES), 1) - first_lane

    def load(kind, step, batch, start):
        for k in range(batch):
            at = start + k
            entry = lists[jnp.minimum(kind * room + k + step * batch, counts[kind])]
            source, slot = entry >> 3, entry & 7
            head = both[source, pl.ds(slot, 1), :]
            tail = both[source, pl.ds(ROOM + (slot >> 1), 1), :]
            meta = both[source, 7:8, :][:, 2 * LANES : 3 * LANES]
            stage[0, at : at + 1, :] = head[:, :rays]
            stage[1, at : at + 1, :LANES] = head[:, rays:]
            stage[1, at : at + 1, LANES:] = jnp.where(
                (slot & 1) == 1, tail[:, 2 * LANES :], tail[:, : 2 * LANES]
            )
            shifts[at : at + 1, :] = jnp.where(lane == slot, meta, 0.0)

    def prepare(begin, end):
        code = jnp.sum(shifts[begin:end, :], axis=1, keepdims=True)
        rowwise = jnp.floor((code + 0.5) / 3.0)
        offsets = (rowwise - 1.0) * (2.0 * TILE), (code - 3.0 * rowwise - 1.0) * (2.0 * TILE)
        for axis in range(2):
            coords = stage[axis, begin:end, :]
            low = jnp.floor(coords)
            facts[4 * axis, begin:end, :] = 1.0 - (coords - low)
            facts[4 * axis + 1, begin:end, :] = 1.0 - ((low + 1.0) - coords)
            here = 2.0 * low + offsets[axis]
            facts[4 * axis + 2, begin:end, :] = here
            facts[4 * axis + 3, begin:end, :] = here + 2.0

    def product(kind, batch, start):
        down, across = (own, edge)[kind // 2], (own, edge)[kind % 2]
        firsts, seconds = [], []
        for at in range(start, start + batch):
            row = [facts[j, at : at + 1, :] for j in range(8)]
            firsts.append(hats(row[:4], down))
            seconds.append(hats(row[4:], across))
        return lax.dot_general(
            jnp.concatenate(firsts, axis=1),
            jnp.concatenate(seconds, axis=1),
            (((1,), (1,)), ((), ())),
            preferred_element_type=jnp.float32,
        )

    def ready(step, *given):
        for kind, batch, start in given:
            load(kind, step, batch, start)
        prepare(given[0][2], given[-1][2] + BATCH)

    def together(one, two):
        def step_one(step, sums, given=one):
            sums = sums + product(*given)
            ready(step + 1, given)
            return sums

        def step_both(step, sums):
            sums = sums[0] + product(*one), sums[1] + product(*two)
            ready(step + 1, one, two)
            return sums

        zeros = [
            jnp.zeros(((TILE, 2 * HALO)[kind // 2], (TILE, 2 * HALO)[kind % 2]), jnp.float32)
            for kind in (one[0], two[0])
        ]
        steps = [(counts[kind] - kind * room + batch - 1) // batch for kind, batch, _ in (one, two)]
        shared = jnp.minimum(steps[0], steps[1])
        sums = lax.fori_loop(0, shared, step_both, tuple(zeros))
        return [
            lax.fori_loop(shared, steps[j], functools.partial(step_one, given=(one, two)[j]), sums[j])
            for j in range(2)
        ]

    pairs = (
        ((0, BATCH, 0), (3, BATCH // 2, BATCH)),
        ((1, 6, 2 * BATCH), (2, 6, 3 * BATCH)),
    )
    for pair in pairs:
        kinds = [kind for kind, _, _ in pair]
        counts = listed(counts, kinds, range(COMMON))
        for kind in kinds:
            lists[counts[kind]] = ROOM
        ready(0, *pair)
    inside, corners = together(*pairs[0])
    beside, above = together(*pairs[1])

    def wide(middle, ends):
        return jnp.concatenate([ends[:, :HALO], middle, ends[:, HALO:]], axis=1)

    middle, ends = wide(inside, beside), wide(above, corners)
    return jnp.concatenate([ends[:HALO], middle, ends[HALO:]], axis=0)


def spread_kernel(scale, mine_ref, other_ref, before_ref, pairs_ref, last_ref, out_ref, total_ref,
                  left, both, *scratch):
    sources = mine_ref.shape[0]
    both[:sources] = mine_ref[...]
    both[sources:] = other_ref[...]
    cells = deposited(both, *scratch)
    if before_ref is not None:
        cells = cells + before_ref[...]
    total_ref[...] = cells
    blocks = [cells[:, at : at + LANES].astype(jnp.bfloat16) for at in (0, SPAN)]
    for h in range(2):
        for u in range(TURNS):
            left[h * LONG : (h + 1) * LONG, u * LANES : (u + 1) * LANES] = blocks[h][
                u * STEP : u * STEP + LONG, :
            ]
    lowest = jnp.concatenate([block[2 * HALO :, :] for block in blocks], axis=0)
    ends = jnp.dot(lowest, last_ref[...], preferred_element_type=jnp.float32)
    evens = [ends[:TILE], ends[TILE:]]
    odds = [jnp.zeros((TILE, LANES), jnp.float32)] * 2
    for p in range(0, STEP * SPAN, 2 * LANES):
        both = jnp.dot(left[...], pairs_ref[:, p : p + 2 * LANES], preferred_element_type=jnp.float32)
        for h in range(2):
            for lanes in (0, LANES):
                s = (p + lanes) // SPAN
                part = both[h * LONG : (h + 1) * LONG, lanes : lanes + LANES]
                evens[h] = evens[h] + part[s : s + TILE]
                odds[h] = odds[h] + part[s + 1 : s + 1 + TILE]
    low = evens[0] + pltpu.roll(odds[0], SPAN, 1)
    high = pltpu.roll(evens[1], SPAN, 1) + odds[1]
    lane = lax.broadcasted_iota(jnp.int32, (TILE, LANES), 1)
    out_ref[...] = jnp.where(lane < SPAN, low, high) / scale


def shards(positions, destination, profile):
    blocks, _, rays = positions.shape
    row_count, col_count = lax.axis_size("row"), lax.axis_size("col")
    tiles = row_count * col_count
    width = -(-(3 * blocks + tiles) // LANES) * LANES

    def exchange(turn, labels, coords):
        kernel, given = pack_kernel, (turn, labels, coords)
        if turn is None:
            kernel, given = functools.partial(pack_kernel, None), (labels, coords)
        outgoing = pl.pallas_call(
            kernel,
            out_shape=jax.ShapeDtypeStruct((8 * tiles, rays + LANES), jnp.float32),
            in_specs=[SMEM, VMEM, VMEM][-len(given) :],
            out_specs=VMEM,
            scratch_shapes=[
                pltpu.VMEM((1, width), jnp.float32),
                pltpu.VMEM((width, rays + LANES), jnp.float32),
            ],
            compiler_params=ALONE if turn is None else LIMIT,
            name="pack",
        )(*given)
        return lax.all_to_all(
            outgoing.reshape(tiles, 8, rays + LANES), ("row", "col"), split_axis=0, concat_axis=0, tiled=True
        )

    def deposit(mine, before, pairs, last):
        other = lax.ppermute(mine, "row", [(i, i ^ 1) for i in range(row_count)])
        scale = blocks * rays / (TILE * TILE)
        kernel, given = functools.partial(spread_kernel, scale), (mine, other, before, pairs, last)
        if before is None:
            kernel = lambda mine, other, *refs: spread_kernel(scale, mine, other, None, *refs)
            given = (mine, other, pairs, last)
        return pl.pallas_call(
            kernel,
            out_shape=(
                jax.ShapeDtypeStruct((TILE, TILE), jnp.float32),
                jax.ShapeDtypeStruct((WIDE, WIDE), jnp.float32),
            ),
            in_specs=[VMEM] * len(given),
            out_specs=(VMEM, VMEM),
            scratch_shapes=[
                pltpu.VMEM((2 * LONG, TURNS * LANES), jnp.bfloat16),
                pltpu.VMEM((2 * tiles, 8, rays + LANES), jnp.float32),
                pltpu.SMEM((4 * (2 * tiles * ROOM + 1),), jnp.int32),
                pltpu.VMEM((2, 4 * BATCH, rays), jnp.float32),
                pltpu.VMEM((4 * BATCH, LANES), jnp.float32),
                pltpu.VMEM((8, 4 * BATCH, rays), jnp.float32),
            ],
            compiler_params=LIMIT,
            name="spread",
        )(*given)

    mine = exchange(None, destination.T, positions)
    pairs, last, labels, coords = pl.pallas_call(
        table_kernel,
        out_shape=(
            jax.ShapeDtypeStruct((TURNS * LANES, STEP * SPAN), jnp.bfloat16),
            jax.ShapeDtypeStruct((LANES, LANES), jnp.bfloat16),
            jax.ShapeDtypeStruct((1, blocks), jnp.int32),
            jax.ShapeDtypeStruct(positions.shape, jnp.float32),
        ),
        in_specs=[VMEM] * 3,
        out_specs=(VMEM,) * 4,
        compiler_params=LIMIT,
        cost_estimate=pl.CostEstimate(flops=10_000_000, bytes_accessed=6_000_000, transcendentals=0),
        name="table",
    )(profile, destination.T, positions)
    mine, pairs, last, labels, coords = lax.optimization_barrier((mine, pairs, last, labels, coords))
    turns = jnp.max(mine[:, 7, 2 * LANES + COUNT]).astype(jnp.int32)
    out, total = deposit(mine, None, pairs, last)

    def more(state):
        turn, _, total = state
        out, total = deposit(
            exchange(jnp.full((1,), turn, jnp.int32), labels, coords), total, pairs, last
        )
        return turn + 1, out, total

    return lax.while_loop(lambda state: state[0] < turns, more, (jnp.int32(1), out, total))[1]


def solution(mesh):
    placed = (P(("maps", "row", "col"), None, None), P(("maps", "row", "col"), None), P())
    return jax.shard_map(
        shards, mesh=mesh, in_specs=placed, out_specs=P(("maps", "row"), "col"), check_vma=False
    )
```

```python
import functools

import jax
import jax.numpy as jnp
from jax import lax
from jax.experimental import pallas as pl
from jax.experimental.pallas import tpu as pltpu
from jax.sharding import PartitionSpec as P

TILE = 128
HALO = 32
MOST = 4
DISC = 2 * HALO + 1
STEP = 16
LONG = TILE + STEP
TURNS = 2 * HALO // STEP
WIDE = TILE + 2 * HALO
LANES = 128
SPAN = 64
BATCH = 8
ROOM = 5
COMMON = 3
COUNT = 16
KINDS = 18
FAR = 1024.0

VMEM = pl.BlockSpec(memory_space=pltpu.VMEM)
SMEM = pl.BlockSpec(memory_space=pltpu.SMEM)
ALONE = pltpu.CompilerParams(vmem_limit_bytes=67_104_000)
LIMIT = pltpu.CompilerParams(vmem_limit_bytes=32 * 1024 * 1024)


def touches(distance, least, most):
    before = (distance == -1.0) & (most > TILE - HALO - 1.0)
    after = (distance == 1.0) & (least < HALO)
    return (distance == 0.0) | before | after


def split(index, size):
    index = index.astype(jnp.float32)
    quotient = jnp.floor((index + 0.5) * (1.0 / size))
    return quotient, index - size * quotient


def pack_kernel(turn_ref, dest_ref, rays_ref, out_ref, labels, parts):
    blocks, _, rays = rays_ref.shape
    tiles = out_ref.shape[0] // 8
    width = parts.shape[0]
    col_count = lax.axis_size("col")
    skip = 0.0 if turn_ref is None else 2.0 * ROOM * turn_ref[0].astype(jnp.float32)
    copy, own = split(lax.broadcasted_iota(jnp.int32, (blocks, width), 1), blocks)
    place = lax.broadcasted_iota(jnp.int32, (blocks, width), 0).astype(jnp.float32)
    there = (own == place) & (copy < 3.0)

    def laid(column):
        return jnp.sum(jnp.where(there, column, 0.0), axis=0, keepdims=True)

    labels[...] = jnp.full(labels.shape, -1.0, jnp.float32)
    for g in range(3):
        labels[0:1, g * blocks : (g + 1) * blocks] = dest_ref[...].astype(jnp.float32)
    label = labels[...]
    label_row = jnp.floor((label + 0.5) * (1.0 / col_count))
    label_col = label - label_row * col_count
    first, second = rays_ref[:, 0, :], rays_ref[:, 1, :]
    least_row, most_row = laid(jnp.min(first, 1, keepdims=True)), laid(jnp.max(first, 1, keepdims=True))
    least_col, most_col = laid(jnp.min(second, 1, keepdims=True)), laid(jnp.max(second, 1, keepdims=True))
    earlier = lax.broadcasted_iota(jnp.int32, (width, width), 0).astype(jnp.float32)
    copy, own = split(lax.broadcasted_iota(jnp.int32, (width, width), 1), blocks)
    earlier = jnp.where((earlier < own) & (copy < 3.0), 1.0, 0.0).astype(jnp.bfloat16)

    def chosen(row, col):
        odd = split(row, 2)[1]
        row = row - odd
        dc = label_col - col
        aside = touches(dc, least_col, most_col) & (label >= 0.0)

        def coded(dr):
            reach = aside & touches(dr, least_row, most_row)
            return reach, jnp.where(reach, 3.0 * dr + dc + 4.0, FAR)

        even, odds = coded(label_row - row), coded(label_row - row - 1.0)
        reach = jnp.where(even[0] | odds[0], 1.0, 0.0)
        rank = jnp.dot(reach.astype(jnp.bfloat16), earlier, preferred_element_type=jnp.float32)
        left = rank - skip - odd
        slot = jnp.floor(left * 0.5)
        mine = (reach > 0.0) & (slot * 2.0 == left) & (slot >= 0.0) & (slot < ROOM)
        return jnp.where(mine, slot, -1.0), even[1], odds[1], (rank + 1.0) * reach

    tile = lax.broadcasted_iota(jnp.int32, (tiles, width), 0)
    slot, even, odds, most = chosen(*split(tile, col_count))
    most = jnp.max(jnp.max(most, axis=1, keepdims=True), axis=0, keepdims=True)
    turns = jnp.floor((most + (2.0 * ROOM - 0.5)) / (2.0 * ROOM))
    lane = lax.broadcasted_iota(jnp.int32, (tiles, width), 1)
    meta = jnp.where(lane == COUNT, turns, FAR)
    for k in range(ROOM):
        here = (slot == k) & (lane < blocks)
        for at, code in ((k, even), (8 + k, odds)):
            found = jnp.sum(jnp.where(here, code - FAR, 0.0), axis=1, keepdims=True) + FAR
            meta = jnp.where(lane == at, found, meta)
    for at, code in ((KINDS, even), (KINDS + 1, odds)):
        rowwise, colwise = split(code, 3)
        kind = jnp.where(rowwise == 1.0, 0.0, 2.0) + jnp.where(colwise == 1.0, 0.0, 1.0)
        bit = 1 << jnp.clip(5.0 * kind + slot, 0.0, 23.0).astype(jnp.int32)
        here = (slot >= 0.0) & (code < FAR) & (lane < blocks)
        word = jnp.sum(jnp.where(here, bit.astype(jnp.float32), 0.0), axis=1, keepdims=True)
        meta = jnp.where(lane == at, word, meta)

    parts[...] = jnp.zeros(parts.shape, jnp.float32)
    parts[:blocks, :rays] = first
    parts[:blocks, rays:] = second[:, :LANES]
    parts[blocks : 2 * blocks, : 2 * LANES] = second[:, LANES:]
    parts[2 * blocks : 3 * blocks, 2 * LANES :] = second[:, LANES:]
    parts[3 * blocks : 3 * blocks + tiles, 2 * LANES : 3 * LANES] = meta[:, :LANES]

    tile, within = split(lax.broadcasted_iota(jnp.int32, (8 * tiles, width), 0), 8)
    lane = lax.broadcasted_iota(jnp.int32, (8 * tiles, width), 1)
    copy = split(lane, blocks)[0]
    slot = chosen(*split(tile, col_count))[0]
    low = 2.0 * (within - ROOM)
    wanted = jnp.where(copy == 0.0, within, jnp.where(copy == 1.0, low, low + 1.0))
    place = ((copy == 0.0) & (within < ROOM)) | ((copy > 0.0) & (copy < 3.0) & (within >= ROOM))
    codes = (lane.astype(jnp.float32) - 3.0 * blocks == tile) & (within == 7.0)
    select = jnp.where((place & (slot == wanted)) | codes, 1.0, 0.0).astype(jnp.bfloat16)
    rest = parts[...]
    total = jnp.zeros(out_ref.shape, jnp.float32)
    for _ in range(3):
        part = rest.astype(jnp.bfloat16)
        rest = rest - part.astype(jnp.float32)
        total = total + jnp.dot(select, part, preferred_element_type=jnp.float32)
    out_ref[...] = total


def table_kernel(profile_ref, dest_ref, rays_ref, pairs_ref, last_ref, dest_copy, rays_copy):
    dest_copy[...] = dest_ref[...]
    rays_copy[...] = rays_ref[...]
    a = lax.broadcasted_iota(jnp.int32, (DISC, DISC), 0) - HALO
    c = lax.broadcasted_iota(jnp.int32, (DISC, DISC), 1) - HALO
    weights = jnp.where(a * a + c * c <= HALO * HALO, profile_ref[...], 0.0)
    kernel = (weights / jnp.sum(weights)).astype(jnp.bfloat16)
    source = lax.broadcasted_iota(jnp.int32, (DISC, LANES), 0)
    target = lax.broadcasted_iota(jnp.int32, (DISC, LANES), 1)
    mirror = jnp.where((source + target) % LANES == 0, 1.0, 0.0).astype(jnp.bfloat16)
    mirrored = jnp.dot(kernel, mirror, preferred_element_type=jnp.float32)
    left = lax.broadcasted_iota(jnp.int32, (LANES, LANES), 1) < SPAN

    def band(row, start):
        wide = jnp.broadcast_to(mirrored[row : row + 1, :], (LANES, LANES))
        return pltpu.roll(wide, start, 1, stride=1, stride_axis=0)

    for u in range(TURNS):
        for s in range(0, STEP, 2):
            row = u * STEP + s
            both = jnp.where(left, band(row, 0), band(row + 1, SPAN))
            pairs_ref[u * LANES : (u + 1) * LANES, s * SPAN : (s + 2) * SPAN] = both.astype(jnp.bfloat16)
    last_ref[...] = jnp.where(left, band(2 * HALO, 0), 0.0).astype(jnp.bfloat16)


def hats(row, cell):
    near, far, here, there = (value.astype(jnp.bfloat16) for value in row)
    zero = jnp.zeros((), jnp.bfloat16)
    return jnp.where(cell == here, near, jnp.where(cell == there, far, zero))


def deposited(both, lists, stage, shifts, facts):
    sources = both.shape[0]
    rays = 3 * LANES
    first_lane = lax.axis_index("row") % 2 * 8
    room = sources * ROOM + 1
    lane = lax.broadcasted_iota(jnp.int32, (sources, LANES), 1)
    parity = lax.axis_index("row") % 2
    words = jnp.where(lane == KINDS + parity, both[:, 7, 2 * LANES :][:, :LANES], 0.0)
    words = jnp.sum(words, axis=1, keepdims=True).astype(jnp.int32)
    words = [words[at, 0] for at in range(sources)]

    def listed(counts, kinds, slots):
        counts = list(counts)
        for kind in kinds:
            for at in range(sources):
                for k in slots:
                    lists[counts[kind]] = at * 8 + k
                    bit = (words[at] >> (ROOM * kind + k)) & 1
                    counts[kind] = counts[kind] + bit
        return tuple(counts)

    counts = tuple(jnp.int32(kind * room) for kind in range(4))
    used = functools.reduce(jnp.bitwise_or, words)
    for slot in range(COMMON, ROOM):
        counts = lax.cond(
            used & sum(1 << (ROOM * kind + slot) for kind in range(4)) != 0,
            lambda held, slot=slot: listed(held, range(4), (slot,)),
            lambda held: held,
            counts,
        )

    def doubled(cell):
        return (2 * cell).astype(jnp.float32).astype(jnp.bfloat16)

    own = doubled(lax.broadcasted_iota(jnp.int32, (TILE, rays), 0))
    edge = lax.broadcasted_iota(jnp.int32, (2 * HALO, rays), 0)
    edge = doubled(jnp.where(edge < HALO, edge - HALO, edge + (TILE - HALO)))
    lane = lax.broadcasted_iota(jnp.int32, (1, LANES), 1) - first_lane

    def load(kind, step, batch, start):
        for k in range(batch):
            at = start + k
            entry = lists[jnp.minimum(kind * room + k + step * batch, counts[kind])]
            source, slot = entry >> 3, entry & 7
            head = both[source, pl.ds(slot, 1), :]
            tail = both[source, pl.ds(ROOM + (slot >> 1), 1), :]
            meta = both[source, 7:8, :][:, 2 * LANES : 3 * LANES]
            stage[0, at : at + 1, :] = head[:, :rays]
            stage[1, at : at + 1, :LANES] = head[:, rays:]
            stage[1, at : at + 1, LANES:] = jnp.where(
                (slot & 1) == 1, tail[:, 2 * LANES :], tail[:, : 2 * LANES]
            )
            shifts[at : at + 1, :] = jnp.where(lane == slot, meta, 0.0)

    def prepare(begin, end):
        code = jnp.sum(shifts[begin:end, :], axis=1, keepdims=True)
        rowwise = jnp.floor((code + 0.5) / 3.0)
        offsets = (rowwise - 1.0) * (2.0 * TILE), (code - 3.0 * rowwise - 1.0) * (2.0 * TILE)
        for axis in range(2):
            coords = stage[axis, begin:end, :]
            low = jnp.floor(coords)
            facts[4 * axis, begin:end, :] = 1.0 - (coords - low)
            facts[4 * axis + 1, begin:end, :] = 1.0 - ((low + 1.0) - coords)
            here = 2.0 * low + offsets[axis]
            facts[4 * axis + 2, begin:end, :] = here
            facts[4 * axis + 3, begin:end, :] = here + 2.0

    def product(kind, batch, start):
        down, across = (own, edge)[kind // 2], (own, edge)[kind % 2]
        firsts, seconds = [], []
        for at in range(start, start + batch):
            row = [facts[j, at : at + 1, :] for j in range(8)]
            firsts.append(hats(row[:4], down))
            seconds.append(hats(row[4:], across))
        return lax.dot_general(
            jnp.concatenate(firsts, axis=1),
            jnp.concatenate(seconds, axis=1),
            (((1,), (1,)), ((), ())),
            preferred_element_type=jnp.float32,
        )

    def ready(step, *given):
        for kind, batch, start in given:
            load(kind, step, batch, start)
        prepare(given[0][2], given[-1][2] + BATCH)

    def together(one, two):
        def step_one(step, sums, given=one):
            sums = sums + product(*given)
            ready(step + 1, given)
            return sums

        def step_both(step, sums):
            sums = sums[0] + product(*one), sums[1] + product(*two)
            ready(step + 1, one, two)
            return sums

        zeros = [
            jnp.zeros(((TILE, 2 * HALO)[kind // 2], (TILE, 2 * HALO)[kind % 2]), jnp.float32)
            for kind in (one[0], two[0])
        ]
        steps = [(counts[kind] - kind * room + batch - 1) // batch for kind, batch, _ in (one, two)]
        shared = jnp.minimum(steps[0], steps[1])
        sums = lax.fori_loop(0, shared, step_both, tuple(zeros))
        return [
            lax.fori_loop(shared, steps[j], functools.partial(step_one, given=(one, two)[j]), sums[j])
            for j in range(2)
        ]

    pairs = (
        ((0, BATCH, 0), (3, 6, BATCH)),
        ((1, 6, 2 * BATCH), (2, 6, 3 * BATCH)),
    )
    for pair in pairs:
        kinds = [kind for kind, _, _ in pair]
        counts = listed(counts, kinds, range(COMMON))
        for kind in kinds:
            lists[counts[kind]] = ROOM
        ready(0, *pair)
    inside, corners = together(*pairs[0])
    beside, above = together(*pairs[1])

    def wide(middle, ends):
        return jnp.concatenate([ends[:, :HALO], middle, ends[:, HALO:]], axis=1)

    middle, ends = wide(inside, beside), wide(above, corners)
    return jnp.concatenate([ends[:HALO], middle, ends[HALO:]], axis=0)


def spread_kernel(scale, mine_ref, other_ref, before_ref, pairs_ref, last_ref, out_ref, total_ref,
                  left, both, *scratch):
    sources = mine_ref.shape[0]
    both[:sources] = mine_ref[...]
    both[sources:] = other_ref[...]
    cells = deposited(both, *scratch)
    if before_ref is not None:
        cells = cells + before_ref[...]
    total_ref[...] = cells
    blocks = [cells[:, at : at + LANES].astype(jnp.bfloat16) for at in (0, SPAN)]
    for h in range(2):
        for u in range(TURNS):
            left[h * LONG : (h + 1) * LONG, u * LANES : (u + 1) * LANES] = blocks[h][
                u * STEP : u * STEP + LONG, :
            ]
    lowest = jnp.concatenate([block[2 * HALO :, :] for block in blocks], axis=0)
    ends = jnp.dot(lowest, last_ref[...], preferred_element_type=jnp.float32)
    evens = [ends[:TILE], ends[TILE:]]
    odds = [jnp.zeros((TILE, LANES), jnp.float32)] * 2
    for p in range(0, STEP * SPAN, 2 * LANES):
        both = jnp.dot(left[...], pairs_ref[:, p : p + 2 * LANES], preferred_element_type=jnp.float32)
        for h in range(2):
            for lanes in (0, LANES):
                s = (p + lanes) // SPAN
                part = both[h * LONG : (h + 1) * LONG, lanes : lanes + LANES]
                evens[h] = evens[h] + part[s : s + TILE]
                odds[h] = odds[h] + part[s + 1 : s + 1 + TILE]
    low = evens[0] + pltpu.roll(odds[0], SPAN, 1)
    high = pltpu.roll(evens[1], SPAN, 1) + odds[1]
    lane = lax.broadcasted_iota(jnp.int32, (TILE, LANES), 1)
    out_ref[...] = jnp.where(lane < SPAN, low, high) / scale


def shards(positions, destination, profile):
    blocks, _, rays = positions.shape
    row_count, col_count = lax.axis_size("row"), lax.axis_size("col")
    tiles = row_count * col_count
    width = -(-(3 * blocks + tiles) // LANES) * LANES

    def exchange(turn, labels, coords):
        kernel, given = pack_kernel, (turn, labels, coords)
        if turn is None:
            kernel, given = functools.partial(pack_kernel, None), (labels, coords)
        outgoing = pl.pallas_call(
            kernel,
            out_shape=jax.ShapeDtypeStruct((8 * tiles, rays + LANES), jnp.float32),
            in_specs=[SMEM, VMEM, VMEM][-len(given) :],
            out_specs=VMEM,
            scratch_shapes=[
                pltpu.VMEM((1, width), jnp.float32),
                pltpu.VMEM((width, rays + LANES), jnp.float32),
            ],
            compiler_params=ALONE if turn is None else LIMIT,
            name="pack",
        )(*given)
        return lax.all_to_all(
            outgoing.reshape(tiles, 8, rays + LANES), ("row", "col"), split_axis=0, concat_axis=0, tiled=True
        )

    def deposit(mine, before, pairs, last):
        other = lax.ppermute(mine, "row", [(i, i ^ 1) for i in range(row_count)])
        scale = blocks * rays / (TILE * TILE)
        kernel, given = functools.partial(spread_kernel, scale), (mine, other, before, pairs, last)
        if before is None:
            kernel = lambda mine, other, *refs: spread_kernel(scale, mine, other, None, *refs)
            given = (mine, other, pairs, last)
        return pl.pallas_call(
            kernel,
            out_shape=(
                jax.ShapeDtypeStruct((TILE, TILE), jnp.float32),
                jax.ShapeDtypeStruct((WIDE, WIDE), jnp.float32),
            ),
            in_specs=[VMEM] * len(given),
            out_specs=(VMEM, VMEM),
            scratch_shapes=[
                pltpu.VMEM((2 * LONG, TURNS * LANES), jnp.bfloat16),
                pltpu.VMEM((2 * tiles, 8, rays + LANES), jnp.float32),
                pltpu.SMEM((4 * (2 * tiles * ROOM + 1),), jnp.int32),
                pltpu.VMEM((2, 4 * BATCH, rays), jnp.float32),
                pltpu.VMEM((4 * BATCH, LANES), jnp.float32),
                pltpu.VMEM((8, 4 * BATCH, rays), jnp.float32),
            ],
            compiler_params=LIMIT,
            name="spread",
        )(*given)

    mine = exchange(None, destination.T, positions)
    pairs, last, labels, coords = pl.pallas_call(
        table_kernel,
        out_shape=(
            jax.ShapeDtypeStruct((TURNS * LANES, STEP * SPAN), jnp.bfloat16),
            jax.ShapeDtypeStruct((LANES, LANES), jnp.bfloat16),
            jax.ShapeDtypeStruct((1, blocks), jnp.int32),
            jax.ShapeDtypeStruct(positions.shape, jnp.float32),
        ),
        in_specs=[VMEM] * 3,
        out_specs=(VMEM,) * 4,
        compiler_params=LIMIT,
        cost_estimate=pl.CostEstimate(flops=10_000_000, bytes_accessed=6_000_000, transcendentals=0),
        name="table",
    )(profile, destination.T, positions)
    mine, pairs, last, labels, coords = lax.optimization_barrier((mine, pairs, last, labels, coords))
    turns = jnp.max(mine[:, 7, 2 * LANES + COUNT]).astype(jnp.int32)
    out, total = deposit(mine, None, pairs, last)

    def more(state):
        turn, _, total = state
        out, total = deposit(
            exchange(jnp.full((1,), turn, jnp.int32), labels, coords), total, pairs, last
        )
        return turn + 1, out, total

    return lax.while_loop(lambda state: state[0] < turns, more, (jnp.int32(1), out, total))[1]


def solution(mesh):
    placed = (P(("maps", "row", "col"), None, None), P(("maps", "row", "col"), None), P())
    return jax.shard_map(
        shards, mesh=mesh, in_specs=placed, out_specs=P(("maps", "row"), "col"), check_vma=False
    )
```

```python
import functools

import jax
import jax.numpy as jnp
from jax import lax
from jax.experimental import pallas as pl
from jax.experimental.pallas import tpu as pltpu
from jax.sharding import PartitionSpec as P

TILE = 128
HALO = 32
MOST = 4
DISC = 2 * HALO + 1
STEP = 16
LONG = TILE + STEP
TURNS = 2 * HALO // STEP
WIDE = TILE + 2 * HALO
LANES = 128
SPAN = 64
BATCH = 8
ROOM = 5
COMMON = 3
COUNT = 16
KINDS = 18
FAR = 1024.0

VMEM = pl.BlockSpec(memory_space=pltpu.VMEM)
SMEM = pl.BlockSpec(memory_space=pltpu.SMEM)
ALONE = pltpu.CompilerParams(vmem_limit_bytes=67_104_000)
LIMIT = pltpu.CompilerParams(vmem_limit_bytes=32 * 1024 * 1024)


def touches(distance, least, most):
    before = (distance == -1.0) & (most > TILE - HALO - 1.0)
    after = (distance == 1.0) & (least < HALO)
    return (distance == 0.0) | before | after


def split(index, size):
    index = index.astype(jnp.float32)
    quotient = jnp.floor((index + 0.5) * (1.0 / size))
    return quotient, index - size * quotient


def pack_kernel(turn_ref, dest_ref, rays_ref, out_ref, labels, parts):
    blocks, _, rays = rays_ref.shape
    tiles = out_ref.shape[0] // 8
    width = parts.shape[0]
    col_count = lax.axis_size("col")
    skip = 0.0 if turn_ref is None else 2.0 * ROOM * turn_ref[0].astype(jnp.float32)
    copy, own = split(lax.broadcasted_iota(jnp.int32, (blocks, width), 1), blocks)
    place = lax.broadcasted_iota(jnp.int32, (blocks, width), 0).astype(jnp.float32)
    there = (own == place) & (copy < 3.0)

    def laid(column):
        return jnp.sum(jnp.where(there, column, 0.0), axis=0, keepdims=True)

    labels[...] = jnp.full(labels.shape, -1.0, jnp.float32)
    for g in range(3):
        labels[0:1, g * blocks : (g + 1) * blocks] = dest_ref[...].astype(jnp.float32)
    label = labels[...]
    label_row = jnp.floor((label + 0.5) * (1.0 / col_count))
    label_col = label - label_row * col_count
    first, second = rays_ref[:, 0, :], rays_ref[:, 1, :]
    least_row, most_row = laid(jnp.min(first, 1, keepdims=True)), laid(jnp.max(first, 1, keepdims=True))
    least_col, most_col = laid(jnp.min(second, 1, keepdims=True)), laid(jnp.max(second, 1, keepdims=True))
    earlier = lax.broadcasted_iota(jnp.int32, (width, width), 0).astype(jnp.float32)
    copy, own = split(lax.broadcasted_iota(jnp.int32, (width, width), 1), blocks)
    earlier = jnp.where((earlier < own) & (copy < 3.0), 1.0, 0.0).astype(jnp.bfloat16)

    def chosen(row, col):
        odd = split(row, 2)[1]
        row = row - odd
        dc = label_col - col
        aside = touches(dc, least_col, most_col) & (label >= 0.0)

        def coded(dr):
            reach = aside & touches(dr, least_row, most_row)
            return reach, jnp.where(reach, 3.0 * dr + dc + 4.0, FAR)

        even, odds = coded(label_row - row), coded(label_row - row - 1.0)
        reach = jnp.where(even[0] | odds[0], 1.0, 0.0)
        rank = jnp.dot(reach.astype(jnp.bfloat16), earlier, preferred_element_type=jnp.float32)
        left = rank - skip - odd
        slot = jnp.floor(left * 0.5)
        mine = (reach > 0.0) & (slot * 2.0 == left) & (slot >= 0.0) & (slot < ROOM)
        return jnp.where(mine, slot, -1.0), even[1], odds[1], (rank + 1.0) * reach

    tile = lax.broadcasted_iota(jnp.int32, (tiles, width), 0)
    slot, even, odds, most = chosen(*split(tile, col_count))
    most = jnp.max(jnp.max(most, axis=1, keepdims=True), axis=0, keepdims=True)
    turns = jnp.floor((most + (2.0 * ROOM - 0.5)) / (2.0 * ROOM))
    lane = lax.broadcasted_iota(jnp.int32, (tiles, width), 1)
    meta = jnp.where(lane == COUNT, turns, FAR)
    for k in range(ROOM):
        here = (slot == k) & (lane < blocks)
        for at, code in ((k, even), (8 + k, odds)):
            found = jnp.sum(jnp.where(here, code - FAR, 0.0), axis=1, keepdims=True) + FAR
            meta = jnp.where(lane == at, found, meta)
    for at, code in ((KINDS, even), (KINDS + 1, odds)):
        rowwise, colwise = split(code, 3)
        kind = jnp.where(rowwise == 1.0, 0.0, 2.0) + jnp.where(colwise == 1.0, 0.0, 1.0)
        bit = 1 << jnp.clip(5.0 * kind + slot, 0.0, 23.0).astype(jnp.int32)
        here = (slot >= 0.0) & (code < FAR) & (lane < blocks)
        word = jnp.sum(jnp.where(here, bit.astype(jnp.float32), 0.0), axis=1, keepdims=True)
        meta = jnp.where(lane == at, word, meta)

    parts[...] = jnp.zeros(parts.shape, jnp.float32)
    parts[:blocks, :rays] = first
    parts[:blocks, rays:] = second[:, :LANES]
    parts[blocks : 2 * blocks, : 2 * LANES] = second[:, LANES:]
    parts[2 * blocks : 3 * blocks, 2 * LANES :] = second[:, LANES:]
    parts[3 * blocks : 3 * blocks + tiles, 2 * LANES : 3 * LANES] = meta[:, :LANES]

    tile, within = split(lax.broadcasted_iota(jnp.int32, (8 * tiles, width), 0), 8)
    lane = lax.broadcasted_iota(jnp.int32, (8 * tiles, width), 1)
    copy = split(lane, blocks)[0]
    slot = chosen(*split(tile, col_count))[0]
    low = 2.0 * (within - ROOM)
    wanted = jnp.where(copy == 0.0, within, jnp.where(copy == 1.0, low, low + 1.0))
    place = ((copy == 0.0) & (within < ROOM)) | ((copy > 0.0) & (copy < 3.0) & (within >= ROOM))
    codes = (lane.astype(jnp.float32) - 3.0 * blocks == tile) & (within == 7.0)
    select = jnp.where((place & (slot == wanted)) | codes, 1.0, 0.0).astype(jnp.bfloat16)
    rest = parts[...]
    total = jnp.zeros(out_ref.shape, jnp.float32)
    for _ in range(3):
        part = rest.astype(jnp.bfloat16)
        rest = rest - part.astype(jnp.float32)
        total = total + jnp.dot(select, part, preferred_element_type=jnp.float32)
    out_ref[...] = total


def table_kernel(profile_ref, dest_ref, rays_ref, pairs_ref, last_ref, dest_copy, rays_copy):
    dest_copy[...] = dest_ref[...]
    rays_copy[...] = rays_ref[...]
    a = lax.broadcasted_iota(jnp.int32, (DISC, DISC), 0) - HALO
    c = lax.broadcasted_iota(jnp.int32, (DISC, DISC), 1) - HALO
    weights = jnp.where(a * a + c * c <= HALO * HALO, profile_ref[...], 0.0)
    kernel = (weights / jnp.sum(weights)).astype(jnp.bfloat16)
    source = lax.broadcasted_iota(jnp.int32, (DISC, LANES), 0)
    target = lax.broadcasted_iota(jnp.int32, (DISC, LANES), 1)
    mirror = jnp.where((source + target) % LANES == 0, 1.0, 0.0).astype(jnp.bfloat16)
    mirrored = jnp.dot(kernel, mirror, preferred_element_type=jnp.float32)
    left = lax.broadcasted_iota(jnp.int32, (LANES, LANES), 1) < SPAN

    def band(row, start):
        wide = jnp.broadcast_to(mirrored[row : row + 1, :], (LANES, LANES))
        return pltpu.roll(wide, start, 1, stride=1, stride_axis=0)

    for u in range(TURNS):
        for s in range(0, STEP, 2):
            row = u * STEP + s
            both = jnp.where(left, band(row, 0), band(row + 1, SPAN))
            pairs_ref[u * LANES : (u + 1) * LANES, s * SPAN : (s + 2) * SPAN] = both.astype(jnp.bfloat16)
    last_ref[...] = jnp.where(left, band(2 * HALO, 0), 0.0).astype(jnp.bfloat16)


def hats(row, cell):
    near, far, here, there = (value.astype(jnp.bfloat16) for value in row)
    zero = jnp.zeros((), jnp.bfloat16)
    return jnp.where(cell == here, near, jnp.where(cell == there, far, zero))


def deposited(both, lists, stage, shifts, facts):
    sources = both.shape[0]
    rays = 3 * LANES
    first_lane = lax.axis_index("row") % 2 * 8
    room = sources * ROOM + 1
    lane = lax.broadcasted_iota(jnp.int32, (sources, LANES), 1)
    parity = lax.axis_index("row") % 2
    words = jnp.where(lane == KINDS + parity, both[:, 7, 2 * LANES :][:, :LANES], 0.0)
    words = jnp.sum(words, axis=1, keepdims=True).astype(jnp.int32)
    words = [words[at, 0] for at in range(sources)]

    def listed(counts, kinds, slots):
        counts = list(counts)
        for kind in kinds:
            for at in range(sources):
                for k in slots:
                    lists[counts[kind]] = at * 8 + k
                    bit = (words[at] >> (ROOM * kind + k)) & 1
                    counts[kind] = counts[kind] + bit
        return tuple(counts)

    counts = tuple(jnp.int32(kind * room) for kind in range(4))
    used = functools.reduce(jnp.bitwise_or, words)
    for slot in range(COMMON, ROOM):
        counts = lax.cond(
            used & sum(1 << (ROOM * kind + slot) for kind in range(4)) != 0,
            lambda held, slot=slot: listed(held, range(4), (slot,)),
            lambda held: held,
            counts,
        )

    def doubled(cell):
        return (2 * cell).astype(jnp.float32).astype(jnp.bfloat16)

    own = doubled(lax.broadcasted_iota(jnp.int32, (TILE, rays), 0))
    edge = lax.broadcasted_iota(jnp.int32, (2 * HALO, rays), 0)
    edge = doubled(jnp.where(edge < HALO, edge - HALO, edge + (TILE - HALO)))
    lane = lax.broadcasted_iota(jnp.int32, (1, LANES), 1) - first_lane

    def load(kind, step, batch, start):
        for k in range(batch):
            at = start + k
            entry = lists[jnp.minimum(kind * room + k + step * batch, counts[kind])]
            source, slot = entry >> 3, entry & 7
            head = both[source, pl.ds(slot, 1), :]
            tail = both[source, pl.ds(ROOM + (slot >> 1), 1), :]
            meta = both[source, 7:8, :][:, 2 * LANES : 3 * LANES]
            stage[0, at : at + 1, :] = head[:, :rays]
            stage[1, at : at + 1, :LANES] = head[:, rays:]
            stage[1, at : at + 1, LANES:] = jnp.where(
                (slot & 1) == 1, tail[:, 2 * LANES :], tail[:, : 2 * LANES]
            )
            shifts[at : at + 1, :] = jnp.where(lane == slot, meta, 0.0)

    def prepare(begin, end):
        code = jnp.sum(shifts[begin:end, :], axis=1, keepdims=True)
        rowwise = jnp.floor((code + 0.5) / 3.0)
        offsets = (rowwise - 1.0) * (2.0 * TILE), (code - 3.0 * rowwise - 1.0) * (2.0 * TILE)
        for axis in range(2):
            coords = stage[axis, begin:end, :]
            low = jnp.floor(coords)
            facts[4 * axis, begin:end, :] = 1.0 - (coords - low)
            facts[4 * axis + 1, begin:end, :] = 1.0 - ((low + 1.0) - coords)
            here = 2.0 * low + offsets[axis]
            facts[4 * axis + 2, begin:end, :] = here
            facts[4 * axis + 3, begin:end, :] = here + 2.0

    def product(kind, batch, start):
        down, across = (own, edge)[kind // 2], (own, edge)[kind % 2]
        firsts, seconds = [], []
        for at in range(start, start + batch):
            row = [facts[j, at : at + 1, :] for j in range(8)]
            firsts.append(hats(row[:4], down))
            seconds.append(hats(row[4:], across))
        return lax.dot_general(
            jnp.concatenate(firsts, axis=1),
            jnp.concatenate(seconds, axis=1),
            (((1,), (1,)), ((), ())),
            preferred_element_type=jnp.float32,
        )

    def ready(step, *given):
        for kind, batch, start in given:
            load(kind, step, batch, start)
        prepare(given[0][2], given[-1][2] + BATCH)

    def together(one, two):
        def step_one(step, sums, given=one):
            sums = sums + product(*given)
            ready(step + 1, given)
            return sums

        def step_both(step, sums):
            sums = sums[0] + product(*one), sums[1] + product(*two)
            ready(step + 1, one, two)
            return sums

        zeros = [
            jnp.zeros(((TILE, 2 * HALO)[kind // 2], (TILE, 2 * HALO)[kind % 2]), jnp.float32)
            for kind in (one[0], two[0])
        ]
        steps = [(counts[kind] - kind * room + batch - 1) // batch for kind, batch, _ in (one, two)]
        shared = jnp.minimum(steps[0], steps[1])
        sums = lax.fori_loop(0, shared, step_both, tuple(zeros))
        return [
            lax.fori_loop(shared, steps[j], functools.partial(step_one, given=(one, two)[j]), sums[j])
            for j in range(2)
        ]

    pairs = (
        ((0, BATCH, 0), (3, BATCH // 2, BATCH)),
        ((1, BATCH, 2 * BATCH), (2, BATCH, 3 * BATCH)),
    )
    for pair in pairs:
        kinds = [kind for kind, _, _ in pair]
        counts = listed(counts, kinds, range(COMMON))
        for kind in kinds:
            lists[counts[kind]] = ROOM
        ready(0, *pair)
    inside, corners = together(*pairs[0])
    beside, above = together(*pairs[1])

    def wide(middle, ends):
        return jnp.concatenate([ends[:, :HALO], middle, ends[:, HALO:]], axis=1)

    middle, ends = wide(inside, beside), wide(above, corners)
    return jnp.concatenate([ends[:HALO], middle, ends[HALO:]], axis=0)


def spread_kernel(scale, mine_ref, other_ref, before_ref, pairs_ref, last_ref, out_ref, total_ref,
                  left, both, *scratch):
    sources = mine_ref.shape[0]
    both[:sources] = mine_ref[...]
    both[sources:] = other_ref[...]
    cells = deposited(both, *scratch)
    if before_ref is not None:
        cells = cells + before_ref[...]
    total_ref[...] = cells
    blocks = [cells[:, at : at + LANES].astype(jnp.bfloat16) for at in (0, SPAN)]
    for h in range(2):
        for u in range(TURNS):
            left[h * LONG : (h + 1) * LONG, u * LANES : (u + 1) * LANES] = blocks[h][
                u * STEP : u * STEP + LONG, :
            ]
    lowest = jnp.concatenate([block[2 * HALO :, :] for block in blocks], axis=0)
    ends = jnp.dot(lowest, last_ref[...], preferred_element_type=jnp.float32)
    evens = [ends[:TILE], ends[TILE:]]
    odds = [jnp.zeros((TILE, LANES), jnp.float32)] * 2
    for p in range(0, STEP * SPAN, 2 * LANES):
        both = jnp.dot(left[...], pairs_ref[:, p : p + 2 * LANES], preferred_element_type=jnp.float32)
        for h in range(2):
            for lanes in (0, LANES):
                s = (p + lanes) // SPAN
                part = both[h * LONG : (h + 1) * LONG, lanes : lanes + LANES]
                evens[h] = evens[h] + part[s : s + TILE]
                odds[h] = odds[h] + part[s + 1 : s + 1 + TILE]
    low = evens[0] + pltpu.roll(odds[0], SPAN, 1)
    high = pltpu.roll(evens[1], SPAN, 1) + odds[1]
    lane = lax.broadcasted_iota(jnp.int32, (TILE, LANES), 1)
    out_ref[...] = jnp.where(lane < SPAN, low, high) / scale


def shards(positions, destination, profile):
    blocks, _, rays = positions.shape
    row_count, col_count = lax.axis_size("row"), lax.axis_size("col")
    tiles = row_count * col_count
    width = -(-(3 * blocks + tiles) // LANES) * LANES

    def exchange(turn, labels, coords):
        kernel, given = pack_kernel, (turn, labels, coords)
        if turn is None:
            kernel, given = functools.partial(pack_kernel, None), (labels, coords)
        outgoing = pl.pallas_call(
            kernel,
            out_shape=jax.ShapeDtypeStruct((8 * tiles, rays + LANES), jnp.float32),
            in_specs=[SMEM, VMEM, VMEM][-len(given) :],
            out_specs=VMEM,
            scratch_shapes=[
                pltpu.VMEM((1, width), jnp.float32),
                pltpu.VMEM((width, rays + LANES), jnp.float32),
            ],
            compiler_params=ALONE if turn is None else LIMIT,
            name="pack",
        )(*given)
        return lax.all_to_all(
            outgoing.reshape(tiles, 8, rays + LANES), ("row", "col"), split_axis=0, concat_axis=0, tiled=True
        )

    def deposit(mine, before, pairs, last):
        other = lax.ppermute(mine, "row", [(i, i ^ 1) for i in range(row_count)])
        scale = blocks * rays / (TILE * TILE)
        kernel, given = functools.partial(spread_kernel, scale), (mine, other, before, pairs, last)
        if before is None:
            kernel = lambda mine, other, *refs: spread_kernel(scale, mine, other, None, *refs)
            given = (mine, other, pairs, last)
        return pl.pallas_call(
            kernel,
            out_shape=(
                jax.ShapeDtypeStruct((TILE, TILE), jnp.float32),
                jax.ShapeDtypeStruct((WIDE, WIDE), jnp.float32),
            ),
            in_specs=[VMEM] * len(given),
            out_specs=(VMEM, VMEM),
            scratch_shapes=[
                pltpu.VMEM((2 * LONG, TURNS * LANES), jnp.bfloat16),
                pltpu.VMEM((2 * tiles, 8, rays + LANES), jnp.float32),
                pltpu.SMEM((4 * (2 * tiles * ROOM + 1),), jnp.int32),
                pltpu.VMEM((2, 4 * BATCH, rays), jnp.float32),
                pltpu.VMEM((4 * BATCH, LANES), jnp.float32),
                pltpu.VMEM((8, 4 * BATCH, rays), jnp.float32),
            ],
            compiler_params=LIMIT,
            name="spread",
        )(*given)

    mine = exchange(None, destination.T, positions)
    pairs, last, labels, coords = pl.pallas_call(
        table_kernel,
        out_shape=(
            jax.ShapeDtypeStruct((TURNS * LANES, STEP * SPAN), jnp.bfloat16),
            jax.ShapeDtypeStruct((LANES, LANES), jnp.bfloat16),
            jax.ShapeDtypeStruct((1, blocks), jnp.int32),
            jax.ShapeDtypeStruct(positions.shape, jnp.float32),
        ),
        in_specs=[VMEM] * 3,
        out_specs=(VMEM,) * 4,
        compiler_params=LIMIT,
        cost_estimate=pl.CostEstimate(flops=10_000_000, bytes_accessed=6_000_000, transcendentals=0),
        name="table",
    )(profile, destination.T, positions)
    mine, pairs, last, labels, coords = lax.optimization_barrier((mine, pairs, last, labels, coords))
    turns = jnp.max(mine[:, 7, 2 * LANES + COUNT]).astype(jnp.int32)
    out, total = deposit(mine, None, pairs, last)

    def more(state):
        turn, _, total = state
        out, total = deposit(
            exchange(jnp.full((1,), turn, jnp.int32), labels, coords), total, pairs, last
        )
        return turn + 1, out, total

    return lax.while_loop(lambda state: state[0] < turns, more, (jnp.int32(1), out, total))[1]


def solution(mesh):
    placed = (P(("maps", "row", "col"), None, None), P(("maps", "row", "col"), None), P())
    return jax.shard_map(
        shards, mesh=mesh, in_specs=placed, out_specs=P(("maps", "row"), "col"), check_vma=False
    )
```
